32 devices in a mesh: grp: 2 (over core), blk: 16 (over z, y, x).
Axes of the slice: x: 2, y: 2, z: 4, core: 2. Of those that a mesh axis runs over, the one named last changes fastest.
Arguments:
- hidden_in: bfloat16 [4352, 1024], P(('grp', 'blk')), may hold values from -6 to 6
- segment_ids: int32 [4352], P(('grp', 'blk')), may hold values from 0 to 3, as said below
- order_ids: int32 [4352], P(('grp', 'blk')), may hold values from 0 to 127
- box_ids: int32 [2, 4352], P(None, ('grp', 'blk')), may hold values from 0 to 63
- qkv_weight: bfloat16 [3, 1024, 1024], P(None, ('grp', 'blk')), may hold values from -0.25 to 0.25
- qkv_bias: bfloat16 [2, 1024], P(None, ('grp', 'blk')), may hold values from -0.59765625 to 0.59765625
- rel_tables: bfloat16 [3, 128, 1024], P(None, None, ('grp', 'blk')), may hold values from -8 to 8
- out_weight: bfloat16 [1024, 1024], P(('grp', 'blk')), may hold values from -0.75 to 0.75
- branch_bias: bfloat16 [2, 1024], P(None, ('grp', 'blk')), may hold values from -1.796875 to 1.796875
- norm_gains: bfloat16 [2, 1024], P(None, ('grp', 'blk')), may hold values from 0.25 to 1.75
- norm_shifts: bfloat16 [2, 1024], P(None, ('grp', 'blk')), may hold values from -1.796875 to 1.796875
- ffn_in: bfloat16 [1024, 4096], P(('grp', 'blk')), may hold values from -0.1875 to 0.1875
- ffn_in_bias: bfloat16 [4096], P(('grp', 'blk')), may hold values from -1.796875 to 1.796875
- ffn_out: bfloat16 [4096, 1024], P(('grp', 'blk')), may hold values from -0.125 to 0.125
- out_grad: bfloat16 [4352, 1024], P(('grp', 'blk')), may hold values from -6 to 6
Outputs:
- hidden_out: bfloat16 [4352, 1024], P(('grp', 'blk'))
- hidden_grad: bfloat16 [4352, 1024], P(('grp', 'blk'))
- qkv_weight_grad: float32 [3, 1024, 1024], P(None, ('grp', 'blk'))
- qkv_bias_grad: float32 [2, 1024], P(None, ('grp', 'blk'))
- rel_tables_grad: float32 [3, 128, 1024], P(None, None, ('grp', 'blk'))
- out_weight_grad: float32 [1024, 1024], P(('grp', 'blk'))
- branch_bias_grad: float32 [2, 1024], P(None, ('grp', 'blk'))
- norm_gains_grad: float32 [2, 1024], P(None, ('grp', 'blk'))
- norm_shifts_grad: float32 [2, 1024], P(None, ('grp', 'blk'))
- ffn_in_grad: float32 [1024, 4096], P(('grp', 'blk'))
- ffn_in_bias_grad: float32 [4096], P(('grp', 'blk'))
- ffn_out_grad: float32 [4096, 1024], P(('grp', 'blk'))
The draws below stay inside these ranges and needn't reach their ends.
Inputs may be any that keep to these rules, and one draw needn't show every extreme that they name: `segment_ids`: one label for each page of 544 consecutive tokens; pages of a batch group with equal labels form one document; in every batch group the first and the last page carry the same label, and some page carries another.
All inputs are finite; a program needn't handle non-finite values.
Results may differ from the reference program's by a relative error of at most 0.02.
Values may be sent and summed in bfloat16 or wider, within the bound.
A program may use at most 256 MiB of HBM per device.

```python
import math
import jax
import jax.numpy as jnp
from jax import lax

D = 1024
H = 16
HD = 64
FF = 4096
NB = 128
ORDER_RANGE = 128
BOX_RANGE = 64
PAGE = 544
DOCS = 4
TOK_DEV = 136
TOKENS = 4352
N_GRP = 2
N_BLK = 16


def draw_segment_ids(key, part):
    key = jax.random.fold_in(key, 11)
    page_count = TOK_DEV * N_BLK // PAGE
    spanning = jax.random.randint(jax.random.fold_in(key, 1), (N_GRP, 1), 0, DOCS)
    labels = jax.random.randint(jax.random.fold_in(key, 2), (N_GRP, page_count), 0, DOCS)
    offset = jax.random.randint(jax.random.fold_in(key, 3), (N_GRP, 1), 1, DOCS)
    other = (spanning + offset) % DOCS
    labels = labels.at[:, 0:1].set(spanning).at[:, page_count - 1:page_count].set(spanning).at[:, 1:2].set(other)
    return jnp.repeat(labels, PAGE, axis=1).reshape(N_GRP * page_count * PAGE).astype(jnp.int32)


def touch_ends(drawn, key, smallest, high):
    shape = drawn.shape
    index_at = [jax.random.randint(jax.random.fold_in(key, axis), (), 0, shape[axis]) for axis in range(len(shape))]
    drawn = drawn.at[tuple(index_at)].set(smallest)
    longest = shape.index(max(shape))
    index_at[longest] = (index_at[longest] + 1) % shape[longest]
    return drawn.at[tuple(index_at)].set(high)


def block_scale(stream_key, shape, shards, smallest, top_value):
    def one(axis_at, parts):
        draws = jax.random.uniform(jax.random.fold_in(jax.random.fold_in(stream_key, 6), axis_at), (parts,), jnp.float32, smallest / len(shards), top_value / len(shards))
        return jnp.repeat(jnp.exp(draws), shape[axis_at] // parts).reshape((-1,) + (1,) * (len(shape) - axis_at - 1))

    loudness = one(*shards[0])
    for cut in shards[1:]:
        loudness = loudness * one(*cut)
    return loudness


def normal_values(own_key, shape, deviation, limit, shards=(), held_as=jnp.bfloat16):
    array = jax.random.normal(own_key, shape, jnp.float32) * deviation
    if len(shards) > 0:
        array = block_scale(own_key, shape, shards, -0.22, 0.18) * array
    return jnp.clip(array, min=-limit, max=limit).astype(held_as)


def setup_inputs(seed: int = 0) -> dict:
    key_of = jax.random.split(jax.random.key(seed), 16)
    hidden_in = normal_values(key_of[0], (TOKENS, D), 1.0, 6.0, ((0, 32),))
    segment_ids = draw_segment_ids(jax.random.fold_in(key_of[15], 71), 0)
    order_ids = touch_ends(jax.random.randint(key_of[2], (TOKENS,), 0, ORDER_RANGE), jax.random.fold_in(key_of[2], 1), 0, ORDER_RANGE - 1).astype(jnp.int32)
    box_ids = touch_ends(jax.random.randint(key_of[3], (2, TOKENS), 0, BOX_RANGE), jax.random.fold_in(key_of[3], 1), 0, BOX_RANGE - 1).astype(jnp.int32)
    qkv_weight = normal_values(key_of[4], (3, D, D), (D // 2) ** -0.5, 0.25, ((1, 32),))
    qkv_bias = normal_values(key_of[5], (2, D), 0.1, 0.59765625, ((1, 32),))
    rel_tables = normal_values(key_of[6], (3, NB, D), 1.4, 8.0, ((2, 32),))
    out_weight = normal_values(key_of[7], (D, D), (D // 16) ** -0.5, 0.75, ((0, 32),))
    branch_bias = normal_values(key_of[8], (2, D), 0.3, 1.796875, ((1, 32),))
    norm_gains = jnp.clip(1.0 + 0.15 * jax.random.normal(key_of[9], (2, D), jnp.float32), 0.25, 1.75).astype(jnp.bfloat16)
    norm_shifts = normal_values(key_of[10], (2, D), 0.3, 1.796875, ((1, 32),))
    ffn_in = normal_values(key_of[11], (D, FF), D ** -0.5, 0.1875, ((0, 32),))
    ffn_in_bias = normal_values(key_of[12], (FF,), 0.3, 1.796875, ((0, 32),))
    ffn_out = normal_values(key_of[13], (FF, D), (FF // 2) ** -0.5, 0.125, ((0, 32),))
    out_grad = normal_values(key_of[14], (TOKENS, D), 1.0, 6.0, ((0, 32),))
    return dict(hidden_in=hidden_in, segment_ids=segment_ids, order_ids=order_ids, box_ids=box_ids, qkv_weight=qkv_weight, qkv_bias=qkv_bias, rel_tables=rel_tables, out_weight=out_weight, branch_bias=branch_bias, norm_gains=norm_gains, norm_shifts=norm_shifts, ffn_in=ffn_in, ffn_in_bias=ffn_in_bias, ffn_out=ffn_out, out_grad=out_grad)


@jax.custom_vjp
def low(v):
    return lax.optimization_barrier(v.astype(jnp.bfloat16)).astype(jnp.float32)

@jax.custom_vjp
def low_back(v):
    return v

def low_keep(v):
    return (low(v), None)

def low_pass(kept, grad):
    return (grad,)

def back_keep(v):
    return (v, None)

def back_low(kept, grad):
    return (low(grad),)
low.defvjp(low_keep, low_pass)
low_back.defvjp(back_keep, back_low)

def matmul_high(left, right):
    return jnp.dot(left, right, precision=lax.Precision.HIGHEST)

def layer_norm(values_in, norm_gain, norm_shift):
    center = values_in - lax.optimization_barrier(jnp.mean(values_in, axis=-1, keepdims=True))
    spread = lax.optimization_barrier(jnp.mean(center * center, axis=-1, keepdims=True))
    return center * lax.rsqrt(spread + 1e-05) * norm_gain + norm_shift

def kind_ranges():
    return (ORDER_RANGE, BOX_RANGE, BOX_RANGE)

def key_onehot_high(layout_group):
    pieces_out = []
    for column, extent in enumerate(kind_ranges()):
        match_rows = layout_group[:, column][:, None] == jnp.arange(extent, dtype=jnp.int32)[None, :]
        pieces_out.append(match_rows.astype(jnp.float32))
    return jnp.concatenate(pieces_out, axis=1)

def attend_block(query_block, layout_block, seg_block, key_group, value_group, onehot_group, seg_group, w_rel):
    row_count = query_block.shape[0]
    query_heads = query_block.reshape(row_count, H, HD)
    tables = jnp.einsum('thd,nbhd->nthb', query_heads, w_rel.reshape(3, NB, H, HD), precision=lax.Precision.HIGHEST)
    tables = low(low_back(tables))
    pieces_out = []
    for column, extent in enumerate(kind_ranges()):
        offsets = layout_block[:, column][:, None] - jnp.arange(extent, dtype=jnp.int32)[None, :]
        bucket = jnp.clip(offsets, -(NB // 2), NB // 2 - 1) + NB // 2
        bucket = jnp.broadcast_to(bucket[:, None, :], (row_count, H, extent)).astype(jnp.int32)
        pieces_out.append(jnp.take_along_axis(tables[column], bucket, axis=2))
    selector = jnp.concatenate(pieces_out, axis=2)
    key_heads = key_group.reshape(key_group.shape[0], H, HD)
    content = jnp.einsum('thd,khd->htk', query_heads, key_heads, precision=lax.Precision.HIGHEST)
    rel_bias = jnp.einsum('thv,kv->htk', selector, onehot_group, precision=lax.Precision.HIGHEST)
    logits = low_back((content + rel_bias) * (1.0 / math.sqrt(4.0 * HD)))
    allowed = seg_block[:, None] == seg_group[None, :]
    logits = jnp.where(allowed[None], logits, -1e+30)
    row_top = lax.optimization_barrier(jnp.max(logits, axis=2, keepdims=True))
    exponent = jnp.exp(logits - row_top)
    probs = exponent / lax.optimization_barrier(jnp.sum(exponent, axis=2, keepdims=True))
    value_heads = value_group.reshape(value_group.shape[0], H, HD)
    context = jnp.einsum('htk,khd->thd', low(probs), value_heads, precision=lax.Precision.HIGHEST)
    return context.reshape(row_count, H * HD)

def attend_all(query_rows, key_rows, value_rows, w_rel, layout, seg_all):
    group_rows = TOK_DEV * N_BLK
    blocks = group_rows // PAGE
    width = query_rows.shape[1]

    def one_group(members):
        query_group, key_group, value_group, layout_group, seg_group = members
        onehot_group = key_onehot_high(layout_group)

        def one_block(block_members):
            query_block, layout_block, seg_block = block_members
            return attend_block(query_block, layout_block, seg_block, key_group, value_group, onehot_group, seg_group, w_rel)
        result = lax.map(jax.checkpoint(one_block), (query_group.reshape(blocks, PAGE, width), layout_group.reshape(blocks, PAGE, 3), seg_group.reshape(blocks, PAGE)))
        return result.reshape(group_rows, width)
    grouped = (query_rows.reshape(N_GRP, group_rows, width), key_rows.reshape(N_GRP, group_rows, width), value_rows.reshape(N_GRP, group_rows, width), layout.reshape(N_GRP, group_rows, 3), seg_all.reshape(N_GRP, group_rows))
    return lax.map(one_group, grouped).reshape(N_GRP * group_rows, width)

def reference(hidden_in, segment_ids, order_ids, box_ids, qkv_weight, qkv_bias, rel_tables, out_weight, branch_bias, norm_gains, norm_shifts, ffn_in, ffn_in_bias, ffn_out, out_grad):
    layout = jnp.stack([order_ids, box_ids[0], box_ids[1]], axis=1).astype(jnp.int32)
    seg_all = segment_ids.astype(jnp.int32)

    def forward(inputs, w_qkv, b_qkv, w_rel, w_out, b_branch, gains, shifts, w_in, b_in, w_down):
        projected = jnp.einsum('td,cde->cte', inputs, w_qkv, precision=lax.Precision.HIGHEST)
        query_rows = low(low_back(projected[0] + b_qkv[0]))
        key_rows = low(low_back(projected[1]))
        value_rows = low(low_back(projected[2] + b_qkv[1]))
        context = attend_all(query_rows, key_rows, value_rows, w_rel, layout, seg_all)
        context = low(low_back(context))
        branch = low_back(matmul_high(context, w_out) + b_branch[0])
        first = layer_norm(inputs + branch, gains[0], shifts[0])
        inner = low_back(matmul_high(low(first), w_in) + b_in)
        second = low_back(matmul_high(low(jax.nn.gelu(inner, approximate=False)), w_down) + b_branch[1])
        return layer_norm(first + second, gains[1], shifts[1])
    floats = tuple((member.astype(jnp.float32) for member in (hidden_in, qkv_weight, qkv_bias, rel_tables, out_weight, branch_bias, norm_gains, norm_shifts, ffn_in, ffn_in_bias, ffn_out)))
    outputs, pullback = jax.vjp(forward, *floats)
    grads = pullback(out_grad.astype(jnp.float32))
    return (outputs.astype(jnp.bfloat16), grads[0].astype(jnp.bfloat16), grads[1], grads[2], grads[3], grads[4], grads[5], grads[6], grads[7], grads[8], grads[9], grads[10])
```

```python
import functools
import math

import jax
import jax.numpy as jnp
from jax import lax
from jax.experimental import pallas as pl
from jax.experimental.pallas import tpu as pltpu
from jax.sharding import PartitionSpec as P

H = 16
HD = 64
NB = 128
ORDER_RANGE = 128
BOX_RANGE = 64


NEGATIVE = -1e30
EPSILON = 1e-05


def shifted(x, axis, by):
    devices = lax.axis_size(axis)
    return lax.ppermute(x, axis, [(i, (i + by) % devices) for i in range(devices)])


def block_size(row_count):
    chosen = 1
    for option in range(1, min(row_count, 544) + 1):
        if row_count % option == 0:
            chosen = option
    return chosen


def kind_ranges():
    return (ORDER_RANGE, BOX_RANGE, BOX_RANGE)


def query_maps(layout_ids):
    maps_out = []
    for column, extent in enumerate(kind_ranges()):
        offsets = layout_ids[:, column][:, None] - jnp.arange(extent, dtype=jnp.int32)[None, :]
        bucket = jnp.clip(offsets, -(NB // 2), NB // 2 - 1) + NB // 2
        maps_out.append(bucket[:, :, None] == jnp.arange(NB, dtype=jnp.int32)[None, None, :])
    return maps_out


def key_onehot(key_ids):
    pieces_out = []
    for column, extent in enumerate(kind_ranges()):
        pieces_out.append(
            key_ids[:, column + 1][:, None] == jnp.arange(extent, dtype=jnp.int32)[None, :]
        )
    return jnp.concatenate(pieces_out, axis=1).astype(jnp.bfloat16)


def norm_forward(values_in, norm_gain, norm_shift):
    center = values_in - jnp.mean(values_in, axis=-1, keepdims=True)
    inverse = lax.rsqrt(jnp.mean(center * center, axis=-1, keepdims=True) + EPSILON)
    normed = center * inverse
    return (normed * norm_gain + norm_shift, normed, inverse)


def norm_backward(upstream, normed, inverse, norm_gain):
    scaled = upstream * norm_gain
    inner_part = (
        scaled
        - jnp.mean(scaled, axis=-1, keepdims=True)
        - normed * jnp.mean(scaled * normed, axis=-1, keepdims=True)
    )
    return (inner_part * inverse, jnp.sum(upstream * normed, axis=0), jnp.sum(upstream, axis=0))


def block_logits(query_heads, selector, query_seg, key_part, meta_part, scaling):
    key_ids = meta_part.astype(jnp.int32)
    row_count = key_part.shape[0]
    key_heads = key_part.reshape(row_count, H, HD)
    content = jnp.einsum("thd,khd->htk", query_heads, key_heads, preferred_element_type=jnp.float32)
    onehot = key_onehot(key_ids)
    rel_bias = jnp.einsum("thv,kv->htk", selector, onehot, preferred_element_type=jnp.float32)
    allowed = query_seg[:, None] == key_ids[None, :, 0]
    logits = jnp.where(allowed[None], (content + rel_bias) * scaling, NEGATIVE)
    return (logits, allowed, onehot, key_heads)


def over_blocks(advance, carry, piece, start):
    row_count = piece[0].shape[0]
    stride = block_size(row_count)

    def one_step(block_index, running):
        portion = tuple(
            (lax.dynamic_slice_in_dim(member, block_index * stride, stride, 0) for member in piece)
        )
        return advance(running, portion, start + block_index * stride)

    return lax.fori_loop(0, row_count // stride, one_step, carry)


def shards(
    hidden_in,
    segment_ids,
    order_ids,
    box_ids,
    qkv_weight,
    qkv_bias,
    rel_tables,
    out_weight,
    branch_bias,
    norm_gains,
    norm_shifts,
    ffn_in,
    ffn_in_bias,
    ffn_out,
    out_grad,
):
    gathered = (
        lax.all_gather(qkv_weight, ("grp", "blk"), axis=1, tiled=True),
        lax.all_gather(qkv_bias, ("grp", "blk"), axis=1, tiled=True),
        lax.all_gather(rel_tables, ("grp", "blk"), axis=2, tiled=True),
        lax.all_gather(out_weight, ("grp", "blk"), axis=0, tiled=True),
        lax.all_gather(branch_bias, ("grp", "blk"), axis=1, tiled=True),
        lax.all_gather(norm_gains, ("grp", "blk"), axis=1, tiled=True),
        lax.all_gather(norm_shifts, ("grp", "blk"), axis=1, tiled=True),
        lax.all_gather(ffn_in, ("grp", "blk"), axis=0, tiled=True),
        lax.all_gather(ffn_in_bias, ("grp", "blk"), axis=0, tiled=True),
        lax.all_gather(ffn_out, ("grp", "blk"), axis=0, tiled=True),
    )
    w_qkv, b_qkv, w_rel, w_out, b_branch, gains, shifts, w_in, b_in, w_down = gathered
    row_count = hidden_in.shape[0]
    width = hidden_in.shape[1]
    scaling = 1.0 / math.sqrt(4.0 * HD)
    select_width = ORDER_RANGE + 2 * BOX_RANGE
    projected = jnp.einsum("td,cde->cte", hidden_in, w_qkv, preferred_element_type=jnp.float32)
    bias_qkv = b_qkv.astype(jnp.float32)
    query_rows = (projected[0] + bias_qkv[0]).astype(jnp.bfloat16)
    key_rows = projected[1].astype(jnp.bfloat16)
    value_rows = (projected[2] + bias_qkv[1]).astype(jnp.bfloat16)
    layout_ids = jnp.stack([order_ids, box_ids[0], box_ids[1]], axis=1)
    key_meta = jnp.stack([segment_ids, order_ids, box_ids[0], box_ids[1]], axis=1).astype(
        jnp.bfloat16
    )
    query_heads = query_rows.reshape(row_count, H, HD)
    rel_heads = w_rel.reshape(3, NB, H, HD)
    tables = jnp.einsum(
        "thd,nbhd->thnb", query_heads, rel_heads, preferred_element_type=jnp.float32
    ).astype(jnp.bfloat16)
    maps_list = query_maps(layout_ids)
    selector = jnp.concatenate(
        [
            jnp.einsum(
                "thb,tvb->thv",
                tables[:, :, column],
                maps_list[column].astype(jnp.bfloat16),
                preferred_element_type=jnp.float32,
            )
            for column in range(3)
        ],
        axis=2,
    ).astype(jnp.bfloat16)

    def forward_step(running, portion, offset):
        row_top, row_total, weighted = running
        key_part, value_part, meta_part = portion
        logits, allowed, onehot, key_heads = block_logits(
            query_heads, selector, segment_ids, key_part, meta_part, scaling
        )
        new_top = jnp.maximum(row_top, jnp.max(logits, axis=2))
        rescale = jnp.exp(row_top - new_top)
        weights = jnp.where(allowed[None], jnp.exp(logits - new_top[:, :, None]), 0.0)
        value_heads = value_part.reshape(value_part.shape[0], H, HD)
        weighted = weighted * rescale.T[:, :, None] + jnp.einsum(
            "htk,khd->thd",
            weights.astype(jnp.bfloat16),
            value_heads,
            preferred_element_type=jnp.float32,
        )
        return (new_top, row_total * rescale + jnp.sum(weights, axis=2), weighted)

    start_state = (
        jnp.full((H, row_count), NEGATIVE, jnp.float32),
        jnp.zeros((H, row_count), jnp.float32),
        jnp.zeros((row_count, H, HD), jnp.float32),
    )
    row_top, row_total, weighted = over_blocks(
        forward_step,
        start_state,
        (
            lax.all_gather(key_rows, "blk", axis=0, tiled=True),
            lax.all_gather(value_rows, "blk", axis=0, tiled=True),
            lax.all_gather(key_meta, "blk", axis=0, tiled=True),
        ),
        jnp.int32(0),
    )
    context_full = weighted / row_total.T[:, :, None]
    log_total = row_top + jnp.log(row_total)
    context = context_full.reshape(row_count, width).astype(jnp.bfloat16)
    branch = jnp.dot(context, w_out, preferred_element_type=jnp.float32) + b_branch[0].astype(
        jnp.float32
    )
    first, normed_one, inverse_one = norm_forward(
        hidden_in.astype(jnp.float32) + branch,
        gains[0].astype(jnp.float32),
        shifts[0].astype(jnp.float32),
    )
    first_low = first.astype(jnp.bfloat16)
    inner_pre = jnp.dot(first_low, w_in, preferred_element_type=jnp.float32) + b_in.astype(
        jnp.float32
    )
    activated, gelu_pull = jax.vjp(
        lambda pre_act: jax.nn.gelu(pre_act, approximate=False), inner_pre
    )
    activated_low = activated.astype(jnp.bfloat16)
    second = jnp.dot(activated_low, w_down, preferred_element_type=jnp.float32) + b_branch[
        1
    ].astype(jnp.float32)
    result, normed_two, inverse_two = norm_forward(
        first + second, gains[1].astype(jnp.float32), shifts[1].astype(jnp.float32)
    )
    hidden_out = result.astype(jnp.bfloat16)
    grad_sum2, gain_grad2, shift_grad2 = norm_backward(
        out_grad.astype(jnp.float32), normed_two, inverse_two, gains[1].astype(jnp.float32)
    )
    grad_second = grad_sum2.astype(jnp.bfloat16)
    grad_w_down = jnp.einsum(
        "tf,td->fd", activated_low, grad_second, preferred_element_type=jnp.float32
    )
    grad_bias_two = jnp.sum(grad_second.astype(jnp.float32), axis=0)
    grad_act = jnp.einsum("td,fd->tf", grad_second, w_down, preferred_element_type=jnp.float32)
    grad_inner = gelu_pull(grad_act)[0].astype(jnp.bfloat16)
    grad_b_in = jnp.sum(grad_inner.astype(jnp.float32), axis=0)
    grad_w_in = jnp.einsum("td,tf->df", first_low, grad_inner, preferred_element_type=jnp.float32)
    grad_first = grad_sum2 + jnp.einsum(
        "tf,df->td", grad_inner, w_in, preferred_element_type=jnp.float32
    )
    grad_sum1, gain_grad1, shift_grad1 = norm_backward(
        grad_first, normed_one, inverse_one, gains[0].astype(jnp.float32)
    )
    grad_branch = grad_sum1.astype(jnp.bfloat16)
    grad_w_out = jnp.einsum("td,te->de", context, grad_branch, preferred_element_type=jnp.float32)
    grad_bias_one = jnp.sum(grad_branch.astype(jnp.float32), axis=0)
    grad_context = jnp.einsum(
        "te,de->td", grad_branch, w_out, preferred_element_type=jnp.float32
    ).astype(jnp.bfloat16)
    grad_heads = grad_context.reshape(row_count, H, HD)
    delta = jnp.einsum("thd,thd->ht", grad_heads.astype(jnp.float32), context_full)

    def backward_core(grad_query, grad_select, portion):
        key_part, value_part, meta_part = portion
        logits, allowed, onehot, key_heads = block_logits(
            query_heads, selector, segment_ids, key_part, meta_part, scaling
        )
        probs = jnp.where(allowed[None], jnp.exp(logits - log_total[:, :, None]), 0.0)
        part_rows = key_part.shape[0]
        value_heads = value_part.reshape(part_rows, H, HD)
        grad_probs = jnp.einsum(
            "thd,khd->htk", grad_heads, value_heads, preferred_element_type=jnp.float32
        )
        grad_logits = (probs * (grad_probs - delta[:, :, None])).astype(jnp.bfloat16)
        grad_query = grad_query + scaling * jnp.einsum(
            "htk,khd->thd", grad_logits, key_heads, preferred_element_type=jnp.float32
        )
        grad_select = grad_select + scaling * jnp.einsum(
            "htk,kv->thv", grad_logits, onehot, preferred_element_type=jnp.float32
        )
        grad_key = scaling * jnp.einsum(
            "htk,thd->khd", grad_logits, query_heads, preferred_element_type=jnp.float32
        )
        grad_value = jnp.einsum(
            "htk,thd->khd",
            probs.astype(jnp.bfloat16),
            grad_heads,
            preferred_element_type=jnp.float32,
        )
        update = jnp.concatenate(
            [grad_key.reshape(part_rows, width), grad_value.reshape(part_rows, width)], axis=1
        )
        return (grad_query, grad_select, update)

    query_zero = jnp.zeros((row_count, H, HD), jnp.float32)
    select_zero = jnp.zeros((row_count, H, select_width), jnp.float32)

    def cycle_turn(turn, carry):
        grad_query, grad_select, key_part, value_part, meta_part, carried = carry
        portion = (key_part, value_part, meta_part)
        grad_query, grad_select, update = backward_core(grad_query, grad_select, portion)
        carried = carried + update
        key_part, value_part, meta_part = shifted((key_part, value_part, meta_part), "blk", 1)
        carried = shifted(carried.astype(jnp.bfloat16), "blk", 1).astype(carried.dtype)
        return (grad_query, grad_select, key_part, value_part, meta_part, carried)

    cycle_start = (
        query_zero,
        select_zero,
        key_rows,
        value_rows,
        key_meta,
        jnp.zeros((row_count, 2 * width), jnp.float32),
    )
    cycle_end = lax.fori_loop(0, lax.axis_size("blk"), cycle_turn, cycle_start)
    grad_query, grad_select, own_pairs = (cycle_end[0], cycle_end[1], cycle_end[5])
    grad_key_rows = own_pairs[:, :width].astype(jnp.bfloat16)
    grad_value_rows = own_pairs[:, width:].astype(jnp.bfloat16)
    cursor = 0
    table_parts = []
    for column, extent in enumerate(kind_ranges()):
        table_parts.append(
            jnp.einsum(
                "thv,tvb->thb",
                grad_select[:, :, cursor : cursor + extent],
                maps_list[column].astype(jnp.float32),
                precision=lax.Precision.HIGHEST,
            )
        )
        cursor = cursor + extent
    grad_tables = jnp.stack(table_parts, axis=2).astype(jnp.bfloat16)
    grad_query_total = grad_query + jnp.einsum(
        "thnb,nbhd->thd", grad_tables, rel_heads, preferred_element_type=jnp.float32
    )
    grad_query_rows = grad_query_total.reshape(row_count, width).astype(jnp.bfloat16)
    grad_rel = jnp.einsum(
        "thnb,thd->nbhd", grad_tables, query_heads, preferred_element_type=jnp.float32
    ).reshape(3, NB, width)
    grad_stack = jnp.stack([grad_query_rows, grad_key_rows, grad_value_rows])
    grad_w_qkv = jnp.einsum(
        "td,cte->cde", hidden_in, grad_stack, preferred_element_type=jnp.float32
    )
    grad_b_qkv = jnp.stack(
        [
            jnp.sum(grad_query_rows.astype(jnp.float32), axis=0),
            jnp.sum(grad_value_rows.astype(jnp.float32), axis=0),
        ]
    )
    grad_input = grad_sum1 + jnp.einsum(
        "cte,cde->td", grad_stack, w_qkv, preferred_element_type=jnp.float32
    )
    summed = (
        lax.psum_scatter(grad_w_qkv, ("grp", "blk"), scatter_dimension=1, tiled=True),
        lax.psum_scatter(grad_b_qkv, ("grp", "blk"), scatter_dimension=1, tiled=True),
        lax.psum_scatter(grad_rel, ("grp", "blk"), scatter_dimension=2, tiled=True),
        lax.psum_scatter(grad_w_out, ("grp", "blk"), scatter_dimension=0, tiled=True),
        lax.psum_scatter(
            jnp.stack([grad_bias_one, grad_bias_two]),
            ("grp", "blk"),
            scatter_dimension=1,
            tiled=True,
        ),
        lax.psum_scatter(
            jnp.stack([gain_grad1, gain_grad2]), ("grp", "blk"), scatter_dimension=1, tiled=True
        ),
        lax.psum_scatter(
            jnp.stack([shift_grad1, shift_grad2]), ("grp", "blk"), scatter_dimension=1, tiled=True
        ),
        lax.psum_scatter(grad_w_in, ("grp", "blk"), scatter_dimension=0, tiled=True),
        lax.psum_scatter(grad_b_in, ("grp", "blk"), scatter_dimension=0, tiled=True),
        lax.psum_scatter(grad_w_down, ("grp", "blk"), scatter_dimension=0, tiled=True),
    )
    return (
        hidden_out,
        grad_input.astype(jnp.bfloat16),
        summed[0],
        summed[1],
        summed[2],
        summed[3],
        summed[4],
        summed[5],
        summed[6],
        summed[7],
        summed[8],
        summed[9],
    )


MESH = pl.DeviceIdType.MESH
LOW = jnp.bfloat16
HIGH = jnp.float32
CHIPS = 16
HALF = 8
BLOCK = 256
MASKED = -1e30
VMEM_LIMIT = 60 * 2**20


def dot(left, right, dims=((1,), (0,))):
    return lax.dot_general(left, right, (dims, ((), ())), preferred_element_type=HIGH)


NT = ((1,), (1,))
TN = ((0,), (0,))


def place():
    core = lax.axis_index("grp")
    chip = lax.axis_index("blk")
    return core, chip


def coordinates(chip):
    return lax.div(chip, 4), lax.rem(lax.div(chip, 2), 2), lax.rem(chip, 2)


def chip_at(z, y, x):
    return z * 4 + y * 2 + x


def meet():
    core, chip = place()
    me = core * CHIPS + chip
    barrier = pltpu.get_barrier_semaphore()

    def greet(ahead, carry):
        other = lax.rem(me + ahead, 2 * CHIPS)
        pl.semaphore_signal(
            barrier,
            inc=1,
            device_id=(lax.div(other, CHIPS), lax.rem(other, CHIPS)),
            device_id_type=MESH,
        )
        return carry

    lax.fori_loop(1, 2 * CHIPS, greet, 0)
    pl.semaphore_wait(barrier, 2 * CHIPS - 1)


def remote(source, target, send, recv, device):
    return pltpu.make_async_remote_copy(
        src_ref=source,
        dst_ref=target,
        send_sem=send,
        recv_sem=recv,
        device_id=device,
        device_id_type=MESH,
    )


def gather_steps(pick, send, recv, across):
    core, chip = place()
    z, y, x = coordinates(chip)
    started = []

    def flip(far_p, far_q, ahead):
        p_y, p_x = (0, far_p) if across == "x" else (far_p, 0)
        q_y, q_x = (far_q, 0) if across == "x" else (0, far_q)
        y_to = 1 - y if p_y + q_y else y
        x_to = 1 - x if p_x + q_x else x
        return chip_at(lax.rem(z + ahead, 4), y_to, x_to)

    def ship(slot, to):
        copy = remote(
            pick(slot), pick(slot), send.at[len(started)], recv.at[slot], (core, to)
        )
        copy.start()
        started.append(copy)

    def landed(slot):
        remote(pick(slot), pick(slot), send.at[0], recv.at[slot], (core, flip(1, 0, 0))).wait_recv()

    def own():
        for ahead in (1, 3, 2):
            ship(chip, flip(0, 0, ahead))
        ship(chip, flip(1, 0, 0))
        ship(chip, flip(0, 1, 0))

    def line(ahead):
        slot = flip(0, 0, ahead)
        landed(slot)
        ship(slot, flip(1, 0, 0))
        ship(slot, flip(0, 1, 0))

    def side(ahead):
        slot = flip(1, 0, ahead)
        landed(slot)
        ship(slot, flip(0, 1, 0))

    def finish():
        for ahead in (0, 1, 3, 2):
            for far_p in (0, 1):
                landed(flip(far_p, 1, ahead))
        for copy in started:
            copy.wait_send()

    return [
        own,
        lambda: side(0),
        lambda: line(1),
        lambda: side(1),
        lambda: line(3),
        lambda: side(3),
        lambda: line(2),
        lambda: side(2),
        finish,
    ]


def run_together(*plans):
    for steps in zip(*plans):
        for step in steps:
            step()


def to_tokens(source, target, send, recv):
    core, chip = place()
    to_core = lax.div(chip, HALF)
    mine = core * HALF + lax.rem(chip, HALF)
    here = to_core == core

    def copy_to(ahead):
        chip_to = lax.rem(chip + ahead, CHIPS)
        return remote(
            source.at[chip_to], target.at[mine], send.at[ahead], recv.at[mine], (to_core, chip_to)
        )

    @pl.when(here)
    def _():
        pltpu.make_async_copy(source.at[chip], target.at[mine], recv.at[mine]).start()

    @pl.when(jnp.logical_not(here))
    def _():
        copy_to(0).start()

    for ahead in range(1, CHIPS):
        copy_to(ahead).start()

    def finish():
        for slot in range(CHIPS):
            pltpu.make_async_copy(source.at[slot], target.at[slot], recv.at[slot]).wait()

        @pl.when(jnp.logical_not(here))
        def _():
            copy_to(0).wait_send()

        for ahead in range(1, CHIPS):
            copy_to(ahead).wait_send()

    return finish


def to_heads(source, target, send, recv):
    core, chip = place()

    def copy_to(group, ahead):
        head = lax.rem(chip + ahead, HALF)
        return remote(
            source.at[group * HALF + head],
            target.at[chip],
            send.at[group * HALF + ahead],
            recv.at[chip],
            (group, core * HALF + head),
        )

    here = lax.div(chip, HALF) == core

    def each(act):
        for group in range(2):
            for ahead in range(HALF):
                if ahead == 0:
                    itself = jnp.logical_and(here, core == group)
                    pl.when(jnp.logical_not(itself))(lambda: act(copy_to(group, 0)))
                else:
                    act(copy_to(group, ahead))

    @pl.when(here)
    def _():
        pltpu.make_async_copy(
            source.at[core * HALF + lax.rem(chip, HALF)], target.at[chip], recv.at[chip]
        ).start()

    each(lambda copy: copy.start())

    def finish():
        for slot in range(CHIPS):
            pltpu.make_async_copy(source.at[slot], target.at[slot], recv.at[slot]).wait()
        each(lambda copy: copy.wait_send())

    return finish


def lanes(rows, width=128):
    return lax.broadcasted_iota(jnp.int32, (rows, width), 1)


def fold(rows_in):
    half = rows_in.shape[0] // 2
    both = jnp.where(lanes(half) < HD, rows_in[:half], pltpu.roll(rows_in[half:], HD, 1))
    pad = -half % 16
    if pad:
        both = jnp.concatenate([both, jnp.zeros((pad, 128), HIGH)], axis=0)
    return both.astype(LOW)


def gather_tokens(slot_rows, x_in, w_in, rel_in, x_all, w_all, rel_all, *sems):
    x_send, x_recv, w_send, w_recv, rel_send, rel_recv, pair_sem, own_sem = sems
    core, chip = place()
    me = core * CHIPS + chip
    to_chip = lax.div(me, 2)
    side = lax.rem(chip, 2)
    depth = rel_in.shape[0]
    half = x_in.shape[1] // 2
    own_x = pltpu.make_async_copy(x_in, x_all.at[pl.ds(chip * slot_rows, slot_rows)], own_sem.at[0])
    own_w = pltpu.make_async_copy(w_in.at[chip], w_all.at[me], own_sem.at[1])
    own_x.start()
    own_w.start()
    meet()
    rel_slot = rel_all.at[pl.ds(side * depth, depth)]

    def rel_copy(to_core):
        return remote(
            rel_in, rel_slot, rel_send.at[to_core], rel_recv.at[side], (to_core, to_chip)
        )

    def rel_each(act_remote, act_own):
        for to_core in range(2):
            itself = jnp.logical_and(to_chip == chip, core == to_core)
            pl.when(jnp.logical_not(itself))(lambda: act_remote(rel_copy(to_core)))
            if act_own is not None:
                pl.when(itself)(act_own)

    rel_each(
        lambda copy: copy.start(),
        lambda: pltpu.make_async_copy(rel_in, rel_slot, rel_recv.at[side]).start(),
    )

    def w_copy(ahead):
        chip_to = lax.rem(chip + ahead, CHIPS)
        return remote(w_in.at[chip_to], w_all.at[me], w_send.at[ahead], w_recv.at[chip], (core, chip_to))

    for ahead in range(1, CHIPS):
        w_copy(ahead).start()

    def pick(part):
        return lambda slot: x_all.at[
            pl.ds(pl.multiple_of(slot * slot_rows, 16), slot_rows), pl.ds(part * half, half)
        ]

    own_x.wait()
    run_together(
        gather_steps(pick(0), x_send.at[0], x_recv.at[0], "x"),
        gather_steps(pick(1), x_send.at[1], x_recv.at[1], "y"),
    )
    own_w.wait()
    for ahead in range(1, CHIPS):
        chip_from = lax.rem(chip + ahead, CHIPS)
        remote(
            w_in.at[0], w_all.at[core * CHIPS + chip_from], w_send.at[0], w_recv.at[chip_from], (core, chip_from)
        ).wait_recv()
    mine = w_all.at[pl.ds(core * CHIPS, CHIPS)]
    pair = remote(mine, mine, pair_sem.at[0], pair_sem.at[1], (1 - core, chip))
    pair.start()
    for ahead in range(1, CHIPS):
        w_copy(ahead).wait_send()
    rel_each(lambda copy: copy.wait_send(), None)
    for slot in range(2):
        pltpu.make_async_copy(
            rel_in, rel_all.at[pl.ds(slot * depth, depth)], rel_recv.at[slot]
        ).wait()
    pair.wait()


def gather_weights(in_in, down_in, out_in, qkv_in, small_in, w_in, w_down, w_out, w_qkv, small, *sems):
    in_send, in_recv, down_send, down_recv, out_send, out_recv, qkv_send, qkv_recv, pair_sem, own_sem = sems
    core, chip = place()
    other = 1 - core
    wide = in_in.shape[1] // 2
    narrow = qkv_in.shape[2] // 2

    def columns(half, width):
        return pl.ds(pl.multiple_of(half * width, 128), width)

    own = [
        pltpu.make_async_copy(in_in.at[:, columns(core, wide)], w_in.at[core, chip], own_sem.at[0]),
        pltpu.make_async_copy(qkv_in.at[:, :, columns(core, narrow)], w_qkv.at[:, core, chip], own_sem.at[1]),
        pltpu.make_async_copy(down_in, w_down.at[chip], own_sem.at[2]),
        pltpu.make_async_copy(out_in, w_out.at[chip], own_sem.at[3]),
        pltpu.make_async_copy(small_in, small.at[core], own_sem.at[4]),
    ]
    for copy in own:
        copy.start()
    meet()
    pair = [
        remote(in_in.at[:, columns(other, wide)], w_in.at[core, chip], pair_sem.at[0], pair_sem.at[1], (other, chip)),
        remote(
            qkv_in.at[:, :, columns(other, narrow)],
            w_qkv.at[:, core, chip],
            pair_sem.at[2],
            pair_sem.at[3],
            (other, chip),
        ),
        remote(small_in, small.at[core], pair_sem.at[4], pair_sem.at[5], (other, chip)),
    ]
    for copy in pair:
        copy.start()
    for copy in own:
        copy.wait()
    plans = (
        gather_steps(lambda slot: w_out.at[slot], out_send, out_recv, "x"),
        gather_steps(lambda slot: w_down.at[slot], down_send, down_recv, "y"),
        gather_steps(lambda slot: w_in.at[:, slot], in_send, in_recv, "x"),
        gather_steps(lambda slot: w_qkv.at[:, :, slot], qkv_send, qkv_recv, "y"),
    )
    plans[0][0]()
    plans[1][0]()
    for copy in pair:
        copy.wait()
    plans[2][0]()
    plans[3][0]()
    run_together(*(plan[1:] for plan in plans))


def attend_forward(
    slot_rows, token_rows, x_all, w_all, rel_all, left, right, right_t, value, value_t, kept, arrived, *scratch
):
    meta, message, send, recv = scratch
    total = x_all.shape[0]
    eye = (
        lax.broadcasted_iota(jnp.int32, (slot_rows, 2 * 128), 0)
        == lax.broadcasted_iota(jnp.int32, (slot_rows, 2 * 128), 1)
    ).astype(LOW)
    for slot in range(CHIPS):
        end = (slot + 1) * slot_rows
        labels = x_all[end - 16 : end, 0:256]
        meta[end - slot_rows : end, 0:16] = dot(eye, labels, NT)
    rel = rel_all[...]
    table_t = rel[:, 0 : 3 * NB]
    depth = rel.shape[0]
    eye_small = lax.broadcasted_iota(jnp.int32, (depth, 128), 0) == lax.broadcasted_iota(
        jnp.int32, (depth, 128), 1
    )
    eye_next = lax.broadcasted_iota(jnp.int32, (depth, 128), 0) + depth == lax.broadcasted_iota(
        jnp.int32, (depth, 128), 1
    )
    extra = rel[:, 3 * NB : 4 * NB].astype(HIGH)
    bias = jnp.sum(
        jnp.where(eye_small, extra[:, 0:1], 0.0) + jnp.where(eye_next, extra[:, 1:2], 0.0),
        axis=0,
        keepdims=True,
    )
    lane = lanes(BLOCK)
    first_half = lane < HD
    scale = 1.0 / math.sqrt(4.0 * HD)

    def prepare(index, carry):
        rows = pl.ds(pl.multiple_of(index * BLOCK, BLOCK), BLOCK)
        projected = dot(x_all[rows, :], w_all[...])
        query_value = (projected[:, 0:128] + bias).astype(LOW).astype(HIGH)
        key = projected[:, 128:256].astype(LOW).astype(HIGH)
        query = query_value[:, 0:HD].astype(LOW)
        tables = dot(query, table_t).astype(LOW).astype(HIGH)
        ids = meta[rows, 8:12].astype(jnp.int32)
        segment, order, box_x, box_y = ids[:, 0:1], ids[:, 1:2], ids[:, 2:3], ids[:, 3:4]

        def selected(column, ids_of, values):
            bucket = jnp.clip(ids_of - values, -(NB // 2), NB // 2 - 1) + NB // 2
            return jnp.take_along_axis(tables[:, column * NB : (column + 1) * NB], bucket, axis=1)

        wide = selected(0, order, lane)
        narrow = jnp.where(
            first_half, selected(1, box_x, lane), selected(2, box_y, lane - HD)
        )
        label = lane - HD
        query_side = jnp.where(
            first_half,
            query_value * scale,
            jnp.where(jnp.logical_and(label != segment, label < 8), MASKED, 0.0),
        )
        key_side = jnp.where(first_half, key, (label == segment).astype(HIGH))
        left[rows, 0:128] = (wide * scale).astype(LOW)
        left[rows, 128:256] = (narrow * scale).astype(LOW)
        left[rows, 256:384] = query_side.astype(LOW)
        order_hot = (lane == order).astype(HIGH)
        box_hot = (jnp.where(first_half, box_x, box_y + HD) == lane).astype(HIGH)
        right[rows, 0:128] = order_hot.astype(LOW)
        right[rows, 128:256] = box_hot.astype(LOW)
        right[rows, 256:384] = key_side.astype(LOW)
        right_t[0:128, rows] = order_hot.T.astype(LOW)
        right_t[128:256, rows] = box_hot.T.astype(LOW)
        right_t[256:384, rows] = key_side.T.astype(LOW)
        held = jnp.where(first_half, pltpu.roll(query_value, HD, 1), (label == 0).astype(HIGH))
        value[rows, :] = held.astype(LOW)
        value_t[:, rows] = held.T.astype(LOW)
        return carry

    lax.fori_loop(0, total // BLOCK, prepare, 0)

    def attend(index, carry):
        rows = pl.ds(pl.multiple_of(index * BLOCK, BLOCK), BLOCK)
        logits = dot(left[rows, :], right_t[...])
        top = jnp.max(logits, axis=1, keepdims=True)
        weights = jnp.exp(logits - top).astype(LOW)
        mixed = dot(weights, value[...])
        row_sum = mixed[:, HD : HD + 1]
        ids = meta[rows, 8:12]
        facts = jnp.where(lane == HD, top + jnp.log(row_sum), ids[:, 3:4])
        facts = jnp.where(lane == HD + 1, ids[:, 1:2], facts)
        facts = jnp.where(lane == HD + 2, ids[:, 2:3], facts)
        kept[rows, :] = jnp.where(first_half, mixed / row_sum, facts)
        return carry

    lax.fori_loop(0, total // BLOCK, attend, 0)
    for slot in range(CHIPS):
        message[slot] = fold(kept[slot * slot_rows : (slot + 1) * slot_rows, :])
    meet()
    to_tokens(message, arrived, send, recv)()


def gelu_parts(pre):
    cdf = 0.5 * (1.0 + lax.erf(pre * math.sqrt(0.5)))
    density = jnp.exp(-0.5 * pre * pre) * (1.0 / math.sqrt(2.0 * math.pi))
    return pre * cdf, cdf + pre * density


def feed_forward(slot_rows, *refs):
    inputs, refs = refs[:8], refs[8:]
    outputs, refs = refs[:7], refs[7:]
    context_in, x_in, grad_in, vectors, bias_in, w_in, w_down, w_out = inputs
    out, d_sum1, g_in, g_down, g_out, g_small, arrived = outputs
    (context_wide, context, low_first, act, slope, d_second, d_inner, d_branch) = refs[:8]
    (out_part, in_part, d_message, pair_send, pair_recv, send, recv) = refs[8:]
    core, chip = place()
    own = pl.ds(pl.multiple_of(core * slot_rows, 16), slot_rows)
    far = pl.ds(pl.multiple_of((1 - core) * slot_rows, 16), slot_rows)
    width = x_in.shape[1]
    hidden = w_in.shape[1]
    tile = 512
    half = slot_rows // 2
    meet()
    count = [0]

    def swap(source, target):
        copy = remote(
            source, target, pair_send.at[count[0]], pair_recv.at[count[0]], (1 - core, chip)
        )
        count[0] += 1
        copy.start()
        return copy

    def swap_sum(index, full):
        copy = swap(out_part.at[index], in_part.at[index])
        copy.wait()
        return full[...] + in_part[index]

    left_half = lanes(half) < HD
    for group in range(2):
        for pair in range(HALF // 2):
            even = context_in[group * HALF + 2 * pair].astype(HIGH)[:half]
            odd = context_in[group * HALF + 2 * pair + 1].astype(HIGH)[:half]
            top = group * slot_rows
            columns = slice(pair * 128, pair * 128 + 128)
            context_wide[top : top + half, columns] = jnp.where(left_half, even, pltpu.roll(odd, HD, 1))
            context_wide[top + half : top + slot_rows, columns] = jnp.where(
                left_half, pltpu.roll(even, HD, 1), odd
            )
    context[...] = context_wide[...].astype(LOW)

    def product(index, lhs, rhs):
        out_part[index] = dot(lhs[far, :], rhs[...])
        copy = swap(out_part.at[index], in_part.at[index])
        mine = dot(lhs[own, :], rhs[...])
        copy.wait()
        return mine + in_part[index]

    def normalize(v, gain, shift):
        center = v - jnp.mean(v, axis=1, keepdims=True)
        inverse = lax.rsqrt(jnp.mean(center * center, axis=1, keepdims=True) + EPSILON)
        normed = center * inverse
        return normed * gain + shift, normed, inverse

    def normalize_back(c, normed, inverse, gain):
        scaled = c * gain
        inner = (
            scaled
            - jnp.mean(scaled, axis=1, keepdims=True)
            - normed * jnp.mean(scaled * normed, axis=1, keepdims=True)
        )
        return inner * inverse

    def column_sums(v):
        return jnp.sum(v, axis=0, keepdims=True)

    branch = product(0, context, w_out) + vectors[0:1]
    first, normed1, inverse1 = normalize(x_in[...].astype(HIGH) + branch, vectors[2:3], vectors[4:5])
    low_first[own, :] = first.astype(LOW)
    swap(low_first.at[own], low_first.at[own]).wait()

    def widen(index, carry):
        columns = pl.ds(pl.multiple_of(index * tile, tile), tile)
        pre = dot(low_first[...], w_in[:, columns]) + bias_in[:, columns]
        value, derivative = gelu_parts(pre)
        act[:, columns] = value.astype(LOW)
        slope[:, columns] = derivative
        return carry

    lax.fori_loop(0, hidden // tile, widen, 0)
    second = product(1, act, w_down) + vectors[1:2]
    result, normed2, inverse2 = normalize(first + second, vectors[3:4], vectors[5:6])
    out[...] = result.astype(LOW)
    upstream = grad_in[...].astype(HIGH)
    g_small[...] = jnp.zeros_like(g_small)
    d_sum2 = normalize_back(upstream, normed2, inverse2, vectors[3:4])
    low_second = d_sum2.astype(LOW)
    d_second[own, :] = low_second
    copy = swap(d_second.at[own], d_second.at[own])
    g_small[1:2, 0:width] = column_sums(low_second.astype(HIGH))
    g_small[3:4, 0:width] = column_sums(upstream * normed2)
    g_small[5:6, 0:width] = column_sums(upstream)
    copy.wait()

    def narrow_back(index, carry):
        columns = pl.ds(pl.multiple_of(index * tile, tile), tile)
        d_act = dot(d_second[...], w_down[columns, :], NT)
        low = (d_act * slope[:, columns]).astype(LOW)
        d_inner[:, columns] = low
        g_small[pl.ds(8, 1), columns] = column_sums(low.astype(HIGH))
        g_down[columns, :] = dot(act[:, columns], d_second[...], TN).astype(LOW)
        return carry

    lax.fori_loop(0, hidden // tile, narrow_back, 0)
    out_part[2] = dot(d_inner[far, :], w_in[...], NT)
    copy = swap(out_part.at[2], in_part.at[2])
    mine = dot(d_inner[own, :], w_in[...], NT)

    def widen_grad(index, carry):
        rows = pl.ds(pl.multiple_of(index * 256, 256), 256)
        g_in[rows, :] = dot(low_first[:, rows], d_inner[...], TN).astype(LOW)
        return carry

    lax.fori_loop(0, width // 256, widen_grad, 0)
    copy.wait()
    d_first = d_sum2 + mine + in_part[2]
    grad1 = normalize_back(d_first, normed1, inverse1, vectors[2:3])
    d_sum1[...] = grad1
    low_branch = grad1.astype(LOW)
    d_branch[own, :] = low_branch
    copy = swap(d_branch.at[own], d_branch.at[own])
    g_small[0:1, 0:width] = column_sums(low_branch.astype(HIGH))
    g_small[2:3, 0:width] = column_sums(d_first * normed1)
    g_small[4:5, 0:width] = column_sums(d_first)
    copy.wait()
    context_wide[...] = dot(d_branch[...], w_out[...], NT)
    for group in range(2):
        for pair in range(HALF // 2):
            both = context_wide[
                group * slot_rows : (group + 1) * slot_rows, pair * 128 : pair * 128 + 128
            ]
            d_message[group * HALF + 2 * pair] = fold(both)
            d_message[group * HALF + 2 * pair + 1] = fold(pltpu.roll(both, HD, 1))
    finish = to_heads(d_message, arrived, send, recv)
    g_out[...] = dot(context[...], d_branch[...], TN).astype(LOW)
    finish()


def attend_backward(slot_rows, *refs):
    left, right, right_t, value_t, kept, rel_all, x_all, message_in = refs[:8]
    tokens_out, w_out, rel_out = refs[8:11]
    d_context, d_query, d_query_t, d_pair_t, rel_grad, message, w_mine, w_far, w_low = refs[11:20]
    rel_far, rel_sum, send, recv, w_send, w_recv, pair_sem, rel_sem, own_sem = refs[20:]
    core, chip = place()
    total = x_all.shape[0]
    width = x_all.shape[1]
    half = slot_rows // 2
    scale = 1.0 / math.sqrt(4.0 * HD)
    left_half = lanes(half) < HD
    for slot in range(CHIPS):
        both = message_in[slot].astype(HIGH)[:half]
        top = slot * slot_rows
        d_context[top : top + half, :] = jnp.where(left_half, both, 0.0)
        d_context[top + half : top + slot_rows, :] = jnp.where(left_half, pltpu.roll(both, HD, 1), 0.0)
    table_t = rel_all[:, 0 : 3 * NB]
    lane = lanes(BLOCK)
    first_half = lane < HD
    d_pair_t[...] = jnp.zeros_like(d_pair_t)
    rel_grad[...] = jnp.zeros_like(rel_grad)

    def step(index, carry):
        rows = pl.ds(pl.multiple_of(index * BLOCK, BLOCK), BLOCK)
        facts = kept[rows, :]
        grad = d_context[rows, :]
        delta = jnp.sum(grad * facts, axis=1, keepdims=True)
        probs = jnp.exp(dot(left[rows, :], right_t[...]) - facts[:, HD : HD + 1])
        d_probs = dot(grad.astype(LOW), value_t[...])
        d_logits = (probs * (d_probs - delta)).astype(LOW)
        query_t = jnp.where(first_half, left[rows, 256:384].astype(HIGH), 0.0).T[0:HD]
        d_pair_t[0:HD, :] += dot(grad.T[0:HD].astype(LOW), probs.astype(LOW))
        d_pair_t[HD : 2 * HD, :] += dot(query_t.astype(LOW), d_logits)
        back = dot(d_logits, right[...]) * scale
        ids = facts.astype(jnp.int32)
        order, box_x, box_y = (ids[:, HD + k : HD + k + 1] for k in (1, 2, 3))

        def placed(column, ids_of, extent, start):
            value = ids_of + NB // 2 - lane
            found = jnp.take_along_axis(
                back[:, column * 128 : column * 128 + 128], jnp.clip(value, 0, extent - 1) + start, axis=1
            )
            return jnp.where(jnp.logical_and(value >= 0, value < extent), found, 0.0)

        wide = back[:, 0:128]
        low_end = jnp.sum(jnp.where(lane >= order + NB // 2, wide, 0.0), axis=1, keepdims=True)
        high_end = jnp.sum(jnp.where(lane <= order - (NB // 2 - 1), wide, 0.0), axis=1, keepdims=True)
        first = placed(0, order, ORDER_RANGE, 0)
        first = jnp.where(lane == 0, low_end, jnp.where(lane == NB - 1, high_end, first))
        d_tables = jnp.concatenate(
            [first, placed(1, box_x, BOX_RANGE, 0), placed(1, box_y, BOX_RANGE, BOX_RANGE)], axis=1
        ).astype(LOW)
        from_tables = dot(d_tables, table_t, NT)
        content = back[:, 256:384]
        d_query[rows, :] = jnp.where(
            first_half, content + jnp.concatenate([from_tables, from_tables], axis=1), 0.0
        )
        d_query_t[0:HD, rows] = d_query[rows, :].T[0:HD].astype(LOW)
        rel_grad[:, 0 : 3 * NB] += dot((query_t / scale).astype(LOW), d_tables)
        return carry

    lax.fori_loop(0, total // BLOCK, step, 0)
    d_query_t[HD : 3 * HD, :] = d_pair_t[...].astype(LOW)
    d_columns = d_query_t[...]
    sums = jnp.sum(d_columns[0 : 2 * HD].astype(HIGH), axis=1, keepdims=True)
    rel_grad[:, 3 * NB : 4 * NB] = jnp.where(
        lanes(HD) == 0, sums[0:HD], jnp.where(lanes(HD) == 1, sums[HD : 2 * HD], 0.0)
    )
    slot_lane = lanes(slot_rows)
    for slot in range(CHIPS):
        top = slot * slot_rows
        if slot % 8 == 0:
            turned = d_pair_t[:, top : top + 8 * slot_rows].T
        pair = turned[(slot % 8) * slot_rows : (slot % 8 + 1) * slot_rows]
        turned_pair = pltpu.roll(pair, HD, 1)
        message[slot, 0:slot_rows, :] = jnp.where(
            slot_lane < HD, d_query[top : top + slot_rows, :], pair
        ).astype(LOW)
        message[slot, slot_rows:, :] = fold(pair)
    meet()
    finish_tokens = to_tokens(message, tokens_out, send, recv)
    w_grad = dot(d_columns, x_all[...])
    half_width = width // 2
    for part in range(2):
        w_mine[part] = w_grad[:, part * half_width : (part + 1) * half_width]
    w_pair = remote(w_mine.at[1 - core], w_far, pair_sem.at[0], pair_sem.at[1], (1 - core, chip))
    w_pair.start()
    depth = rel_sum.shape[0]
    rel_rows = pl.ds(pl.multiple_of((1 - core) * depth, 8), depth)
    rel_pair = remote(rel_grad.at[rel_rows], rel_far, pair_sem.at[2], pair_sem.at[3], (1 - core, chip))
    rel_pair.start()
    w_pair.wait()
    w_sum = (w_mine[core] + w_far[...]).T
    rows_each = w_low.shape[1]
    for slot in range(CHIPS):
        w_low[slot] = w_sum[slot * rows_each : (slot + 1) * rows_each].astype(LOW)

    def w_copy(ahead):
        to = lax.rem(chip + ahead, CHIPS)
        return remote(w_low.at[to], w_out.at[chip], w_send.at[ahead], w_recv.at[chip], (core, to))

    own_w = pltpu.make_async_copy(w_low.at[chip], w_out.at[chip], own_sem.at[0])
    own_w.start()
    for ahead in range(1, CHIPS):
        w_copy(ahead).start()
    rel_pair.wait()
    rel_sum[...] = rel_grad[pl.ds(pl.multiple_of(core * depth, 8), depth), :] + rel_far[...]
    rel_to = (lax.div(chip, HALF), lax.rem(2 * chip + core, CHIPS))
    itself = jnp.logical_and(rel_to[0] == core, rel_to[1] == chip)
    rel_copy = remote(rel_sum, rel_out, rel_sem.at[0], rel_sem.at[1], rel_to)
    own_rel = pltpu.make_async_copy(rel_sum, rel_out, rel_sem.at[1])
    pl.when(itself)(lambda: own_rel.start())
    pl.when(jnp.logical_not(itself))(lambda: rel_copy.start())
    own_rel.wait()
    pl.when(jnp.logical_not(itself))(lambda: rel_copy.wait_send())
    own_w.wait()
    for ahead in range(1, CHIPS):
        came = lax.rem(chip + ahead, CHIPS)
        remote(w_low.at[0], w_out.at[came], w_send.at[0], w_recv.at[came], (core, came)).wait_recv()
        w_copy(ahead).wait_send()
    finish_tokens()


def input_gradient(slot_rows, message_in, w_qkv, d_sum1, out, wide, low, out_part, in_part, sems):
    core, chip = place()
    own = pl.ds(pl.multiple_of(core * slot_rows, 16), slot_rows)
    far = pl.ds(pl.multiple_of((1 - core) * slot_rows, 16), slot_rows)
    half = slot_rows // 2
    pad = message_in.shape[1] - slot_rows
    lane_all = lanes(slot_rows) < HD
    lane_half = lanes(half) < HD
    for group in range(2):
        top = group * slot_rows
        for pair in range(HALF // 2):
            columns = slice(pair * 128, pair * 128 + 128)
            even = message_in[group * HALF + 2 * pair].astype(HIGH)
            odd = message_in[group * HALF + 2 * pair + 1].astype(HIGH)
            even_main, odd_main = even[:slot_rows], odd[:slot_rows]
            wide[0, top : top + slot_rows, columns] = jnp.where(
                lane_all, even_main, pltpu.roll(odd_main, HD, 1)
            )
            wide[1, top : top + slot_rows, columns] = jnp.where(
                lane_all, pltpu.roll(even_main, HD, 1), odd_main
            )
            even_last, odd_last = even[slot_rows : slot_rows + half], odd[slot_rows : slot_rows + half]
            wide[2, top : top + half, columns] = jnp.where(
                lane_half, even_last, pltpu.roll(odd_last, HD, 1)
            )
            wide[2, top + half : top + slot_rows, columns] = jnp.where(
                lane_half, pltpu.roll(even_last, HD, 1), odd_last
            )
    low[...] = wide[...].astype(LOW)
    meet()

    def part(rows):
        return (
            dot(low[0, rows, :], w_qkv[0], NT)
            + dot(low[1, rows, :], w_qkv[1], NT)
            + dot(low[2, rows, :], w_qkv[2], NT)
        )

    out_part[...] = part(far)
    copy = remote(out_part, in_part, sems.at[0], sems.at[1], (1 - core, chip))
    copy.start()
    mine = part(own) + d_sum1[...]
    copy.wait()
    out[...] = (mine + in_part[...]).astype(LOW)


def reduce_steps(own, slot_of, stages, send, recv, across, result):
    core, chip = place()
    z, y, x = coordinates(chip)
    first, second, third = stages
    started = []
    order = (1, 3, 2, 0)

    def at(far_p, far_q, ahead):
        far_y, far_x = (far_q, far_p) if across == "x" else (far_p, far_q)
        return chip_at(lax.rem(z + ahead, 4), 1 - y if far_y else y, 1 - x if far_x else x)

    def ship(source, target, slot, to):
        copy = remote(source, target, send.at[len(started)], recv.at[slot], (core, to))
        copy.start()
        started.append(copy)

    def landed(target, slot):
        remote(target, target, send.at[0], recv.at[slot], (core, at(1, 0, 0))).wait_recv()

    def start():
        for ahead in order:
            for far_p in (1, 0):
                place_at = ahead * 2 + far_p
                ship(slot_of(own, at(far_p, 1, ahead)), first.at[place_at], place_at, at(0, 1, 0))

    def side(ahead):
        place_at = ahead * 2 + 1
        landed(first.at[place_at], place_at)
        mine = slot_of(own, at(1, 0, ahead))
        first[place_at] = (first[place_at].astype(HIGH) + mine[...].astype(HIGH)).astype(LOW)
        ship(first.at[place_at], second.at[ahead], 8 + ahead, at(1, 0, 0))

    def line(ahead):
        place_at = ahead * 2
        landed(first.at[place_at], place_at)
        landed(second.at[ahead], 8 + ahead)
        mine = slot_of(own, at(0, 0, ahead))
        total = (
            first[place_at].astype(HIGH) + second[ahead].astype(HIGH) + mine[...].astype(HIGH)
        )
        if ahead:
            first[place_at] = total.astype(LOW)
            ship(first.at[place_at], third.at[ahead - 1], 11 + ahead, at(0, 0, ahead))
        else:
            result[...] = total

    def finish():
        for ahead in (1, 3, 2):
            landed(third.at[ahead - 1], 11 + ahead)
            result[...] += third[ahead - 1].astype(HIGH)
        for copy in started:
            copy.wait_send()

    return [start] + [step for ahead in order for step in (functools.partial(side, ahead), functools.partial(line, ahead))] + [finish]


def reduce_gradients(*refs):
    g_in, g_down, g_out, g_small = refs[:4]
    in_result, down_result, out_result, small_result = refs[4:8]
    in_stages, down_stages, out_stages, refs = refs[8:11], refs[11:14], refs[14:17], refs[17:]
    in_total, in_far, small_sum, small_in = refs[:4]
    in_send, in_recv, down_send, down_recv, out_send, out_recv, small_send, small_recv, pair_sem = refs[4:]
    core, chip = place()
    z, y, x = coordinates(chip)
    meet()
    plans = (
        reduce_steps(g_down, lambda ref, slot: ref.at[slot], down_stages, down_send, down_recv, "y", down_result),
        reduce_steps(g_in, lambda ref, slot: ref.at[:, slot], in_stages, in_send, in_recv, "x", in_total),
        reduce_steps(g_out, lambda ref, slot: ref.at[slot], out_stages, out_send, out_recv, "y", out_result),
    )
    small_sum[...] = g_small[...]
    waiting = []

    def small_ship(index, device):
        copy = remote(small_sum, small_in.at[index], small_send.at[index], small_recv.at[index], device)
        copy.start()
        return copy

    def small_pair():
        copy = small_ship(0, (1 - core, chip))
        copy.wait()
        small_sum[0:8, :] += small_in[0, 0:8, :]

    def small_side(index, to):
        copy = small_ship(index, (core, to))
        copy.wait()
        small_sum[...] += small_in[index]

    def small_line():
        copies = [small_ship(2 + ahead, (core, chip_at(lax.rem(z + ahead, 4), y, x))) for ahead in (1, 2, 3)]
        for copy in copies:
            copy.wait()
        small_result[...] = small_sum[...] + small_in[3] + small_in[4] + small_in[5]

    nothing = lambda: None
    small_steps = [
        nothing,
        small_pair,
        nothing,
        lambda: small_side(1, chip_at(z, 1 - y, x)),
        nothing,
        lambda: small_side(2, chip_at(z, y, 1 - x)),
        nothing,
        small_line,
        nothing,
        nothing,
    ]
    run_together(*plans, small_steps)
    pair = remote(in_total.at[1 - core], in_far, pair_sem.at[0], pair_sem.at[1], (1 - core, chip))
    pair.start()
    wide = in_total.shape[2]

    def columns(half):
        return pl.ds(pl.multiple_of(half * wide, 128), wide)

    in_result[:, columns(core)] = in_total[core]
    pair.wait()
    in_result[:, columns(1 - core)] = in_far[...]


def communicate(kernel, name, number, outputs, scratch, in_memory, out_memory):
    return pl.pallas_call(
        kernel,
        out_shape=outputs,
        in_specs=[pl.BlockSpec(memory_space=space) for space in in_memory],
        out_specs=[pl.BlockSpec(memory_space=space) for space in out_memory],
        scratch_shapes=scratch,
        compiler_params=pltpu.CompilerParams(
            collective_id=number, has_side_effects=True, vmem_limit_bytes=VMEM_LIMIT
        ),
        name=name,
    )


def head_shards(
    hidden_in,
    segment_ids,
    order_ids,
    box_ids,
    qkv_weight,
    qkv_bias,
    rel_tables,
    out_weight,
    branch_bias,
    norm_gains,
    norm_shifts,
    ffn_in,
    ffn_in_bias,
    ffn_out,
    out_grad,
):
    rows, width = hidden_in.shape
    slot_rows = -(-(rows + 5) // 16) * 16
    total = CHIPS * slot_rows
    depth = qkv_weight.shape[1]
    hidden = ffn_in.shape[1]
    half_hidden, half_width = hidden // 2, width // 2
    down_rows = ffn_out.shape[0]
    core = lax.axis_index("grp")
    chip = lax.axis_index("blk")
    shape = jax.ShapeDtypeStruct
    any_, vmem = pl.ANY, pltpu.VMEM
    dma = pltpu.SemaphoreType.DMA

    def row(values):
        return jnp.pad(values.astype(LOW), (0, width - values.shape[0]))[None]

    pad_label = jnp.full((slot_rows - rows,), 4, jnp.int32)
    extra = jnp.concatenate(
        [
            row(jnp.concatenate([segment_ids, pad_label])),
            row(order_ids),
            row(box_ids[0]),
            row(box_ids[1]),
            row(
                jnp.concatenate(
                    [branch_bias.reshape(-1), norm_gains.reshape(-1), norm_shifts.reshape(-1), ffn_in_bias]
                )
            ),
            jnp.zeros((slot_rows - rows - 5, width), LOW),
        ],
        axis=0,
    )
    x_slot = jnp.concatenate([hidden_in, extra], axis=0)
    w_heads = jnp.concatenate(
        [
            qkv_weight[0].reshape(depth, H, HD),
            qkv_weight[2].reshape(depth, H, HD),
            qkv_weight[1].reshape(depth, H, HD),
            jnp.zeros((depth, H, HD), LOW),
        ],
        axis=2,
    ).transpose(1, 0, 2)
    rel_part = jnp.concatenate(
        [
            rel_tables.reshape(3 * NB, depth).T,
            qkv_bias.T,
            jnp.zeros((depth, NB - 2), LOW),
        ],
        axis=1,
    )
    x_all, w_all, rel_all = communicate(
        functools.partial(gather_tokens, slot_rows),
        "gather_tokens",
        0,
        (
            shape((total, width), LOW),
            shape((2 * CHIPS, depth, 4 * HD), LOW),
            shape((2 * depth, 4 * NB), LOW),
        ),
        [dma((2, 16)), dma((2, 16)), dma((16,)), dma((16,)), dma((2,)), dma((2,)), dma((2,)), dma((2,))],
        [any_] * 3,
        [any_] * 3,
    )(x_slot, w_heads, rel_part)
    small_in = x_all.reshape(CHIPS, slot_rows, width)[:, rows + 4, : 6 * depth + down_rows]
    w_in, w_down, w_out, w_qkv, small = communicate(
        gather_weights,
        "gather_weights",
        1,
        (
            shape((2, CHIPS, depth, half_hidden), LOW),
            shape((CHIPS, down_rows, width), LOW),
            shape((CHIPS, depth, width), LOW),
            shape((3, 2, CHIPS, depth, half_width), LOW),
            shape((2,) + small_in.shape, LOW),
        ),
        [dma((16,))] * 8 + [dma((6,)), dma((5,))],
        [any_] * 5,
        [any_] * 5,
    )(ffn_in, ffn_out, out_weight, qkv_weight, small_in)
    left, right, right_t, value, value_t, kept, context = communicate(
        functools.partial(attend_forward, slot_rows, rows),
        "attend_forward",
        2,
        (
            shape((total, 384), LOW),
            shape((total, 384), LOW),
            shape((384, total), LOW),
            shape((total, 128), LOW),
            shape((128, total), LOW),
            shape((total, 128), HIGH),
            shape((CHIPS, 80, 128), LOW),
        ),
        [vmem((total, 128), HIGH), vmem((CHIPS, 80, 128), LOW), dma((16,)), dma((16,))],
        [vmem] * 3,
        [vmem] * 7,
    )(x_all, w_all.reshape(width, 4 * HD), rel_all)
    vectors = (
        small[:, :, : 6 * depth].astype(HIGH).reshape(2, CHIPS, 6, depth).transpose(2, 0, 1, 3).reshape(6, width)
    )
    vectors = jnp.pad(vectors, ((0, 2), (0, 0)))
    bias_in = small_in[:, 6 * depth :].astype(HIGH).reshape(1, half_hidden)
    pad_rows = ((0, slot_rows - rows), (0, 0))
    both = 2 * slot_rows
    hidden_out, d_sum1, g_in, g_down, g_out, g_small, d_context = communicate(
        functools.partial(feed_forward, slot_rows),
        "feed_forward",
        3,
        (
            shape((slot_rows, width), LOW),
            shape((slot_rows, width), HIGH),
            shape((width, half_hidden), LOW),
            shape((half_hidden, width), LOW),
            shape((half_width, width), LOW),
            shape((16, half_hidden), HIGH),
            shape((CHIPS, 80, 128), LOW),
        ),
        [
            vmem((both, half_width), HIGH),
            vmem((both, half_width), LOW),
            vmem((both, width), LOW),
            vmem((both, half_hidden), LOW),
            vmem((both, half_hidden), HIGH),
            vmem((both, width), LOW),
            vmem((both, half_hidden), LOW),
            vmem((both, width), LOW),
            vmem((3, slot_rows, width), HIGH),
            vmem((3, slot_rows, width), HIGH),
            vmem((CHIPS, 80, 128), LOW),
            dma((6,)),
            dma((6,)),
            dma((16,)),
            dma((16,)),
        ],
        [vmem] * 8,
        [vmem] * 7,
    )(
        context,
        jnp.pad(hidden_in, pad_rows),
        jnp.pad(out_grad, pad_rows),
        vectors,
        bias_in,
        w_in.reshape(width, half_hidden),
        w_down.reshape(half_hidden, width),
        w_out.reshape(half_width, width),
    )
    token_grads, w_grad, rel_grad = communicate(
        functools.partial(attend_backward, slot_rows),
        "attend_backward",
        4,
        (
            shape((CHIPS, slot_rows + 80, 128), LOW),
            shape((CHIPS, depth, 3 * HD), LOW),
            shape((depth, 4 * NB), HIGH),
        ),
        [
            vmem((total, 128), HIGH),
            vmem((total, 128), HIGH),
            vmem((3 * HD, total), LOW),
            vmem((2 * HD, total), HIGH),
            vmem((2 * depth, 4 * NB), HIGH),
            vmem((CHIPS, slot_rows + 80, 128), LOW),
            vmem((2, 3 * HD, half_width), HIGH),
            vmem((3 * HD, half_width), HIGH),
            vmem((CHIPS, depth, 3 * HD), LOW),
            vmem((depth, 4 * NB), HIGH),
            vmem((depth, 4 * NB), HIGH),
            dma((16,)),
            dma((16,)),
            dma((16,)),
            dma((16,)),
            dma((4,)),
            dma((2,)),
            dma((1,)),
        ],
        [vmem] * 8,
        [vmem] * 3,
    )(left, right, right_t, value_t, kept, rel_all, x_all, d_context)
    hidden_grad = communicate(
        functools.partial(input_gradient, slot_rows),
        "input_gradient",
        5,
        (shape((slot_rows, width), LOW),),
        [
            vmem((3, both, half_width), HIGH),
            vmem((3, both, half_width), LOW),
            vmem((slot_rows, width), HIGH),
            vmem((slot_rows, width), HIGH),
            dma((2,)),
        ],
        [vmem] * 3,
        [vmem],
    )(token_grads, w_qkv.reshape(3, width, half_width), d_sum1)[0]

    def stages(block):
        return [vmem((count,) + block, LOW) for count in (8, 4, 3)]

    in_grad, down_grad, out_w_grad, small_grad = communicate(
        reduce_gradients,
        "reduce_gradients",
        6,
        (
            shape((depth, hidden), HIGH),
            shape((down_rows, width), HIGH),
            shape((depth, width), HIGH),
            shape((16, half_hidden), HIGH),
        ),
        stages((2, depth, half_hidden))
        + stages((down_rows, width))
        + stages((depth, width))
        + [
            vmem((2, depth, half_hidden), HIGH),
            vmem((depth, half_hidden), HIGH),
            vmem((16, half_hidden), HIGH),
            vmem((6, 16, half_hidden), HIGH),
        ]
        + [dma((16,))] * 6
        + [dma((6,)), dma((6,)), dma((2,))],
        [vmem] * 4,
        [vmem] * 4,
    )(
        g_in.reshape(2, CHIPS, depth, half_hidden),
        g_down.reshape(CHIPS, down_rows, width),
        g_out.reshape(CHIPS, depth, width),
        g_small,
    )
    qkv_grad = w_grad.reshape(H, depth, 3, HD).transpose(2, 1, 0, 3).reshape(3, depth, width).astype(HIGH)
    mine = lax.dynamic_slice_in_dim(small_grad[0:6], (core * CHIPS + chip) * depth, depth, 1)
    bias_grad = lax.dynamic_slice_in_dim(small_grad[8], chip * down_rows, down_rows, 0)
    return (
        hidden_out[:rows],
        hidden_grad[:rows],
        jnp.stack([qkv_grad[0], qkv_grad[2], qkv_grad[1]]),
        rel_grad[:, 3 * NB : 3 * NB + 2].T,
        rel_grad[:, : 3 * NB].T.reshape(3, NB, depth),
        out_w_grad,
        mine[0:2],
        mine[2:4],
        mine[4:6],
        in_grad,
        bias_grad,
        down_grad,
    )


def solution(mesh):
    by_heads = mesh.shape["grp"] == 2 and mesh.shape["blk"] == CHIPS == H
    return jax.shard_map(
        head_shards if by_heads else shards,
        mesh=mesh,
        in_specs=(
            P(("grp", "blk"), None),
            P(("grp", "blk")),
            P(("grp", "blk")),
            P(None, ("grp", "blk")),
            P(None, ("grp", "blk"), None),
            P(None, ("grp", "blk")),
            P(None, None, ("grp", "blk")),
            P(("grp", "blk"), None),
            P(None, ("grp", "blk")),
            P(None, ("grp", "blk")),
            P(None, ("grp", "blk")),
            P(("grp", "blk"), None),
            P(("grp", "blk")),
            P(("grp", "blk"), None),
            P(("grp", "blk"), None),
        ),
        out_specs=(
            P(("grp", "blk"), None),
            P(("grp", "blk"), None),
            P(None, ("grp", "blk"), None),
            P(None, ("grp", "blk")),
            P(None, None, ("grp", "blk")),
            P(("grp", "blk"), None),
            P(None, ("grp", "blk")),
            P(None, ("grp", "blk")),
            P(None, ("grp", "blk")),
            P(("grp", "blk"), None),
            P(("grp", "blk")),
            P(("grp", "blk"), None),
        ),
        check_vma=False,
    )
```

```python
import functools
import math
import types

import jax
import jax.numpy as jnp
from jax import lax
from jax.experimental import pallas as pl
from jax.experimental.pallas import tpu as pltpu
from jax.sharding import PartitionSpec as P

H = 16
HD = 64
NB = 128
ORDER_RANGE = 128
BOX_RANGE = 64


NEGATIVE = -1e30
EPSILON = 1e-05


def shifted(x, axis, by):
    devices = lax.axis_size(axis)
    return lax.ppermute(x, axis, [(i, (i + by) % devices) for i in range(devices)])


def block_size(row_count):
    chosen = 1
    for option in range(1, min(row_count, 544) + 1):
        if row_count % option == 0:
            chosen = option
    return chosen


def kind_ranges():
    return (ORDER_RANGE, BOX_RANGE, BOX_RANGE)


def query_maps(layout_ids):
    maps_out = []
    for column, extent in enumerate(kind_ranges()):
        offsets = layout_ids[:, column][:, None] - jnp.arange(extent, dtype=jnp.int32)[None, :]
        bucket = jnp.clip(offsets, -(NB // 2), NB // 2 - 1) + NB // 2
        maps_out.append(bucket[:, :, None] == jnp.arange(NB, dtype=jnp.int32)[None, None, :])
    return maps_out


def key_onehot(key_ids):
    pieces_out = []
    for column, extent in enumerate(kind_ranges()):
        pieces_out.append(
            key_ids[:, column + 1][:, None] == jnp.arange(extent, dtype=jnp.int32)[None, :]
        )
    return jnp.concatenate(pieces_out, axis=1).astype(jnp.bfloat16)


def norm_forward(values_in, norm_gain, norm_shift):
    center = values_in - jnp.mean(values_in, axis=-1, keepdims=True)
    inverse = lax.rsqrt(jnp.mean(center * center, axis=-1, keepdims=True) + EPSILON)
    normed = center * inverse
    return (normed * norm_gain + norm_shift, normed, inverse)


def norm_backward(upstream, normed, inverse, norm_gain):
    scaled = upstream * norm_gain
    inner_part = (
        scaled
        - jnp.mean(scaled, axis=-1, keepdims=True)
        - normed * jnp.mean(scaled * normed, axis=-1, keepdims=True)
    )
    return (inner_part * inverse, jnp.sum(upstream * normed, axis=0), jnp.sum(upstream, axis=0))


def block_logits(query_heads, selector, query_seg, key_part, meta_part, scaling):
    key_ids = meta_part.astype(jnp.int32)
    row_count = key_part.shape[0]
    key_heads = key_part.reshape(row_count, H, HD)
    content = jnp.einsum("thd,khd->htk", query_heads, key_heads, preferred_element_type=jnp.float32)
    onehot = key_onehot(key_ids)
    rel_bias = jnp.einsum("thv,kv->htk", selector, onehot, preferred_element_type=jnp.float32)
    allowed = query_seg[:, None] == key_ids[None, :, 0]
    logits = jnp.where(allowed[None], (content + rel_bias) * scaling, NEGATIVE)
    return (logits, allowed, onehot, key_heads)


def over_blocks(advance, carry, piece, start):
    row_count = piece[0].shape[0]
    stride = block_size(row_count)

    def one_step(block_index, running):
        portion = tuple(
            (lax.dynamic_slice_in_dim(member, block_index * stride, stride, 0) for member in piece)
        )
        return advance(running, portion, start + block_index * stride)

    return lax.fori_loop(0, row_count // stride, one_step, carry)


def shards(
    hidden_in,
    segment_ids,
    order_ids,
    box_ids,
    qkv_weight,
    qkv_bias,
    rel_tables,
    out_weight,
    branch_bias,
    norm_gains,
    norm_shifts,
    ffn_in,
    ffn_in_bias,
    ffn_out,
    out_grad,
):
    gathered = (
        lax.all_gather(qkv_weight, ("grp", "blk"), axis=1, tiled=True),
        lax.all_gather(qkv_bias, ("grp", "blk"), axis=1, tiled=True),
        lax.all_gather(rel_tables, ("grp", "blk"), axis=2, tiled=True),
        lax.all_gather(out_weight, ("grp", "blk"), axis=0, tiled=True),
        lax.all_gather(branch_bias, ("grp", "blk"), axis=1, tiled=True),
        lax.all_gather(norm_gains, ("grp", "blk"), axis=1, tiled=True),
        lax.all_gather(norm_shifts, ("grp", "blk"), axis=1, tiled=True),
        lax.all_gather(ffn_in, ("grp", "blk"), axis=0, tiled=True),
        lax.all_gather(ffn_in_bias, ("grp", "blk"), axis=0, tiled=True),
        lax.all_gather(ffn_out, ("grp", "blk"), axis=0, tiled=True),
    )
    w_qkv, b_qkv, w_rel, w_out, b_branch, gains, shifts, w_in, b_in, w_down = gathered
    row_count = hidden_in.shape[0]
    width = hidden_in.shape[1]
    scaling = 1.0 / math.sqrt(4.0 * HD)
    select_width = ORDER_RANGE + 2 * BOX_RANGE
    projected = jnp.einsum("td,cde->cte", hidden_in, w_qkv, preferred_element_type=jnp.float32)
    bias_qkv = b_qkv.astype(jnp.float32)
    query_rows = (projected[0] + bias_qkv[0]).astype(jnp.bfloat16)
    key_rows = projected[1].astype(jnp.bfloat16)
    value_rows = (projected[2] + bias_qkv[1]).astype(jnp.bfloat16)
    layout_ids = jnp.stack([order_ids, box_ids[0], box_ids[1]], axis=1)
    key_meta = jnp.stack([segment_ids, order_ids, box_ids[0], box_ids[1]], axis=1).astype(
        jnp.bfloat16
    )
    query_heads = query_rows.reshape(row_count, H, HD)
    rel_heads = w_rel.reshape(3, NB, H, HD)
    tables = jnp.einsum(
        "thd,nbhd->thnb", query_heads, rel_heads, preferred_element_type=jnp.float32
    ).astype(jnp.bfloat16)
    maps_list = query_maps(layout_ids)
    selector = jnp.concatenate(
        [
            jnp.einsum(
                "thb,tvb->thv",
                tables[:, :, column],
                maps_list[column].astype(jnp.bfloat16),
                preferred_element_type=jnp.float32,
            )
            for column in range(3)
        ],
        axis=2,
    ).astype(jnp.bfloat16)

    def forward_step(running, portion, offset):
        row_top, row_total, weighted = running
        key_part, value_part, meta_part = portion
        logits, allowed, onehot, key_heads = block_logits(
            query_heads, selector, segment_ids, key_part, meta_part, scaling
        )
        new_top = jnp.maximum(row_top, jnp.max(logits, axis=2))
        rescale = jnp.exp(row_top - new_top)
        weights = jnp.where(allowed[None], jnp.exp(logits - new_top[:, :, None]), 0.0)
        value_heads = value_part.reshape(value_part.shape[0], H, HD)
        weighted = weighted * rescale.T[:, :, None] + jnp.einsum(
            "htk,khd->thd",
            weights.astype(jnp.bfloat16),
            value_heads,
            preferred_element_type=jnp.float32,
        )
        return (new_top, row_total * rescale + jnp.sum(weights, axis=2), weighted)

    start_state = (
        jnp.full((H, row_count), NEGATIVE, jnp.float32),
        jnp.zeros((H, row_count), jnp.float32),
        jnp.zeros((row_count, H, HD), jnp.float32),
    )
    row_top, row_total, weighted = over_blocks(
        forward_step,
        start_state,
        (
            lax.all_gather(key_rows, "blk", axis=0, tiled=True),
            lax.all_gather(value_rows, "blk", axis=0, tiled=True),
            lax.all_gather(key_meta, "blk", axis=0, tiled=True),
        ),
        jnp.int32(0),
    )
    context_full = weighted / row_total.T[:, :, None]
    log_total = row_top + jnp.log(row_total)
    context = context_full.reshape(row_count, width).astype(jnp.bfloat16)
    branch = jnp.dot(context, w_out, preferred_element_type=jnp.float32) + b_branch[0].astype(
        jnp.float32
    )
    first, normed_one, inverse_one = norm_forward(
        hidden_in.astype(jnp.float32) + branch,
        gains[0].astype(jnp.float32),
        shifts[0].astype(jnp.float32),
    )
    first_low = first.astype(jnp.bfloat16)
    inner_pre = jnp.dot(first_low, w_in, preferred_element_type=jnp.float32) + b_in.astype(
        jnp.float32
    )
    activated, gelu_pull = jax.vjp(
        lambda pre_act: jax.nn.gelu(pre_act, approximate=False), inner_pre
    )
    activated_low = activated.astype(jnp.bfloat16)
    second = jnp.dot(activated_low, w_down, preferred_element_type=jnp.float32) + b_branch[
        1
    ].astype(jnp.float32)
    result, normed_two, inverse_two = norm_forward(
        first + second, gains[1].astype(jnp.float32), shifts[1].astype(jnp.float32)
    )
    hidden_out = result.astype(jnp.bfloat16)
    grad_sum2, gain_grad2, shift_grad2 = norm_backward(
        out_grad.astype(jnp.float32), normed_two, inverse_two, gains[1].astype(jnp.float32)
    )
    grad_second = grad_sum2.astype(jnp.bfloat16)
    grad_w_down = jnp.einsum(
        "tf,td->fd", activated_low, grad_second, preferred_element_type=jnp.float32
    )
    grad_bias_two = jnp.sum(grad_second.astype(jnp.float32), axis=0)
    grad_act = jnp.einsum("td,fd->tf", grad_second, w_down, preferred_element_type=jnp.float32)
    grad_inner = gelu_pull(grad_act)[0].astype(jnp.bfloat16)
    grad_b_in = jnp.sum(grad_inner.astype(jnp.float32), axis=0)
    grad_w_in = jnp.einsum("td,tf->df", first_low, grad_inner, preferred_element_type=jnp.float32)
    grad_first = grad_sum2 + jnp.einsum(
        "tf,df->td", grad_inner, w_in, preferred_element_type=jnp.float32
    )
    grad_sum1, gain_grad1, shift_grad1 = norm_backward(
        grad_first, normed_one, inverse_one, gains[0].astype(jnp.float32)
    )
    grad_branch = grad_sum1.astype(jnp.bfloat16)
    grad_w_out = jnp.einsum("td,te->de", context, grad_branch, preferred_element_type=jnp.float32)
    grad_bias_one = jnp.sum(grad_branch.astype(jnp.float32), axis=0)
    grad_context = jnp.einsum(
        "te,de->td", grad_branch, w_out, preferred_element_type=jnp.float32
    ).astype(jnp.bfloat16)
    grad_heads = grad_context.reshape(row_count, H, HD)
    delta = jnp.einsum("thd,thd->ht", grad_heads.astype(jnp.float32), context_full)

    def backward_core(grad_query, grad_select, portion):
        key_part, value_part, meta_part = portion
        logits, allowed, onehot, key_heads = block_logits(
            query_heads, selector, segment_ids, key_part, meta_part, scaling
        )
        probs = jnp.where(allowed[None], jnp.exp(logits - log_total[:, :, None]), 0.0)
        part_rows = key_part.shape[0]
        value_heads = value_part.reshape(part_rows, H, HD)
        grad_probs = jnp.einsum(
            "thd,khd->htk", grad_heads, value_heads, preferred_element_type=jnp.float32
        )
        grad_logits = (probs * (grad_probs - delta[:, :, None])).astype(jnp.bfloat16)
        grad_query = grad_query + scaling * jnp.einsum(
            "htk,khd->thd", grad_logits, key_heads, preferred_element_type=jnp.float32
        )
        grad_select = grad_select + scaling * jnp.einsum(
            "htk,kv->thv", grad_logits, onehot, preferred_element_type=jnp.float32
        )
        grad_key = scaling * jnp.einsum(
            "htk,thd->khd", grad_logits, query_heads, preferred_element_type=jnp.float32
        )
        grad_value = jnp.einsum(
            "htk,thd->khd",
            probs.astype(jnp.bfloat16),
            grad_heads,
            preferred_element_type=jnp.float32,
        )
        update = jnp.concatenate(
            [grad_key.reshape(part_rows, width), grad_value.reshape(part_rows, width)], axis=1
        )
        return (grad_query, grad_select, update)

    query_zero = jnp.zeros((row_count, H, HD), jnp.float32)
    select_zero = jnp.zeros((row_count, H, select_width), jnp.float32)

    def cycle_turn(turn, carry):
        grad_query, grad_select, key_part, value_part, meta_part, carried = carry
        portion = (key_part, value_part, meta_part)
        grad_query, grad_select, update = backward_core(grad_query, grad_select, portion)
        carried = carried + update
        key_part, value_part, meta_part = shifted((key_part, value_part, meta_part), "blk", 1)
        carried = shifted(carried.astype(jnp.bfloat16), "blk", 1).astype(carried.dtype)
        return (grad_query, grad_select, key_part, value_part, meta_part, carried)

    cycle_start = (
        query_zero,
        select_zero,
        key_rows,
        value_rows,
        key_meta,
        jnp.zeros((row_count, 2 * width), jnp.float32),
    )
    cycle_end = lax.fori_loop(0, lax.axis_size("blk"), cycle_turn, cycle_start)
    grad_query, grad_select, own_pairs = (cycle_end[0], cycle_end[1], cycle_end[5])
    grad_key_rows = own_pairs[:, :width].astype(jnp.bfloat16)
    grad_value_rows = own_pairs[:, width:].astype(jnp.bfloat16)
    cursor = 0
    table_parts = []
    for column, extent in enumerate(kind_ranges()):
        table_parts.append(
            jnp.einsum(
                "thv,tvb->thb",
                grad_select[:, :, cursor : cursor + extent],
                maps_list[column].astype(jnp.float32),
                precision=lax.Precision.HIGHEST,
            )
        )
        cursor = cursor + extent
    grad_tables = jnp.stack(table_parts, axis=2).astype(jnp.bfloat16)
    grad_query_total = grad_query + jnp.einsum(
        "thnb,nbhd->thd", grad_tables, rel_heads, preferred_element_type=jnp.float32
    )
    grad_query_rows = grad_query_total.reshape(row_count, width).astype(jnp.bfloat16)
    grad_rel = jnp.einsum(
        "thnb,thd->nbhd", grad_tables, query_heads, preferred_element_type=jnp.float32
    ).reshape(3, NB, width)
    grad_stack = jnp.stack([grad_query_rows, grad_key_rows, grad_value_rows])
    grad_w_qkv = jnp.einsum(
        "td,cte->cde", hidden_in, grad_stack, preferred_element_type=jnp.float32
    )
    grad_b_qkv = jnp.stack(
        [
            jnp.sum(grad_query_rows.astype(jnp.float32), axis=0),
            jnp.sum(grad_value_rows.astype(jnp.float32), axis=0),
        ]
    )
    grad_input = grad_sum1 + jnp.einsum(
        "cte,cde->td", grad_stack, w_qkv, preferred_element_type=jnp.float32
    )
    summed = (
        lax.psum_scatter(grad_w_qkv, ("grp", "blk"), scatter_dimension=1, tiled=True),
        lax.psum_scatter(grad_b_qkv, ("grp", "blk"), scatter_dimension=1, tiled=True),
        lax.psum_scatter(grad_rel, ("grp", "blk"), scatter_dimension=2, tiled=True),
        lax.psum_scatter(grad_w_out, ("grp", "blk"), scatter_dimension=0, tiled=True),
        lax.psum_scatter(
            jnp.stack([grad_bias_one, grad_bias_two]),
            ("grp", "blk"),
            scatter_dimension=1,
            tiled=True,
        ),
        lax.psum_scatter(
            jnp.stack([gain_grad1, gain_grad2]), ("grp", "blk"), scatter_dimension=1, tiled=True
        ),
        lax.psum_scatter(
            jnp.stack([shift_grad1, shift_grad2]), ("grp", "blk"), scatter_dimension=1, tiled=True
        ),
        lax.psum_scatter(grad_w_in, ("grp", "blk"), scatter_dimension=0, tiled=True),
        lax.psum_scatter(grad_b_in, ("grp", "blk"), scatter_dimension=0, tiled=True),
        lax.psum_scatter(grad_w_down, ("grp", "blk"), scatter_dimension=0, tiled=True),
    )
    return (
        hidden_out,
        grad_input.astype(jnp.bfloat16),
        summed[0],
        summed[1],
        summed[2],
        summed[3],
        summed[4],
        summed[5],
        summed[6],
        summed[7],
        summed[8],
        summed[9],
    )


MESH = pl.DeviceIdType.MESH
LOW = jnp.bfloat16
HIGH = jnp.float32
CHIPS = 16
HALF = 8
BLOCK = 256
MASKED = -1e30
VMEM_LIMIT = 62 * 2**20
NT = ((1,), (1,))
TN = ((0,), (0,))


def dot(left, right, dims=((1,), (0,))):
    return lax.dot_general(left, right, (dims, ((), ())), preferred_element_type=HIGH)


def place():
    return lax.axis_index("grp"), lax.axis_index("blk")


def coordinates(chip):
    return lax.div(chip, 4), lax.rem(lax.div(chip, 2), 2), lax.rem(chip, 2)


def meet():
    core, chip = place()
    me = core * CHIPS + chip
    barrier = pltpu.get_barrier_semaphore()

    def greet(ahead, carry):
        other = lax.rem(me + ahead, 2 * CHIPS)
        pl.semaphore_signal(
            barrier,
            inc=1,
            device_id=(lax.div(other, CHIPS), lax.rem(other, CHIPS)),
            device_id_type=MESH,
        )
        return carry

    lax.fori_loop(1, 2 * CHIPS, greet, 0)
    pl.semaphore_wait(barrier, 2 * CHIPS - 1)


def remote(source, target, send, recv, device):
    return pltpu.make_async_remote_copy(
        src_ref=source,
        dst_ref=target,
        send_sem=send,
        recv_sem=recv,
        device_id=device,
        device_id_type=MESH,
    )


def local(source, target, sem):
    return pltpu.make_async_copy(source, target, sem)


def neighbours(across):
    core, chip = place()
    z, y, x = coordinates(chip)
    planes = (z + 1 - 2 * lax.rem(z, 2), 2 - lax.div(z, 2), 3 - 3 * lax.div(z, 2))

    def slot(far_p, far_q, line):
        far_y, far_x = (far_q, far_p) if across == "x" else (far_p, far_q)
        plane = z if line is None else planes[line]
        return plane * 4 + (1 - y if far_y else y) * 2 + (1 - x if far_x else x)

    return slot


class Shipments:
    def __init__(self, send, recv):
        self.send, self.recv, self.made = send, recv, []
        self.core = lax.axis_index("grp")

    def ship(self, source, target, recv_index, to):
        index = len(self.made)

        def make():
            return remote(
                source(), target(), self.send.at[index], self.recv.at[recv_index()], (self.core, to())
            )

        self.made.append(make)
        make().start()

    def landed(self, target, recv_index, near):
        remote(target, target, self.send.at[0], self.recv.at[recv_index], (self.core, near)).wait_recv()

    def all_sent(self):
        assert len(self.made) == 15
        for make in self.made:
            make().wait_send()


class Gather:
    def __init__(self, pick, send, recv, across):
        self.pick, self.at = pick, neighbours(across)
        self.moves = Shipments(send, recv)

    def ship(self, what, to):
        slot = lambda: self.at(*what)
        ref = lambda: self.pick(slot())
        self.moves.ship(ref, ref, slot, lambda: self.at(*to))

    def landed(self, *what):
        slot = self.at(*what)
        self.moves.landed(self.pick(slot), slot, self.at(1, 0, None))

    def own_line(self, line):
        self.ship((0, 0, None), (0, 0, line))

    def own_plane(self):
        self.ship((0, 0, None), (1, 0, None))
        self.ship((0, 0, None), (0, 1, None))

    def line(self, line):
        self.landed(0, 0, line)
        self.ship((0, 0, line), (1, 0, None))
        self.ship((0, 0, line), (0, 1, None))

    def side(self, line):
        self.landed(1, 0, line)
        self.ship((1, 0, line), (0, 1, None))

    def arrive(self):
        for line in (None, 0, 1, 2):
            for far_p in (0, 1):
                self.landed(far_p, 1, line)

    def finish(self):
        self.moves.all_sent()


class Reduce:
    def __init__(self, sent, own, pick, stages, send, recv, across):
        self.sent, self.own, self.pick, self.at = sent, own, pick, neighbours(across)
        self.first, self.second, self.third = stages
        self.moves = Shipments(send, recv)

    @staticmethod
    def number(line):
        return 3 if line is None else line

    def ship(self, source, target, index, to):
        self.moves.ship(source, target, lambda: index, lambda: self.at(*to))

    def landed(self, target, index):
        self.moves.landed(target, index, self.at(1, 0, None))

    def start(self, line):
        for far_p in (1, 0):
            index = self.number(line) * 2 + far_p
            self.ship(
                lambda far_p=far_p: self.pick(self.sent, self.at(far_p, 1, line)),
                lambda index=index: self.first.at[index],
                index,
                (0, 1, None),
            )

    def mine(self, *what):
        return self.pick(self.own, self.at(*what))[...].astype(HIGH)

    def side(self, line):
        number = self.number(line)
        index = number * 2 + 1
        self.landed(self.first.at[index], index)
        self.first[index] = (self.first[index].astype(HIGH) + self.mine(1, 0, line)).astype(LOW)
        self.ship(
            lambda: self.first.at[index], lambda: self.second.at[number], 8 + number, (1, 0, None)
        )

    def line(self, line):
        number = self.number(line)
        index = number * 2
        self.landed(self.first.at[index], index)
        self.landed(self.second.at[number], 8 + number)
        total = (
            self.first[index].astype(HIGH)
            + self.second[number].astype(HIGH)
            + self.mine(0, 0, line)
        )
        if line is None:
            return total
        self.first[index] = total.astype(LOW)
        ahead = lambda: lax.rem(lax.div(self.at(0, 0, None), 4) - lax.div(self.at(0, 0, line), 4) + 4, 4) - 1
        self.moves.ship(
            lambda: self.first.at[index],
            lambda: self.third.at[ahead()],
            lambda: 12 + ahead(),
            lambda: self.at(0, 0, line),
        )

    def finish(self, result):
        result[...] = self.line(None)
        for ahead in range(3):
            self.landed(self.third.at[ahead], 12 + ahead)
            result[...] += self.third[ahead].astype(HIGH)
        self.moves.all_sent()


def each(plans, act, *arguments):
    for plan in plans:
        act(plan, *arguments)


def to_tokens(source, target, send, recv):
    core, chip = place()
    to_core = lax.div(chip, HALF)
    mine = core * HALF + lax.rem(chip, HALF)
    here = to_core == core

    def copy_to(ahead):
        chip_to = lax.rem(chip + ahead, CHIPS)
        return remote(
            source.at[chip_to], target.at[mine], send.at[ahead], recv.at[mine], (to_core, chip_to)
        )

    pl.when(here)(lambda: local(source.at[chip], target.at[mine], recv.at[mine]).start())
    pl.when(jnp.logical_not(here))(lambda: copy_to(0).start())
    for ahead in range(1, CHIPS):
        copy_to(ahead).start()

    def arrive():
        for slot in range(CHIPS):
            local(source.at[slot], target.at[slot], recv.at[slot]).wait()

    def finish():
        pl.when(jnp.logical_not(here))(lambda: copy_to(0).wait_send())
        for ahead in range(1, CHIPS):
            copy_to(ahead).wait_send()

    return arrive, finish


def to_heads(source, target, send, recv):
    core, chip = place()
    here = lax.div(chip, HALF) == core

    def copy_to(group, ahead):
        head = lax.rem(chip + ahead, HALF)
        return remote(
            source.at[group * HALF + head],
            target.at[chip],
            send.at[group * HALF + ahead],
            recv.at[chip],
            (group, core * HALF + head),
        )

    def every(act):
        for group in range(2):
            for ahead in range(HALF):
                if ahead == 0:
                    itself = jnp.logical_and(here, core == group)
                    pl.when(jnp.logical_not(itself))(lambda: act(copy_to(group, 0)))
                else:
                    act(copy_to(group, ahead))

    pl.when(here)(
        lambda: local(
            source.at[core * HALF + lax.rem(chip, HALF)], target.at[chip], recv.at[chip]
        ).start()
    )
    every(lambda copy: copy.start())

    def arrive():
        for slot in range(CHIPS):
            local(source.at[slot], target.at[slot], recv.at[slot]).wait()

    return arrive, lambda: every(lambda copy: copy.wait_send())


def lanes(rows, width=128):
    return lax.broadcasted_iota(jnp.int32, (rows, width), 1)


def turn(values):
    return pltpu.roll(values, HD, 1)


def fold(rows_in):
    half = rows_in.shape[0] // 2
    both = jnp.where(lanes(half) < HD, rows_in[:half], turn(rows_in[half:]))
    pad = -half % 16
    if pad:
        both = jnp.concatenate([both, jnp.zeros((pad, 128), HIGH)], axis=0)
    return both.astype(LOW)


def column_sums(v):
    return jnp.sum(v, axis=0, keepdims=True)


def gelu_parts(pre):
    cdf = 0.5 * (1.0 + lax.erf(pre * math.sqrt(0.5)))
    density = jnp.exp(-0.5 * pre * pre) * (1.0 / math.sqrt(2.0 * math.pi))
    return pre * cdf, cdf + pre * density


def normalize(v, gain, shift):
    center = v - jnp.mean(v, axis=1, keepdims=True)
    inverse = lax.rsqrt(jnp.mean(center * center, axis=1, keepdims=True) + EPSILON)
    normed = center * inverse
    return normed * gain + shift, normed, inverse


def normalize_back(c, normed, inverse, gain):
    scaled = c * gain
    inner = (
        scaled
        - jnp.mean(scaled, axis=1, keepdims=True)
        - normed * jnp.mean(scaled * normed, axis=1, keepdims=True)
    )
    return inner * inverse


def at_steps(index, steps):
    for number, acts in steps.items():

        def run(acts=acts):
            for act in acts:
                act()

        pl.when(index == number)(run)


def columns_of(half, width):
    return pl.ds(pl.multiple_of(half * width, 128), width)


LABEL_AT, BRANCH_AT, GAIN_AT, SHIFT_AT, BIAS_AT = 0, 256, 384, 512, 640


def first_kernel(names, *refs):
    r = types.SimpleNamespace(**dict(zip(names, refs)))
    hidden, x_all, w_all, rel_all = r.hidden_in, r.x_vmem, r.w_all, r.rel_all
    token_rows, width = hidden.shape
    total = x_all.shape[0]
    slot_rows = total // CHIPS
    depth = r.out_weight.shape[0]
    w_in, w_down, w_out, w_qkv = r.w_in, r.w_down, r.w_out, r.w_qkv
    half_hidden = w_in.shape[3]
    half_width = width // 2
    core, chip = place()
    other = 1 - core
    me = core * CHIPS + chip
    keep = r.keep_sem

    loads = [
        local(r.ffn_in.at[:, columns_of(core, half_hidden)], w_in.at[core, chip], keep.at[0]),
        local(r.ffn_out, w_down.at[chip], keep.at[1]),
        local(r.out_weight, w_out.at[chip], keep.at[2]),
        local(r.qkv_any.at[:, :, columns_of(core, half_width)], w_qkv.at[:, core, chip], keep.at[3]),
    ]
    for copy in loads:
        copy.start()

    own_slot = pl.ds(pl.multiple_of(chip * slot_rows, 16), slot_rows)
    extra = r.extra
    extra[...] = jnp.zeros_like(extra)
    extra[0:1, 0:256] = jnp.full((1, 256), 4.0, HIGH)
    extra[0:1, 0:token_rows] = r.segment_ids[...].astype(HIGH)
    extra[1:2, 0:token_rows] = r.order_ids[...].astype(HIGH)
    extra[2:4, 0:token_rows] = r.box_ids[...].astype(HIGH)
    for start, pair in ((BRANCH_AT, r.branch_bias), (GAIN_AT, r.norm_gains), (SHIFT_AT, r.norm_shifts)):
        extra[0:2, start : start + depth] = pair[...].astype(HIGH)
    extra[0:1, BIAS_AT : BIAS_AT + 128] = r.ffn_in_bias[...].astype(HIGH)
    tail = token_rows - token_rows % 16
    x_own = r.x_own
    x_own[0:tail, :] = hidden[0:tail, :]
    x_own[tail:slot_rows, :] = jnp.concatenate(
        [hidden[tail:token_rows, :].astype(HIGH), extra[...]], axis=0
    ).astype(LOW)
    weight = r.qkv_weight
    w_own = r.w_own
    lane_depth = lanes(depth) < HD
    for pair in range(H // 2):
        columns = slice(pair * 128, pair * 128 + 128)
        query, key, value = (weight[n, :, columns].astype(HIGH) for n in range(3))
        w_own[2 * pair, :, 0:128] = jnp.where(lane_depth, query, turn(value)).astype(LOW)
        w_own[2 * pair + 1, :, 0:128] = jnp.where(lane_depth, turn(query), value).astype(LOW)
        w_own[2 * pair, :, 128:256] = jnp.where(lane_depth, key, 0.0).astype(LOW)
        w_own[2 * pair + 1, :, 128:256] = jnp.where(lane_depth, turn(key), 0.0).astype(LOW)
    rel_own = r.rel_own
    eye_depth = (
        lax.broadcasted_iota(jnp.int32, (depth, depth), 0)
        == lax.broadcasted_iota(jnp.int32, (depth, depth), 1)
    ).astype(LOW)
    for kind in range(3):
        rel_own[:, kind * NB : (kind + 1) * NB] = dot(eye_depth, r.rel_tables[kind], NT).astype(LOW)
    bias_columns = dot(eye_depth, r.qkv_bias[...], NT)
    rel_own[:, 3 * NB : 4 * NB] = jnp.where(
        lanes(depth) == 0, bias_columns[:, 0:1], jnp.where(lanes(depth) == 1, bias_columns[:, 1:2], 0.0)
    ).astype(LOW)
    own_x = local(x_own, x_all.at[own_slot], keep.at[4])
    own_w = local(w_own.at[chip], w_all.at[me], keep.at[5])
    own_x.start()
    own_w.start()
    meet()

    to_chip = lax.div(me, 2)
    parity = lax.rem(chip, 2)
    rel_slot = rel_all.at[pl.ds(parity * depth, depth)]

    def rel_each(act_remote, act_own):
        for to_core in range(2):
            itself = jnp.logical_and(to_chip == chip, core == to_core)
            copy = lambda: remote(
                rel_own, rel_slot, r.rel_send.at[to_core], r.rel_recv.at[parity], (to_core, to_chip)
            )
            pl.when(jnp.logical_not(itself))(lambda: act_remote(copy()))
            if act_own is not None:
                pl.when(itself)(act_own)

    rel_each(
        lambda copy: copy.start(), lambda: local(rel_own, rel_slot, r.rel_recv.at[parity]).start()
    )

    def w_copy(ahead):
        to = lax.rem(chip + ahead, CHIPS)
        return remote(
            w_own.at[to], w_all.at[me], r.w_send.at[ahead], r.w_recv.at[chip], (core, to)
        )

    half = width // 2

    def pick_x(part):
        return lambda slot: x_all.at[
            pl.ds(pl.multiple_of(slot * slot_rows, 16), slot_rows), pl.ds(part * half, half)
        ]

    x_plans = [
        Gather(pick_x(part), r.x_send.at[part], r.x_recv.at[part], across)
        for part, across in enumerate("xy")
    ]

    own_x.wait()
    each(x_plans, Gather.own_line, 0)
    each(x_plans, Gather.own_plane)
    for ahead in range(1, CHIPS):
        w_copy(ahead).start()
    each(x_plans, Gather.own_line, 1)
    each(x_plans, Gather.own_line, 2)
    swaps = [
        remote(
            r.ffn_in.at[:, columns_of(other, half_hidden)],
            w_in.at[core, chip],
            r.pair_send.at[0],
            r.pair_recv.at[0],
            (other, chip),
        ),
        remote(
            r.qkv_any.at[:, :, columns_of(other, half_width)],
            w_qkv.at[:, core, chip],
            r.pair_send.at[1],
            r.pair_recv.at[1],
            (other, chip),
        ),
    ]
    for copy in swaps:
        copy.start()
    each(x_plans, Gather.side, None)
    for line in range(3):
        each(x_plans, Gather.line, line)
        each(x_plans, Gather.side, line)

    plan_out = Gather(lambda slot: w_out.at[slot], r.out_send, r.out_recv, "x")
    plan_in = Gather(lambda slot: w_in.at[:, slot], r.in_send, r.in_recv, "x")
    plan_down = Gather(lambda slot: w_down.at[slot], r.down_send, r.down_recv, "y")
    plan_qkv = Gather(lambda slot: w_qkv.at[:, :, slot], r.qkv_send, r.qkv_recv, "y")
    plans = (plan_out, plan_in, plan_down)
    for copy in loads:
        copy.wait()
    for copy in swaps:
        copy.wait()
    each(plans, Gather.own_line, 0)
    each(plans, Gather.own_plane)
    each(plans, Gather.own_line, 1)
    each(plans, Gather.own_line, 2)

    own_w.wait()
    for ahead in range(1, CHIPS):
        came = lax.rem(chip + ahead, CHIPS)
        remote(
            w_own.at[0], w_all.at[core * CHIPS + came], r.w_send.at[0], r.w_recv.at[came], (core, came)
        ).wait_recv()
    mine = w_all.at[pl.ds(core * CHIPS, CHIPS)]
    pair_w = remote(mine, mine, r.pair_send.at[2], r.pair_recv.at[2], (other, chip))
    pair_w.start()
    for slot in range(2):
        local(rel_own, rel_all.at[pl.ds(slot * depth, depth)], r.rel_recv.at[slot]).wait()
    each(x_plans, Gather.arrive)
    keep_x = local(x_all, r.x_out, keep.at[6])
    keep_x.start()
    keep_rel = local(rel_all, r.rel_out, keep.at[7])
    keep_rel.start()

    meta, shares, bias_in = r.meta, r.shares, r.bias_in
    eye = (
        lax.broadcasted_iota(jnp.int32, (slot_rows, 256), 0)
        == lax.broadcasted_iota(jnp.int32, (slot_rows, 256), 1)
    ).astype(LOW)
    shares[core] = jnp.zeros(shares.shape[1:], HIGH)
    for slot in range(CHIPS):
        end = (slot + 1) * slot_rows
        labels = x_all[end - 16 : end, 0:256]
        meta[end - slot_rows : end, 0:16] = dot(eye, labels, NT)
        small = x_all[end - 16 : end, BRANCH_AT:768].astype(HIGH)[8:16]
        target = slice(slot * depth // 128 * 128, slot * depth // 128 * 128 + 128)
        for number in range(3):
            piece = jnp.where(lanes(8) < depth, small[:, number * 128 : number * 128 + 128], 0.0)
            if slot * depth % 128:
                piece = pltpu.roll(piece, slot * depth % 128, 1)
            shares[core, number, :, target] += piece
        bias_in[:, slot * 128 : slot * 128 + 128] = small[0:1, 384:512]
    pair_small = remote(
        shares.at[core], shares.at[core], r.pair_send.at[3], r.pair_recv.at[3], (other, chip)
    )
    pair_small.start()
    rel = rel_all[...]
    table_t = rel[:, 0 : 3 * NB]
    extra_columns = rel[:, 3 * NB : 4 * NB].astype(HIGH)
    row_at = lax.broadcasted_iota(jnp.int32, (2 * depth, 128), 0)
    column_at = lanes(2 * depth)
    bias = column_sums(
        jnp.where(row_at == column_at, extra_columns[:, 0:1], 0.0)
        + jnp.where(row_at + 2 * depth == column_at, extra_columns[:, 1:2], 0.0)
    )
    lane = lanes(BLOCK)
    first_half = lane < HD
    scale = 1.0 / math.sqrt(4.0 * HD)
    left, right, right_t = r.left, r.right, r.right_t
    value, value_t, kept = r.value, r.value_t, r.kept
    pair_w.wait()

    def prepare(index, carry):
        rows = pl.ds(pl.multiple_of(index * BLOCK, BLOCK), BLOCK)
        at_steps(
            index,
            {
                3: [lambda: each(plans, Gather.side, None)],
                7: [lambda: each(plans, Gather.line, 0)],
            },
        )
        projected = dot(x_all[rows, :], w_all[...].reshape(width, 4 * HD))
        query_value = (projected[:, 0:128] + bias).astype(LOW).astype(HIGH)
        key = projected[:, 128:256].astype(LOW).astype(HIGH)
        query = query_value[:, 0:HD].astype(LOW)
        tables = dot(query, table_t).astype(LOW).astype(HIGH)
        ids = meta[rows, 8:12].astype(jnp.int32)
        segment, order, box_x, box_y = ids[:, 0:1], ids[:, 1:2], ids[:, 2:3], ids[:, 3:4]

        def selected(column, ids_of, values):
            bucket = jnp.clip(ids_of - values, -(NB // 2), NB // 2 - 1) + NB // 2
            return jnp.take_along_axis(tables[:, column * NB : (column + 1) * NB], bucket, axis=1)

        wide = selected(0, order, lane)
        narrow = jnp.where(first_half, selected(1, box_x, lane), selected(2, box_y, lane - HD))
        label = lane - HD
        query_side = jnp.where(
            first_half,
            query_value * scale,
            jnp.where(jnp.logical_and(label != segment, label < 8), MASKED, 0.0),
        )
        key_side = jnp.where(first_half, key, (label == segment).astype(HIGH))
        left[rows, 0:128] = (wide * scale).astype(LOW)
        left[rows, 128:256] = (narrow * scale).astype(LOW)
        left[rows, 256:384] = query_side.astype(LOW)
        order_hot = (lane == order).astype(HIGH)
        box_hot = (jnp.where(first_half, box_x, box_y + HD) == lane).astype(HIGH)
        right[rows, 0:128] = order_hot.astype(LOW)
        right[rows, 128:256] = box_hot.astype(LOW)
        right[rows, 256:384] = key_side.astype(LOW)
        right_t[0:128, rows] = order_hot.T.astype(LOW)
        right_t[128:256, rows] = box_hot.T.astype(LOW)
        right_t[256:384, rows] = key_side.T.astype(LOW)
        held = jnp.where(first_half, turn(query_value), (label == 0).astype(HIGH))
        value[rows, :] = held.astype(LOW)
        value_t[:, rows] = held.T.astype(LOW)
        return carry

    lax.fori_loop(0, total // BLOCK, prepare, 0)
    stash = [
        local(held, out, keep.at[8 + k])
        for k, (held, out) in enumerate(
            (
                (left, r.left_out),
                (right, r.right_out),
                (right_t, r.right_t_out),
                (value_t, r.value_t_out),
            )
        )
    ]
    for copy in stash:
        copy.start()

    def attend(index, carry):
        rows = pl.ds(pl.multiple_of(index * BLOCK, BLOCK), BLOCK)
        at_steps(
            index,
            {
                1: [lambda: each(plans, Gather.side, 0)],
                4: [lambda: each(plans, Gather.line, 1)],
                7: [lambda: each(plans, Gather.side, 1)],
            },
        )
        logits = dot(left[rows, :], right_t[...])
        top = jnp.max(logits, axis=1, keepdims=True)
        weights = jnp.exp(logits - top).astype(LOW)
        mixed = dot(weights, value[...])
        row_sum = mixed[:, HD : HD + 1]
        ids = meta[rows, 8:12]
        facts = jnp.where(lane == HD, top + jnp.log(row_sum), ids[:, 3:4])
        facts = jnp.where(lane == HD + 1, ids[:, 1:2], facts)
        facts = jnp.where(lane == HD + 2, ids[:, 2:3], facts)
        kept[rows, :] = jnp.where(first_half, mixed / row_sum, facts)
        return carry

    lax.fori_loop(0, total // BLOCK, attend, 0)
    keep_facts = local(kept, r.kept_out, keep.at[12])
    keep_facts.start()
    message, context_in = r.message, r.context_in
    for slot in range(CHIPS):
        message[slot] = fold(kept[slot * slot_rows : (slot + 1) * slot_rows, :])
    context_arrives, context_sent = to_tokens(message, context_in, r.msg_send, r.msg_recv)
    each(plans, Gather.line, 2)
    each(plans, Gather.side, 2)
    plan_qkv.own_line(0)
    plan_qkv.own_plane()
    plan_qkv.own_line(1)
    plan_qkv.own_line(2)
    context_arrives()
    pair_small.wait()

    vectors = [
        [jnp.concatenate([shares[0, number, k : k + 1], shares[1, number, k : k + 1]], axis=1) for k in range(2)]
        for number in range(3)
    ]
    branch_bias, gains, shifts = vectors
    context_wide, context, low_first = r.context_wide, r.context, r.low_first
    act, slope, d_second, d_inner, d_branch = r.act, r.slope, r.d_second, r.d_inner, r.d_branch
    out_part, in_part, g_small = r.out_part, r.in_part, r.g_small
    own = pl.ds(pl.multiple_of(core * slot_rows, 16), slot_rows)
    far = pl.ds(pl.multiple_of(other * slot_rows, 16), slot_rows)
    tile = 512
    half_slot = slot_rows // 2
    count = [4]

    def swap(source, target):
        copy = remote(
            source, target, r.pair_send.at[count[0]], r.pair_recv.at[count[0]], (other, chip)
        )
        count[0] += 1
        copy.start()
        return copy

    left_half = lanes(half_slot) < HD
    for group in range(2):
        for pair in range(HALF // 2):
            even = context_in[group * HALF + 2 * pair].astype(HIGH)[:half_slot]
            odd = context_in[group * HALF + 2 * pair + 1].astype(HIGH)[:half_slot]
            top = group * slot_rows
            columns = slice(pair * 128, pair * 128 + 128)
            context_wide[top : top + half_slot, columns] = jnp.where(left_half, even, turn(odd))
            context_wide[top + half_slot : top + slot_rows, columns] = jnp.where(
                left_half, turn(even), odd
            )
    context[...] = context_wide[...].astype(LOW)

    def product(index, lhs, rhs):
        out_part[index] = dot(lhs[far, :], rhs)
        copy = swap(out_part.at[index], in_part.at[index])
        mine = dot(lhs[own, :], rhs)
        copy.wait()
        return mine + in_part[index]

    plan_out.arrive()
    branch = product(0, context, w_out[...].reshape(half_width, width)) + branch_bias[0]
    row_index = lax.broadcasted_iota(jnp.int32, (slot_rows, 1), 0)
    tokens = row_index < token_rows
    x_mine = jnp.where(tokens, x_own[...].astype(HIGH), 0.0)
    first, normed1, inverse1 = normalize(x_mine + branch, gains[0], shifts[0])
    low_first[own, :] = first.astype(LOW)
    copy = swap(low_first.at[own], low_first.at[own])
    plan_qkv.side(None)
    plan_in.arrive()
    copy.wait()

    def widen(index, carry):
        columns = pl.ds(pl.multiple_of(index * tile, tile), tile)
        pre = dot(low_first[...], w_in[:, :, :, columns].reshape(width, tile)) + bias_in[:, columns]
        found, derivative = gelu_parts(pre)
        act[:, columns] = found.astype(LOW)
        slope[:, columns] = derivative
        return carry

    lax.fori_loop(0, half_hidden // tile, widen, 0)
    plan_down.arrive()
    second = product(1, act, w_down[...].reshape(half_hidden, width)) + branch_bias[1]
    plan_qkv.line(0)
    plan_qkv.side(0)
    result, normed2, inverse2 = normalize(first + second, gains[1], shifts[1])
    r.hidden_out[...] = result[:token_rows].astype(LOW)
    given = r.out_grad
    upstream = jnp.concatenate(
        [given[...].astype(HIGH), jnp.zeros((slot_rows - token_rows, width), HIGH)], axis=0
    )
    d_sum2 = normalize_back(upstream, normed2, inverse2, gains[1])
    low_second = d_sum2.astype(LOW)
    d_second[own, :] = low_second
    copy = swap(d_second.at[own], d_second.at[own])
    g_small[...] = jnp.zeros_like(g_small)
    g_small[1:2, 0:width] = column_sums(low_second.astype(HIGH))
    g_small[3:4, 0:width] = column_sums(upstream * normed2)
    g_small[5:6, 0:width] = column_sums(upstream)
    plan_qkv.line(1)
    plan_qkv.side(1)
    copy.wait()
    g_down, g_in, g_out = r.g_down, r.g_in, r.g_out

    def narrow_back(index, carry):
        columns = pl.ds(pl.multiple_of(index * tile, tile), tile)
        down = w_down[pl.ds(index * (tile // 128), tile // 128)].reshape(tile, width)
        low = (dot(d_second[...], down, NT) * slope[:, columns]).astype(LOW)
        d_inner[:, columns] = low
        g_small[pl.ds(8, 1), columns] = column_sums(low.astype(HIGH))
        g_down[columns, :] = dot(act[:, columns], d_second[...], TN).astype(LOW)
        return carry

    lax.fori_loop(0, half_hidden // tile, narrow_back, 0)
    keep_down = local(g_down, r.g_down_out, keep.at[13])
    keep_down.start()
    plan_qkv.line(2)
    plan_qkv.side(2)
    w_in_all = w_in[...].reshape(width, half_hidden)
    out_part[2] = dot(d_inner[far, :], w_in_all, NT)
    copy = swap(out_part.at[2], in_part.at[2])
    mine = dot(d_inner[own, :], w_in_all, NT)

    def widen_grad(index, carry):
        rows = pl.ds(pl.multiple_of(index * 256, 256), 256)
        g_in[rows, :] = dot(low_first[:, rows], d_inner[...], TN).astype(LOW)
        return carry

    lax.fori_loop(0, width // 256, widen_grad, 0)
    keep_in = local(g_in, r.g_in_out, keep.at[14])
    keep_in.start()
    copy.wait()
    d_first = d_sum2 + mine + in_part[2]
    d_sum1 = normalize_back(d_first, normed1, inverse1, gains[0])
    r.d_sum1[...] = d_sum1
    low_branch = d_sum1.astype(LOW)
    d_branch[own, :] = low_branch
    copy = swap(d_branch.at[own], d_branch.at[own])
    g_small[0:1, 0:width] = column_sums(low_branch.astype(HIGH))
    g_small[2:3, 0:width] = column_sums(d_first * normed1)
    g_small[4:5, 0:width] = column_sums(d_first)
    copy.wait()
    w_out_all = w_out[...].reshape(half_width, width)
    context_wide[...] = dot(d_branch[...], w_out_all, NT)
    for group in range(2):
        for pair in range(HALF // 2):
            both = context_wide[
                group * slot_rows : (group + 1) * slot_rows, pair * 128 : pair * 128 + 128
            ]
            r.d_message[group * HALF + 2 * pair] = fold(both)
            r.d_message[group * HALF + 2 * pair + 1] = fold(turn(both))
    g_out[...] = dot(context[...], d_branch[...], TN).astype(LOW)
    plan_qkv.arrive()
    keep_qkv = local(w_qkv, r.w_qkv_out, keep.at[15])
    keep_qkv.start()

    for ahead in range(1, CHIPS):
        w_copy(ahead).wait_send()
    rel_each(lambda copy: copy.wait_send(), None)
    context_sent()
    each(x_plans, Gather.finish)
    each(plans + (plan_qkv,), Gather.finish)
    for copy in stash + [keep_x, keep_rel, keep_facts, keep_down, keep_in, keep_qkv]:
        copy.wait()


def second_kernel(names, *refs):
    r = types.SimpleNamespace(**dict(zip(names, refs)))
    core, chip = place()
    other = 1 - core
    left, right, right_t, value_t, kept = r.left, r.right, r.right_t, r.value_t, r.kept
    rel_all, x_all, w_qkv = r.rel_all, r.x_all, r.w_qkv
    g_in, g_down, g_out = r.g_in, r.g_down, r.g_out
    total, width = x_all.shape
    slot_rows = total // CHIPS
    half_slot = slot_rows // 2
    half_width = width // 2
    depth = w_qkv.shape[3]
    token_rows = r.hidden_grad.shape[0]
    scale = 1.0 / math.sqrt(4.0 * HD)
    keep = r.keep_sem
    loads = [
        local(there, held, keep.at[k])
        for k, (there, held) in enumerate(
            (
                (r.left_any, left),
                (r.right_t_any, right_t),
                (r.value_t_any, value_t),
                (r.kept_any, kept),
                (r.right_any, right),
                (r.g_down_any, g_down),
                (r.g_in_any, g_in),
                (r.g_out_any, g_out),
                (r.x_all_any, x_all),
                (r.w_qkv_any, w_qkv),
            )
        )
    ]
    for copy in loads:
        copy.start()
    meet()
    d_arrived = r.d_arrived
    grad_arrives, grad_sent = to_heads(r.d_message, d_arrived, r.d_send, r.d_recv)
    plan_down = Reduce(
        r.g_down_any,
        g_down,
        lambda ref, slot: ref.at[slot],
        [r.down_1, r.down_2, r.down_3],
        r.down_send,
        r.down_recv,
        "y",
    )
    plan_in = Reduce(
        r.g_in_any,
        g_in,
        lambda ref, slot: ref.at[:, slot],
        [r.in_1, r.in_2, r.in_3],
        r.in_send,
        r.in_recv,
        "x",
    )
    plan_out = Reduce(
        r.g_out_any,
        g_out,
        lambda ref, slot: ref.at[slot],
        [r.out_1, r.out_2, r.out_3],
        r.out_send,
        r.out_recv,
        "y",
    )
    plans = (plan_down, plan_in, plan_out)

    each(plans, Reduce.start, 2)
    each(plans, Reduce.start, 1)

    z, y, x = coordinates(chip)
    small_sum, small_in = r.small_sum, r.small_in
    small_sum[...] = r.g_small[...]

    def small_copy(index, to_core, to_chip):
        return remote(
            small_sum, small_in.at[index], r.small_send.at[index], r.small_recv.at[index], (to_core, to_chip)
        )

    def small_turn(index):
        if index == 0:
            return [small_copy(0, other, chip)]
        if index == 1:
            return [small_copy(1, core, z * 4 + (1 - y) * 2 + x)]
        if index == 2:
            return [small_copy(2, core, z * 4 + y * 2 + 1 - x)]
        return [
            small_copy(2 + ahead, core, lax.rem(z + ahead, 4) * 4 + y * 2 + x) for ahead in (1, 2, 3)
        ]

    def small_start(index):
        for copy in small_turn(index):
            copy.start()

    def small_end(index):
        for copy in small_turn(index):
            copy.wait()
        if index == 0:
            small_sum[0:8, :] += small_in[0, 0:8, :]
        elif index < 3:
            small_sum[...] += small_in[index]

    small_start(0)
    left_half = lanes(half_slot) < HD
    d_context = r.d_context
    grad_arrives()
    for slot in range(CHIPS):
        both = d_arrived[slot].astype(HIGH)[:half_slot]
        top = slot * slot_rows
        d_context[top : top + half_slot, :] = jnp.where(left_half, both, 0.0)
        d_context[top + half_slot : top + slot_rows, :] = jnp.where(left_half, turn(both), 0.0)
    table_t = rel_all[:, 0 : 3 * NB]
    lane = lanes(BLOCK)
    first_half = lane < HD
    d_query, d_query_t, d_pair_t, rel_grad = r.d_query, r.d_query_t, r.d_pair_t, r.rel_grad
    d_pair_t[...] = jnp.zeros_like(d_pair_t)
    rel_grad[...] = jnp.zeros_like(rel_grad)
    for copy in loads:
        copy.wait()

    def step(index, carry):
        rows = pl.ds(pl.multiple_of(index * BLOCK, BLOCK), BLOCK)
        at_steps(
            index,
            {
                1: [
                    lambda: each(plans, Reduce.side, 2),
                    lambda: each(plans, Reduce.start, 0),
                    lambda: small_end(0),
                    lambda: small_start(1),
                ],
                2: [lambda: each(plans, Reduce.line, 2)],
                4: [
                    lambda: each(plans, Reduce.side, 1),
                    lambda: each(plans, Reduce.start, None),
                    lambda: small_end(1),
                    lambda: small_start(2),
                ],
                5: [lambda: each(plans, Reduce.line, 1)],
                7: [lambda: each(plans, Reduce.side, 0), lambda: small_end(2), lambda: small_start(3)],
                8: [lambda: each(plans, Reduce.line, 0)],
            },
        )
        facts = kept[rows, :]
        grad = d_context[rows, :]
        delta = jnp.sum(grad * facts, axis=1, keepdims=True)
        probs = jnp.exp(dot(left[rows, :], right_t[...]) - facts[:, HD : HD + 1])
        d_probs = dot(grad.astype(LOW), value_t[...])
        d_logits = (probs * (d_probs - delta)).astype(LOW)
        query_t = jnp.where(first_half, left[rows, 256:384].astype(HIGH), 0.0).T[0:HD]
        d_pair_t[0:HD, :] += dot(grad.T[0:HD].astype(LOW), probs.astype(LOW))
        d_pair_t[HD : 2 * HD, :] += dot(query_t.astype(LOW), d_logits)
        back = dot(d_logits, right[...]) * scale
        ids = facts.astype(jnp.int32)
        order, box_x, box_y = (ids[:, HD + k : HD + k + 1] for k in (1, 2, 3))

        def placed(column, ids_of, extent, start):
            found_at = ids_of + NB // 2 - lane
            found = jnp.take_along_axis(
                back[:, column * 128 : column * 128 + 128], jnp.clip(found_at, 0, extent - 1) + start, axis=1
            )
            return jnp.where(jnp.logical_and(found_at >= 0, found_at < extent), found, 0.0)

        wide = back[:, 0:128]
        low_end = jnp.sum(jnp.where(lane >= order + NB // 2, wide, 0.0), axis=1, keepdims=True)
        high_end = jnp.sum(jnp.where(lane <= order - (NB // 2 - 1), wide, 0.0), axis=1, keepdims=True)
        first = placed(0, order, ORDER_RANGE, 0)
        first = jnp.where(lane == 0, low_end, jnp.where(lane == NB - 1, high_end, first))
        d_tables = jnp.concatenate(
            [first, placed(1, box_x, BOX_RANGE, 0), placed(1, box_y, BOX_RANGE, BOX_RANGE)], axis=1
        ).astype(LOW)
        from_tables = dot(d_tables, table_t, NT)
        d_query[rows, :] = jnp.where(
            first_half,
            back[:, 256:384] + jnp.concatenate([from_tables, from_tables], axis=1),
            0.0,
        )
        d_query_t[0:HD, rows] = d_query[rows, :].T[0:HD].astype(LOW)
        rel_grad[:, 0 : 3 * NB] += dot((query_t / scale).astype(LOW), d_tables)
        return carry

    lax.fori_loop(0, total // BLOCK, step, 0)
    message = r.message
    slot_lane = lanes(slot_rows) < HD
    for slot in range(CHIPS):
        top = slot * slot_rows
        if slot % 8 == 0:
            turned = d_pair_t[:, top : top + 8 * slot_rows].T
        pair = turned[(slot % 8) * slot_rows : (slot % 8 + 1) * slot_rows]
        message[slot, 0:slot_rows, :] = jnp.where(
            slot_lane, d_query[top : top + slot_rows, :], pair
        ).astype(LOW)
        message[slot, slot_rows:, :] = fold(pair)
    tokens_in = r.tokens_in
    tokens_arrive, tokens_sent = to_tokens(message, tokens_in, r.msg_send, r.msg_recv)
    each(plans, Reduce.side, None)

    d_query_t[HD : 3 * HD, :] = d_pair_t[...].astype(LOW)
    d_columns = d_query_t[...]
    sums = jnp.sum(d_columns[0 : 2 * HD].astype(HIGH), axis=1, keepdims=True)
    rel_grad[:, 3 * NB : 4 * NB] = jnp.where(
        lanes(HD) == 0, sums[0:HD], jnp.where(lanes(HD) == 1, sums[HD : 2 * HD], 0.0)
    )
    rel_far, rel_sum = r.rel_far, r.rel_sum
    rel_rows = pl.ds(pl.multiple_of(other * depth, 8), depth)
    rel_pair = remote(
        rel_grad.at[rel_rows], rel_far, r.pair_send.at[0], r.pair_recv.at[0], (other, chip)
    )
    rel_pair.start()
    w_mine, w_far, w_low, w_came = r.w_mine, r.w_far, r.w_low, r.w_came
    w_grad = dot(d_columns, x_all[...])
    for part in range(2):
        w_mine[part] = w_grad[:, part * half_width : (part + 1) * half_width]
    w_pair = remote(
        w_mine.at[other], w_far, r.pair_send.at[1], r.pair_recv.at[1], (other, chip)
    )
    w_pair.start()
    rel_pair.wait()
    rel_sum[...] = rel_grad[pl.ds(pl.multiple_of(core * depth, 8), depth), :] + rel_far[...]
    rel_to = (lax.div(chip, HALF), lax.rem(2 * chip + core, CHIPS))
    rel_here = jnp.logical_and(rel_to[0] == core, rel_to[1] == chip)
    rel_came = r.rel_came
    rel_copy = lambda: remote(rel_sum, rel_came, r.rel_send.at[0], r.rel_recv.at[0], rel_to)
    own_rel = lambda: local(rel_sum, rel_came, r.rel_recv.at[0])
    pl.when(rel_here)(lambda: own_rel().start())
    pl.when(jnp.logical_not(rel_here))(lambda: rel_copy().start())
    w_pair.wait()
    w_sum = (w_mine[core] + w_far[...]).T
    w_low[...] = jnp.zeros_like(w_low)
    for slot in range(CHIPS):
        w_low[slot, :, 0 : 3 * HD] = w_sum[slot * depth : (slot + 1) * depth].astype(LOW)

    def w_copy(ahead):
        to = lax.rem(chip + ahead, CHIPS)
        return remote(w_low.at[to], w_came.at[chip], r.w_send.at[ahead], r.w_recv.at[chip], (core, to))

    own_w = local(w_low.at[chip], w_came.at[chip], keep.at[10])
    own_w.start()
    for ahead in range(1, CHIPS):
        w_copy(ahead).start()

    wide, low = r.wide, r.low
    tokens_arrive()
    for group in range(2):
        top = group * slot_rows
        for pair in range(HALF // 2):
            columns = slice(pair * 128, pair * 128 + 128)
            even = tokens_in[group * HALF + 2 * pair].astype(HIGH)
            odd = tokens_in[group * HALF + 2 * pair + 1].astype(HIGH)
            even_main, odd_main = even[:slot_rows], odd[:slot_rows]
            low[0, top : top + slot_rows, columns] = jnp.where(
                slot_lane, even_main, turn(odd_main)
            ).astype(LOW)
            low[1, top : top + slot_rows, columns] = jnp.where(
                slot_lane, turn(even_main), odd_main
            ).astype(LOW)
            even_last = even[slot_rows : slot_rows + half_slot]
            odd_last = odd[slot_rows : slot_rows + half_slot]
            wide[top : top + half_slot, columns] = jnp.where(left_half, even_last, turn(odd_last))
            wide[top + half_slot : top + slot_rows, columns] = jnp.where(
                left_half, turn(even_last), odd_last
            )
    low[2] = wide[...].astype(LOW)
    own = pl.ds(pl.multiple_of(core * slot_rows, 16), slot_rows)
    far = pl.ds(pl.multiple_of(other * slot_rows, 16), slot_rows)
    weights = [w_qkv[n].reshape(width, half_width) for n in range(3)]

    def part(rows):
        return (
            dot(low[0, rows, :], weights[0], NT)
            + dot(low[1, rows, :], weights[1], NT)
            + dot(low[2, rows, :], weights[2], NT)
        )

    out_part, in_part = r.out_part, r.in_part
    out_part[...] = part(far)
    x_pair = remote(out_part, in_part, r.pair_send.at[2], r.pair_recv.at[2], (other, chip))
    x_pair.start()
    mine = part(own) + r.d_sum1[...]
    x_pair.wait()
    r.hidden_grad[...] = (mine + in_part[...])[:token_rows].astype(LOW)

    plan_down.finish(r.down_grad)
    in_total, in_far = r.in_total, r.in_far
    plan_in.finish(in_total)
    in_pair = remote(
        in_total.at[other], in_far, r.pair_send.at[3], r.pair_recv.at[3], (other, chip)
    )
    in_pair.start()
    plan_out.finish(r.out_grad)
    half_hidden = in_total.shape[2]
    in_grad = r.in_grad
    in_grad[:, columns_of(core, half_hidden)] = in_total[core]
    small_end(3)
    me = core * CHIPS + chip
    small_all = lambda rows, columns: (
        small_sum[rows, columns] + small_in[3, rows, columns] + small_in[4, rows, columns] + small_in[5, rows, columns]
    )
    strip = columns_of(lax.div(me * depth, 128), 128)
    shares = pltpu.roll(small_all(pl.ds(0, 8), strip), 128 - lax.rem(me * depth, 128), 1)
    for number, result in enumerate((r.branch_grad, r.gain_grad, r.shift_grad)):
        result[...] = shares[2 * number : 2 * number + 2, 0:depth]
    r.bias_grad[...] = small_all(pl.ds(8, 1), columns_of(chip, 128))
    own_rel().wait()
    pl.when(jnp.logical_not(rel_here))(lambda: rel_copy().wait_send())
    tables = rel_came[...].T
    for kind in range(3):
        r.rel_tables_grad[kind] = tables[kind * NB : (kind + 1) * NB]
    r.qkv_bias_grad[...] = tables[3 * NB : 3 * NB + 2]
    own_w.wait()
    for ahead in range(1, CHIPS):
        came = lax.rem(chip + ahead, CHIPS)
        remote(w_low.at[0], w_came.at[came], r.w_send.at[0], r.w_recv.at[came], (core, came)).wait_recv()
        w_copy(ahead).wait_send()
    lane_depth = lanes(depth) < HD
    for pair in range(H // 2):
        columns = slice(pair * 128, pair * 128 + 128)
        even = w_came[2 * pair].astype(HIGH)
        odd = w_came[2 * pair + 1].astype(HIGH)
        w_out = r.qkv_grad
        w_out[0, :, columns] = jnp.where(lane_depth, even[:, 0:128], turn(odd[:, 0:128]))
        w_out[2, :, columns] = jnp.where(lane_depth, turn(even[:, 0:128]), odd[:, 0:128])
        w_out[1, :, columns] = jnp.where(lane_depth, even[:, 128:256], turn(odd[:, 128:256]))
    in_pair.wait()
    in_grad[:, columns_of(other, half_hidden)] = in_far[...]
    grad_sent()
    tokens_sent()


def call(kernel, name, number, inputs, outputs, scratch):
    names = list(inputs) + list(outputs) + list(scratch)
    results = pl.pallas_call(
        functools.partial(kernel, names),
        out_shape=[jax.ShapeDtypeStruct(shape, dtype) for shape, dtype, _ in outputs.values()],
        in_specs=[pl.BlockSpec(memory_space=space) for _, space in inputs.values()],
        out_specs=[pl.BlockSpec(memory_space=space) for _, _, space in outputs.values()],
        scratch_shapes=list(scratch.values()),
        compiler_params=pltpu.CompilerParams(
            collective_id=number, has_side_effects=True, vmem_limit_bytes=VMEM_LIMIT
        ),
        name=name,
    )(*(array for array, _ in inputs.values()))
    return types.SimpleNamespace(**dict(zip(outputs, results)))


def head_shards(
    hidden_in,
    segment_ids,
    order_ids,
    box_ids,
    qkv_weight,
    qkv_bias,
    rel_tables,
    out_weight,
    branch_bias,
    norm_gains,
    norm_shifts,
    ffn_in,
    ffn_in_bias,
    ffn_out,
    out_grad,
):
    rows, width = hidden_in.shape
    slot_rows = -(-rows // 16) * 16
    total = CHIPS * slot_rows
    depth = qkv_weight.shape[1]
    hidden = ffn_in.shape[1]
    half_hidden, half_width = hidden // 2, width // 2
    down_rows = ffn_out.shape[0]
    both = 2 * slot_rows
    fold_rows = -(-(slot_rows // 2) // 16) * 16
    any_, vmem, dma = pl.ANY, pltpu.VMEM, pltpu.SemaphoreType.DMA
    message = (CHIPS, fold_rows, 128)
    made = call(
        first_kernel,
        "forward_and_feed_forward",
        0,
        dict(
            hidden_in=(hidden_in, vmem),
            segment_ids=(segment_ids.reshape(1, rows), vmem),
            order_ids=(order_ids.reshape(1, rows), vmem),
            box_ids=(box_ids, vmem),
            qkv_weight=(qkv_weight, vmem),
            qkv_any=(qkv_weight, any_),
            qkv_bias=(qkv_bias, vmem),
            rel_tables=(rel_tables, vmem),
            out_weight=(out_weight, any_),
            branch_bias=(branch_bias, vmem),
            norm_gains=(norm_gains, vmem),
            norm_shifts=(norm_shifts, vmem),
            ffn_in=(ffn_in, any_),
            ffn_in_bias=(ffn_in_bias.reshape(1, down_rows), vmem),
            ffn_out=(ffn_out, any_),
            out_grad=(out_grad, vmem),
        ),
        dict(
            hidden_out=((rows, width), LOW, vmem),
            x_out=((total, width), LOW, any_),
            rel_out=((2 * depth, 4 * NB), LOW, any_),
            left_out=((total, 384), LOW, any_),
            right_out=((total, 384), LOW, any_),
            right_t_out=((384, total), LOW, any_),
            value_t_out=((128, total), LOW, any_),
            kept_out=((total, 128), HIGH, any_),
            g_down_out=((half_hidden, width), LOW, any_),
            g_in_out=((width, half_hidden), LOW, any_),
            g_out=((half_width, width), LOW, vmem),
            g_small=((16, half_hidden), HIGH, vmem),
            d_sum1=((slot_rows, width), HIGH, vmem),
            d_message=(message, LOW, vmem),
            w_qkv_out=((3, 2, CHIPS, depth, half_width), LOW, any_),
        ),
        dict(
            x_own=vmem((slot_rows, width), LOW),
            x_vmem=vmem((total, width), LOW),
            extra=vmem((slot_rows - rows, width), HIGH),
            w_own=vmem((H, depth, 4 * HD), LOW),
            w_all=vmem((2 * CHIPS, depth, 4 * HD), LOW),
            rel_own=vmem((depth, 4 * NB), LOW),
            rel_all=vmem((2 * depth, 4 * NB), LOW),
            w_in=vmem((2, CHIPS, depth, half_hidden), LOW),
            w_down=vmem((CHIPS, down_rows, width), LOW),
            w_out=vmem((CHIPS, depth, width), LOW),
            w_qkv=vmem((3, 2, CHIPS, depth, half_width), LOW),
            meta=vmem((total, 128), HIGH),
            shares=vmem((2, 3, 8, half_width), HIGH),
            bias_in=vmem((1, half_hidden), HIGH),
            left=vmem((total, 384), LOW),
            right=vmem((total, 384), LOW),
            right_t=vmem((384, total), LOW),
            value=vmem((total, 128), LOW),
            value_t=vmem((128, total), LOW),
            kept=vmem((total, 128), HIGH),
            message=vmem(message, LOW),
            context_in=vmem(message, LOW),
            context_wide=vmem((both, half_width), HIGH),
            context=vmem((both, half_width), LOW),
            low_first=vmem((both, width), LOW),
            act=vmem((both, half_hidden), LOW),
            slope=vmem((both, half_hidden), HIGH),
            d_second=vmem((both, width), LOW),
            d_inner=vmem((both, half_hidden), LOW),
            d_branch=vmem((both, width), LOW),
            g_down=vmem((half_hidden, width), LOW),
            g_in=vmem((width, half_hidden), LOW),
            out_part=vmem((3, slot_rows, width), HIGH),
            in_part=vmem((3, slot_rows, width), HIGH),
            keep_sem=dma((16,)),
            x_send=dma((2, 16)),
            x_recv=dma((2, 16)),
            w_send=dma((16,)),
            w_recv=dma((16,)),
            rel_send=dma((2,)),
            rel_recv=dma((2,)),
            out_send=dma((16,)),
            out_recv=dma((16,)),
            in_send=dma((16,)),
            in_recv=dma((16,)),
            down_send=dma((16,)),
            down_recv=dma((16,)),
            qkv_send=dma((16,)),
            qkv_recv=dma((16,)),
            msg_send=dma((16,)),
            msg_recv=dma((16,)),
            pair_send=dma((10,)),
            pair_recv=dma((10,)),
        ),
    )
    g_down = made.g_down_out.reshape(CHIPS, down_rows, width)
    g_in = made.g_in_out.reshape(2, CHIPS, depth, half_hidden)
    g_out = made.g_out.reshape(CHIPS, depth, width)
    out_message = (CHIPS, slot_rows + fold_rows, 128)
    in_block, down_block, out_block = (2, depth, half_hidden), (down_rows, width), (depth, width)
    ended = call(
        second_kernel,
        "backward_and_sums",
        1,
        dict(
            left_any=(made.left_out, any_),
            right_any=(made.right_out, any_),
            right_t_any=(made.right_t_out, any_),
            value_t_any=(made.value_t_out, any_),
            kept_any=(made.kept_out, any_),
            rel_all=(made.rel_out, vmem),
            x_all_any=(made.x_out, any_),
            w_qkv_any=(made.w_qkv_out, any_),
            g_down_any=(g_down, any_),
            g_in_any=(g_in, any_),
            g_out_any=(g_out, any_),
            g_small=(made.g_small, vmem),
            d_sum1=(made.d_sum1, vmem),
            d_message=(made.d_message, vmem),
        ),
        dict(
            hidden_grad=((rows, width), LOW, vmem),
            qkv_grad=((3, depth, width), HIGH, vmem),
            qkv_bias_grad=((2, depth), HIGH, vmem),
            rel_tables_grad=((3, NB, depth), HIGH, vmem),
            out_grad=((depth, width), HIGH, vmem),
            branch_grad=((2, depth), HIGH, vmem),
            gain_grad=((2, depth), HIGH, vmem),
            shift_grad=((2, depth), HIGH, vmem),
            in_grad=((depth, hidden), HIGH, vmem),
            bias_grad=((1, down_rows), HIGH, vmem),
            down_grad=((down_rows, width), HIGH, vmem),
        ),
        dict(
            left=vmem((total, 384), LOW),
            right=vmem((total, 384), LOW),
            right_t=vmem((384, total), LOW),
            value_t=vmem((128, total), LOW),
            kept=vmem((total, 128), HIGH),
            x_all=vmem((total, width), LOW),
            w_qkv=vmem((3, 2, CHIPS, depth, half_width), LOW),
            g_down=vmem((CHIPS,) + down_block, LOW),
            g_in=vmem((2, CHIPS, depth, half_hidden), LOW),
            g_out=vmem((CHIPS,) + out_block, LOW),
            in_1=vmem((8,) + in_block, LOW),
            in_2=vmem((4,) + in_block, LOW),
            in_3=vmem((3,) + in_block, LOW),
            down_1=vmem((8,) + down_block, LOW),
            down_2=vmem((4,) + down_block, LOW),
            down_3=vmem((3,) + down_block, LOW),
            out_1=vmem((8,) + out_block, LOW),
            out_2=vmem((4,) + out_block, LOW),
            out_3=vmem((3,) + out_block, LOW),
            in_total=vmem(in_block, HIGH),
            in_far=vmem((depth, half_hidden), HIGH),
            small_sum=vmem((16, half_hidden), HIGH),
            small_in=vmem((6, 16, half_hidden), HIGH),
            d_arrived=vmem(message, LOW),
            d_context=vmem((total, 128), HIGH),
            d_query=vmem((total, 128), HIGH),
            d_query_t=vmem((3 * HD, total), LOW),
            d_pair_t=vmem((2 * HD, total), HIGH),
            rel_grad=vmem((2 * depth, 4 * NB), HIGH),
            rel_far=vmem((depth, 4 * NB), HIGH),
            rel_sum=vmem((depth, 4 * NB), HIGH),
            rel_came=vmem((depth, 4 * NB), HIGH),
            message=vmem(out_message, LOW),
            tokens_in=vmem(out_message, LOW),
            w_mine=vmem((2, 3 * HD, half_width), HIGH),
            w_far=vmem((3 * HD, half_width), HIGH),
            w_low=vmem((CHIPS, depth, 4 * HD), LOW),
            w_came=vmem((CHIPS, depth, 4 * HD), LOW),
            wide=vmem((both, half_width), HIGH),
            low=vmem((3, both, half_width), LOW),
            out_part=vmem((slot_rows, width), HIGH),
            in_part=vmem((slot_rows, width), HIGH),
            keep_sem=dma((11,)),
            d_send=dma((16,)),
            d_recv=dma((16,)),
            in_send=dma((16,)),
            in_recv=dma((16,)),
            down_send=dma((16,)),
            down_recv=dma((16,)),
            out_send=dma((16,)),
            out_recv=dma((16,)),
            small_send=dma((6,)),
            small_recv=dma((6,)),
            msg_send=dma((16,)),
            msg_recv=dma((16,)),
            w_send=dma((16,)),
            w_recv=dma((16,)),
            rel_send=dma((1,)),
            rel_recv=dma((1,)),
            pair_send=dma((4,)),
            pair_recv=dma((4,)),
        ),
    )
    return (
        made.hidden_out,
        ended.hidden_grad,
        ended.qkv_grad,
        ended.qkv_bias_grad,
        ended.rel_tables_grad,
        ended.out_grad,
        ended.branch_grad,
        ended.gain_grad,
        ended.shift_grad,
        ended.in_grad,
        ended.bias_grad.reshape(down_rows),
        ended.down_grad,
    )


def solution(mesh):
    by_heads = mesh.shape["grp"] == 2 and mesh.shape["blk"] == CHIPS == H
    return jax.shard_map(
        head_shards if by_heads else shards,
        mesh=mesh,
        in_specs=(
            P(("grp", "blk"), None),
            P(("grp", "blk")),
            P(("grp", "blk")),
            P(None, ("grp", "blk")),
            P(None, ("grp", "blk"), None),
            P(None, ("grp", "blk")),
            P(None, None, ("grp", "blk")),
            P(("grp", "blk"), None),
            P(None, ("grp", "blk")),
            P(None, ("grp", "blk")),
            P(None, ("grp", "blk")),
            P(("grp", "blk"), None),
            P(("grp", "blk")),
            P(("grp", "blk"), None),
            P(("grp", "blk"), None),
        ),
        out_specs=(
            P(("grp", "blk"), None),
            P(("grp", "blk"), None),
            P(None, ("grp", "blk"), None),
            P(None, ("grp", "blk")),
            P(None, None, ("grp", "blk")),
            P(("grp", "blk"), None),
            P(None, ("grp", "blk")),
            P(None, ("grp", "blk")),
            P(None, ("grp", "blk")),
            P(("grp", "blk"), None),
            P(("grp", "blk")),
            P(("grp", "blk"), None),
        ),
        check_vma=False,
    )
```

```python
import functools
import math
import types

import jax
import jax.numpy as jnp
from jax import lax
from jax.experimental import pallas as pl
from jax.experimental.pallas import tpu as pltpu
from jax.sharding import PartitionSpec as P

H = 16
HD = 64
NB = 128
ORDER_RANGE = 128
BOX_RANGE = 64


NEGATIVE = -1e30
EPSILON = 1e-05


def shifted(x, axis, by):
    devices = lax.axis_size(axis)
    return lax.ppermute(x, axis, [(i, (i + by) % devices) for i in range(devices)])


def block_size(row_count):
    chosen = 1
    for option in range(1, min(row_count, 544) + 1):
        if row_count % option == 0:
            chosen = option
    return chosen


def kind_ranges():
    return (ORDER_RANGE, BOX_RANGE, BOX_RANGE)


def query_maps(layout_ids):
    maps_out = []
    for column, extent in enumerate(kind_ranges()):
        offsets = layout_ids[:, column][:, None] - jnp.arange(extent, dtype=jnp.int32)[None, :]
        bucket = jnp.clip(offsets, -(NB // 2), NB // 2 - 1) + NB // 2
        maps_out.append(bucket[:, :, None] == jnp.arange(NB, dtype=jnp.int32)[None, None, :])
    return maps_out


def key_onehot(key_ids):
    pieces_out = []
    for column, extent in enumerate(kind_ranges()):
        pieces_out.append(
            key_ids[:, column + 1][:, None] == jnp.arange(extent, dtype=jnp.int32)[None, :]
        )
    return jnp.concatenate(pieces_out, axis=1).astype(jnp.bfloat16)


def norm_forward(values_in, norm_gain, norm_shift):
    center = values_in - jnp.mean(values_in, axis=-1, keepdims=True)
    inverse = lax.rsqrt(jnp.mean(center * center, axis=-1, keepdims=True) + EPSILON)
    normed = center * inverse
    return (normed * norm_gain + norm_shift, normed, inverse)


def norm_backward(upstream, normed, inverse, norm_gain):
    scaled = upstream * norm_gain
    inner_part = (
        scaled
        - jnp.mean(scaled, axis=-1, keepdims=True)
        - normed * jnp.mean(scaled * normed, axis=-1, keepdims=True)
    )
    return (inner_part * inverse, jnp.sum(upstream * normed, axis=0), jnp.sum(upstream, axis=0))


def block_logits(query_heads, selector, query_seg, key_part, meta_part, scaling):
    key_ids = meta_part.astype(jnp.int32)
    row_count = key_part.shape[0]
    key_heads = key_part.reshape(row_count, H, HD)
    content = jnp.einsum("thd,khd->htk", query_heads, key_heads, preferred_element_type=jnp.float32)
    onehot = key_onehot(key_ids)
    rel_bias = jnp.einsum("thv,kv->htk", selector, onehot, preferred_element_type=jnp.float32)
    allowed = query_seg[:, None] == key_ids[None, :, 0]
    logits = jnp.where(allowed[None], (content + rel_bias) * scaling, NEGATIVE)
    return (logits, allowed, onehot, key_heads)


def over_blocks(advance, carry, piece, start):
    row_count = piece[0].shape[0]
    stride = block_size(row_count)

    def one_step(block_index, running):
        portion = tuple(
            (lax.dynamic_slice_in_dim(member, block_index * stride, stride, 0) for member in piece)
        )
        return advance(running, portion, start + block_index * stride)

    return lax.fori_loop(0, row_count // stride, one_step, carry)


def shards(
    hidden_in,
    segment_ids,
    order_ids,
    box_ids,
    qkv_weight,
    qkv_bias,
    rel_tables,
    out_weight,
    branch_bias,
    norm_gains,
    norm_shifts,
    ffn_in,
    ffn_in_bias,
    ffn_out,
    out_grad,
):
    gathered = (
        lax.all_gather(qkv_weight, ("grp", "blk"), axis=1, tiled=True),
        lax.all_gather(qkv_bias, ("grp", "blk"), axis=1, tiled=True),
        lax.all_gather(rel_tables, ("grp", "blk"), axis=2, tiled=True),
        lax.all_gather(out_weight, ("grp", "blk"), axis=0, tiled=True),
        lax.all_gather(branch_bias, ("grp", "blk"), axis=1, tiled=True),
        lax.all_gather(norm_gains, ("grp", "blk"), axis=1, tiled=True),
        lax.all_gather(norm_shifts, ("grp", "blk"), axis=1, tiled=True),
        lax.all_gather(ffn_in, ("grp", "blk"), axis=0, tiled=True),
        lax.all_gather(ffn_in_bias, ("grp", "blk"), axis=0, tiled=True),
        lax.all_gather(ffn_out, ("grp", "blk"), axis=0, tiled=True),
    )
    w_qkv, b_qkv, w_rel, w_out, b_branch, gains, shifts, w_in, b_in, w_down = gathered
    row_count = hidden_in.shape[0]
    width = hidden_in.shape[1]
    scaling = 1.0 / math.sqrt(4.0 * HD)
    select_width = ORDER_RANGE + 2 * BOX_RANGE
    projected = jnp.einsum("td,cde->cte", hidden_in, w_qkv, preferred_element_type=jnp.float32)
    bias_qkv = b_qkv.astype(jnp.float32)
    query_rows = (projected[0] + bias_qkv[0]).astype(jnp.bfloat16)
    key_rows = projected[1].astype(jnp.bfloat16)
    value_rows = (projected[2] + bias_qkv[1]).astype(jnp.bfloat16)
    layout_ids = jnp.stack([order_ids, box_ids[0], box_ids[1]], axis=1)
    key_meta = jnp.stack([segment_ids, order_ids, box_ids[0], box_ids[1]], axis=1).astype(
        jnp.bfloat16
    )
    query_heads = query_rows.reshape(row_count, H, HD)
    rel_heads = w_rel.reshape(3, NB, H, HD)
    tables = jnp.einsum(
        "thd,nbhd->thnb", query_heads, rel_heads, preferred_element_type=jnp.float32
    ).astype(jnp.bfloat16)
    maps_list = query_maps(layout_ids)
    selector = jnp.concatenate(
        [
            jnp.einsum(
                "thb,tvb->thv",
                tables[:, :, column],
                maps_list[column].astype(jnp.bfloat16),
                preferred_element_type=jnp.float32,
            )
            for column in range(3)
        ],
        axis=2,
    ).astype(jnp.bfloat16)

    def forward_step(running, portion, offset):
        row_top, row_total, weighted = running
        key_part, value_part, meta_part = portion
        logits, allowed, onehot, key_heads = block_logits(
            query_heads, selector, segment_ids, key_part, meta_part, scaling
        )
        new_top = jnp.maximum(row_top, jnp.max(logits, axis=2))
        rescale = jnp.exp(row_top - new_top)
        weights = jnp.where(allowed[None], jnp.exp(logits - new_top[:, :, None]), 0.0)
        value_heads = value_part.reshape(value_part.shape[0], H, HD)
        weighted = weighted * rescale.T[:, :, None] + jnp.einsum(
            "htk,khd->thd",
            weights.astype(jnp.bfloat16),
            value_heads,
            preferred_element_type=jnp.float32,
        )
        return (new_top, row_total * rescale + jnp.sum(weights, axis=2), weighted)

    start_state = (
        jnp.full((H, row_count), NEGATIVE, jnp.float32),
        jnp.zeros((H, row_count), jnp.float32),
        jnp.zeros((row_count, H, HD), jnp.float32),
    )
    row_top, row_total, weighted = over_blocks(
        forward_step,
        start_state,
        (
            lax.all_gather(key_rows, "blk", axis=0, tiled=True),
            lax.all_gather(value_rows, "blk", axis=0, tiled=True),
            lax.all_gather(key_meta, "blk", axis=0, tiled=True),
        ),
        jnp.int32(0),
    )
    context_full = weighted / row_total.T[:, :, None]
    log_total = row_top + jnp.log(row_total)
    context = context_full.reshape(row_count, width).astype(jnp.bfloat16)
    branch = jnp.dot(context, w_out, preferred_element_type=jnp.float32) + b_branch[0].astype(
        jnp.float32
    )
    first, normed_one, inverse_one = norm_forward(
        hidden_in.astype(jnp.float32) + branch,
        gains[0].astype(jnp.float32),
        shifts[0].astype(jnp.float32),
    )
    first_low = first.astype(jnp.bfloat16)
    inner_pre = jnp.dot(first_low, w_in, preferred_element_type=jnp.float32) + b_in.astype(
        jnp.float32
    )
    activated, gelu_pull = jax.vjp(
        lambda pre_act: jax.nn.gelu(pre_act, approximate=False), inner_pre
    )
    activated_low = activated.astype(jnp.bfloat16)
    second = jnp.dot(activated_low, w_down, preferred_element_type=jnp.float32) + b_branch[
        1
    ].astype(jnp.float32)
    result, normed_two, inverse_two = norm_forward(
        first + second, gains[1].astype(jnp.float32), shifts[1].astype(jnp.float32)
    )
    hidden_out = result.astype(jnp.bfloat16)
    grad_sum2, gain_grad2, shift_grad2 = norm_backward(
        out_grad.astype(jnp.float32), normed_two, inverse_two, gains[1].astype(jnp.float32)
    )
    grad_second = grad_sum2.astype(jnp.bfloat16)
    grad_w_down = jnp.einsum(
        "tf,td->fd", activated_low, grad_second, preferred_element_type=jnp.float32
    )
    grad_bias_two = jnp.sum(grad_second.astype(jnp.float32), axis=0)
    grad_act = jnp.einsum("td,fd->tf", grad_second, w_down, preferred_element_type=jnp.float32)
    grad_inner = gelu_pull(grad_act)[0].astype(jnp.bfloat16)
    grad_b_in = jnp.sum(grad_inner.astype(jnp.float32), axis=0)
    grad_w_in = jnp.einsum("td,tf->df", first_low, grad_inner, preferred_element_type=jnp.float32)
    grad_first = grad_sum2 + jnp.einsum(
        "tf,df->td", grad_inner, w_in, preferred_element_type=jnp.float32
    )
    grad_sum1, gain_grad1, shift_grad1 = norm_backward(
        grad_first, normed_one, inverse_one, gains[0].astype(jnp.float32)
    )
    grad_branch = grad_sum1.astype(jnp.bfloat16)
    grad_w_out = jnp.einsum("td,te->de", context, grad_branch, preferred_element_type=jnp.float32)
    grad_bias_one = jnp.sum(grad_branch.astype(jnp.float32), axis=0)
    grad_context = jnp.einsum(
        "te,de->td", grad_branch, w_out, preferred_element_type=jnp.float32
    ).astype(jnp.bfloat16)
    grad_heads = grad_context.reshape(row_count, H, HD)
    delta = jnp.einsum("thd,thd->ht", grad_heads.astype(jnp.float32), context_full)

    def backward_core(grad_query, grad_select, portion):
        key_part, value_part, meta_part = portion
        logits, allowed, onehot, key_heads = block_logits(
            query_heads, selector, segment_ids, key_part, meta_part, scaling
        )
        probs = jnp.where(allowed[None], jnp.exp(logits - log_total[:, :, None]), 0.0)
        part_rows = key_part.shape[0]
        value_heads = value_part.reshape(part_rows, H, HD)
        grad_probs = jnp.einsum(
            "thd,khd->htk", grad_heads, value_heads, preferred_element_type=jnp.float32
        )
        grad_logits = (probs * (grad_probs - delta[:, :, None])).astype(jnp.bfloat16)
        grad_query = grad_query + scaling * jnp.einsum(
            "htk,khd->thd", grad_logits, key_heads, preferred_element_type=jnp.float32
        )
        grad_select = grad_select + scaling * jnp.einsum(
            "htk,kv->thv", grad_logits, onehot, preferred_element_type=jnp.float32
        )
        grad_key = scaling * jnp.einsum(
            "htk,thd->khd", grad_logits, query_heads, preferred_element_type=jnp.float32
        )
        grad_value = jnp.einsum(
            "htk,thd->khd",
            probs.astype(jnp.bfloat16),
            grad_heads,
            preferred_element_type=jnp.float32,
        )
        update = jnp.concatenate(
            [grad_key.reshape(part_rows, width), grad_value.reshape(part_rows, width)], axis=1
        )
        return (grad_query, grad_select, update)

    query_zero = jnp.zeros((row_count, H, HD), jnp.float32)
    select_zero = jnp.zeros((row_count, H, select_width), jnp.float32)

    def cycle_turn(turn, carry):
        grad_query, grad_select, key_part, value_part, meta_part, carried = carry
        portion = (key_part, value_part, meta_part)
        grad_query, grad_select, update = backward_core(grad_query, grad_select, portion)
        carried = carried + update
        key_part, value_part, meta_part = shifted((key_part, value_part, meta_part), "blk", 1)
        carried = shifted(carried.astype(jnp.bfloat16), "blk", 1).astype(carried.dtype)
        return (grad_query, grad_select, key_part, value_part, meta_part, carried)

    cycle_start = (
        query_zero,
        select_zero,
        key_rows,
        value_rows,
        key_meta,
        jnp.zeros((row_count, 2 * width), jnp.float32),
    )
    cycle_end = lax.fori_loop(0, lax.axis_size("blk"), cycle_turn, cycle_start)
    grad_query, grad_select, own_pairs = (cycle_end[0], cycle_end[1], cycle_end[5])
    grad_key_rows = own_pairs[:, :width].astype(jnp.bfloat16)
    grad_value_rows = own_pairs[:, width:].astype(jnp.bfloat16)
    cursor = 0
    table_parts = []
    for column, extent in enumerate(kind_ranges()):
        table_parts.append(
            jnp.einsum(
                "thv,tvb->thb",
                grad_select[:, :, cursor : cursor + extent],
                maps_list[column].astype(jnp.float32),
                precision=lax.Precision.HIGHEST,
            )
        )
        cursor = cursor + extent
    grad_tables = jnp.stack(table_parts, axis=2).astype(jnp.bfloat16)
    grad_query_total = grad_query + jnp.einsum(
        "thnb,nbhd->thd", grad_tables, rel_heads, preferred_element_type=jnp.float32
    )
    grad_query_rows = grad_query_total.reshape(row_count, width).astype(jnp.bfloat16)
    grad_rel = jnp.einsum(
        "thnb,thd->nbhd", grad_tables, query_heads, preferred_element_type=jnp.float32
    ).reshape(3, NB, width)
    grad_stack = jnp.stack([grad_query_rows, grad_key_rows, grad_value_rows])
    grad_w_qkv = jnp.einsum(
        "td,cte->cde", hidden_in, grad_stack, preferred_element_type=jnp.float32
    )
    grad_b_qkv = jnp.stack(
        [
            jnp.sum(grad_query_rows.astype(jnp.float32), axis=0),
            jnp.sum(grad_value_rows.astype(jnp.float32), axis=0),
        ]
    )
    grad_input = grad_sum1 + jnp.einsum(
        "cte,cde->td", grad_stack, w_qkv, preferred_element_type=jnp.float32
    )
    summed = (
        lax.psum_scatter(grad_w_qkv, ("grp", "blk"), scatter_dimension=1, tiled=True),
        lax.psum_scatter(grad_b_qkv, ("grp", "blk"), scatter_dimension=1, tiled=True),
        lax.psum_scatter(grad_rel, ("grp", "blk"), scatter_dimension=2, tiled=True),
        lax.psum_scatter(grad_w_out, ("grp", "blk"), scatter_dimension=0, tiled=True),
        lax.psum_scatter(
            jnp.stack([grad_bias_one, grad_bias_two]),
            ("grp", "blk"),
            scatter_dimension=1,
            tiled=True,
        ),
        lax.psum_scatter(
            jnp.stack([gain_grad1, gain_grad2]), ("grp", "blk"), scatter_dimension=1, tiled=True
        ),
        lax.psum_scatter(
            jnp.stack([shift_grad1, shift_grad2]), ("grp", "blk"), scatter_dimension=1, tiled=True
        ),
        lax.psum_scatter(grad_w_in, ("grp", "blk"), scatter_dimension=0, tiled=True),
        lax.psum_scatter(grad_b_in, ("grp", "blk"), scatter_dimension=0, tiled=True),
        lax.psum_scatter(grad_w_down, ("grp", "blk"), scatter_dimension=0, tiled=True),
    )
    return (
        hidden_out,
        grad_input.astype(jnp.bfloat16),
        summed[0],
        summed[1],
        summed[2],
        summed[3],
        summed[4],
        summed[5],
        summed[6],
        summed[7],
        summed[8],
        summed[9],
    )


MESH = pl.DeviceIdType.MESH
LOW = jnp.bfloat16
HIGH = jnp.float32
CHIPS = 16
HALF = 8
BLOCK = 256
MASKED = -1e30
VMEM_LIMIT = 62 * 2**20
NT = ((1,), (1,))
TN = ((0,), (0,))


def dot(left, right, dims=((1,), (0,))):
    return lax.dot_general(left, right, (dims, ((), ())), preferred_element_type=HIGH)


def place():
    return lax.axis_index("grp"), lax.axis_index("blk")


def coordinates(chip):
    return lax.div(chip, 4), lax.rem(lax.div(chip, 2), 2), lax.rem(chip, 2)


def meet():
    core, chip = place()
    me = core * CHIPS + chip
    barrier = pltpu.get_barrier_semaphore()

    def greet(ahead, carry):
        other = lax.rem(me + ahead, 2 * CHIPS)
        pl.semaphore_signal(
            barrier,
            inc=1,
            device_id=(lax.div(other, CHIPS), lax.rem(other, CHIPS)),
            device_id_type=MESH,
        )
        return carry

    lax.fori_loop(1, 2 * CHIPS, greet, 0)
    pl.semaphore_wait(barrier, 2 * CHIPS - 1)


def remote(source, target, send, recv, device):
    return pltpu.make_async_remote_copy(
        src_ref=source,
        dst_ref=target,
        send_sem=send,
        recv_sem=recv,
        device_id=device,
        device_id_type=MESH,
    )


def local(source, target, sem):
    return pltpu.make_async_copy(source, target, sem)


def neighbours(across):
    core, chip = place()
    z, y, x = coordinates(chip)
    planes = (z + 1 - 2 * lax.rem(z, 2), 2 - lax.div(z, 2), 3 - 3 * lax.div(z, 2))

    def slot(far_p, far_q, line):
        far_y, far_x = (far_q, far_p) if across == "x" else (far_p, far_q)
        plane = z if line is None else planes[line]
        return plane * 4 + (1 - y if far_y else y) * 2 + (1 - x if far_x else x)

    return slot


class Shipments:
    def __init__(self, send, recv):
        self.send, self.recv, self.made = send, recv, []
        self.core = lax.axis_index("grp")

    def ship(self, source, target, recv_index, to):
        index = len(self.made)

        def make():
            return remote(
                source(), target(), self.send.at[index], self.recv.at[recv_index()], (self.core, to())
            )

        self.made.append(make)
        make().start()

    def landed(self, target, recv_index, near):
        remote(target, target, self.send.at[0], self.recv.at[recv_index], (self.core, near)).wait_recv()

    def all_sent(self):
        assert len(self.made) == 15
        for make in self.made:
            make().wait_send()


class Gather:
    def __init__(self, pick, send, recv, across):
        self.pick, self.at = pick, neighbours(across)
        self.moves = Shipments(send, recv)

    def ship(self, what, to):
        slot = lambda: self.at(*what)
        ref = lambda: self.pick(slot())
        self.moves.ship(ref, ref, slot, lambda: self.at(*to))

    def landed(self, *what):
        slot = self.at(*what)
        self.moves.landed(self.pick(slot), slot, self.at(1, 0, None))

    def own_line(self, line):
        self.ship((0, 0, None), (0, 0, line))

    def own_plane(self):
        self.ship((0, 0, None), (1, 0, None))
        self.ship((0, 0, None), (0, 1, None))

    def line(self, line):
        self.landed(0, 0, line)
        self.ship((0, 0, line), (1, 0, None))
        self.ship((0, 0, line), (0, 1, None))

    def side(self, line):
        self.landed(1, 0, line)
        self.ship((1, 0, line), (0, 1, None))

    def arrive(self):
        for line in (None, 0, 1, 2):
            for far_p in (0, 1):
                self.landed(far_p, 1, line)

    def finish(self):
        self.moves.all_sent()


class GatherLate(Gather):
    def first(self):
        self.ship((0, 0, None), (1, 0, None))
        self.ship((0, 0, None), (0, 1, None))

    def second(self):
        self.landed(1, 0, None)
        self.ship((1, 0, None), (0, 1, None))

    def third(self):
        for far_p in (0, 1):
            self.landed(far_p, 1, None)
        for line in range(3):
            for what in ((0, 0), (1, 0), (0, 1), (1, 1)):
                self.ship(what + (None,), (0, 0, line))

    def arrive(self):
        for line in range(3):
            for what in ((0, 0), (1, 0), (0, 1), (1, 1)):
                self.landed(*what, line)


class Reduce:
    def __init__(self, sent, own, pick, stages, send, recv, across):
        self.sent, self.own, self.pick, self.at = sent, own, pick, neighbours(across)
        self.first, self.second, self.third_in = stages
        self.moves = Shipments(send, recv)

    @staticmethod
    def number(line):
        return 3 if line is None else line

    def ship(self, source, target, index, to):
        self.moves.ship(source, target, lambda: index, lambda: self.at(*to))

    def landed(self, target, index):
        self.moves.landed(target, index, self.at(1, 0, None))

    def start(self, line):
        for far_p in (1, 0):
            index = self.number(line) * 2 + far_p
            self.ship(
                lambda far_p=far_p: self.pick(self.sent, self.at(far_p, 1, line)),
                lambda index=index: self.first.at[index],
                index,
                (0, 1, None),
            )

    def mine(self, *what):
        return self.pick(self.own, self.at(*what))[...].astype(HIGH)

    def side(self, line):
        number = self.number(line)
        index = number * 2 + 1
        self.landed(self.first.at[index], index)
        self.first[index] = (self.first[index].astype(HIGH) + self.mine(1, 0, line)).astype(LOW)
        self.ship(
            lambda: self.first.at[index], lambda: self.second.at[number], 8 + number, (1, 0, None)
        )

    def line(self, line):
        number = self.number(line)
        index = number * 2
        self.landed(self.first.at[index], index)
        self.landed(self.second.at[number], 8 + number)
        total = (
            self.first[index].astype(HIGH)
            + self.second[number].astype(HIGH)
            + self.mine(0, 0, line)
        )
        if line is None:
            return total
        self.first[index] = total.astype(LOW)
        ahead = lambda: lax.rem(lax.div(self.at(0, 0, None), 4) - lax.div(self.at(0, 0, line), 4) + 4, 4) - 1
        self.moves.ship(
            lambda: self.first.at[index],
            lambda: self.third_in.at[ahead()],
            lambda: 12 + ahead(),
            lambda: self.at(0, 0, line),
        )

    def finish(self, result):
        result[...] = self.line(None)
        for ahead in range(3):
            self.landed(self.third_in.at[ahead], 12 + ahead)
            result[...] += self.third_in[ahead].astype(HIGH)
        self.moves.all_sent()


class ReduceEarly(Reduce):
    PLANE = ((0, 0), (1, 0), (0, 1), (1, 1))

    def ahead(self, line):
        return lax.rem(lax.div(self.at(0, 0, None), 4) - lax.div(self.at(0, 0, line), 4) + 4, 4) - 1

    def start(self):
        for line in (2, 1, 0):
            for number, what in enumerate(self.PLANE):
                index = lambda number=number, line=line: self.ahead(line) * 4 + number
                self.moves.ship(
                    lambda what=what, line=line: self.pick(self.sent, self.at(*what, line)),
                    lambda index=index: self.first.at[index()],
                    index,
                    lambda line=line: self.at(0, 0, line),
                )

    def plane_sum(self, number):
        total = self.mine(*self.PLANE[number], None)
        for ahead in range(3):
            index = ahead * 4 + number
            self.landed(self.first.at[index], index)
            total += self.first[index].astype(HIGH)
        return total

    def third(self):
        for number, far_p in ((3, 1), (2, 0)):
            self.first[number] = self.plane_sum(number).astype(LOW)
            self.ship(
                lambda number=number: self.first.at[number],
                lambda far_p=far_p: self.second.at[far_p],
                12 + far_p,
                (0, 1, None),
            )

    def across(self):
        total = self.plane_sum(1)
        self.landed(self.second.at[1], 13)
        self.first[1] = (total + self.second[1].astype(HIGH)).astype(LOW)
        self.ship(lambda: self.first.at[1], lambda: self.third_in.at[0], 14, (1, 0, None))

    def finish(self, result):
        total = self.plane_sum(0)
        self.landed(self.second.at[0], 12)
        self.landed(self.third_in.at[0], 14)
        result[...] = total + self.second[0].astype(HIGH) + self.third_in[0].astype(HIGH)
        self.moves.all_sent()


def each(plans, act, *arguments):
    for plan in plans:
        act(plan, *arguments)


def to_tokens(source, target, send, recv):
    core, chip = place()
    to_core = lax.div(chip, HALF)
    mine = core * HALF + lax.rem(chip, HALF)
    here = to_core == core

    def copy_to(ahead):
        chip_to = lax.rem(chip + ahead, CHIPS)
        return remote(
            source.at[chip_to], target.at[mine], send.at[ahead], recv.at[mine], (to_core, chip_to)
        )

    pl.when(here)(lambda: local(source.at[chip], target.at[mine], recv.at[mine]).start())
    pl.when(jnp.logical_not(here))(lambda: copy_to(0).start())
    for ahead in range(1, CHIPS):
        copy_to(ahead).start()

    def arrive():
        for slot in range(CHIPS):
            local(source.at[slot], target.at[slot], recv.at[slot]).wait()

    def finish():
        pl.when(jnp.logical_not(here))(lambda: copy_to(0).wait_send())
        for ahead in range(1, CHIPS):
            copy_to(ahead).wait_send()

    return arrive, finish


def to_heads(source, target, send, recv):
    core, chip = place()
    here = lax.div(chip, HALF) == core

    def copy_to(group, ahead):
        head = lax.rem(chip + ahead, HALF)
        return remote(
            source.at[group * HALF + head],
            target.at[chip],
            send.at[group * HALF + ahead],
            recv.at[chip],
            (group, core * HALF + head),
        )

    def every(act):
        for group in range(2):
            for ahead in range(HALF):
                if ahead == 0:
                    itself = jnp.logical_and(here, core == group)
                    pl.when(jnp.logical_not(itself))(lambda: act(copy_to(group, 0)))
                else:
                    act(copy_to(group, ahead))

    pl.when(here)(
        lambda: local(
            source.at[core * HALF + lax.rem(chip, HALF)], target.at[chip], recv.at[chip]
        ).start()
    )
    every(lambda copy: copy.start())

    def arrive():
        for slot in range(CHIPS):
            local(source.at[slot], target.at[slot], recv.at[slot]).wait()

    return arrive, lambda: every(lambda copy: copy.wait_send())


def lanes(rows, width=128):
    return lax.broadcasted_iota(jnp.int32, (rows, width), 1)


def turn(values):
    return pltpu.roll(values, HD, 1)


def fold(rows_in):
    half = rows_in.shape[0] // 2
    both = jnp.where(lanes(half) < HD, rows_in[:half], turn(rows_in[half:]))
    pad = -half % 16
    if pad:
        both = jnp.concatenate([both, jnp.zeros((pad, 128), HIGH)], axis=0)
    return both.astype(LOW)


def column_sums(v):
    return jnp.sum(v, axis=0, keepdims=True)


def gelu_parts(pre):
    cdf = 0.5 * (1.0 + lax.erf(pre * math.sqrt(0.5)))
    density = jnp.exp(-0.5 * pre * pre) * (1.0 / math.sqrt(2.0 * math.pi))
    return pre * cdf, cdf + pre * density


def normalize(v, gain, shift):
    center = v - jnp.mean(v, axis=1, keepdims=True)
    inverse = lax.rsqrt(jnp.mean(center * center, axis=1, keepdims=True) + EPSILON)
    normed = center * inverse
    return normed * gain + shift, normed, inverse


def normalize_back(c, normed, inverse, gain):
    scaled = c * gain
    inner = (
        scaled
        - jnp.mean(scaled, axis=1, keepdims=True)
        - normed * jnp.mean(scaled * normed, axis=1, keepdims=True)
    )
    return inner * inverse


def at_steps(index, steps):
    for number, acts in steps.items():

        def run(acts=acts):
            for act in acts:
                act()

        pl.when(index == number)(run)


def columns_of(half, width):
    return pl.ds(pl.multiple_of(half * width, 128), width)


LABEL_AT, BRANCH_AT, GAIN_AT, SHIFT_AT, BIAS_AT = 0, 256, 384, 512, 640


def first_kernel(names, *refs):
    r = types.SimpleNamespace(**dict(zip(names, refs)))
    hidden, x_all, w_all, rel_all = r.hidden_in, r.x_vmem, r.w_all, r.rel_all
    token_rows, width = hidden.shape
    total = x_all.shape[0]
    slot_rows = total // CHIPS
    depth = r.out_weight.shape[0]
    w_in, w_down, w_out, w_qkv = r.w_in, r.w_down, r.w_out, r.w_qkv
    half_hidden = w_in.shape[3]
    half_width = width // 2
    core, chip = place()
    other = 1 - core
    me = core * CHIPS + chip
    keep = r.keep_sem

    loads = [
        local(r.ffn_in.at[:, columns_of(core, half_hidden)], w_in.at[core, chip], keep.at[0]),
        local(r.ffn_out, w_down.at[chip], keep.at[1]),
        local(r.out_weight, w_out.at[chip], keep.at[2]),
        local(r.qkv_any.at[:, :, columns_of(core, half_width)], w_qkv.at[:, core, chip], keep.at[3]),
    ]
    for copy in loads:
        copy.start()

    own_slot = pl.ds(pl.multiple_of(chip * slot_rows, 16), slot_rows)
    extra = r.extra
    extra[...] = jnp.zeros_like(extra)
    extra[0:1, 0:256] = jnp.full((1, 256), 4.0, HIGH)
    extra[0:1, 0:token_rows] = r.segment_ids[...].astype(HIGH)
    extra[1:2, 0:token_rows] = r.order_ids[...].astype(HIGH)
    extra[2:4, 0:token_rows] = r.box_ids[...].astype(HIGH)
    for start, pair in ((BRANCH_AT, r.branch_bias), (GAIN_AT, r.norm_gains), (SHIFT_AT, r.norm_shifts)):
        extra[0:2, start : start + depth] = pair[...].astype(HIGH)
    extra[0:1, BIAS_AT : BIAS_AT + 128] = r.ffn_in_bias[...].astype(HIGH)
    tail = token_rows - token_rows % 16
    x_own = r.x_own
    x_own[0:tail, :] = hidden[0:tail, :]
    x_own[tail:slot_rows, :] = jnp.concatenate(
        [hidden[tail:token_rows, :].astype(HIGH), extra[...]], axis=0
    ).astype(LOW)
    weight = r.qkv_weight
    w_own = r.w_own
    lane_depth = lanes(depth) < HD
    for pair in range(H // 2):
        columns = slice(pair * 128, pair * 128 + 128)
        query, key, value = (weight[n, :, columns].astype(HIGH) for n in range(3))
        w_own[2 * pair, :, 0:128] = jnp.where(lane_depth, query, turn(value)).astype(LOW)
        w_own[2 * pair + 1, :, 0:128] = jnp.where(lane_depth, turn(query), value).astype(LOW)
        w_own[2 * pair, :, 128:256] = jnp.where(lane_depth, key, 0.0).astype(LOW)
        w_own[2 * pair + 1, :, 128:256] = jnp.where(lane_depth, turn(key), 0.0).astype(LOW)
    rel_own = r.rel_own
    eye_depth = (
        lax.broadcasted_iota(jnp.int32, (depth, depth), 0)
        == lax.broadcasted_iota(jnp.int32, (depth, depth), 1)
    ).astype(LOW)
    for kind in range(3):
        rel_own[:, kind * NB : (kind + 1) * NB] = r.rel_tables[kind]
    bias_columns = dot(eye_depth, r.qkv_bias[...], NT)
    rel_own[:, 3 * NB : 4 * NB] = jnp.where(
        lanes(depth) == 0, bias_columns[:, 0:1], jnp.where(lanes(depth) == 1, bias_columns[:, 1:2], 0.0)
    ).astype(LOW)
    own_x = local(x_own, x_all.at[own_slot], keep.at[4])
    own_w = local(w_own.at[chip], w_all.at[me], keep.at[5])
    own_x.start()
    own_w.start()
    meet()

    to_chip = lax.div(me, 2)
    parity = lax.rem(chip, 2)
    rel_slot = rel_all.at[pl.ds(parity * depth, depth)]

    def rel_each(act_remote, act_own):
        for to_core in range(2):
            itself = jnp.logical_and(to_chip == chip, core == to_core)
            copy = lambda: remote(
                rel_own, rel_slot, r.rel_send.at[to_core], r.rel_recv.at[parity], (to_core, to_chip)
            )
            pl.when(jnp.logical_not(itself))(lambda: act_remote(copy()))
            if act_own is not None:
                pl.when(itself)(act_own)

    rel_each(
        lambda copy: copy.start(), lambda: local(rel_own, rel_slot, r.rel_recv.at[parity]).start()
    )

    def w_copy(ahead):
        to = lax.rem(chip + ahead, CHIPS)
        return remote(
            w_own.at[to], w_all.at[me], r.w_send.at[ahead], r.w_recv.at[chip], (core, to)
        )

    half = width // 2

    def pick_x(part):
        return lambda slot: x_all.at[
            pl.ds(pl.multiple_of(slot * slot_rows, 16), slot_rows), pl.ds(part * half, half)
        ]

    x_plans = [
        Gather(pick_x(part), r.x_send.at[part], r.x_recv.at[part], across)
        for part, across in enumerate("xy")
    ]

    own_x.wait()
    each(x_plans, Gather.own_line, 0)
    each(x_plans, Gather.own_plane)
    for ahead in range(1, CHIPS):
        w_copy(ahead).start()
    each(x_plans, Gather.own_line, 1)
    each(x_plans, Gather.own_line, 2)
    swaps = [
        remote(
            r.ffn_in.at[:, columns_of(other, half_hidden)],
            w_in.at[core, chip],
            r.pair_send.at[0],
            r.pair_recv.at[0],
            (other, chip),
        ),
        remote(
            r.qkv_any.at[:, :, columns_of(other, half_width)],
            w_qkv.at[:, core, chip],
            r.pair_send.at[1],
            r.pair_recv.at[1],
            (other, chip),
        ),
    ]
    for copy in swaps:
        copy.start()
    each(x_plans, Gather.side, None)
    for line in range(3):
        each(x_plans, Gather.line, line)
        each(x_plans, Gather.side, line)

    half_tile = half_hidden // 2
    plan_out = GatherLate(lambda slot: w_out.at[slot], r.out_send, r.out_recv, "x")
    plan_qkv = Gather(lambda slot: w_qkv.at[:, :, slot], r.qkv_send, r.qkv_recv, "y")

    def halves(ref, wide, sends, recvs):
        return [
            Gather(
                lambda slot, part=part: ref(slot, pl.ds(part * wide, wide)), sends.at[part], recvs.at[part], across
            )
            for part, across in enumerate("xy")
        ]

    plans_in = halves(lambda slot, columns: w_in.at[:, slot, :, columns], half_tile, r.in_send, r.in_recv)
    plans_down = halves(lambda slot, columns: w_down.at[slot, :, columns], half, r.down_send, r.down_recv)
    for copy in loads:
        copy.wait()
    for copy in swaps:
        copy.wait()
    each(plans_in, Gather.own_line, 0)
    each(plans_in, Gather.own_plane)
    plan_out.first()
    each(plans_in, Gather.own_line, 1)
    each(plans_in, Gather.own_line, 2)

    own_w.wait()
    for ahead in range(1, CHIPS):
        came = lax.rem(chip + ahead, CHIPS)
        remote(
            w_own.at[0], w_all.at[core * CHIPS + came], r.w_send.at[0], r.w_recv.at[came], (core, came)
        ).wait_recv()
    mine = w_all.at[pl.ds(core * CHIPS, CHIPS)]
    pair_w = remote(mine, mine, r.pair_send.at[2], r.pair_recv.at[2], (other, chip))
    pair_w.start()
    for slot in range(2):
        local(rel_own, rel_all.at[pl.ds(slot * depth, depth)], r.rel_recv.at[slot]).wait()
    each(x_plans, Gather.arrive)
    keep_x = local(x_all, r.x_out, keep.at[6])
    keep_x.start()
    keep_rel = local(rel_all, r.rel_out, keep.at[7])
    keep_rel.start()

    meta, shares, bias_in = r.meta, r.shares, r.bias_in
    eye = (
        lax.broadcasted_iota(jnp.int32, (slot_rows, 256), 0)
        == lax.broadcasted_iota(jnp.int32, (slot_rows, 256), 1)
    ).astype(LOW)
    shares[core] = jnp.zeros(shares.shape[1:], HIGH)
    for slot in range(CHIPS):
        end = (slot + 1) * slot_rows
        labels = x_all[end - 16 : end, 0:256]
        meta[end - slot_rows : end, 0:16] = dot(eye, labels, NT)
        small = x_all[end - 16 : end, BRANCH_AT:768].astype(HIGH)[8:16]
        target = slice(slot * depth // 128 * 128, slot * depth // 128 * 128 + 128)
        for number in range(3):
            piece = jnp.where(lanes(8) < depth, small[:, number * 128 : number * 128 + 128], 0.0)
            if slot * depth % 128:
                piece = pltpu.roll(piece, slot * depth % 128, 1)
            shares[core, number, :, target] += piece
        bias_in[:, slot * 128 : slot * 128 + 128] = small[0:1, 384:512]
    pair_small = remote(
        shares.at[core], shares.at[core], r.pair_send.at[3], r.pair_recv.at[3], (other, chip)
    )
    pair_small.start()
    rel = rel_all[...]
    table_t = rel[:, 0 : 3 * NB]
    extra_columns = rel[:, 3 * NB : 4 * NB].astype(HIGH)
    row_at = lax.broadcasted_iota(jnp.int32, (2 * depth, 128), 0)
    column_at = lanes(2 * depth)
    bias = column_sums(
        jnp.where(row_at == column_at, extra_columns[:, 0:1], 0.0)
        + jnp.where(row_at + 2 * depth == column_at, extra_columns[:, 1:2], 0.0)
    )
    lane = lanes(BLOCK)
    first_half = lane < HD
    scale = 1.0 / math.sqrt(4.0 * HD)
    left, right, right_t = r.left, r.right, r.right_t
    value, value_t, kept = r.value, r.value_t, r.kept
    pair_w.wait()

    def prepare(index, carry):
        rows = pl.ds(pl.multiple_of(index * BLOCK, BLOCK), BLOCK)
        at_steps(
            index,
            {
                1: [
                    lambda: each(plans_in, Gather.side, None),
                    plan_out.second,
                    lambda: each(plans_down, Gather.own_line, 0),
                    lambda: each(plans_down, Gather.own_plane),
                ],
                4: [lambda: each(plans_in, Gather.line, 0), plan_out.third],
                7: [
                    lambda: each(plans_in, Gather.side, 0),
                    lambda: each(plans_down, Gather.own_line, 1),
                    lambda: each(plans_down, Gather.own_line, 2),
                ],
            },
        )
        projected = dot(x_all[rows, :], w_all[...].reshape(width, 4 * HD))
        query_value = (projected[:, 0:128] + bias).astype(LOW).astype(HIGH)
        key = projected[:, 128:256].astype(LOW).astype(HIGH)
        query = query_value[:, 0:HD].astype(LOW)
        tables = dot(query, table_t).astype(LOW).astype(HIGH)
        ids = meta[rows, 8:12].astype(jnp.int32)
        segment, order, box_x, box_y = ids[:, 0:1], ids[:, 1:2], ids[:, 2:3], ids[:, 3:4]

        def selected(column, ids_of, values):
            bucket = jnp.clip(ids_of - values, -(NB // 2), NB // 2 - 1) + NB // 2
            return jnp.take_along_axis(tables[:, column * NB : (column + 1) * NB], bucket, axis=1)

        wide = selected(0, order, lane)
        narrow = jnp.where(first_half, selected(1, box_x, lane), selected(2, box_y, lane - HD))
        label = lane - HD
        query_side = jnp.where(
            first_half,
            query_value * scale,
            jnp.where(jnp.logical_and(label != segment, label < 8), MASKED, 0.0),
        )
        key_side = jnp.where(first_half, key, (label == segment).astype(HIGH))
        left[rows, 0:128] = (wide * scale).astype(LOW)
        left[rows, 128:256] = (narrow * scale).astype(LOW)
        left[rows, 256:384] = query_side.astype(LOW)
        order_hot = (lane == order).astype(HIGH)
        box_hot = (jnp.where(first_half, box_x, box_y + HD) == lane).astype(HIGH)
        right[rows, 0:128] = order_hot.astype(LOW)
        right[rows, 128:256] = box_hot.astype(LOW)
        right[rows, 256:384] = key_side.astype(LOW)
        right_t[0:128, rows] = order_hot.T.astype(LOW)
        right_t[128:256, rows] = box_hot.T.astype(LOW)
        right_t[256:384, rows] = key_side.T.astype(LOW)
        held = jnp.where(first_half, turn(query_value), (label == 0).astype(HIGH))
        value[rows, :] = held.astype(LOW)
        value_t[:, rows] = held.T.astype(LOW)
        return carry

    lax.fori_loop(0, total // BLOCK, prepare, 0)
    stash = [
        local(held, out, keep.at[8 + k])
        for k, (held, out) in enumerate(
            (
                (left, r.left_out),
                (right, r.right_out),
                (right_t, r.right_t_out),
                (value_t, r.value_t_out),
            )
        )
    ]
    for copy in stash:
        copy.start()

    def attend(index, carry):
        rows = pl.ds(pl.multiple_of(index * BLOCK, BLOCK), BLOCK)
        at_steps(
            index,
            {
                0: [lambda: each(plans_in, Gather.line, 1), lambda: each(plans_down, Gather.side, None)],
                3: [lambda: each(plans_in, Gather.side, 1)],
                6: [lambda: each(plans_in, Gather.line, 2), lambda: each(plans_down, Gather.line, 0)],
            },
        )
        logits = dot(left[rows, :], right_t[...])
        top = jnp.max(logits, axis=1, keepdims=True)
        weights = jnp.exp(logits - top).astype(LOW)
        mixed = dot(weights, value[...])
        row_sum = mixed[:, HD : HD + 1]
        ids = meta[rows, 8:12]
        facts = jnp.where(lane == HD, top + jnp.log(row_sum), ids[:, 3:4])
        facts = jnp.where(lane == HD + 1, ids[:, 1:2], facts)
        facts = jnp.where(lane == HD + 2, ids[:, 2:3], facts)
        kept[rows, :] = jnp.where(first_half, mixed / row_sum, facts)
        return carry

    lax.fori_loop(0, total // BLOCK, attend, 0)
    keep_facts = local(kept, r.kept_out, keep.at[12])
    keep_facts.start()
    message, context_in = r.message, r.context_in
    for slot in range(CHIPS):
        message[slot] = fold(kept[slot * slot_rows : (slot + 1) * slot_rows, :])
    context_arrives, context_sent = to_tokens(message, context_in, r.msg_send, r.msg_recv)
    each(plans_in, Gather.side, 2)
    each(plans_down, Gather.side, 0)
    each(plans_down, Gather.line, 1)
    each(plans_down, Gather.side, 1)
    context_arrives()
    pair_small.wait()

    vectors = [
        [jnp.concatenate([shares[0, number, k : k + 1], shares[1, number, k : k + 1]], axis=1) for k in range(2)]
        for number in range(3)
    ]
    branch_bias, gains, shifts = vectors
    context_wide, context, low_first = r.context_wide, r.context, r.low_first
    act, slope, d_second, d_inner, d_branch = r.act, r.slope, r.d_second, r.d_inner, r.d_branch
    out_part, in_part, g_small = r.out_part, r.in_part, r.g_small
    own = pl.ds(pl.multiple_of(core * slot_rows, 16), slot_rows)
    far = pl.ds(pl.multiple_of(other * slot_rows, 16), slot_rows)
    tile = 512
    half_slot = slot_rows // 2
    count = [4]

    def swap(source, target):
        copy = remote(
            source, target, r.pair_send.at[count[0]], r.pair_recv.at[count[0]], (other, chip)
        )
        count[0] += 1
        copy.start()
        return copy

    left_half = lanes(half_slot) < HD
    for group in range(2):
        for pair in range(HALF // 2):
            even = context_in[group * HALF + 2 * pair].astype(HIGH)[:half_slot]
            odd = context_in[group * HALF + 2 * pair + 1].astype(HIGH)[:half_slot]
            top = group * slot_rows
            columns = slice(pair * 128, pair * 128 + 128)
            context_wide[top : top + half_slot, columns] = jnp.where(left_half, even, turn(odd))
            context_wide[top + half_slot : top + slot_rows, columns] = jnp.where(
                left_half, turn(even), odd
            )
    context[...] = context_wide[...].astype(LOW)

    def product(index, lhs, rhs):
        out_part[index] = dot(lhs[far, :], rhs)
        copy = swap(out_part.at[index], in_part.at[index])
        mine = dot(lhs[own, :], rhs)
        copy.wait()
        return mine + in_part[index]

    plan_out.arrive()
    branch = product(0, context, w_out[...].reshape(half_width, width)) + branch_bias[0]
    row_index = lax.broadcasted_iota(jnp.int32, (slot_rows, 1), 0)
    tokens = row_index < token_rows
    x_mine = jnp.where(tokens, x_own[...].astype(HIGH), 0.0)
    first, normed1, inverse1 = normalize(x_mine + branch, gains[0], shifts[0])
    low_first[own, :] = first.astype(LOW)
    copy = swap(low_first.at[own], low_first.at[own])
    each(plans_down, Gather.line, 2)
    each(plans_down, Gather.side, 2)
    plan_qkv.own_line(0)
    plan_qkv.own_plane()
    plan_qkv.own_line(1)
    plan_qkv.own_line(2)
    each(plans_in, Gather.arrive)
    copy.wait()

    def widen(index, carry):
        columns = pl.ds(pl.multiple_of(index * tile, tile), tile)
        pre = dot(low_first[...], w_in[:, :, :, columns].reshape(width, tile)) + bias_in[:, columns]
        found, derivative = gelu_parts(pre)
        act[:, columns] = found.astype(LOW)
        slope[:, columns] = derivative
        return carry

    lax.fori_loop(0, half_hidden // tile, widen, 0)
    plan_qkv.side(None)
    each(plans_down, Gather.arrive)
    second = product(1, act, w_down[...].reshape(half_hidden, width)) + branch_bias[1]
    plan_qkv.line(0)
    plan_qkv.side(0)
    result, normed2, inverse2 = normalize(first + second, gains[1], shifts[1])
    r.hidden_out[...] = result[:token_rows].astype(LOW)
    given = r.out_grad
    upstream = jnp.concatenate(
        [given[...].astype(HIGH), jnp.zeros((slot_rows - token_rows, width), HIGH)], axis=0
    )
    d_sum2 = normalize_back(upstream, normed2, inverse2, gains[1])
    low_second = d_sum2.astype(LOW)
    d_second[own, :] = low_second
    copy = swap(d_second.at[own], d_second.at[own])
    g_small[...] = jnp.zeros_like(g_small)
    g_small[1:2, 0:width] = column_sums(low_second.astype(HIGH))
    g_small[3:4, 0:width] = column_sums(upstream * normed2)
    g_small[5:6, 0:width] = column_sums(upstream)
    plan_qkv.line(1)
    plan_qkv.side(1)
    copy.wait()
    g_down, g_in, g_out = r.g_down, r.g_in, r.g_out

    def narrow_back(index, carry):
        columns = pl.ds(pl.multiple_of(index * tile, tile), tile)
        down = w_down[pl.ds(index * (tile // 128), tile // 128)].reshape(tile, width)
        low = (dot(d_second[...], down, NT) * slope[:, columns]).astype(LOW)
        d_inner[:, columns] = low
        g_small[pl.ds(8, 1), columns] = column_sums(low.astype(HIGH))
        g_down[columns, :] = dot(act[:, columns], d_second[...], TN).astype(LOW)
        return carry

    lax.fori_loop(0, half_hidden // tile, narrow_back, 0)
    keep_down = local(g_down, r.g_down_out, keep.at[13])
    keep_down.start()
    plan_qkv.line(2)
    plan_qkv.side(2)
    w_in_all = w_in[...].reshape(width, half_hidden)
    out_part[2] = dot(d_inner[far, :], w_in_all, NT)
    copy = swap(out_part.at[2], in_part.at[2])
    mine = dot(d_inner[own, :], w_in_all, NT)

    def widen_grad(index, carry):
        rows = pl.ds(pl.multiple_of(index * 256, 256), 256)
        g_in[rows, :] = dot(low_first[:, rows], d_inner[...], TN).astype(LOW)
        return carry

    lax.fori_loop(0, width // 256, widen_grad, 0)
    keep_in = local(g_in, r.g_in_out, keep.at[14])
    keep_in.start()
    copy.wait()
    d_first = d_sum2 + mine + in_part[2]
    d_sum1 = normalize_back(d_first, normed1, inverse1, gains[0])
    r.d_sum1[...] = d_sum1
    low_branch = d_sum1.astype(LOW)
    d_branch[own, :] = low_branch
    copy = swap(d_branch.at[own], d_branch.at[own])
    g_small[0:1, 0:width] = column_sums(low_branch.astype(HIGH))
    g_small[2:3, 0:width] = column_sums(d_first * normed1)
    g_small[4:5, 0:width] = column_sums(d_first)
    copy.wait()
    w_out_all = w_out[...].reshape(half_width, width)
    context_wide[...] = dot(d_branch[...], w_out_all, NT)
    for group in range(2):
        for pair in range(HALF // 2):
            both = context_wide[
                group * slot_rows : (group + 1) * slot_rows, pair * 128 : pair * 128 + 128
            ]
            r.d_message[group * HALF + 2 * pair] = fold(both)
            r.d_message[group * HALF + 2 * pair + 1] = fold(turn(both))
    g_out[...] = dot(context[...], d_branch[...], TN).astype(LOW)
    plan_qkv.arrive()
    keep_qkv = local(w_qkv, r.w_qkv_out, keep.at[15])
    keep_qkv.start()

    for ahead in range(1, CHIPS):
        w_copy(ahead).wait_send()
    rel_each(lambda copy: copy.wait_send(), None)
    context_sent()
    each(x_plans, Gather.finish)
    each(plans_in + plans_down + [plan_out, plan_qkv], Gather.finish)
    for copy in stash + [keep_x, keep_rel, keep_facts, keep_down, keep_in, keep_qkv]:
        copy.wait()


def second_kernel(names, *refs):
    r = types.SimpleNamespace(**dict(zip(names, refs)))
    core, chip = place()
    other = 1 - core
    left, right, right_t, value_t, kept = r.left, r.right, r.right_t, r.value_t, r.kept
    rel_all, x_all, w_qkv = r.rel_all, r.x_all, r.w_qkv
    g_in, g_down, g_out = r.g_in, r.g_down, r.g_out
    total, width = x_all.shape
    slot_rows = total // CHIPS
    half_slot = slot_rows // 2
    half_width = width // 2
    depth = w_qkv.shape[3]
    token_rows = r.hidden_grad.shape[0]
    scale = 1.0 / math.sqrt(4.0 * HD)
    keep = r.keep_sem
    loads = [
        local(there, held, keep.at[k])
        for k, (there, held) in enumerate(
            (
                (r.left_any, left),
                (r.right_t_any, right_t),
                (r.value_t_any, value_t),
                (r.kept_any, kept),
                (r.right_any, right),
                (r.g_down_any, g_down),
                (r.g_in_any, g_in),
                (r.g_out_any, g_out),
                (r.x_all_any, x_all),
                (r.w_qkv_any, w_qkv),
            )
        )
    ]
    for copy in loads:
        copy.start()
    meet()
    d_arrived = r.d_arrived
    grad_arrives, grad_sent = to_heads(r.d_message, d_arrived, r.d_send, r.d_recv)
    plan_down = Reduce(
        r.g_down_any,
        g_down,
        lambda ref, slot: ref.at[slot],
        [r.down_1, r.down_2, r.down_3],
        r.down_send,
        r.down_recv,
        "y",
    )
    plan_in = Reduce(
        r.g_in_any,
        g_in,
        lambda ref, slot: ref.at[:, slot],
        [r.in_1, r.in_2, r.in_3],
        r.in_send,
        r.in_recv,
        "x",
    )
    plan_out = ReduceEarly(
        r.g_out_any,
        g_out,
        lambda ref, slot: ref.at[slot],
        [r.out_1, r.out_2, r.out_3],
        r.out_send,
        r.out_recv,
        "y",
    )
    plans = (plan_down, plan_in)
    plan_out.start()

    each(plans, Reduce.start, 2)
    each(plans, Reduce.start, 1)

    z, y, x = coordinates(chip)
    small_sum, small_in = r.small_sum, r.small_in
    small_sum[...] = r.g_small[...]

    def small_copy(index, to_core, to_chip):
        return remote(
            small_sum, small_in.at[index], r.small_send.at[index], r.small_recv.at[index], (to_core, to_chip)
        )

    def small_turn(index):
        if index == 0:
            return [small_copy(0, other, chip)]
        if index == 1:
            return [small_copy(1, core, z * 4 + (1 - y) * 2 + x)]
        if index == 2:
            return [small_copy(2, core, z * 4 + y * 2 + 1 - x)]
        return [
            small_copy(2 + ahead, core, lax.rem(z + ahead, 4) * 4 + y * 2 + x) for ahead in (1, 2, 3)
        ]

    def small_start(index):
        for copy in small_turn(index):
            copy.start()

    def small_end(index):
        for copy in small_turn(index):
            copy.wait()
        if index == 0:
            small_sum[0:8, :] += small_in[0, 0:8, :]
        elif index < 3:
            small_sum[...] += small_in[index]

    small_start(0)
    left_half = lanes(half_slot) < HD
    d_context = r.d_context
    grad_arrives()
    for slot in range(CHIPS):
        both = d_arrived[slot].astype(HIGH)[:half_slot]
        top = slot * slot_rows
        d_context[top : top + half_slot, :] = jnp.where(left_half, both, 0.0)
        d_context[top + half_slot : top + slot_rows, :] = jnp.where(left_half, turn(both), 0.0)
    table_t = rel_all[:, 0 : 3 * NB]
    lane = lanes(BLOCK)
    first_half = lane < HD
    d_query, d_query_t, d_pair_t, rel_grad = r.d_query, r.d_query_t, r.d_pair_t, r.rel_grad
    d_pair_t[...] = jnp.zeros_like(d_pair_t)
    rel_grad[...] = jnp.zeros_like(rel_grad)
    for copy in loads:
        copy.wait()

    def step(index, carry):
        rows = pl.ds(pl.multiple_of(index * BLOCK, BLOCK), BLOCK)
        at_steps(
            index,
            {
                1: [
                    lambda: each(plans, Reduce.side, 2),
                    lambda: each(plans, Reduce.start, 0),
                    lambda: small_end(0),
                    lambda: small_start(1),
                ],
                2: [lambda: each(plans, Reduce.line, 2), plan_out.third],
                4: [
                    lambda: each(plans, Reduce.side, 1),
                    lambda: each(plans, Reduce.start, None),
                    lambda: small_end(1),
                    lambda: small_start(2),
                ],
                5: [lambda: each(plans, Reduce.line, 1), plan_out.across],
                7: [lambda: each(plans, Reduce.side, 0), lambda: small_end(2), lambda: small_start(3)],
                8: [lambda: each(plans, Reduce.line, 0)],
            },
        )
        facts = kept[rows, :]
        grad = d_context[rows, :]
        delta = jnp.sum(grad * facts, axis=1, keepdims=True)
        probs = jnp.exp(dot(left[rows, :], right_t[...]) - facts[:, HD : HD + 1])
        d_probs = dot(grad.astype(LOW), value_t[...])
        d_logits = (probs * (d_probs - delta)).astype(LOW)
        query_t = jnp.where(first_half, left[rows, 256:384].astype(HIGH), 0.0).T[0:HD]
        d_pair_t[0:HD, :] += dot(grad.T[0:HD].astype(LOW), probs.astype(LOW))
        d_pair_t[HD : 2 * HD, :] += dot(query_t.astype(LOW), d_logits)
        back = dot(d_logits, right[...]) * scale
        ids = facts.astype(jnp.int32)
        order, box_x, box_y = (ids[:, HD + k : HD + k + 1] for k in (1, 2, 3))

        def placed(column, ids_of, extent, start):
            found_at = ids_of + NB // 2 - lane
            found = jnp.take_along_axis(
                back[:, column * 128 : column * 128 + 128], jnp.clip(found_at, 0, extent - 1) + start, axis=1
            )
            return jnp.where(jnp.logical_and(found_at >= 0, found_at < extent), found, 0.0)

        wide = back[:, 0:128]
        low_end = jnp.sum(jnp.where(lane >= order + NB // 2, wide, 0.0), axis=1, keepdims=True)
        high_end = jnp.sum(jnp.where(lane <= order - (NB // 2 - 1), wide, 0.0), axis=1, keepdims=True)
        first = placed(0, order, ORDER_RANGE, 0)
        first = jnp.where(lane == 0, low_end, jnp.where(lane == NB - 1, high_end, first))
        d_tables = jnp.concatenate(
            [first, placed(1, box_x, BOX_RANGE, 0), placed(1, box_y, BOX_RANGE, BOX_RANGE)], axis=1
        ).astype(LOW)
        from_tables = dot(d_tables, table_t, NT)
        d_query[rows, :] = jnp.where(
            first_half,
            back[:, 256:384] + jnp.concatenate([from_tables, from_tables], axis=1),
            0.0,
        )
        d_query_t[0:HD, rows] = d_query[rows, :].T[0:HD].astype(LOW)
        rel_grad[:, 0 : 3 * NB] += dot((query_t / scale).astype(LOW), d_tables)
        return carry

    lax.fori_loop(0, total // BLOCK, step, 0)
    message = r.message
    slot_lane = lanes(slot_rows) < HD
    for slot in range(CHIPS):
        top = slot * slot_rows
        if slot % 8 == 0:
            turned = d_pair_t[:, top : top + 8 * slot_rows].T
        pair = turned[(slot % 8) * slot_rows : (slot % 8 + 1) * slot_rows]
        message[slot, 0:slot_rows, :] = jnp.where(
            slot_lane, d_query[top : top + slot_rows, :], pair
        ).astype(LOW)
        message[slot, slot_rows:, :] = fold(pair)
    tokens_in = r.tokens_in
    tokens_arrive, tokens_sent = to_tokens(message, tokens_in, r.msg_send, r.msg_recv)
    each(plans, Reduce.side, None)

    d_query_t[HD : 3 * HD, :] = d_pair_t[...].astype(LOW)
    d_columns = d_query_t[...]
    sums = jnp.sum(d_columns[0 : 2 * HD].astype(HIGH), axis=1, keepdims=True)
    rel_grad[:, 3 * NB : 4 * NB] = jnp.where(
        lanes(HD) == 0, sums[0:HD], jnp.where(lanes(HD) == 1, sums[HD : 2 * HD], 0.0)
    )
    rel_far, rel_sum = r.rel_far, r.rel_sum
    rel_rows = pl.ds(pl.multiple_of(other * depth, 8), depth)
    rel_pair = remote(
        rel_grad.at[rel_rows], rel_far, r.pair_send.at[0], r.pair_recv.at[0], (other, chip)
    )
    rel_pair.start()
    w_mine, w_far, w_low, w_came = r.w_mine, r.w_far, r.w_low, r.w_came
    w_grad = dot(d_columns, x_all[...])
    for part in range(2):
        w_mine[part] = w_grad[:, part * half_width : (part + 1) * half_width]
    w_pair = remote(
        w_mine.at[other], w_far, r.pair_send.at[1], r.pair_recv.at[1], (other, chip)
    )
    w_pair.start()
    rel_pair.wait()
    rel_sum[...] = rel_grad[pl.ds(pl.multiple_of(core * depth, 8), depth), :] + rel_far[...]
    rel_to = (lax.div(chip, HALF), lax.rem(2 * chip + core, CHIPS))
    rel_here = jnp.logical_and(rel_to[0] == core, rel_to[1] == chip)
    rel_came = r.rel_came
    rel_copy = lambda: remote(rel_sum, rel_came, r.rel_send.at[0], r.rel_recv.at[0], rel_to)
    own_rel = lambda: local(rel_sum, rel_came, r.rel_recv.at[0])
    pl.when(rel_here)(lambda: own_rel().start())
    pl.when(jnp.logical_not(rel_here))(lambda: rel_copy().start())
    w_pair.wait()
    w_sum = (w_mine[core] + w_far[...]).T
    w_low[...] = jnp.zeros_like(w_low)
    for slot in range(CHIPS):
        w_low[slot, :, 0 : 3 * HD] = w_sum[slot * depth : (slot + 1) * depth].astype(LOW)

    def w_copy(ahead):
        to = lax.rem(chip + ahead, CHIPS)
        return remote(w_low.at[to], w_came.at[chip], r.w_send.at[ahead], r.w_recv.at[chip], (core, to))

    own_w = local(w_low.at[chip], w_came.at[chip], keep.at[10])
    own_w.start()
    for ahead in range(1, CHIPS):
        w_copy(ahead).start()

    wide, low = r.wide, r.low
    tokens_arrive()
    for group in range(2):
        top = group * slot_rows
        for pair in range(HALF // 2):
            columns = slice(pair * 128, pair * 128 + 128)
            even = tokens_in[group * HALF + 2 * pair].astype(HIGH)
            odd = tokens_in[group * HALF + 2 * pair + 1].astype(HIGH)
            even_main, odd_main = even[:slot_rows], odd[:slot_rows]
            low[0, top : top + slot_rows, columns] = jnp.where(
                slot_lane, even_main, turn(odd_main)
            ).astype(LOW)
            low[1, top : top + slot_rows, columns] = jnp.where(
                slot_lane, turn(even_main), odd_main
            ).astype(LOW)
            even_last = even[slot_rows : slot_rows + half_slot]
            odd_last = odd[slot_rows : slot_rows + half_slot]
            wide[top : top + half_slot, columns] = jnp.where(left_half, even_last, turn(odd_last))
            wide[top + half_slot : top + slot_rows, columns] = jnp.where(
                left_half, turn(even_last), odd_last
            )
    low[2] = wide[...].astype(LOW)
    own = pl.ds(pl.multiple_of(core * slot_rows, 16), slot_rows)
    far = pl.ds(pl.multiple_of(other * slot_rows, 16), slot_rows)
    weights = [w_qkv[n].reshape(width, half_width) for n in range(3)]

    def part(rows):
        return (
            dot(low[0, rows, :], weights[0], NT)
            + dot(low[1, rows, :], weights[1], NT)
            + dot(low[2, rows, :], weights[2], NT)
        )

    out_part, in_part = r.out_part, r.in_part
    out_part[...] = part(far)
    x_pair = remote(out_part, in_part, r.pair_send.at[2], r.pair_recv.at[2], (other, chip))
    x_pair.start()
    mine = part(own) + r.d_sum1[...]
    x_pair.wait()
    r.hidden_grad[...] = (mine + in_part[...])[:token_rows].astype(LOW)

    plan_down.finish(r.down_grad)
    in_total, in_far = r.in_total, r.in_far
    plan_in.finish(in_total)
    in_pair = remote(
        in_total.at[other], in_far, r.pair_send.at[3], r.pair_recv.at[3], (other, chip)
    )
    in_pair.start()
    plan_out.finish(r.out_grad)
    half_hidden = in_total.shape[2]
    in_grad = r.in_grad
    in_grad[:, columns_of(core, half_hidden)] = in_total[core]
    small_end(3)
    me = core * CHIPS + chip
    small_all = lambda rows, columns: (
        small_sum[rows, columns] + small_in[3, rows, columns] + small_in[4, rows, columns] + small_in[5, rows, columns]
    )
    strip = columns_of(lax.div(me * depth, 128), 128)
    shares = pltpu.roll(small_all(pl.ds(0, 8), strip), 128 - lax.rem(me * depth, 128), 1)
    for number, result in enumerate((r.branch_grad, r.gain_grad, r.shift_grad)):
        result[...] = shares[2 * number : 2 * number + 2, 0:depth]
    r.bias_grad[...] = small_all(pl.ds(8, 1), columns_of(chip, 128))
    own_rel().wait()
    pl.when(jnp.logical_not(rel_here))(lambda: rel_copy().wait_send())
    for kind in range(3):
        r.rel_tables_grad[kind] = rel_came[:, kind * NB : (kind + 1) * NB]
    r.qkv_bias_grad[...] = rel_came[:, 3 * NB : 4 * NB].T[0:2]
    own_w.wait()
    for ahead in range(1, CHIPS):
        came = lax.rem(chip + ahead, CHIPS)
        remote(w_low.at[0], w_came.at[came], r.w_send.at[0], r.w_recv.at[came], (core, came)).wait_recv()
        w_copy(ahead).wait_send()
    lane_depth = lanes(depth) < HD
    for pair in range(H // 2):
        columns = slice(pair * 128, pair * 128 + 128)
        even = w_came[2 * pair].astype(HIGH)
        odd = w_came[2 * pair + 1].astype(HIGH)
        w_out = r.qkv_grad
        w_out[0, :, columns] = jnp.where(lane_depth, even[:, 0:128], turn(odd[:, 0:128]))
        w_out[2, :, columns] = jnp.where(lane_depth, turn(even[:, 0:128]), odd[:, 0:128])
        w_out[1, :, columns] = jnp.where(lane_depth, even[:, 128:256], turn(odd[:, 128:256]))
    in_pair.wait()
    in_grad[:, columns_of(other, half_hidden)] = in_far[...]
    grad_sent()
    tokens_sent()


def hand_over(count, *refs):
    for source, target in zip(refs[:count], refs[count:]):
        target[...] = source[...]


def handed_over(arrays):
    return pl.pallas_call(
        functools.partial(hand_over, len(arrays)),
        out_shape=[jax.ShapeDtypeStruct(array.shape, array.dtype) for array in arrays],
        name="hand_over",
    )(*arrays)


def call(kernel, name, number, inputs, outputs, scratch):
    names = list(inputs) + list(outputs) + list(scratch)
    results = pl.pallas_call(
        functools.partial(kernel, names),
        out_shape=[jax.ShapeDtypeStruct(shape, dtype) for shape, dtype, _ in outputs.values()],
        in_specs=[pl.BlockSpec(memory_space=space) for _, space in inputs.values()],
        out_specs=[pl.BlockSpec(memory_space=space) for _, _, space in outputs.values()],
        scratch_shapes=list(scratch.values()),
        compiler_params=pltpu.CompilerParams(
            collective_id=number, has_side_effects=True, vmem_limit_bytes=VMEM_LIMIT
        ),
        name=name,
    )(*(array for array, _ in inputs.values()))
    return types.SimpleNamespace(**dict(zip(outputs, results)))


def head_shards(
    hidden_in,
    segment_ids,
    order_ids,
    box_ids,
    qkv_weight,
    qkv_bias,
    rel_tables,
    out_weight,
    branch_bias,
    norm_gains,
    norm_shifts,
    ffn_in,
    ffn_in_bias,
    ffn_out,
    out_grad,
):
    rows, width = hidden_in.shape
    slot_rows = -(-rows // 16) * 16
    total = CHIPS * slot_rows
    depth = qkv_weight.shape[1]
    hidden = ffn_in.shape[1]
    half_hidden, half_width = hidden // 2, width // 2
    down_rows = ffn_out.shape[0]
    both = 2 * slot_rows
    fold_rows = -(-(slot_rows // 2) // 16) * 16
    any_, vmem, dma = pl.ANY, pltpu.VMEM, pltpu.SemaphoreType.DMA
    message = (CHIPS, fold_rows, 128)
    made = call(
        first_kernel,
        "forward_and_feed_forward",
        0,
        dict(
            hidden_in=(hidden_in, vmem),
            segment_ids=(segment_ids.reshape(1, rows), vmem),
            order_ids=(order_ids.reshape(1, rows), vmem),
            box_ids=(box_ids, vmem),
            qkv_weight=(qkv_weight, vmem),
            qkv_any=(qkv_weight, any_),
            qkv_bias=(qkv_bias, vmem),
            rel_tables=(rel_tables.transpose(0, 2, 1), vmem),
            out_weight=(out_weight, any_),
            branch_bias=(branch_bias, vmem),
            norm_gains=(norm_gains, vmem),
            norm_shifts=(norm_shifts, vmem),
            ffn_in=(ffn_in, any_),
            ffn_in_bias=(ffn_in_bias.reshape(1, down_rows), vmem),
            ffn_out=(ffn_out, any_),
            out_grad=(out_grad, vmem),
        ),
        dict(
            hidden_out=((rows, width), LOW, vmem),
            x_out=((total, width), LOW, any_),
            rel_out=((2 * depth, 4 * NB), LOW, any_),
            left_out=((total, 384), LOW, any_),
            right_out=((total, 384), LOW, any_),
            right_t_out=((384, total), LOW, any_),
            value_t_out=((128, total), LOW, any_),
            kept_out=((total, 128), HIGH, any_),
            g_down_out=((half_hidden, width), LOW, any_),
            g_in_out=((width, half_hidden), LOW, any_),
            g_out=((half_width, width), LOW, vmem),
            g_small=((16, half_hidden), HIGH, vmem),
            d_sum1=((slot_rows, width), HIGH, vmem),
            d_message=(message, LOW, vmem),
            w_qkv_out=((3, 2, CHIPS, depth, half_width), LOW, any_),
        ),
        dict(
            x_own=vmem((slot_rows, width), LOW),
            x_vmem=vmem((total, width), LOW),
            extra=vmem((slot_rows - rows, width), HIGH),
            w_own=vmem((H, depth, 4 * HD), LOW),
            w_all=vmem((2 * CHIPS, depth, 4 * HD), LOW),
            rel_own=vmem((depth, 4 * NB), LOW),
            rel_all=vmem((2 * depth, 4 * NB), LOW),
            w_in=vmem((2, CHIPS, depth, half_hidden), LOW),
            w_down=vmem((CHIPS, down_rows, width), LOW),
            w_out=vmem((CHIPS, depth, width), LOW),
            w_qkv=vmem((3, 2, CHIPS, depth, half_width), LOW),
            meta=vmem((total, 128), HIGH),
            shares=vmem((2, 3, 8, half_width), HIGH),
            bias_in=vmem((1, half_hidden), HIGH),
            left=vmem((total, 384), LOW),
            right=vmem((total, 384), LOW),
            right_t=vmem((384, total), LOW),
            value=vmem((total, 128), LOW),
            value_t=vmem((128, total), LOW),
            kept=vmem((total, 128), HIGH),
            message=vmem(message, LOW),
            context_in=vmem(message, LOW),
            context_wide=vmem((both, half_width), HIGH),
            context=vmem((both, half_width), LOW),
            low_first=vmem((both, width), LOW),
            act=vmem((both, half_hidden), LOW),
            slope=vmem((both, half_hidden), HIGH),
            d_second=vmem((both, width), LOW),
            d_inner=vmem((both, half_hidden), LOW),
            d_branch=vmem((both, width), LOW),
            g_down=vmem((half_hidden, width), LOW),
            g_in=vmem((width, half_hidden), LOW),
            out_part=vmem((3, slot_rows, width), HIGH),
            in_part=vmem((3, slot_rows, width), HIGH),
            keep_sem=dma((16,)),
            x_send=dma((2, 16)),
            x_recv=dma((2, 16)),
            w_send=dma((16,)),
            w_recv=dma((16,)),
            rel_send=dma((2,)),
            rel_recv=dma((2,)),
            out_send=dma((16,)),
            out_recv=dma((16,)),
            in_send=dma((2, 16)),
            in_recv=dma((2, 16)),
            down_send=dma((2, 16)),
            down_recv=dma((2, 16)),
            qkv_send=dma((16,)),
            qkv_recv=dma((16,)),
            msg_send=dma((16,)),
            msg_recv=dma((16,)),
            pair_send=dma((10,)),
            pair_recv=dma((10,)),
        ),
    )
    g_down = made.g_down_out.reshape(CHIPS, down_rows, width)
    g_in = made.g_in_out.reshape(2, CHIPS, depth, half_hidden)
    g_out = made.g_out.reshape(CHIPS, depth, width)
    out_message = (CHIPS, slot_rows + fold_rows, 128)
    in_block, down_block, out_block = (2, depth, half_hidden), (down_rows, width), (depth, width)
    ended = call(
        second_kernel,
        "backward_and_sums",
        1,
        dict(
            left_any=(made.left_out, any_),
            right_any=(made.right_out, any_),
            right_t_any=(made.right_t_out, any_),
            value_t_any=(made.value_t_out, any_),
            kept_any=(made.kept_out, any_),
            rel_all=(made.rel_out, vmem),
            x_all_any=(made.x_out, any_),
            w_qkv_any=(made.w_qkv_out, any_),
            g_down_any=(g_down, any_),
            g_in_any=(g_in, any_),
            g_out_any=(g_out, any_),
            g_small=(made.g_small, vmem),
            d_sum1=(made.d_sum1, vmem),
            d_message=(made.d_message, vmem),
        ),
        dict(
            hidden_grad=((rows, width), LOW, vmem),
            qkv_grad=((3, depth, width), HIGH, vmem),
            qkv_bias_grad=((2, depth), HIGH, vmem),
            rel_tables_grad=((3, depth, NB), HIGH, vmem),
            out_grad=((depth, width), HIGH, vmem),
            branch_grad=((2, depth), HIGH, vmem),
            gain_grad=((2, depth), HIGH, vmem),
            shift_grad=((2, depth), HIGH, vmem),
            in_grad=((depth, hidden), HIGH, vmem),
            bias_grad=((1, down_rows), HIGH, vmem),
            down_grad=((down_rows, width), HIGH, vmem),
        ),
        dict(
            left=vmem((total, 384), LOW),
            right=vmem((total, 384), LOW),
            right_t=vmem((384, total), LOW),
            value_t=vmem((128, total), LOW),
            kept=vmem((total, 128), HIGH),
            x_all=vmem((total, width), LOW),
            w_qkv=vmem((3, 2, CHIPS, depth, half_width), LOW),
            g_down=vmem((CHIPS,) + down_block, LOW),
            g_in=vmem((2, CHIPS, depth, half_hidden), LOW),
            g_out=vmem((CHIPS,) + out_block, LOW),
            in_1=vmem((8,) + in_block, LOW),
            in_2=vmem((4,) + in_block, LOW),
            in_3=vmem((3,) + in_block, LOW),
            down_1=vmem((8,) + down_block, LOW),
            down_2=vmem((4,) + down_block, LOW),
            down_3=vmem((3,) + down_block, LOW),
            out_1=vmem((12,) + out_block, LOW),
            out_2=vmem((2,) + out_block, LOW),
            out_3=vmem((1,) + out_block, LOW),
            in_total=vmem(in_block, HIGH),
            in_far=vmem((depth, half_hidden), HIGH),
            small_sum=vmem((16, half_hidden), HIGH),
            small_in=vmem((6, 16, half_hidden), HIGH),
            d_arrived=vmem(message, LOW),
            d_context=vmem((total, 128), HIGH),
            d_query=vmem((total, 128), HIGH),
            d_query_t=vmem((3 * HD, total), LOW),
            d_pair_t=vmem((2 * HD, total), HIGH),
            rel_grad=vmem((2 * depth, 4 * NB), HIGH),
            rel_far=vmem((depth, 4 * NB), HIGH),
            rel_sum=vmem((depth, 4 * NB), HIGH),
            rel_came=vmem((depth, 4 * NB), HIGH),
            message=vmem(out_message, LOW),
            tokens_in=vmem(out_message, LOW),
            w_mine=vmem((2, 3 * HD, half_width), HIGH),
            w_far=vmem((3 * HD, half_width), HIGH),
            w_low=vmem((CHIPS, depth, 4 * HD), LOW),
            w_came=vmem((CHIPS, depth, 4 * HD), LOW),
            wide=vmem((both, half_width), HIGH),
            low=vmem((3, both, half_width), LOW),
            out_part=vmem((slot_rows, width), HIGH),
            in_part=vmem((slot_rows, width), HIGH),
            keep_sem=dma((11,)),
            d_send=dma((16,)),
            d_recv=dma((16,)),
            in_send=dma((16,)),
            in_recv=dma((16,)),
            down_send=dma((16,)),
            down_recv=dma((16,)),
            out_send=dma((16,)),
            out_recv=dma((16,)),
            small_send=dma((6,)),
            small_recv=dma((6,)),
            msg_send=dma((16,)),
            msg_recv=dma((16,)),
            w_send=dma((16,)),
            w_recv=dma((16,)),
            rel_send=dma((1,)),
            rel_recv=dma((1,)),
            pair_send=dma((4,)),
            pair_recv=dma((4,)),
        ),
    )
    results = list(handed_over(
        [
            made.hidden_out,
            ended.hidden_grad,
            ended.qkv_grad,
            ended.qkv_bias_grad,
            ended.rel_tables_grad,
            ended.out_grad,
            ended.branch_grad,
            ended.gain_grad,
            ended.shift_grad,
            ended.in_grad,
            ended.bias_grad,
            ended.down_grad,
        ]
    ))
    results[4] = results[4].transpose(0, 2, 1)
    results[10] = results[10].reshape(down_rows)
    return tuple(results)


def solution(mesh):
    by_heads = mesh.shape["grp"] == 2 and mesh.shape["blk"] == CHIPS == H
    return jax.shard_map(
        head_shards if by_heads else shards,
        mesh=mesh,
        in_specs=(
            P(("grp", "blk"), None),
            P(("grp", "blk")),
            P(("grp", "blk")),
            P(None, ("grp", "blk")),
            P(None, ("grp", "blk"), None),
            P(None, ("grp", "blk")),
            P(None, None, ("grp", "blk")),
            P(("grp", "blk"), None),
            P(None, ("grp", "blk")),
            P(None, ("grp", "blk")),
            P(None, ("grp", "blk")),
            P(("grp", "blk"), None),
            P(("grp", "blk")),
            P(("grp", "blk"), None),
            P(("grp", "blk"), None),
        ),
        out_specs=(
            P(("grp", "blk"), None),
            P(("grp", "blk"), None),
            P(None, ("grp", "blk"), None),
            P(None, ("grp", "blk")),
            P(None, None, ("grp", "blk")),
            P(("grp", "blk"), None),
            P(None, ("grp", "blk")),
            P(None, ("grp", "blk")),
            P(None, ("grp", "blk")),
            P(("grp", "blk"), None),
            P(("grp", "blk")),
            P(("grp", "blk"), None),
        ),
        check_vma=False,
    )
```

```python
import functools
import math
import types

import jax
import jax.numpy as jnp
from jax import lax
from jax.experimental import pallas as pl
from jax.experimental.pallas import tpu as pltpu
from jax.sharding import PartitionSpec as P

H = 16
HD = 64
NB = 128
ORDER_RANGE = 128
BOX_RANGE = 64


NEGATIVE = -1e30
EPSILON = 1e-05


def shifted(x, axis, by):
    devices = lax.axis_size(axis)
    return lax.ppermute(x, axis, [(i, (i + by) % devices) for i in range(devices)])


def block_size(row_count):
    chosen = 1
    for option in range(1, min(row_count, 544) + 1):
        if row_count % option == 0:
            chosen = option
    return chosen


def kind_ranges():
    return (ORDER_RANGE, BOX_RANGE, BOX_RANGE)


def query_maps(layout_ids):
    maps_out = []
    for column, extent in enumerate(kind_ranges()):
        offsets = layout_ids[:, column][:, None] - jnp.arange(extent, dtype=jnp.int32)[None, :]
        bucket = jnp.clip(offsets, -(NB // 2), NB // 2 - 1) + NB // 2
        maps_out.append(bucket[:, :, None] == jnp.arange(NB, dtype=jnp.int32)[None, None, :])
    return maps_out


def key_onehot(key_ids):
    pieces_out = []
    for column, extent in enumerate(kind_ranges()):
        pieces_out.append(
            key_ids[:, column + 1][:, None] == jnp.arange(extent, dtype=jnp.int32)[None, :]
        )
    return jnp.concatenate(pieces_out, axis=1).astype(jnp.bfloat16)


def norm_forward(values_in, norm_gain, norm_shift):
    center = values_in - jnp.mean(values_in, axis=-1, keepdims=True)
    inverse = lax.rsqrt(jnp.mean(center * center, axis=-1, keepdims=True) + EPSILON)
    normed = center * inverse
    return (normed * norm_gain + norm_shift, normed, inverse)


def norm_backward(upstream, normed, inverse, norm_gain):
    scaled = upstream * norm_gain
    inner_part = (
        scaled
        - jnp.mean(scaled, axis=-1, keepdims=True)
        - normed * jnp.mean(scaled * normed, axis=-1, keepdims=True)
    )
    return (inner_part * inverse, jnp.sum(upstream * normed, axis=0), jnp.sum(upstream, axis=0))


def block_logits(query_heads, selector, query_seg, key_part, meta_part, scaling):
    key_ids = meta_part.astype(jnp.int32)
    row_count = key_part.shape[0]
    key_heads = key_part.reshape(row_count, H, HD)
    content = jnp.einsum("thd,khd->htk", query_heads, key_heads, preferred_element_type=jnp.float32)
    onehot = key_onehot(key_ids)
    rel_bias = jnp.einsum("thv,kv->htk", selector, onehot, preferred_element_type=jnp.float32)
    allowed = query_seg[:, None] == key_ids[None, :, 0]
    logits = jnp.where(allowed[None], (content + rel_bias) * scaling, NEGATIVE)
    return (logits, allowed, onehot, key_heads)


def over_blocks(advance, carry, piece, start):
    row_count = piece[0].shape[0]
    stride = block_size(row_count)

    def one_step(block_index, running):
        portion = tuple(
            (lax.dynamic_slice_in_dim(member, block_index * stride, stride, 0) for member in piece)
        )
        return advance(running, portion, start + block_index * stride)

    return lax.fori_loop(0, row_count // stride, one_step, carry)


def shards(
    hidden_in,
    segment_ids,
    order_ids,
    box_ids,
    qkv_weight,
    qkv_bias,
    rel_tables,
    out_weight,
    branch_bias,
    norm_gains,
    norm_shifts,
    ffn_in,
    ffn_in_bias,
    ffn_out,
    out_grad,
):
    gathered = (
        lax.all_gather(qkv_weight, ("grp", "blk"), axis=1, tiled=True),
        lax.all_gather(qkv_bias, ("grp", "blk"), axis=1, tiled=True),
        lax.all_gather(rel_tables, ("grp", "blk"), axis=2, tiled=True),
        lax.all_gather(out_weight, ("grp", "blk"), axis=0, tiled=True),
        lax.all_gather(branch_bias, ("grp", "blk"), axis=1, tiled=True),
        lax.all_gather(norm_gains, ("grp", "blk"), axis=1, tiled=True),
        lax.all_gather(norm_shifts, ("grp", "blk"), axis=1, tiled=True),
        lax.all_gather(ffn_in, ("grp", "blk"), axis=0, tiled=True),
        lax.all_gather(ffn_in_bias, ("grp", "blk"), axis=0, tiled=True),
        lax.all_gather(ffn_out, ("grp", "blk"), axis=0, tiled=True),
    )
    w_qkv, b_qkv, w_rel, w_out, b_branch, gains, shifts, w_in, b_in, w_down = gathered
    row_count = hidden_in.shape[0]
    width = hidden_in.shape[1]
    scaling = 1.0 / math.sqrt(4.0 * HD)
    select_width = ORDER_RANGE + 2 * BOX_RANGE
    projected = jnp.einsum("td,cde->cte", hidden_in, w_qkv, preferred_element_type=jnp.float32)
    bias_qkv = b_qkv.astype(jnp.float32)
    query_rows = (projected[0] + bias_qkv[0]).astype(jnp.bfloat16)
    key_rows = projected[1].astype(jnp.bfloat16)
    value_rows = (projected[2] + bias_qkv[1]).astype(jnp.bfloat16)
    layout_ids = jnp.stack([order_ids, box_ids[0], box_ids[1]], axis=1)
    key_meta = jnp.stack([segment_ids, order_ids, box_ids[0], box_ids[1]], axis=1).astype(
        jnp.bfloat16
    )
    query_heads = query_rows.reshape(row_count, H, HD)
    rel_heads = w_rel.reshape(3, NB, H, HD)
    tables = jnp.einsum(
        "thd,nbhd->thnb", query_heads, rel_heads, preferred_element_type=jnp.float32
    ).astype(jnp.bfloat16)
    maps_list = query_maps(layout_ids)
    selector = jnp.concatenate(
        [
            jnp.einsum(
                "thb,tvb->thv",
                tables[:, :, column],
                maps_list[column].astype(jnp.bfloat16),
                preferred_element_type=jnp.float32,
            )
            for column in range(3)
        ],
        axis=2,
    ).astype(jnp.bfloat16)

    def forward_step(running, portion, offset):
        row_top, row_total, weighted = running
        key_part, value_part, meta_part = portion
        logits, allowed, onehot, key_heads = block_logits(
            query_heads, selector, segment_ids, key_part, meta_part, scaling
        )
        new_top = jnp.maximum(row_top, jnp.max(logits, axis=2))
        rescale = jnp.exp(row_top - new_top)
        weights = jnp.where(allowed[None], jnp.exp(logits - new_top[:, :, None]), 0.0)
        value_heads = value_part.reshape(value_part.shape[0], H, HD)
        weighted = weighted * rescale.T[:, :, None] + jnp.einsum(
            "htk,khd->thd",
            weights.astype(jnp.bfloat16),
            value_heads,
            preferred_element_type=jnp.float32,
        )
        return (new_top, row_total * rescale + jnp.sum(weights, axis=2), weighted)

    start_state = (
        jnp.full((H, row_count), NEGATIVE, jnp.float32),
        jnp.zeros((H, row_count), jnp.float32),
        jnp.zeros((row_count, H, HD), jnp.float32),
    )
    row_top, row_total, weighted = over_blocks(
        forward_step,
        start_state,
        (
            lax.all_gather(key_rows, "blk", axis=0, tiled=True),
            lax.all_gather(value_rows, "blk", axis=0, tiled=True),
            lax.all_gather(key_meta, "blk", axis=0, tiled=True),
        ),
        jnp.int32(0),
    )
    context_full = weighted / row_total.T[:, :, None]
    log_total = row_top + jnp.log(row_total)
    context = context_full.reshape(row_count, width).astype(jnp.bfloat16)
    branch = jnp.dot(context, w_out, preferred_element_type=jnp.float32) + b_branch[0].astype(
        jnp.float32
    )
    first, normed_one, inverse_one = norm_forward(
        hidden_in.astype(jnp.float32) + branch,
        gains[0].astype(jnp.float32),
        shifts[0].astype(jnp.float32),
    )
    first_low = first.astype(jnp.bfloat16)
    inner_pre = jnp.dot(first_low, w_in, preferred_element_type=jnp.float32) + b_in.astype(
        jnp.float32
    )
    activated, gelu_pull = jax.vjp(
        lambda pre_act: jax.nn.gelu(pre_act, approximate=False), inner_pre
    )
    activated_low = activated.astype(jnp.bfloat16)
    second = jnp.dot(activated_low, w_down, preferred_element_type=jnp.float32) + b_branch[
        1
    ].astype(jnp.float32)
    result, normed_two, inverse_two = norm_forward(
        first + second, gains[1].astype(jnp.float32), shifts[1].astype(jnp.float32)
    )
    hidden_out = result.astype(jnp.bfloat16)
    grad_sum2, gain_grad2, shift_grad2 = norm_backward(
        out_grad.astype(jnp.float32), normed_two, inverse_two, gains[1].astype(jnp.float32)
    )
    grad_second = grad_sum2.astype(jnp.bfloat16)
    grad_w_down = jnp.einsum(
        "tf,td->fd", activated_low, grad_second, preferred_element_type=jnp.float32
    )
    grad_bias_two = jnp.sum(grad_second.astype(jnp.float32), axis=0)
    grad_act = jnp.einsum("td,fd->tf", grad_second, w_down, preferred_element_type=jnp.float32)
    grad_inner = gelu_pull(grad_act)[0].astype(jnp.bfloat16)
    grad_b_in = jnp.sum(grad_inner.astype(jnp.float32), axis=0)
    grad_w_in = jnp.einsum("td,tf->df", first_low, grad_inner, preferred_element_type=jnp.float32)
    grad_first = grad_sum2 + jnp.einsum(
        "tf,df->td", grad_inner, w_in, preferred_element_type=jnp.float32
    )
    grad_sum1, gain_grad1, shift_grad1 = norm_backward(
        grad_first, normed_one, inverse_one, gains[0].astype(jnp.float32)
    )
    grad_branch = grad_sum1.astype(jnp.bfloat16)
    grad_w_out = jnp.einsum("td,te->de", context, grad_branch, preferred_element_type=jnp.float32)
    grad_bias_one = jnp.sum(grad_branch.astype(jnp.float32), axis=0)
    grad_context = jnp.einsum(
        "te,de->td", grad_branch, w_out, preferred_element_type=jnp.float32
    ).astype(jnp.bfloat16)
    grad_heads = grad_context.reshape(row_count, H, HD)
    delta = jnp.einsum("thd,thd->ht", grad_heads.astype(jnp.float32), context_full)

    def backward_core(grad_query, grad_select, portion):
        key_part, value_part, meta_part = portion
        logits, allowed, onehot, key_heads = block_logits(
            query_heads, selector, segment_ids, key_part, meta_part, scaling
        )
        probs = jnp.where(allowed[None], jnp.exp(logits - log_total[:, :, None]), 0.0)
        part_rows = key_part.shape[0]
        value_heads = value_part.reshape(part_rows, H, HD)
        grad_probs = jnp.einsum(
            "thd,khd->htk", grad_heads, value_heads, preferred_element_type=jnp.float32
        )
        grad_logits = (probs * (grad_probs - delta[:, :, None])).astype(jnp.bfloat16)
        grad_query = grad_query + scaling * jnp.einsum(
            "htk,khd->thd", grad_logits, key_heads, preferred_element_type=jnp.float32
        )
        grad_select = grad_select + scaling * jnp.einsum(
            "htk,kv->thv", grad_logits, onehot, preferred_element_type=jnp.float32
        )
        grad_key = scaling * jnp.einsum(
            "htk,thd->khd", grad_logits, query_heads, preferred_element_type=jnp.float32
        )
        grad_value = jnp.einsum(
            "htk,thd->khd",
            probs.astype(jnp.bfloat16),
            grad_heads,
            preferred_element_type=jnp.float32,
        )
        update = jnp.concatenate(
            [grad_key.reshape(part_rows, width), grad_value.reshape(part_rows, width)], axis=1
        )
        return (grad_query, grad_select, update)

    query_zero = jnp.zeros((row_count, H, HD), jnp.float32)
    select_zero = jnp.zeros((row_count, H, select_width), jnp.float32)

    def cycle_turn(turn, carry):
        grad_query, grad_select, key_part, value_part, meta_part, carried = carry
        portion = (key_part, value_part, meta_part)
        grad_query, grad_select, update = backward_core(grad_query, grad_select, portion)
        carried = carried + update
        key_part, value_part, meta_part = shifted((key_part, value_part, meta_part), "blk", 1)
        carried = shifted(carried.astype(jnp.bfloat16), "blk", 1).astype(carried.dtype)
        return (grad_query, grad_select, key_part, value_part, meta_part, carried)

    cycle_start = (
        query_zero,
        select_zero,
        key_rows,
        value_rows,
        key_meta,
        jnp.zeros((row_count, 2 * width), jnp.float32),
    )
    cycle_end = lax.fori_loop(0, lax.axis_size("blk"), cycle_turn, cycle_start)
    grad_query, grad_select, own_pairs = (cycle_end[0], cycle_end[1], cycle_end[5])
    grad_key_rows = own_pairs[:, :width].astype(jnp.bfloat16)
    grad_value_rows = own_pairs[:, width:].astype(jnp.bfloat16)
    cursor = 0
    table_parts = []
    for column, extent in enumerate(kind_ranges()):
        table_parts.append(
            jnp.einsum(
                "thv,tvb->thb",
                grad_select[:, :, cursor : cursor + extent],
                maps_list[column].astype(jnp.float32),
                precision=lax.Precision.HIGHEST,
            )
        )
        cursor = cursor + extent
    grad_tables = jnp.stack(table_parts, axis=2).astype(jnp.bfloat16)
    grad_query_total = grad_query + jnp.einsum(
        "thnb,nbhd->thd", grad_tables, rel_heads, preferred_element_type=jnp.float32
    )
    grad_query_rows = grad_query_total.reshape(row_count, width).astype(jnp.bfloat16)
    grad_rel = jnp.einsum(
        "thnb,thd->nbhd", grad_tables, query_heads, preferred_element_type=jnp.float32
    ).reshape(3, NB, width)
    grad_stack = jnp.stack([grad_query_rows, grad_key_rows, grad_value_rows])
    grad_w_qkv = jnp.einsum(
        "td,cte->cde", hidden_in, grad_stack, preferred_element_type=jnp.float32
    )
    grad_b_qkv = jnp.stack(
        [
            jnp.sum(grad_query_rows.astype(jnp.float32), axis=0),
            jnp.sum(grad_value_rows.astype(jnp.float32), axis=0),
        ]
    )
    grad_input = grad_sum1 + jnp.einsum(
        "cte,cde->td", grad_stack, w_qkv, preferred_element_type=jnp.float32
    )
    summed = (
        lax.psum_scatter(grad_w_qkv, ("grp", "blk"), scatter_dimension=1, tiled=True),
        lax.psum_scatter(grad_b_qkv, ("grp", "blk"), scatter_dimension=1, tiled=True),
        lax.psum_scatter(grad_rel, ("grp", "blk"), scatter_dimension=2, tiled=True),
        lax.psum_scatter(grad_w_out, ("grp", "blk"), scatter_dimension=0, tiled=True),
        lax.psum_scatter(
            jnp.stack([grad_bias_one, grad_bias_two]),
            ("grp", "blk"),
            scatter_dimension=1,
            tiled=True,
        ),
        lax.psum_scatter(
            jnp.stack([gain_grad1, gain_grad2]), ("grp", "blk"), scatter_dimension=1, tiled=True
        ),
        lax.psum_scatter(
            jnp.stack([shift_grad1, shift_grad2]), ("grp", "blk"), scatter_dimension=1, tiled=True
        ),
        lax.psum_scatter(grad_w_in, ("grp", "blk"), scatter_dimension=0, tiled=True),
        lax.psum_scatter(grad_b_in, ("grp", "blk"), scatter_dimension=0, tiled=True),
        lax.psum_scatter(grad_w_down, ("grp", "blk"), scatter_dimension=0, tiled=True),
    )
    return (
        hidden_out,
        grad_input.astype(jnp.bfloat16),
        summed[0],
        summed[1],
        summed[2],
        summed[3],
        summed[4],
        summed[5],
        summed[6],
        summed[7],
        summed[8],
        summed[9],
    )


MESH = pl.DeviceIdType.MESH
LOW = jnp.bfloat16
HIGH = jnp.float32
CHIPS = 16
HALF = 8
BLOCK = 256
MASKED = -1e30
VMEM_LIMIT = 62 * 2**20
NT = ((1,), (1,))
TN = ((0,), (0,))


def dot(left, right, dims=((1,), (0,))):
    return lax.dot_general(left, right, (dims, ((), ())), preferred_element_type=HIGH)


def place():
    return lax.axis_index("grp"), lax.axis_index("blk")


def coordinates(chip):
    return lax.div(chip, 4), lax.rem(lax.div(chip, 2), 2), lax.rem(chip, 2)


def meet():
    core, chip = place()
    me = core * CHIPS + chip
    barrier = pltpu.get_barrier_semaphore()

    def greet(ahead, carry):
        other = lax.rem(me + ahead, 2 * CHIPS)
        pl.semaphore_signal(
            barrier,
            inc=1,
            device_id=(lax.div(other, CHIPS), lax.rem(other, CHIPS)),
            device_id_type=MESH,
        )
        return carry

    lax.fori_loop(1, 2 * CHIPS, greet, 0)
    pl.semaphore_wait(barrier, 2 * CHIPS - 1)


def remote(source, target, send, recv, device):
    return pltpu.make_async_remote_copy(
        src_ref=source,
        dst_ref=target,
        send_sem=send,
        recv_sem=recv,
        device_id=device,
        device_id_type=MESH,
    )


def local(source, target, sem):
    return pltpu.make_async_copy(source, target, sem)


def neighbours(across):
    core, chip = place()
    z, y, x = coordinates(chip)
    planes = (z + 1 - 2 * lax.rem(z, 2), 2 - lax.div(z, 2), 3 - 3 * lax.div(z, 2))

    def slot(far_p, far_q, line):
        far_y, far_x = (far_q, far_p) if across == "x" else (far_p, far_q)
        plane = z if line is None else planes[line]
        return plane * 4 + (1 - y if far_y else y) * 2 + (1 - x if far_x else x)

    return slot


class Shipments:
    def __init__(self, send, recv):
        self.send, self.recv, self.made = send, recv, []
        self.core = lax.axis_index("grp")

    def ship(self, source, target, recv_index, to):
        index = len(self.made)

        def make():
            return remote(
                source(), target(), self.send.at[index], self.recv.at[recv_index()], (self.core, to())
            )

        self.made.append(make)
        make().start()

    def landed(self, target, recv_index, near):
        remote(target, target, self.send.at[0], self.recv.at[recv_index], (self.core, near)).wait_recv()

    def all_sent(self, count=15):
        assert len(self.made) == count
        for make in self.made:
            make().wait_send()


class Gather:
    def __init__(self, pick, send, recv, across):
        self.pick, self.at = pick, neighbours(across)
        self.moves = Shipments(send, recv)

    def ship(self, what, to):
        slot = lambda: self.at(*what)
        ref = lambda: self.pick(slot())
        self.moves.ship(ref, ref, slot, lambda: self.at(*to))

    def landed(self, *what):
        slot = self.at(*what)
        self.moves.landed(self.pick(slot), slot, self.at(1, 0, None))

    def own_line(self, line):
        self.ship((0, 0, None), (0, 0, line))

    def own_plane(self):
        self.ship((0, 0, None), (1, 0, None))
        self.ship((0, 0, None), (0, 1, None))

    def line(self, line):
        self.landed(0, 0, line)
        self.ship((0, 0, line), (1, 0, None))
        self.ship((0, 0, line), (0, 1, None))

    def side(self, line):
        self.landed(1, 0, line)
        self.ship((1, 0, line), (0, 1, None))

    def arrive(self):
        for line in (None, 0, 1, 2):
            for far_p in (0, 1):
                self.landed(far_p, 1, line)

    def finish(self):
        self.moves.all_sent()


class GatherLate(Gather):
    def first(self):
        self.ship((0, 0, None), (1, 0, None))
        self.ship((0, 0, None), (0, 1, None))

    def second(self):
        self.landed(1, 0, None)
        self.ship((1, 0, None), (0, 1, None))

    def third(self):
        for far_p in (0, 1):
            self.landed(far_p, 1, None)
        for line in range(3):
            for what in ((0, 0), (1, 0), (0, 1), (1, 1)):
                self.ship(what + (None,), (0, 0, line))

    def arrive(self):
        for line in range(3):
            for what in ((0, 0), (1, 0), (0, 1), (1, 1)):
                self.landed(*what, line)


class Reduce:
    def __init__(self, sent, own, pick, stages, send, recv, across):
        self.sent, self.own, self.pick, self.at = sent, own, pick, neighbours(across)
        self.first, self.second, self.third_in = stages
        self.moves = Shipments(send, recv)

    @staticmethod
    def number(line):
        return 3 if line is None else line

    def ship(self, source, target, index, to):
        self.moves.ship(source, target, lambda: index, lambda: self.at(*to))

    def landed(self, target, index):
        self.moves.landed(target, index, self.at(1, 0, None))

    def start(self, line):
        for far_p in (1, 0):
            index = self.number(line) * 2 + far_p
            self.ship(
                lambda far_p=far_p: self.pick(self.sent, self.at(far_p, 1, line)),
                lambda index=index: self.first.at[index],
                index,
                (0, 1, None),
            )

    def mine(self, *what):
        return self.pick(self.own, self.at(*what))[...].astype(HIGH)

    def side(self, line):
        number = self.number(line)
        index = number * 2 + 1
        self.landed(self.first.at[index], index)
        self.first[index] = (self.first[index].astype(HIGH) + self.mine(1, 0, line)).astype(LOW)
        self.ship(
            lambda: self.first.at[index], lambda: self.second.at[number], 8 + number, (1, 0, None)
        )

    def line(self, line):
        number = self.number(line)
        index = number * 2
        self.landed(self.first.at[index], index)
        self.landed(self.second.at[number], 8 + number)
        total = (
            self.first[index].astype(HIGH)
            + self.second[number].astype(HIGH)
            + self.mine(0, 0, line)
        )
        if line is None:
            return total
        self.first[index] = total.astype(LOW)
        ahead = lambda: lax.rem(lax.div(self.at(0, 0, None), 4) - lax.div(self.at(0, 0, line), 4) + 4, 4) - 1
        self.moves.ship(
            lambda: self.first.at[index],
            lambda: self.third_in.at[ahead()],
            lambda: 12 + ahead(),
            lambda: self.at(0, 0, line),
        )

    def finish(self, result):
        result[...] = self.line(None)
        for ahead in range(3):
            self.landed(self.third_in.at[ahead], 12 + ahead)
            result[...] += self.third_in[ahead].astype(HIGH)
        self.moves.all_sent()


class ReduceEarly(Reduce):
    PLANE = ((0, 0), (1, 0), (0, 1), (1, 1))

    def ahead(self, line):
        return lax.rem(lax.div(self.at(0, 0, None), 4) - lax.div(self.at(0, 0, line), 4) + 4, 4) - 1

    def start(self):
        for line in (2, 1, 0):
            for number, what in enumerate(self.PLANE):
                index = lambda number=number, line=line: self.ahead(line) * 4 + number
                self.moves.ship(
                    lambda what=what, line=line: self.pick(self.sent, self.at(*what, line)),
                    lambda index=index: self.first.at[index()],
                    index,
                    lambda line=line: self.at(0, 0, line),
                )

    def plane_sum(self, number):
        total = self.mine(*self.PLANE[number], None)
        for ahead in range(3):
            index = ahead * 4 + number
            self.landed(self.first.at[index], index)
            total += self.first[index].astype(HIGH)
        return total

    def third(self):
        for number, far_p in ((3, 1), (2, 0)):
            self.first[number] = self.plane_sum(number).astype(LOW)
            self.ship(
                lambda number=number: self.first.at[number],
                lambda far_p=far_p: self.second.at[far_p],
                12 + far_p,
                (0, 1, None),
            )

    def across(self):
        total = self.plane_sum(1)
        self.landed(self.second.at[1], 13)
        self.first[1] = (total + self.second[1].astype(HIGH)).astype(LOW)
        self.ship(lambda: self.first.at[1], lambda: self.third_in.at[0], 14, (1, 0, None))

    def finish(self, result):
        total = self.plane_sum(0)
        self.landed(self.second.at[0], 12)
        self.landed(self.third_in.at[0], 14)
        result[...] = total + self.second[0].astype(HIGH) + self.third_in[0].astype(HIGH)
        self.moves.all_sent()


def cube_of(order):
    core, chip = place()
    z, y, x = coordinates(chip)

    def at(*flips):
        far = dict(zip(order, flips))
        plane = z + 1 - 2 * lax.rem(z, 2) if far["z"] else z
        return plane * 4 + (1 - y if far["y"] else y) * 2 + (1 - x if far["x"] else x)

    return at


class CubeGather:
    def __init__(self, pick, send, recv, order):
        self.pick, self.at = pick, cube_of(order)
        self.moves = Shipments(send, recv)

    def ship(self, what, to):
        slot = lambda: lax.rem(self.at(*what), HALF)
        ref = lambda: self.pick(slot())
        self.moves.ship(ref, ref, slot, lambda: self.at(*to))

    def landed(self, *what):
        slot = lax.rem(self.at(*what), HALF)
        self.moves.landed(self.pick(slot), slot, self.at(1, 0, 0))

    def own(self):
        for to in ((1, 0, 0), (0, 1, 0), (0, 0, 1)):
            self.ship((0, 0, 0), to)

    def one(self):
        self.landed(1, 0, 0)
        self.ship((1, 0, 0), (0, 1, 0))
        self.ship((1, 0, 0), (0, 0, 1))

    def two(self):
        for what in ((0, 1, 0), (1, 1, 0)):
            self.landed(*what)
            self.ship(what, (0, 0, 1))

    def arrive(self):
        for what in ((0, 0, 1), (1, 0, 1), (0, 1, 1), (1, 1, 1)):
            self.landed(*what)

    def finish(self):
        self.moves.all_sent(7)


class CubeReduce:
    def __init__(self, pick, stage, send, recv, order):
        self.pick, self.stage, self.at = pick, stage, cube_of(order)
        self.moves = Shipments(send, recv)

    def ship(self, source, index, to):
        self.moves.ship(source, lambda: self.stage.at[index], lambda: index, lambda: self.at(*to))

    def mine(self, *what):
        return self.pick(lax.rem(self.at(*what), HALF))

    def term(self, index):
        self.moves.landed(self.stage.at[index], index, self.at(1, 0, 0))
        return self.stage[index].astype(HIGH)

    def own(self):
        for index, (one, two) in enumerate(((1, 1), (0, 1), (1, 0), (0, 0))):
            self.ship(lambda one=one, two=two: self.mine(one, two, 1), index, (0, 0, 1))

    def one(self):
        for index, one in ((0, 1), (1, 0)):
            total = self.mine(one, 1, 0)[...].astype(HIGH) + self.term(index)
            self.stage[index] = total.astype(LOW)
            self.ship(lambda index=index: self.stage.at[index], 4 + index, (0, 1, 0))

    def two(self):
        total = self.mine(1, 0, 0)[...].astype(HIGH) + self.term(2) + self.term(4)
        self.stage[2] = total.astype(LOW)
        self.ship(lambda: self.stage.at[2], 6, (1, 0, 0))

    def arrive(self):
        return self.mine(0, 0, 0)[...].astype(HIGH) + self.term(3) + self.term(5) + self.term(6)

    def finish(self):
        self.moves.all_sent(7)


def each(plans, act, *arguments):
    for plan in plans:
        act(plan, *arguments)


def unit():
    core, chip = place()
    return lax.div(chip, HALF), lax.rem(chip, HALF), core


def to_tokens(source, target, send, recv):
    core, chip = place()
    group, position, _ = unit()
    to_core = lax.div(position, 4)
    mine = group * HALF + 2 * lax.rem(position, 4) + core
    here = to_core == core

    def copy_to(ahead):
        chip_to = lax.rem(chip + ahead, CHIPS)
        return remote(
            source.at[chip_to], target.at[mine], send.at[ahead], recv.at[mine], (to_core, chip_to)
        )

    pl.when(here)(lambda: local(source.at[chip], target.at[mine], recv.at[mine]).start())
    pl.when(jnp.logical_not(here))(lambda: copy_to(0).start())
    for ahead in range(1, CHIPS):
        copy_to(ahead).start()

    def arrive():
        for slot in range(CHIPS):
            local(source.at[slot], target.at[slot], recv.at[slot]).wait()

    def finish():
        pl.when(jnp.logical_not(here))(lambda: copy_to(0).wait_send())
        for ahead in range(1, CHIPS):
            copy_to(ahead).wait_send()

    return arrive, finish


def to_heads(source, target, send, recv):
    core, chip = place()
    group, position, _ = unit()
    here = lax.div(position, 4) == core
    start = 2 * lax.rem(position, 4) + core

    def copy_to(turn_group, ahead):
        to_group = lax.rem(group + turn_group, 2)
        head = lax.rem(start + ahead, HALF)
        return remote(
            source.at[to_group * HALF + head],
            target.at[chip],
            send.at[turn_group * HALF + ahead],
            recv.at[chip],
            (lax.rem(head, 2), to_group * HALF + core * 4 + lax.div(head, 2)),
        )

    def every(act):
        pl.when(jnp.logical_not(here))(lambda: act(copy_to(0, 0)))
        for turn_group in range(2):
            for ahead in range(0 if turn_group else 1, HALF):
                act(copy_to(turn_group, ahead))

    pl.when(here)(
        lambda: local(source.at[group * HALF + start], target.at[chip], recv.at[chip]).start()
    )
    every(lambda copy: copy.start())

    def arrive():
        for slot in range(CHIPS):
            local(source.at[slot], target.at[slot], recv.at[slot]).wait()

    return arrive, lambda: every(lambda copy: copy.wait_send())


def lanes(rows, width=128):
    return lax.broadcasted_iota(jnp.int32, (rows, width), 1)


def turn(values):
    return pltpu.roll(values, HD, 1)


def fold(rows_in):
    half = rows_in.shape[0] // 2
    both = jnp.where(lanes(half) < HD, rows_in[:half], turn(rows_in[half:]))
    pad = -half % 16
    if pad:
        both = jnp.concatenate([both, jnp.zeros((pad, 128), HIGH)], axis=0)
    return both.astype(LOW)


def column_sums(v):
    return jnp.sum(v, axis=0, keepdims=True)


def gelu_parts(pre):
    cdf = 0.5 * (1.0 + lax.erf(pre * math.sqrt(0.5)))
    density = jnp.exp(-0.5 * pre * pre) * (1.0 / math.sqrt(2.0 * math.pi))
    return pre * cdf, cdf + pre * density


def normalize(v, gain, shift):
    center = v - jnp.mean(v, axis=1, keepdims=True)
    inverse = lax.rsqrt(jnp.mean(center * center, axis=1, keepdims=True) + EPSILON)
    normed = center * inverse
    return normed * gain + shift, normed, inverse


def normalize_back(c, normed, inverse, gain):
    scaled = c * gain
    inner = (
        scaled
        - jnp.mean(scaled, axis=1, keepdims=True)
        - normed * jnp.mean(scaled * normed, axis=1, keepdims=True)
    )
    return inner * inverse


def at_steps(index, steps):
    for number, acts in steps.items():

        def run(acts=acts):
            for act in acts:
                act()

        pl.when(index == number)(run)


def columns_of(half, width):
    return pl.ds(pl.multiple_of(half * width, 128), width)


GAIN_AT, SHIFT_AT, BIAS_AT = 128, 256, 384


def first_kernel(names, *refs):
    r = types.SimpleNamespace(**dict(zip(names, refs)))
    hidden, x_all, w_all, rel_all = r.hidden_in, r.x_all, r.w_all, r.rel_all
    token_rows, width = hidden.shape
    slot_rows = x_all.shape[1]
    total = CHIPS * slot_rows
    depth = r.out_weight.shape[0]
    w_in, w_down, w_out = r.w_in, r.w_down, r.w_out
    half_hidden = w_in.shape[3]
    half_width = width // 2
    core, chip = place()
    group, position, _ = unit()
    other = 1 - core
    me = core * CHIPS + chip
    keep = r.keep_sem

    loads = [
        local(r.ffn_in.at[:, columns_of(core, half_hidden)], w_in.at[core, chip], keep.at[0]),
        local(r.ffn_out, w_down.at[chip], keep.at[1]),
        local(r.out_weight, w_out.at[chip, pl.ds(0, depth)], keep.at[2]),
    ]
    for copy in loads:
        copy.start()

    extra = r.extra
    extra[...] = jnp.zeros_like(extra)
    extra[0:1, 0:256] = jnp.full((1, 256), 4.0, HIGH)
    extra[0:1, 0:token_rows] = r.segment_ids[...].astype(HIGH)
    extra[1:2, 0:token_rows] = r.order_ids[...].astype(HIGH)
    extra[2:4, 0:token_rows] = r.box_ids[...].astype(HIGH)
    tail = token_rows - token_rows % 16
    x_own = r.x_own
    x_own[0:tail, :] = hidden[0:tail, :]
    x_own[tail:slot_rows, :] = jnp.concatenate(
        [hidden[tail:token_rows, :].astype(HIGH), extra[...]], axis=0
    ).astype(LOW)
    weight = r.qkv_weight
    rel_own = r.rel_own
    for kind in range(3):
        rel_own[:, kind * NB : (kind + 1) * NB] = r.rel_tables[kind]
    eye_depth = (
        lax.broadcasted_iota(jnp.int32, (depth, depth), 0)
        == lax.broadcasted_iota(jnp.int32, (depth, depth), 1)
    ).astype(LOW)
    bias_columns = dot(eye_depth, r.qkv_bias[...], NT)
    rel_own[:, 3 * NB : 4 * NB] = jnp.where(
        lanes(depth) == 0, bias_columns[:, 0:1], jnp.where(lanes(depth) == 1, bias_columns[:, 1:2], 0.0)
    ).astype(LOW)
    small_own = r.small_own
    small_own[...] = jnp.zeros_like(small_own)
    small_own[0:2, 0:depth] = r.branch_bias[...]
    small_own[0:2, GAIN_AT : GAIN_AT + depth] = r.norm_gains[...]
    small_own[0:2, SHIFT_AT : SHIFT_AT + depth] = r.norm_shifts[...]
    small_own[0:1, BIAS_AT : BIAS_AT + 128] = r.ffn_in_bias[...]
    loads += [
        local(small_own, w_out.at[chip, pl.ds(depth, 16)], keep.at[3]),
        local(weight.at[:, :, columns_of(position, 128)], w_all.at[:, core, chip], keep.at[4]),
    ]
    for copy in loads[3:]:
        copy.start()
    meet()

    at_home = group == core
    away = lax.rem(chip + HALF, CHIPS)
    x_slot = x_all.at[position]
    home = lambda: local(x_own, x_slot, r.home_sem.at[1])
    abroad = lambda: remote(x_own, x_slot, r.home_sem.at[0], r.home_sem.at[1], (other, away))
    pl.when(at_home)(lambda: home().start())
    pl.when(jnp.logical_not(at_home))(lambda: abroad().start())

    rel_head = core * HALF + lax.div(chip, 2)
    parity = lax.rem(chip, 2)
    rel_slot = rel_all.at[pl.ds(parity * depth, depth)]

    def rel_each(act_remote, act_own):
        for to_group in range(2):
            to = (lax.rem(rel_head, 2), to_group * HALF + lax.div(rel_head, 2))
            itself = jnp.logical_and(to[0] == core, to[1] == chip)
            copy = lambda: remote(
                rel_own, rel_slot, r.rel_send.at[to_group], r.rel_recv.at[parity], to
            )
            pl.when(jnp.logical_not(itself))(lambda: act_remote(copy()))
            if act_own is not None:
                pl.when(itself)(act_own)

    rel_each(
        lambda copy: copy.start(), lambda: local(rel_own, rel_slot, r.rel_recv.at[parity]).start()
    )

    def w_copy(ahead):
        to = lax.rem(chip + ahead, CHIPS)
        return remote(
            weight.at[:, :, columns_of(lax.rem(to, HALF), 128)],
            w_all.at[:, core, chip],
            r.w_send.at[ahead],
            r.w_recv.at[chip],
            (core, to),
        )

    for ahead in range(1, CHIPS):
        w_copy(ahead).start()
    swap_in = remote(
        r.ffn_in.at[:, columns_of(other, half_hidden)],
        w_in.at[core, chip],
        r.pair_send.at[0],
        r.pair_recv.at[0],
        (other, chip),
    )
    swap_in.start()

    third = slot_rows // 3
    x_plans = [
        CubeGather(
            lambda slot, part=part: x_all.at[slot, pl.ds(part * third, third)],
            r.x_send.at[part],
            r.x_recv.at[part],
            order,
        )
        for part, order in enumerate(("xyz", "yzx", "zxy"))
    ]
    home().wait()
    each(x_plans, CubeGather.own)
    each(x_plans, CubeGather.one)
    each(x_plans, CubeGather.two)

    half = width // 2
    half_tile = half_hidden // 2
    plan_out = GatherLate(lambda slot: w_out.at[slot], r.out_send, r.out_recv, "x")

    def halves(ref, wide, sends, recvs):
        return [
            Gather(
                lambda slot, part=part: ref(slot, pl.ds(part * wide, wide)), sends.at[part], recvs.at[part], across
            )
            for part, across in enumerate("xy")
        ]

    plans_in = halves(lambda slot, columns: w_in.at[:, slot, :, columns], half_tile, r.in_send, r.in_recv)
    plans_down = halves(lambda slot, columns: w_down.at[slot, :, columns], half, r.down_send, r.down_recv)
    for copy in loads:
        copy.wait()
    swap_in.wait()
    each(plans_in, Gather.own_line, 0)
    each(plans_in, Gather.own_plane)
    plan_out.first()
    each(plans_in, Gather.own_line, 1)
    each(plans_in, Gather.own_line, 2)

    for ahead in range(1, CHIPS):
        came = lax.rem(chip + ahead, CHIPS)
        remote(
            weight.at[:, :, pl.ds(0, 128)], w_all.at[:, core, came], r.w_send.at[0], r.w_recv.at[came], (core, came)
        ).wait_recv()
    pair_w = remote(w_all.at[:, core], w_all.at[:, core], r.pair_send.at[1], r.pair_recv.at[1], (other, chip))
    pair_w.start()
    for slot in range(2):
        local(rel_own, rel_all.at[pl.ds(slot * depth, depth)], r.rel_recv.at[slot]).wait()
    pair_bias = remote(
        rel_all.at[:, pl.ds(3 * NB, NB)], r.bias_far, r.pair_send.at[2], r.pair_recv.at[2], (other, chip)
    )
    pair_bias.start()
    each(x_plans, CubeGather.arrive)

    labels = r.labels
    first_slot = core * HALF
    label_part = x_all.at[:, pl.ds(slot_rows - 16, 16), pl.ds(0, 256)]
    label_slots = labels.at[pl.ds(first_slot, HALF)]
    pair_label = remote(label_part, label_slots, r.pair_send.at[3], r.pair_recv.at[3], (other, chip))
    pair_label.start()
    own_label = local(label_part, label_slots, keep.at[5])
    own_label.start()
    keep_x = local(x_all, r.x_out, keep.at[6])
    keep_x.start()
    keep_rel = local(rel_all, r.rel_out, keep.at[7])
    keep_rel.start()
    pair_w.wait()
    pair_bias.wait()
    keep_w = local(w_all, r.w_all_out, keep.at[15])
    keep_w.start()

    head_rows = 2 * depth
    row_at = lax.broadcasted_iota(jnp.int32, (head_rows, 128), 0)
    column_at = lanes(head_rows)

    def bias_row(columns, number):
        column = columns[:, number : number + 1]
        return column_sums(jnp.where(row_at == column_at, column, 0.0))

    rel = rel_all[...]
    bias_near = rel[:, 3 * NB : 4 * NB].astype(HIGH)
    bias_far = r.bias_far[...].astype(HIGH)
    bias_query, bias_value = (
        bias_row(bias_near, number) + turn(bias_row(bias_far, number)) for number in range(2)
    )
    weights = [w_all[n].reshape(width, 128) for n in range(3)]
    near, far_part = r.near, r.far_part
    pair_rows = 2 * slot_rows
    pair_half = lanes(pair_rows) < HD

    for pair in range(HALF // 2):
        tokens = x_all[2 * pair : 2 * pair + 2].reshape(pair_rows, width)
        query, key, value_rows = (
            pltpu.roll(dot(tokens, weights[n]), core * HD, 1) for n in range(3)
        )
        query, value_rows = query + bias_query, value_rows + bias_value
        rows = pl.ds(pl.multiple_of(core * HALF * slot_rows, 16) + pair * pair_rows, pair_rows)
        near[rows, 0:128] = jnp.where(pair_half, query, turn(value_rows)).astype(LOW)
        near[rows, 128:256] = key.astype(LOW)
        far_rows = slice(pair * pair_rows, (pair + 1) * pair_rows)
        far_part[far_rows, 0:128] = jnp.where(pair_half, turn(query), value_rows).astype(LOW)
        far_part[far_rows, 128:256] = turn(key).astype(LOW)
    pair_qkv = remote(
        far_part,
        near.at[pl.ds(pl.multiple_of(core * HALF * slot_rows, 16), HALF * slot_rows)],
        r.pair_send.at[4],
        r.pair_recv.at[4],
        (other, chip),
    )
    pair_qkv.start()

    meta = r.meta
    eye = (
        lax.broadcasted_iota(jnp.int32, (slot_rows, 256), 0)
        == lax.broadcasted_iota(jnp.int32, (slot_rows, 256), 1)
    ).astype(LOW)
    pair_label.wait()
    own_label.wait()
    for slot in range(CHIPS):
        meta[slot * slot_rows : (slot + 1) * slot_rows, 0:16] = dot(eye, labels[slot], NT)
    table_t = rel[:, 0 : 3 * NB]
    lane = lanes(BLOCK)
    first_half = lane < HD
    scale = 1.0 / math.sqrt(4.0 * HD)
    left, right, right_t = r.left, r.right, r.right_t
    value, value_t, kept = r.value, r.value_t, r.kept
    pair_qkv.wait()

    def prepare(index, carry):
        rows = pl.ds(pl.multiple_of(index * BLOCK, BLOCK), BLOCK)
        at_steps(
            index,
            {
                1: [
                    lambda: each(plans_in, Gather.side, None),
                    plan_out.second,
                    lambda: each(plans_down, Gather.own_line, 0),
                    lambda: each(plans_down, Gather.own_plane),
                ],
                4: [lambda: each(plans_in, Gather.line, 0), plan_out.third],
                7: [
                    lambda: each(plans_in, Gather.side, 0),
                    lambda: each(plans_down, Gather.own_line, 1),
                    lambda: each(plans_down, Gather.own_line, 2),
                ],
            },
        )
        query_value = near[rows, 0:128].astype(HIGH)
        key = near[rows, 128:256].astype(HIGH)
        tables = dot(near[rows, 0:128][:, 0:HD], table_t).astype(LOW).astype(HIGH)
        ids = meta[rows, 8:12].astype(jnp.int32)
        segment, order, box_x, box_y = ids[:, 0:1], ids[:, 1:2], ids[:, 2:3], ids[:, 3:4]

        def selected(column, ids_of, values):
            bucket = jnp.clip(ids_of - values, -(NB // 2), NB // 2 - 1) + NB // 2
            return jnp.take_along_axis(tables[:, column * NB : (column + 1) * NB], bucket, axis=1)

        wide = selected(0, order, lane)
        narrow = jnp.where(first_half, selected(1, box_x, lane), selected(2, box_y, lane - HD))
        label = lane - HD
        query_side = jnp.where(
            first_half,
            query_value * scale,
            jnp.where(jnp.logical_and(label != segment, label < 8), MASKED, 0.0),
        )
        key_side = jnp.where(first_half, key, (label == segment).astype(HIGH))
        left[rows, 0:128] = (wide * scale).astype(LOW)
        left[rows, 128:256] = (narrow * scale).astype(LOW)
        left[rows, 256:384] = query_side.astype(LOW)
        order_hot = (lane == order).astype(HIGH)
        box_hot = (jnp.where(first_half, box_x, box_y + HD) == lane).astype(HIGH)
        right[rows, 0:128] = order_hot.astype(LOW)
        right[rows, 128:256] = box_hot.astype(LOW)
        right[rows, 256:384] = key_side.astype(LOW)
        right_t[0:128, rows] = order_hot.T.astype(LOW)
        right_t[128:256, rows] = box_hot.T.astype(LOW)
        right_t[256:384, rows] = key_side.T.astype(LOW)
        held = jnp.where(first_half, turn(query_value), (label == 0).astype(HIGH))
        value[rows, :] = held.astype(LOW)
        value_t[:, rows] = held.T.astype(LOW)
        return carry

    lax.fori_loop(0, total // BLOCK, prepare, 0)
    stash = [
        local(held, out, keep.at[8 + k])
        for k, (held, out) in enumerate(
            (
                (left, r.left_out),
                (right, r.right_out),
                (right_t, r.right_t_out),
                (value_t, r.value_t_out),
            )
        )
    ]
    for copy in stash:
        copy.start()

    def attend(index, carry):
        rows = pl.ds(pl.multiple_of(index * BLOCK, BLOCK), BLOCK)
        at_steps(
            index,
            {
                0: [lambda: each(plans_in, Gather.line, 1), lambda: each(plans_down, Gather.side, None)],
                3: [lambda: each(plans_in, Gather.side, 1)],
                6: [lambda: each(plans_in, Gather.line, 2), lambda: each(plans_down, Gather.line, 0)],
            },
        )
        logits = dot(left[rows, :], right_t[...])
        top = jnp.max(logits, axis=1, keepdims=True)
        weights = jnp.exp(logits - top).astype(LOW)
        mixed = dot(weights, value[...])
        row_sum = mixed[:, HD : HD + 1]
        ids = meta[rows, 8:12]
        facts = jnp.where(lane == HD, top + jnp.log(row_sum), ids[:, 3:4])
        facts = jnp.where(lane == HD + 1, ids[:, 1:2], facts)
        facts = jnp.where(lane == HD + 2, ids[:, 2:3], facts)
        kept[rows, :] = jnp.where(first_half, mixed / row_sum, facts)
        return carry

    lax.fori_loop(0, total // BLOCK, attend, 0)
    keep_facts = local(kept, r.kept_out, keep.at[12])
    keep_facts.start()
    message, context_in = r.message, r.context_in
    for slot in range(CHIPS):
        message[slot] = fold(kept[slot * slot_rows : (slot + 1) * slot_rows, :])
    context_arrives, context_sent = to_tokens(message, context_in, r.msg_send, r.msg_recv)
    each(plans_in, Gather.side, 2)
    each(plans_down, Gather.side, 0)
    each(plans_down, Gather.line, 1)
    each(plans_down, Gather.side, 1)

    plan_out.arrive()
    keep_out = local(w_out, r.w_out_out, keep.at[13])
    keep_out.start()
    shares, bias_in = r.shares, r.bias_in
    shares[core] = jnp.zeros(shares.shape[1:], HIGH)
    for slot in range(CHIPS):
        small = w_out[slot, depth : depth + 16, 0 : BIAS_AT + 128].astype(HIGH)[0:8]
        target = slice(slot * depth // 128 * 128, slot * depth // 128 * 128 + 128)
        for number in range(3):
            piece = jnp.where(lanes(8) < depth, small[:, number * 128 : number * 128 + 128], 0.0)
            if slot * depth % 128:
                piece = pltpu.roll(piece, slot * depth % 128, 1)
            shares[core, number, :, target] += piece
        bias_in[:, slot * 128 : slot * 128 + 128] = small[0:1, BIAS_AT : BIAS_AT + 128]
    pair_small = remote(
        shares.at[core], shares.at[core], r.pair_send.at[5], r.pair_recv.at[5], (other, chip)
    )
    pair_small.start()
    context_arrives()

    context_wide, context, low_first = r.context_wide, r.context, r.low_first
    act, slope = r.act, r.slope
    out_part, in_part, g_small = r.out_part, r.in_part, r.g_small
    own = pl.ds(pl.multiple_of(core * slot_rows, 16), slot_rows)
    far = pl.ds(pl.multiple_of(other * slot_rows, 16), slot_rows)
    tile = 512
    half_slot = slot_rows // 2
    count = [6]

    def swap(source, target):
        copy = remote(
            source, target, r.pair_send.at[count[0]], r.pair_recv.at[count[0]], (other, chip)
        )
        count[0] += 1
        copy.start()
        return copy

    left_half = lanes(half_slot) < HD
    for slot_group in range(2):
        for pair in range(HALF // 2):
            even = context_in[slot_group * HALF + 2 * pair].astype(HIGH)[:half_slot]
            odd = context_in[slot_group * HALF + 2 * pair + 1].astype(HIGH)[:half_slot]
            top = slot_group * slot_rows
            columns = slice(pair * 128, pair * 128 + 128)
            context_wide[top : top + half_slot, columns] = jnp.where(left_half, even, turn(odd))
            context_wide[top + half_slot : top + slot_rows, columns] = jnp.where(
                left_half, turn(even), odd
            )
    context[...] = context_wide[...].astype(LOW)
    keep_context = local(context, r.context_out, keep.at[14])
    keep_context.start()

    def product(index, lhs, rhs):
        out_part[index] = dot(lhs[far, :], rhs)
        copy = swap(out_part.at[index], in_part.at[index])
        mine = dot(lhs[own, :], rhs)
        copy.wait()
        return mine + in_part[index]

    pair_small.wait()
    branch_bias, gains, shifts = (
        [jnp.concatenate([shares[0, number, k : k + 1], shares[1, number, k : k + 1]], axis=1) for k in range(2)]
        for number in range(3)
    )
    for k in range(2):
        r.gains_out[k : k + 1, :] = gains[k]
    branch = product(0, context, w_out[:, 0:depth, :].reshape(half_width, width)) + branch_bias[0]
    row_index = lax.broadcasted_iota(jnp.int32, (slot_rows, 1), 0)
    x_mine = jnp.where(row_index < token_rows, x_own[...].astype(HIGH), 0.0)
    first, normed1, inverse1 = normalize(x_mine + branch, gains[0], shifts[0])
    low_first[own, :] = first.astype(LOW)
    copy = swap(low_first.at[own], low_first.at[own])
    r.normed1[...] = normed1
    r.inverse1[...] = jnp.broadcast_to(inverse1, r.inverse1.shape)
    each(plans_down, Gather.line, 2)
    each(plans_down, Gather.side, 2)
    each(plans_in, Gather.arrive)
    keep_in = local(w_in, r.w_in_out, keep.at[16])
    keep_in.start()
    copy.wait()
    keep_first = local(low_first, r.low_first_out, keep.at[17])
    keep_first.start()

    def widen(index, carry):
        columns = pl.ds(pl.multiple_of(index * tile, tile), tile)
        pre = dot(low_first[...], w_in[:, :, :, columns].reshape(width, tile)) + bias_in[:, columns]
        found, derivative = gelu_parts(pre)
        act[:, columns] = found.astype(LOW)
        slope[:, columns] = derivative
        return carry

    lax.fori_loop(0, half_hidden // tile, widen, 0)
    keep_act = local(act, r.act_out, keep.at[18])
    keep_act.start()
    keep_slope = local(slope, r.slope_out, keep.at[19])
    keep_slope.start()
    each(plans_down, Gather.arrive)
    keep_down = local(w_down, r.w_down_out, keep.at[20])
    keep_down.start()
    second = product(1, act, w_down[...].reshape(half_hidden, width)) + branch_bias[1]
    result, normed2, inverse2 = normalize(first + second, gains[1], shifts[1])
    r.hidden_out[...] = result[:token_rows].astype(LOW)
    upstream = jnp.concatenate(
        [r.out_grad[...].astype(HIGH), jnp.zeros((slot_rows - token_rows, width), HIGH)], axis=0
    )
    d_sum2 = normalize_back(upstream, normed2, inverse2, gains[1])
    r.d_sum2[...] = d_sum2
    low_second = d_sum2.astype(LOW)
    r.d_second_out[...] = low_second
    g_small[...] = jnp.zeros_like(g_small)
    g_small[1:2, 0:width] = column_sums(low_second.astype(HIGH))
    g_small[3:4, 0:width] = column_sums(upstream * normed2)
    g_small[5:6, 0:width] = column_sums(upstream)

    for ahead in range(1, CHIPS):
        w_copy(ahead).wait_send()
    rel_each(lambda copy: copy.wait_send(), None)
    pl.when(jnp.logical_not(at_home))(lambda: abroad().wait_send())
    context_sent()
    each(x_plans, CubeGather.finish)
    each(plans_in + plans_down + [plan_out], Gather.finish)
    for copy in stash + [
        keep_x,
        keep_rel,
        keep_w,
        keep_facts,
        keep_out,
        keep_context,
        keep_in,
        keep_first,
        keep_act,
        keep_slope,
        keep_down,
    ]:
        copy.wait()


def second_kernel(names, *refs):
    r = types.SimpleNamespace(**dict(zip(names, refs)))
    core, chip = place()
    group, position, _ = unit()
    other = 1 - core
    left, right, right_t, value_t, kept = r.left, r.right, r.right_t, r.value_t, r.kept
    rel_all, x_all, w_all = r.rel_all, r.x_all, r.w_all
    w_in, w_down, w_out = r.w_in, r.w_down, r.w_out
    slot_rows, width = x_all.shape[1:]
    total = CHIPS * slot_rows
    half_total = HALF * slot_rows
    half_slot = slot_rows // 2
    half_hidden = w_in.shape[3]
    half_width = width // 2
    depth = r.g_out.shape[1]
    token_rows = r.hidden_grad.shape[0]
    scale = 1.0 / math.sqrt(4.0 * HD)
    keep = r.keep_sem
    loads = [
        local(there, held, keep.at[k])
        for k, (there, held) in enumerate(
            (
                (r.w_down_any, w_down),
                (r.act_any, r.act),
                (r.slope_any, r.slope),
                (r.w_in_any, w_in),
                (r.low_first_any, r.low_first),
                (r.w_out_any, w_out),
                (r.context_any, r.context),
                (r.left_any, left),
                (r.right_t_any, right_t),
                (r.value_t_any, value_t),
                (r.kept_any, kept),
                (r.right_any, right),
                (r.x_any, x_all),
                (r.w_all_any, w_all),
            )
        )
    ]
    for copy in loads:
        copy.start()
    meet()
    count = [0]

    def swap(source, target):
        copy = remote(
            source, target, r.pair_send.at[count[0]], r.pair_recv.at[count[0]], (other, chip)
        )
        count[0] += 1
        copy.start()
        return copy

    own = pl.ds(pl.multiple_of(core * slot_rows, 16), slot_rows)
    far = pl.ds(pl.multiple_of(other * slot_rows, 16), slot_rows)
    act, slope, low_first, context = r.act, r.slope, r.low_first, r.context
    d_second, d_branch, context_wide = r.d_second, r.d_branch, r.context_wide
    d_inner = act
    out_part, in_part, small_sum = r.out_part, r.in_part, r.small_sum
    plan_down = Reduce(
        w_down,
        w_down,
        lambda ref, slot: ref.at[slot],
        [r.down_1, r.down_2, r.down_3],
        r.down_send,
        r.down_recv,
        "y",
    )
    plan_in = Reduce(
        w_in,
        w_in,
        lambda ref, slot: ref.at[:, slot],
        [r.in_1, r.in_2, r.in_3],
        r.in_send,
        r.in_recv,
        "x",
    )
    plan_out = ReduceEarly(
        r.g_out,
        r.g_out,
        lambda ref, slot: ref.at[slot],
        [r.out_1, r.out_2, r.out_3],
        r.out_send,
        r.out_recv,
        "y",
    )
    plans = (plan_down, plan_in)

    d_second[own, :] = r.d_second_own[...]
    copy = swap(r.d_second_own, d_second.at[own])
    small_sum[...] = r.g_small[...]
    for load in loads[0:3]:
        load.wait()
    copy.wait()
    tile = 512
    slots = tile // w_down.shape[1]

    def narrow_back(index, carry):
        columns = pl.ds(pl.multiple_of(index * tile, tile), tile)
        rows = pl.ds(index * slots, slots)
        low = (dot(d_second[...], w_down[rows].reshape(tile, width), NT) * slope[:, columns]).astype(LOW)
        small_sum[pl.ds(8, 1), columns] = column_sums(low.astype(HIGH))
        w_down[rows] = (
            dot(act[:, columns], d_second[...], TN).astype(LOW).reshape(slots, tile // slots, width)
        )
        d_inner[:, columns] = low
        return carry

    lax.fori_loop(0, half_hidden // tile, narrow_back, 0)
    plan_down.start(2)
    for load in loads[3:5]:
        load.wait()
    w_in_all = w_in[...].reshape(width, half_hidden)
    out_part[...] = dot(d_inner[far, :], w_in_all, NT)
    copy = swap(out_part, in_part)
    mine = dot(d_inner[own, :], w_in_all, NT)
    slots_in = 256 // depth

    def widen_grad(index, carry):
        rows = pl.ds(pl.multiple_of(index * 256, 256), 256)
        parts = CHIPS // slots_in
        w_in[lax.div(index, parts), pl.ds(lax.rem(index, parts) * slots_in, slots_in)] = (
            dot(low_first[:, rows], d_inner[...], TN).astype(LOW).reshape(slots_in, depth, half_hidden)
        )
        return carry

    lax.fori_loop(0, width // 256, widen_grad, 0)
    plan_in.start(2)
    copy.wait()
    d_sum2, gains = r.d_sum2, r.gains
    d_first = d_sum2[...] + mine + in_part[...]
    d_sum1 = normalize_back(d_first, r.normed1[...], r.inverse1[:, 0:1], gains[0:1])
    low_branch = d_sum1.astype(LOW)
    d_branch[own, :] = low_branch
    copy = swap(d_branch.at[own], d_branch.at[own])
    r.d_sum1[...] = d_sum1
    small_sum[0:1, 0:width] = column_sums(low_branch.astype(HIGH))
    small_sum[2:3, 0:width] = column_sums(d_first * r.normed1[...])
    small_sum[4:5, 0:width] = column_sums(d_first)
    for load in loads[5:7]:
        load.wait()
    copy.wait()
    context_wide[...] = dot(d_branch[...], w_out[:, 0:depth, :].reshape(half_width, width), NT)
    for slot_group in range(2):
        for pair in range(HALF // 2):
            both = context_wide[
                slot_group * slot_rows : (slot_group + 1) * slot_rows, pair * 128 : pair * 128 + 128
            ]
            r.d_message[slot_group * HALF + 2 * pair] = fold(both)
            r.d_message[slot_group * HALF + 2 * pair + 1] = fold(turn(both))
    d_arrived = r.d_arrived
    grad_arrives, grad_sent = to_heads(r.d_message, d_arrived, r.d_send, r.d_recv)
    r.g_out[...] = dot(context[...], d_branch[...], TN).astype(LOW).reshape(r.g_out.shape)
    each(plans, Reduce.start, 1)
    plan_out.start()

    z, y, x = coordinates(chip)
    small_in = r.small_in

    def small_copy(index, to_core, to_chip):
        return remote(
            small_sum, small_in.at[index], r.small_send.at[index], r.small_recv.at[index], (to_core, to_chip)
        )

    def small_turn(index):
        if index == 0:
            return [small_copy(0, other, chip)]
        if index == 1:
            return [small_copy(1, core, z * 4 + (1 - y) * 2 + x)]
        if index == 2:
            return [small_copy(2, core, z * 4 + y * 2 + 1 - x)]
        return [
            small_copy(2 + ahead, core, lax.rem(z + ahead, 4) * 4 + y * 2 + x) for ahead in (1, 2, 3)
        ]

    def small_start(index):
        for copy in small_turn(index):
            copy.start()

    def small_end(index):
        for copy in small_turn(index):
            copy.wait()
        if index == 0:
            small_sum[0:8, :] += small_in[0, 0:8, :]
        elif index < 3:
            small_sum[...] += small_in[index]

    small_start(0)
    each(plans, Reduce.side, 2)
    left_half = lanes(half_slot) < HD
    d_context = r.d_context
    grad_arrives()
    for slot in range(CHIPS):
        both = d_arrived[slot].astype(HIGH)[:half_slot]
        top = slot * slot_rows
        d_context[top : top + half_slot, :] = jnp.where(left_half, both, 0.0)
        d_context[top + half_slot : top + slot_rows, :] = jnp.where(left_half, turn(both), 0.0)
    table_t = rel_all[:, 0 : 3 * NB]
    lane = lanes(BLOCK)
    first_half = lane < HD
    d_heads, d_pair_t, rel_grad = r.d_heads, r.d_pair_t, r.rel_grad
    d_pair_t[...] = jnp.zeros_like(d_pair_t)
    rel_grad[...] = jnp.zeros_like(rel_grad)
    for load in loads[7:]:
        load.wait()

    def step(index, carry):
        rows = pl.ds(pl.multiple_of(index * BLOCK, BLOCK), BLOCK)
        at_steps(
            index,
            {
                0: [
                    lambda: each(plans, Reduce.line, 2),
                    lambda: each(plans, Reduce.start, 0),
                    lambda: small_end(0),
                    lambda: small_start(1),
                ],
                2: [plan_out.third],
                3: [
                    lambda: each(plans, Reduce.side, 1),
                    lambda: each(plans, Reduce.start, None),
                    lambda: small_end(1),
                    lambda: small_start(2),
                ],
                5: [plan_out.across],
                6: [lambda: each(plans, Reduce.side, 0)],
                8: [lambda: each(plans, Reduce.line, 1), lambda: small_end(2), lambda: small_start(3)],
            },
        )
        facts = kept[rows, :]
        grad = d_context[rows, :]
        delta = jnp.sum(grad * facts, axis=1, keepdims=True)
        probs = jnp.exp(dot(left[rows, :], right_t[...]) - facts[:, HD : HD + 1])
        d_probs = dot(grad.astype(LOW), value_t[...])
        d_logits = (probs * (d_probs - delta)).astype(LOW)
        query_t = jnp.where(first_half, left[rows, 256:384].astype(HIGH), 0.0).T[0:HD]
        d_pair_t[0:HD, :] += dot(query_t.astype(LOW), d_logits)
        d_pair_t[HD : 2 * HD, :] += dot(grad.T[0:HD].astype(LOW), probs.astype(LOW))
        back = dot(d_logits, right[...]) * scale
        ids = facts.astype(jnp.int32)
        order, box_x, box_y = (ids[:, HD + k : HD + k + 1] for k in (1, 2, 3))

        def placed(column, ids_of, extent, start):
            found_at = ids_of + NB // 2 - lane
            found = jnp.take_along_axis(
                back[:, column * 128 : column * 128 + 128], jnp.clip(found_at, 0, extent - 1) + start, axis=1
            )
            return jnp.where(jnp.logical_and(found_at >= 0, found_at < extent), found, 0.0)

        wide = back[:, 0:128]
        low_end = jnp.sum(jnp.where(lane >= order + NB // 2, wide, 0.0), axis=1, keepdims=True)
        high_end = jnp.sum(jnp.where(lane <= order - (NB // 2 - 1), wide, 0.0), axis=1, keepdims=True)
        first = placed(0, order, ORDER_RANGE, 0)
        first = jnp.where(lane == 0, low_end, jnp.where(lane == NB - 1, high_end, first))
        d_tables = jnp.concatenate(
            [first, placed(1, box_x, BOX_RANGE, 0), placed(1, box_y, BOX_RANGE, BOX_RANGE)], axis=1
        ).astype(LOW)
        from_tables = dot(d_tables, table_t, NT)
        d_query = back[:, 256:384] + jnp.concatenate([from_tables, from_tables], axis=1)
        d_heads[0, :, rows] = d_query.T[0:HD].astype(LOW)
        rel_grad[:, 0 : 3 * NB] += dot((query_t / scale).astype(LOW), d_tables)
        return carry

    lax.fori_loop(0, total // BLOCK, step, 0)

    d_heads[1] = d_pair_t[0:HD, :].astype(LOW)
    d_heads[2] = d_pair_t[HD : 2 * HD, :].astype(LOW)
    d_both = r.d_both
    near_part = pl.ds(pl.multiple_of(core * half_total, 128), half_total)
    far_part = pl.ds(pl.multiple_of(other * half_total, 128), half_total)
    copy = swap(d_heads.at[:, :, far_part], d_both.at[:, core])
    d_both[:, core] = d_heads[:, :, near_part]
    sums = [jnp.sum(d_heads[n].astype(HIGH), axis=1, keepdims=True) for n in (0, 2)]
    rel_grad[:, 3 * NB : 4 * NB] = jnp.where(
        lanes(HD) == 0, sums[0], jnp.where(lanes(HD) == 1, sums[1], 0.0)
    )
    head = 2 * position + core
    rel_came = r.rel_came

    def rel_each(act_remote, act_own):
        for side in range(2):
            to = (lax.div(position, 4), lax.rem(2 * head + side, CHIPS))
            itself = jnp.logical_and(to[0] == core, to[1] == chip)
            source = rel_grad.at[pl.ds(side * depth, depth)]
            act = lambda: act_remote(
                remote(source, rel_came.at[group], r.rel_send.at[side], r.rel_recv.at[group], to)
            )
            pl.when(jnp.logical_not(itself))(act)
            if act_own:
                pl.when(itself)(lambda: local(source, rel_came.at[group], r.rel_recv.at[group]).start())

    rel_each(lambda copy: copy.start(), True)
    copy.wait()
    d_columns = d_both[...].reshape(6 * HD, half_total)

    w_heads = jnp.concatenate([w_all[n].reshape(width, 128) for n in range(3)], axis=1)
    d_rows = d_columns.T
    d_x = r.d_x
    pair_rows = 2 * slot_rows
    for pair in range(HALF // 2):
        d_x[2 * pair : 2 * pair + 2] = (
            dot(d_rows[pair * pair_rows : (pair + 1) * pair_rows], w_heads, NT)
            .astype(LOW)
            .reshape(2, slot_rows, width)
        )
    third = slot_rows // 3
    x_plans = [
        CubeReduce(
            lambda slot, part=part: d_x.at[slot, pl.ds(part * third, third)],
            r.x_stage.at[part],
            r.x_send.at[part],
            r.x_recv.at[part],
            order,
        )
        for part, order in enumerate(("xyz", "yzx", "zxy"))
    ]
    each(x_plans, CubeReduce.own)

    w_grad = dot(d_columns, x_all[...].reshape(half_total, width))
    w_mine, w_far, w_low, w_came = r.w_mine, r.w_far, r.w_low, r.w_came
    for part in range(2):
        w_mine[part] = w_grad[:, part * half_width : (part + 1) * half_width]
    copy = swap(w_mine.at[other], w_far)
    each(x_plans, CubeReduce.one)
    copy.wait()
    w_sum = (w_mine[core] + w_far[...]).T
    for slot in range(CHIPS):
        w_low[slot] = w_sum[slot * depth : (slot + 1) * depth].astype(LOW)

    def w_copy(ahead):
        to = lax.rem(chip + ahead, CHIPS)
        return remote(w_low.at[to], w_came.at[chip], r.w_send.at[ahead], r.w_recv.at[chip], (core, to))

    own_w = local(w_low.at[chip], w_came.at[chip], keep.at[14])
    own_w.start()
    for ahead in range(1, CHIPS):
        w_copy(ahead).start()
    each(x_plans, CubeReduce.two)
    each(plans, Reduce.line, 0)
    each(plans, Reduce.side, None)
    x_total, x_came = r.x_total, r.x_came
    for part, plan in enumerate(x_plans):
        x_total[part * third : (part + 1) * third] = plan.arrive().astype(LOW)
    at_home = group == core
    home = lambda: local(x_total, x_came, r.home_sem.at[1])
    abroad = lambda: remote(
        x_total, x_came, r.home_sem.at[0], r.home_sem.at[1], (other, lax.rem(chip + HALF, CHIPS))
    )
    pl.when(at_home)(lambda: home().start())
    pl.when(jnp.logical_not(at_home))(lambda: abroad().start())

    in_total, in_far = r.in_total, r.in_far
    plan_in.finish(in_total)
    in_pair = swap(in_total.at[other], in_far)
    plan_down.finish(r.down_grad)
    plan_out.finish(r.out_grad)
    in_grad = r.in_grad
    in_grad[:, columns_of(core, half_hidden)] = in_total[core]
    small_end(3)
    me = core * CHIPS + chip
    small_all = lambda rows, columns: (
        small_sum[rows, columns] + small_in[3, rows, columns] + small_in[4, rows, columns] + small_in[5, rows, columns]
    )
    strip = columns_of(lax.div(me * depth, 128), 128)
    shares = pltpu.roll(small_all(pl.ds(0, 8), strip), 128 - lax.rem(me * depth, 128), 1)
    for number, result in enumerate((r.branch_grad, r.gain_grad, r.shift_grad)):
        result[...] = shares[2 * number : 2 * number + 2, 0:depth]
    r.bias_grad[...] = small_all(pl.ds(8, 1), columns_of(chip, 128))
    for slot in range(2):
        local(rel_grad.at[pl.ds(0, depth)], rel_came.at[slot], r.rel_recv.at[slot]).wait()
    rel_each(lambda copy: copy.wait_send(), False)
    rel_total = rel_came[0] + rel_came[1]
    for kind in range(3):
        r.rel_tables_grad[kind] = rel_total[:, kind * NB : (kind + 1) * NB]
    r.qkv_bias_grad[...] = rel_total[:, 3 * NB : 4 * NB].T[0:2]
    own_w.wait()
    for ahead in range(1, CHIPS):
        came = lax.rem(chip + ahead, CHIPS)
        remote(w_low.at[0], w_came.at[came], r.w_send.at[0], r.w_recv.at[came], (core, came)).wait_recv()
        w_copy(ahead).wait_send()
    for pair in range(HALF):
        both = w_came[pair].astype(HIGH) + w_came[HALF + pair].astype(HIGH)
        for n in range(3):
            r.qkv_grad[n, :, pair * 128 : pair * 128 + 128] = both[:, n * 128 : n * 128 + 128]
    home().wait()
    pl.when(jnp.logical_not(at_home))(lambda: abroad().wait_send())
    r.hidden_grad[...] = (r.d_sum1[...] + x_came[...].astype(HIGH))[:token_rows].astype(LOW)
    in_pair.wait()
    in_grad[:, columns_of(other, half_hidden)] = in_far[...]
    grad_sent()
    each(x_plans, CubeReduce.finish)


def hand_over(count, *refs):
    for source, target in zip(refs[:count], refs[count:]):
        target[...] = source[...]


def handed_over(arrays):
    return pl.pallas_call(
        functools.partial(hand_over, len(arrays)),
        out_shape=[jax.ShapeDtypeStruct(array.shape, array.dtype) for array in arrays],
        name="hand_over",
    )(*arrays)


def call(kernel, name, number, inputs, outputs, scratch):
    names = list(inputs) + list(outputs) + list(scratch)
    results = pl.pallas_call(
        functools.partial(kernel, names),
        out_shape=[jax.ShapeDtypeStruct(shape, dtype) for shape, dtype, _ in outputs.values()],
        in_specs=[pl.BlockSpec(memory_space=space) for _, space in inputs.values()],
        out_specs=[pl.BlockSpec(memory_space=space) for _, _, space in outputs.values()],
        scratch_shapes=list(scratch.values()),
        compiler_params=pltpu.CompilerParams(
            collective_id=number, has_side_effects=True, vmem_limit_bytes=VMEM_LIMIT
        ),
        name=name,
    )(*(array for array, _ in inputs.values()))
    return types.SimpleNamespace(**dict(zip(outputs, results)))


def head_shards(
    hidden_in,
    segment_ids,
    order_ids,
    box_ids,
    qkv_weight,
    qkv_bias,
    rel_tables,
    out_weight,
    branch_bias,
    norm_gains,
    norm_shifts,
    ffn_in,
    ffn_in_bias,
    ffn_out,
    out_grad,
):
    rows, width = hidden_in.shape
    slot_rows = -(-rows // 48) * 48
    total = CHIPS * slot_rows
    depth = qkv_weight.shape[1]
    hidden = ffn_in.shape[1]
    half_hidden, half_width = hidden // 2, width // 2
    down_rows = ffn_out.shape[0]
    both = 2 * slot_rows
    fold_rows = -(-(slot_rows // 2) // 16) * 16
    any_, vmem, dma = pl.ANY, pltpu.VMEM, pltpu.SemaphoreType.DMA
    message = (CHIPS, fold_rows, 128)
    x_block, w_block = (HALF, slot_rows, width), (3, 2, CHIPS, depth, 128)
    in_all, down_all = (2, CHIPS, depth, half_hidden), (CHIPS, down_rows, width)
    out_all = (CHIPS, depth + 16, width)
    made = call(
        first_kernel,
        "forward_pass",
        0,
        dict(
            hidden_in=(hidden_in, vmem),
            segment_ids=(segment_ids.reshape(1, rows), vmem),
            order_ids=(order_ids.reshape(1, rows), vmem),
            box_ids=(box_ids, vmem),
            qkv_weight=(qkv_weight, vmem),
            qkv_bias=(qkv_bias, vmem),
            rel_tables=(rel_tables.transpose(0, 2, 1), vmem),
            out_weight=(out_weight, any_),
            branch_bias=(branch_bias, vmem),
            norm_gains=(norm_gains, vmem),
            norm_shifts=(norm_shifts, vmem),
            ffn_in=(ffn_in, any_),
            ffn_in_bias=(ffn_in_bias.reshape(1, down_rows), vmem),
            ffn_out=(ffn_out, any_),
            out_grad=(out_grad, vmem),
        ),
        dict(
            hidden_out=((rows, width), LOW, vmem),
            x_out=(x_block, LOW, any_),
            w_all_out=(w_block, LOW, any_),
            rel_out=((2 * depth, 4 * NB), LOW, any_),
            left_out=((total, 384), LOW, any_),
            right_out=((total, 384), LOW, any_),
            right_t_out=((384, total), LOW, any_),
            value_t_out=((128, total), LOW, any_),
            kept_out=((total, 128), HIGH, any_),
            w_in_out=(in_all, LOW, any_),
            w_down_out=(down_all, LOW, any_),
            w_out_out=(out_all, LOW, any_),
            context_out=((both, half_width), LOW, any_),
            low_first_out=((both, width), LOW, any_),
            act_out=((both, half_hidden), LOW, any_),
            slope_out=((both, half_hidden), HIGH, any_),
            normed1=((slot_rows, width), HIGH, vmem),
            inverse1=((slot_rows, 128), HIGH, vmem),
            d_sum2=((slot_rows, width), HIGH, vmem),
            d_second_out=((slot_rows, width), LOW, vmem),
            gains_out=((2, width), HIGH, vmem),
            g_small=((16, half_hidden), HIGH, vmem),
        ),
        dict(
            x_own=vmem((slot_rows, width), LOW),
            x_all=vmem(x_block, LOW),
            extra=vmem((slot_rows - rows, width), HIGH),
            small_own=vmem((16, width), LOW),
            w_all=vmem(w_block, LOW),
            rel_own=vmem((depth, 4 * NB), LOW),
            rel_all=vmem((2 * depth, 4 * NB), LOW),
            bias_far=vmem((2 * depth, NB), LOW),
            labels=vmem((CHIPS, 16, 256), LOW),
            near=vmem((total, 256), LOW),
            far_part=vmem((total // 2, 256), LOW),
            w_in=vmem(in_all, LOW),
            w_down=vmem(down_all, LOW),
            w_out=vmem(out_all, LOW),
            meta=vmem((total, 128), HIGH),
            shares=vmem((2, 3, 8, half_width), HIGH),
            bias_in=vmem((1, half_hidden), HIGH),
            left=vmem((total, 384), LOW),
            right=vmem((total, 384), LOW),
            right_t=vmem((384, total), LOW),
            value=vmem((total, 128), LOW),
            value_t=vmem((128, total), LOW),
            kept=vmem((total, 128), HIGH),
            message=vmem(message, LOW),
            context_in=vmem(message, LOW),
            context_wide=vmem((both, half_width), HIGH),
            context=vmem((both, half_width), LOW),
            low_first=vmem((both, width), LOW),
            act=vmem((both, half_hidden), LOW),
            slope=vmem((both, half_hidden), HIGH),
            out_part=vmem((2, slot_rows, width), HIGH),
            in_part=vmem((2, slot_rows, width), HIGH),
            keep_sem=dma((21,)),
            home_sem=dma((2,)),
            x_send=dma((3, 8)),
            x_recv=dma((3, 8)),
            w_send=dma((16,)),
            w_recv=dma((16,)),
            rel_send=dma((2,)),
            rel_recv=dma((2,)),
            out_send=dma((16,)),
            out_recv=dma((16,)),
            in_send=dma((2, 16)),
            in_recv=dma((2, 16)),
            down_send=dma((2, 16)),
            down_recv=dma((2, 16)),
            msg_send=dma((16,)),
            msg_recv=dma((16,)),
            pair_send=dma((9,)),
            pair_recv=dma((9,)),
        ),
    )
    in_block, down_block, out_block = (2, depth, half_hidden), (down_rows, width), (depth, width)
    ended = call(
        second_kernel,
        "backward_pass",
        1,
        dict(
            left_any=(made.left_out, any_),
            right_any=(made.right_out, any_),
            right_t_any=(made.right_t_out, any_),
            value_t_any=(made.value_t_out, any_),
            kept_any=(made.kept_out, any_),
            rel_all=(made.rel_out, vmem),
            x_any=(made.x_out, any_),
            w_all_any=(made.w_all_out, any_),
            w_in_any=(made.w_in_out, any_),
            w_down_any=(made.w_down_out, any_),
            w_out_any=(made.w_out_out, any_),
            context_any=(made.context_out, any_),
            low_first_any=(made.low_first_out, any_),
            act_any=(made.act_out, any_),
            slope_any=(made.slope_out, any_),
            normed1=(made.normed1, vmem),
            inverse1=(made.inverse1, vmem),
            d_sum2=(made.d_sum2, vmem),
            d_second_own=(made.d_second_out, vmem),
            gains=(made.gains_out, vmem),
            g_small=(made.g_small, vmem),
        ),
        dict(
            hidden_grad=((rows, width), LOW, vmem),
            qkv_grad=((3, depth, width), HIGH, vmem),
            qkv_bias_grad=((2, depth), HIGH, vmem),
            rel_tables_grad=((3, depth, NB), HIGH, vmem),
            out_grad=((depth, width), HIGH, vmem),
            branch_grad=((2, depth), HIGH, vmem),
            gain_grad=((2, depth), HIGH, vmem),
            shift_grad=((2, depth), HIGH, vmem),
            in_grad=((depth, hidden), HIGH, vmem),
            bias_grad=((1, down_rows), HIGH, vmem),
            down_grad=((down_rows, width), HIGH, vmem),
        ),
        dict(
            left=vmem((total, 384), LOW),
            right=vmem((total, 384), LOW),
            right_t=vmem((384, total), LOW),
            value_t=vmem((128, total), LOW),
            kept=vmem((total, 128), HIGH),
            x_all=vmem(x_block, LOW),
            w_all=vmem(w_block, LOW),
            w_in=vmem(in_all, LOW),
            w_down=vmem(down_all, LOW),
            w_out=vmem(out_all, LOW),
            g_out=vmem((CHIPS,) + out_block, LOW),
            context=vmem((both, half_width), LOW),
            context_wide=vmem((both, half_width), HIGH),
            low_first=vmem((both, width), LOW),
            act=vmem((both, half_hidden), LOW),
            slope=vmem((both, half_hidden), HIGH),
            d_second=vmem((both, width), LOW),
            d_branch=vmem((both, width), LOW),
            d_sum1=vmem((slot_rows, width), HIGH),
            out_part=vmem((slot_rows, width), HIGH),
            in_part=vmem((slot_rows, width), HIGH),
            in_1=vmem((8,) + in_block, LOW),
            in_2=vmem((4,) + in_block, LOW),
            in_3=vmem((3,) + in_block, LOW),
            down_1=vmem((8,) + down_block, LOW),
            down_2=vmem((4,) + down_block, LOW),
            down_3=vmem((3,) + down_block, LOW),
            out_1=vmem((12,) + out_block, LOW),
            out_2=vmem((2,) + out_block, LOW),
            out_3=vmem((1,) + out_block, LOW),
            in_total=vmem(in_block, HIGH),
            in_far=vmem((depth, half_hidden), HIGH),
            small_sum=vmem((16, half_hidden), HIGH),
            small_in=vmem((6, 16, half_hidden), HIGH),
            d_message=vmem(message, LOW),
            d_arrived=vmem(message, LOW),
            d_context=vmem((total, 128), HIGH),
            d_heads=vmem((3, HD, total), LOW),
            d_pair_t=vmem((2 * HD, total), HIGH),
            d_both=vmem((3, 2, HD, total // 2), LOW),
            d_x=vmem(x_block, LOW),
            x_stage=vmem((3, 7, slot_rows // 3, width), LOW),
            x_total=vmem((slot_rows, width), LOW),
            x_came=vmem((slot_rows, width), LOW),
            rel_grad=vmem((2 * depth, 4 * NB), HIGH),
            rel_came=vmem((2, depth, 4 * NB), HIGH),
            w_mine=vmem((2, 6 * HD, half_width), HIGH),
            w_far=vmem((6 * HD, half_width), HIGH),
            w_low=vmem((CHIPS, depth, 6 * HD), LOW),
            w_came=vmem((CHIPS, depth, 6 * HD), LOW),
            keep_sem=dma((15,)),
            home_sem=dma((2,)),
            d_send=dma((16,)),
            d_recv=dma((16,)),
            in_send=dma((16,)),
            in_recv=dma((16,)),
            down_send=dma((16,)),
            down_recv=dma((16,)),
            out_send=dma((16,)),
            out_recv=dma((16,)),
            small_send=dma((6,)),
            small_recv=dma((6,)),
            x_send=dma((3, 8)),
            x_recv=dma((3, 8)),
            w_send=dma((16,)),
            w_recv=dma((16,)),
            rel_send=dma((2,)),
            rel_recv=dma((2,)),
            pair_send=dma((6,)),
            pair_recv=dma((6,)),
        ),
    )
    results = list(
        handed_over(
            [
                made.hidden_out,
                ended.hidden_grad,
                ended.qkv_grad,
                ended.qkv_bias_grad,
                ended.rel_tables_grad,
                ended.out_grad,
                ended.branch_grad,
                ended.gain_grad,
                ended.shift_grad,
                ended.in_grad,
                ended.bias_grad,
                ended.down_grad,
            ]
        )
    )
    results[4] = results[4].transpose(0, 2, 1)
    results[10] = results[10].reshape(down_rows)
    return tuple(results)


def solution(mesh):
    by_heads = mesh.shape["grp"] == 2 and mesh.shape["blk"] == CHIPS == H
    return jax.shard_map(
        head_shards if by_heads else shards,
        mesh=mesh,
        in_specs=(
            P(("grp", "blk"), None),
            P(("grp", "blk")),
            P(("grp", "blk")),
            P(None, ("grp", "blk")),
            P(None, ("grp", "blk"), None),
            P(None, ("grp", "blk")),
            P(None, None, ("grp", "blk")),
            P(("grp", "blk"), None),
            P(None, ("grp", "blk")),
            P(None, ("grp", "blk")),
            P(None, ("grp", "blk")),
            P(("grp", "blk"), None),
            P(("grp", "blk")),
            P(("grp", "blk"), None),
            P(("grp", "blk"), None),
        ),
        out_specs=(
            P(("grp", "blk"), None),
            P(("grp", "blk"), None),
            P(None, ("grp", "blk"), None),
            P(None, ("grp", "blk")),
            P(None, None, ("grp", "blk")),
            P(("grp", "blk"), None),
            P(None, ("grp", "blk")),
            P(None, ("grp", "blk")),
            P(None, ("grp", "blk")),
            P(("grp", "blk"), None),
            P(("grp", "blk")),
            P(("grp", "blk"), None),
        ),
        check_vma=False,
    )
```

```python
import functools
import math
import types

import jax
import jax.numpy as jnp
from jax import lax
from jax.experimental import pallas as pl
from jax.experimental.pallas import tpu as pltpu
from jax.sharding import PartitionSpec as P

H = 16
HD = 64
NB = 128
ORDER_RANGE = 128
BOX_RANGE = 64


NEGATIVE = -1e30
EPSILON = 1e-05


def shifted(x, axis, by):
    devices = lax.axis_size(axis)
    return lax.ppermute(x, axis, [(i, (i + by) % devices) for i in range(devices)])


def block_size(row_count):
    chosen = 1
    for option in range(1, min(row_count, 544) + 1):
        if row_count % option == 0:
            chosen = option
    return chosen


def kind_ranges():
    return (ORDER_RANGE, BOX_RANGE, BOX_RANGE)


def query_maps(layout_ids):
    maps_out = []
    for column, extent in enumerate(kind_ranges()):
        offsets = layout_ids[:, column][:, None] - jnp.arange(extent, dtype=jnp.int32)[None, :]
        bucket = jnp.clip(offsets, -(NB // 2), NB // 2 - 1) + NB // 2
        maps_out.append(bucket[:, :, None] == jnp.arange(NB, dtype=jnp.int32)[None, None, :])
    return maps_out


def key_onehot(key_ids):
    pieces_out = []
    for column, extent in enumerate(kind_ranges()):
        pieces_out.append(
            key_ids[:, column + 1][:, None] == jnp.arange(extent, dtype=jnp.int32)[None, :]
        )
    return jnp.concatenate(pieces_out, axis=1).astype(jnp.bfloat16)


def norm_forward(values_in, norm_gain, norm_shift):
    center = values_in - jnp.mean(values_in, axis=-1, keepdims=True)
    inverse = lax.rsqrt(jnp.mean(center * center, axis=-1, keepdims=True) + EPSILON)
    normed = center * inverse
    return (normed * norm_gain + norm_shift, normed, inverse)


def norm_backward(upstream, normed, inverse, norm_gain):
    scaled = upstream * norm_gain
    inner_part = (
        scaled
        - jnp.mean(scaled, axis=-1, keepdims=True)
        - normed * jnp.mean(scaled * normed, axis=-1, keepdims=True)
    )
    return (inner_part * inverse, jnp.sum(upstream * normed, axis=0), jnp.sum(upstream, axis=0))


def block_logits(query_heads, selector, query_seg, key_part, meta_part, scaling):
    key_ids = meta_part.astype(jnp.int32)
    row_count = key_part.shape[0]
    key_heads = key_part.reshape(row_count, H, HD)
    content = jnp.einsum("thd,khd->htk", query_heads, key_heads, preferred_element_type=jnp.float32)
    onehot = key_onehot(key_ids)
    rel_bias = jnp.einsum("thv,kv->htk", selector, onehot, preferred_element_type=jnp.float32)
    allowed = query_seg[:, None] == key_ids[None, :, 0]
    logits = jnp.where(allowed[None], (content + rel_bias) * scaling, NEGATIVE)
    return (logits, allowed, onehot, key_heads)


def over_blocks(advance, carry, piece, start):
    row_count = piece[0].shape[0]
    stride = block_size(row_count)

    def one_step(block_index, running):
        portion = tuple(
            (lax.dynamic_slice_in_dim(member, block_index * stride, stride, 0) for member in piece)
        )
        return advance(running, portion, start + block_index * stride)

    return lax.fori_loop(0, row_count // stride, one_step, carry)


def shards(
    hidden_in,
    segment_ids,
    order_ids,
    box_ids,
    qkv_weight,
    qkv_bias,
    rel_tables,
    out_weight,
    branch_bias,
    norm_gains,
    norm_shifts,
    ffn_in,
    ffn_in_bias,
    ffn_out,
    out_grad,
):
    gathered = (
        lax.all_gather(qkv_weight, ("grp", "blk"), axis=1, tiled=True),
        lax.all_gather(qkv_bias, ("grp", "blk"), axis=1, tiled=True),
        lax.all_gather(rel_tables, ("grp", "blk"), axis=2, tiled=True),
        lax.all_gather(out_weight, ("grp", "blk"), axis=0, tiled=True),
        lax.all_gather(branch_bias, ("grp", "blk"), axis=1, tiled=True),
        lax.all_gather(norm_gains, ("grp", "blk"), axis=1, tiled=True),
        lax.all_gather(norm_shifts, ("grp", "blk"), axis=1, tiled=True),
        lax.all_gather(ffn_in, ("grp", "blk"), axis=0, tiled=True),
        lax.all_gather(ffn_in_bias, ("grp", "blk"), axis=0, tiled=True),
        lax.all_gather(ffn_out, ("grp", "blk"), axis=0, tiled=True),
    )
    w_qkv, b_qkv, w_rel, w_out, b_branch, gains, shifts, w_in, b_in, w_down = gathered
    row_count = hidden_in.shape[0]
    width = hidden_in.shape[1]
    scaling = 1.0 / math.sqrt(4.0 * HD)
    select_width = ORDER_RANGE + 2 * BOX_RANGE
    projected = jnp.einsum("td,cde->cte", hidden_in, w_qkv, preferred_element_type=jnp.float32)
    bias_qkv = b_qkv.astype(jnp.float32)
    query_rows = (projected[0] + bias_qkv[0]).astype(jnp.bfloat16)
    key_rows = projected[1].astype(jnp.bfloat16)
    value_rows = (projected[2] + bias_qkv[1]).astype(jnp.bfloat16)
    layout_ids = jnp.stack([order_ids, box_ids[0], box_ids[1]], axis=1)
    key_meta = jnp.stack([segment_ids, order_ids, box_ids[0], box_ids[1]], axis=1).astype(
        jnp.bfloat16
    )
    query_heads = query_rows.reshape(row_count, H, HD)
    rel_heads = w_rel.reshape(3, NB, H, HD)
    tables = jnp.einsum(
        "thd,nbhd->thnb", query_heads, rel_heads, preferred_element_type=jnp.float32
    ).astype(jnp.bfloat16)
    maps_list = query_maps(layout_ids)
    selector = jnp.concatenate(
        [
            jnp.einsum(
                "thb,tvb->thv",
                tables[:, :, column],
                maps_list[column].astype(jnp.bfloat16),
                preferred_element_type=jnp.float32,
            )
            for column in range(3)
        ],
        axis=2,
    ).astype(jnp.bfloat16)

    def forward_step(running, portion, offset):
        row_top, row_total, weighted = running
        key_part, value_part, meta_part = portion
        logits, allowed, onehot, key_heads = block_logits(
            query_heads, selector, segment_ids, key_part, meta_part, scaling
        )
        new_top = jnp.maximum(row_top, jnp.max(logits, axis=2))
        rescale = jnp.exp(row_top - new_top)
        weights = jnp.where(allowed[None], jnp.exp(logits - new_top[:, :, None]), 0.0)
        value_heads = value_part.reshape(value_part.shape[0], H, HD)
        weighted = weighted * rescale.T[:, :, None] + jnp.einsum(
            "htk,khd->thd",
            weights.astype(jnp.bfloat16),
            value_heads,
            preferred_element_type=jnp.float32,
        )
        return (new_top, row_total * rescale + jnp.sum(weights, axis=2), weighted)

    start_state = (
        jnp.full((H, row_count), NEGATIVE, jnp.float32),
        jnp.zeros((H, row_count), jnp.float32),
        jnp.zeros((row_count, H, HD), jnp.float32),
    )
    row_top, row_total, weighted = over_blocks(
        forward_step,
        start_state,
        (
            lax.all_gather(key_rows, "blk", axis=0, tiled=True),
            lax.all_gather(value_rows, "blk", axis=0, tiled=True),
            lax.all_gather(key_meta, "blk", axis=0, tiled=True),
        ),
        jnp.int32(0),
    )
    context_full = weighted / row_total.T[:, :, None]
    log_total = row_top + jnp.log(row_total)
    context = context_full.reshape(row_count, width).astype(jnp.bfloat16)
    branch = jnp.dot(context, w_out, preferred_element_type=jnp.float32) + b_branch[0].astype(
        jnp.float32
    )
    first, normed_one, inverse_one = norm_forward(
        hidden_in.astype(jnp.float32) + branch,
        gains[0].astype(jnp.float32),
        shifts[0].astype(jnp.float32),
    )
    first_low = first.astype(jnp.bfloat16)
    inner_pre = jnp.dot(first_low, w_in, preferred_element_type=jnp.float32) + b_in.astype(
        jnp.float32
    )
    activated, gelu_pull = jax.vjp(
        lambda pre_act: jax.nn.gelu(pre_act, approximate=False), inner_pre
    )
    activated_low = activated.astype(jnp.bfloat16)
    second = jnp.dot(activated_low, w_down, preferred_element_type=jnp.float32) + b_branch[
        1
    ].astype(jnp.float32)
    result, normed_two, inverse_two = norm_forward(
        first + second, gains[1].astype(jnp.float32), shifts[1].astype(jnp.float32)
    )
    hidden_out = result.astype(jnp.bfloat16)
    grad_sum2, gain_grad2, shift_grad2 = norm_backward(
        out_grad.astype(jnp.float32), normed_two, inverse_two, gains[1].astype(jnp.float32)
    )
    grad_second = grad_sum2.astype(jnp.bfloat16)
    grad_w_down = jnp.einsum(
        "tf,td->fd", activated_low, grad_second, preferred_element_type=jnp.float32
    )
    grad_bias_two = jnp.sum(grad_second.astype(jnp.float32), axis=0)
    grad_act = jnp.einsum("td,fd->tf", grad_second, w_down, preferred_element_type=jnp.float32)
    grad_inner = gelu_pull(grad_act)[0].astype(jnp.bfloat16)
    grad_b_in = jnp.sum(grad_inner.astype(jnp.float32), axis=0)
    grad_w_in = jnp.einsum("td,tf->df", first_low, grad_inner, preferred_element_type=jnp.float32)
    grad_first = grad_sum2 + jnp.einsum(
        "tf,df->td", grad_inner, w_in, preferred_element_type=jnp.float32
    )
    grad_sum1, gain_grad1, shift_grad1 = norm_backward(
        grad_first, normed_one, inverse_one, gains[0].astype(jnp.float32)
    )
    grad_branch = grad_sum1.astype(jnp.bfloat16)
    grad_w_out = jnp.einsum("td,te->de", context, grad_branch, preferred_element_type=jnp.float32)
    grad_bias_one = jnp.sum(grad_branch.astype(jnp.float32), axis=0)
    grad_context = jnp.einsum(
        "te,de->td", grad_branch, w_out, preferred_element_type=jnp.float32
    ).astype(jnp.bfloat16)
    grad_heads = grad_context.reshape(row_count, H, HD)
    delta = jnp.einsum("thd,thd->ht", grad_heads.astype(jnp.float32), context_full)

    def backward_core(grad_query, grad_select, portion):
        key_part, value_part, meta_part = portion
        logits, allowed, onehot, key_heads = block_logits(
            query_heads, selector, segment_ids, key_part, meta_part, scaling
        )
        probs = jnp.where(allowed[None], jnp.exp(logits - log_total[:, :, None]), 0.0)
        part_rows = key_part.shape[0]
        value_heads = value_part.reshape(part_rows, H, HD)
        grad_probs = jnp.einsum(
            "thd,khd->htk", grad_heads, value_heads, preferred_element_type=jnp.float32
        )
        grad_logits = (probs * (grad_probs - delta[:, :, None])).astype(jnp.bfloat16)
        grad_query = grad_query + scaling * jnp.einsum(
            "htk,khd->thd", grad_logits, key_heads, preferred_element_type=jnp.float32
        )
        grad_select = grad_select + scaling * jnp.einsum(
            "htk,kv->thv", grad_logits, onehot, preferred_element_type=jnp.float32
        )
        grad_key = scaling * jnp.einsum(
            "htk,thd->khd", grad_logits, query_heads, preferred_element_type=jnp.float32
        )
        grad_value = jnp.einsum(
            "htk,thd->khd",
            probs.astype(jnp.bfloat16),
            grad_heads,
            preferred_element_type=jnp.float32,
        )
        update = jnp.concatenate(
            [grad_key.reshape(part_rows, width), grad_value.reshape(part_rows, width)], axis=1
        )
        return (grad_query, grad_select, update)

    query_zero = jnp.zeros((row_count, H, HD), jnp.float32)
    select_zero = jnp.zeros((row_count, H, select_width), jnp.float32)

    def cycle_turn(turn, carry):
        grad_query, grad_select, key_part, value_part, meta_part, carried = carry
        portion = (key_part, value_part, meta_part)
        grad_query, grad_select, update = backward_core(grad_query, grad_select, portion)
        carried = carried + update
        key_part, value_part, meta_part = shifted((key_part, value_part, meta_part), "blk", 1)
        carried = shifted(carried.astype(jnp.bfloat16), "blk", 1).astype(carried.dtype)
        return (grad_query, grad_select, key_part, value_part, meta_part, carried)

    cycle_start = (
        query_zero,
        select_zero,
        key_rows,
        value_rows,
        key_meta,
        jnp.zeros((row_count, 2 * width), jnp.float32),
    )
    cycle_end = lax.fori_loop(0, lax.axis_size("blk"), cycle_turn, cycle_start)
    grad_query, grad_select, own_pairs = (cycle_end[0], cycle_end[1], cycle_end[5])
    grad_key_rows = own_pairs[:, :width].astype(jnp.bfloat16)
    grad_value_rows = own_pairs[:, width:].astype(jnp.bfloat16)
    cursor = 0
    table_parts = []
    for column, extent in enumerate(kind_ranges()):
        table_parts.append(
            jnp.einsum(
                "thv,tvb->thb",
                grad_select[:, :, cursor : cursor + extent],
                maps_list[column].astype(jnp.float32),
                precision=lax.Precision.HIGHEST,
            )
        )
        cursor = cursor + extent
    grad_tables = jnp.stack(table_parts, axis=2).astype(jnp.bfloat16)
    grad_query_total = grad_query + jnp.einsum(
        "thnb,nbhd->thd", grad_tables, rel_heads, preferred_element_type=jnp.float32
    )
    grad_query_rows = grad_query_total.reshape(row_count, width).astype(jnp.bfloat16)
    grad_rel = jnp.einsum(
        "thnb,thd->nbhd", grad_tables, query_heads, preferred_element_type=jnp.float32
    ).reshape(3, NB, width)
    grad_stack = jnp.stack([grad_query_rows, grad_key_rows, grad_value_rows])
    grad_w_qkv = jnp.einsum(
        "td,cte->cde", hidden_in, grad_stack, preferred_element_type=jnp.float32
    )
    grad_b_qkv = jnp.stack(
        [
            jnp.sum(grad_query_rows.astype(jnp.float32), axis=0),
            jnp.sum(grad_value_rows.astype(jnp.float32), axis=0),
        ]
    )
    grad_input = grad_sum1 + jnp.einsum(
        "cte,cde->td", grad_stack, w_qkv, preferred_element_type=jnp.float32
    )
    summed = (
        lax.psum_scatter(grad_w_qkv, ("grp", "blk"), scatter_dimension=1, tiled=True),
        lax.psum_scatter(grad_b_qkv, ("grp", "blk"), scatter_dimension=1, tiled=True),
        lax.psum_scatter(grad_rel, ("grp", "blk"), scatter_dimension=2, tiled=True),
        lax.psum_scatter(grad_w_out, ("grp", "blk"), scatter_dimension=0, tiled=True),
        lax.psum_scatter(
            jnp.stack([grad_bias_one, grad_bias_two]),
            ("grp", "blk"),
            scatter_dimension=1,
            tiled=True,
        ),
        lax.psum_scatter(
            jnp.stack([gain_grad1, gain_grad2]), ("grp", "blk"), scatter_dimension=1, tiled=True
        ),
        lax.psum_scatter(
            jnp.stack([shift_grad1, shift_grad2]), ("grp", "blk"), scatter_dimension=1, tiled=True
        ),
        lax.psum_scatter(grad_w_in, ("grp", "blk"), scatter_dimension=0, tiled=True),
        lax.psum_scatter(grad_b_in, ("grp", "blk"), scatter_dimension=0, tiled=True),
        lax.psum_scatter(grad_w_down, ("grp", "blk"), scatter_dimension=0, tiled=True),
    )
    return (
        hidden_out,
        grad_input.astype(jnp.bfloat16),
        summed[0],
        summed[1],
        summed[2],
        summed[3],
        summed[4],
        summed[5],
        summed[6],
        summed[7],
        summed[8],
        summed[9],
    )


MESH = pl.DeviceIdType.MESH
LOW = jnp.bfloat16
HIGH = jnp.float32
CHIPS = 16
HALF = 8
BLOCK = 256
MASKED = -1e30
VMEM_LIMIT = 62 * 2**20
NT = ((1,), (1,))
TN = ((0,), (0,))


def dot(left, right, dims=((1,), (0,))):
    return lax.dot_general(left, right, (dims, ((), ())), preferred_element_type=HIGH)


def place():
    return lax.axis_index("grp"), lax.axis_index("blk")


def coordinates(chip):
    return lax.div(chip, 4), lax.rem(lax.div(chip, 2), 2), lax.rem(chip, 2)


def greet_all():
    core, chip = place()
    me = core * CHIPS + chip
    barrier = pltpu.get_barrier_semaphore()

    def greet(ahead, carry):
        other = lax.rem(me + ahead, 2 * CHIPS)
        pl.semaphore_signal(
            barrier,
            inc=1,
            device_id=(lax.div(other, CHIPS), lax.rem(other, CHIPS)),
            device_id_type=MESH,
        )
        return carry

    lax.fori_loop(1, 2 * CHIPS, greet, 0)


def await_all():
    pl.semaphore_wait(pltpu.get_barrier_semaphore(), 2 * CHIPS - 1)


def remote(source, target, send, recv, device):
    return pltpu.make_async_remote_copy(
        src_ref=source,
        dst_ref=target,
        send_sem=send,
        recv_sem=recv,
        device_id=device,
        device_id_type=MESH,
    )


def local(source, target, sem):
    return pltpu.make_async_copy(source, target, sem)


MIRROR = 3


def in_the_middle():
    z, _, _ = coordinates(lax.axis_index("blk"))
    return jnp.logical_and(z > 0, z < 3)


def neighbours(across):
    core, chip = place()
    z, y, x = coordinates(chip)
    planes = (z + 1 - 2 * lax.rem(z, 2), 2 - lax.div(z, 2), 3 - 3 * lax.div(z, 2), 3 - z)

    def slot(far_p, far_q, line):
        far_y, far_x = (far_q, far_p) if across == "x" else (far_p, far_q)
        plane = z if line is None else planes[line]
        return plane * 4 + (1 - y if far_y else y) * 2 + (1 - x if far_x else x)

    return slot


class Shipments:
    def __init__(self, send, recv):
        self.send, self.recv, self.made = send, recv, []
        self.core = lax.axis_index("grp")

    def ship(self, source, target, recv_index, to, when=None):
        index = len(self.made)

        def make():
            return remote(
                source(), target(), self.send.at[index], self.recv.at[recv_index()], (self.core, to())
            )

        self.made.append((make, when))
        self.on(when, lambda: make().start())

    @staticmethod
    def on(when, act):
        if when is None:
            act()
        else:
            pl.when(when)(act)

    def landed(self, target, recv_index, near):
        remote(target, target, self.send.at[0], self.recv.at[recv_index], (self.core, near)).wait_recv()

    def all_sent(self, count):
        assert len(self.made) == count
        for make, when in self.made:
            self.on(when, lambda make=make: make().wait_send())


class Gather:
    def __init__(self, pick, send, recv, across):
        self.pick, self.at = pick, neighbours(across)
        self.moves = Shipments(send, recv)
        self.middle = in_the_middle()

    def ship(self, what, to, when=None):
        slot = lambda: self.at(*what)
        ref = lambda: self.pick(slot())
        self.moves.ship(ref, ref, slot, lambda: self.at(*to), when)

    def landed(self, *what):
        slot = self.at(*what)
        self.moves.landed(self.pick(slot), slot, self.at(1, 0, None))

    def pass_on(self, what, line):
        self.ship(what, (0, 0, MIRROR if line == 0 else 0), self.middle)

    def own_line(self, number):
        if number == 0:
            self.ship((0, 0, None), (0, 0, 0))
        else:
            self.ship((0, 0, None), (0, 0, MIRROR), self.middle)

    def own_plane(self):
        self.ship((0, 0, None), (1, 0, None))
        self.ship((0, 0, None), (0, 1, None))

    def line(self, line):
        self.landed(0, 0, line)
        self.pass_on((0, 0, line), line)
        self.ship((0, 0, line), (1, 0, None))
        self.ship((0, 0, line), (0, 1, None))

    def side(self, line):
        self.landed(1, 0, line)
        self.ship((1, 0, line), (0, 1, None))

    def arrive(self):
        for line in (None, 0, 1, 2):
            for far_p in (0, 1):
                self.landed(far_p, 1, line)

    def finish(self):
        self.moves.all_sent(17)


class GatherLate(Gather):
    PLANE = ((0, 0), (1, 0), (0, 1), (1, 1))

    def first(self):
        self.own_plane()

    def second(self):
        self.landed(1, 0, None)
        self.ship((1, 0, None), (0, 1, None))

    def third(self):
        for far_p in (0, 1):
            self.landed(far_p, 1, None)
        for what in self.PLANE:
            self.ship(what + (None,), (0, 0, 0))
        for what in self.PLANE:
            self.ship(what + (None,), (0, 0, MIRROR), self.middle)

    def late_line(self, line):
        for what in self.PLANE:
            self.landed(*what, line)
            self.pass_on(what + (line,), line)

    def finish(self):
        self.moves.all_sent(23)


class Reduce:
    def __init__(self, sent, own, pick, stages, send, recv, across):
        self.sent, self.own, self.pick, self.at = sent, own, pick, neighbours(across)
        self.first, self.second, self.third_in = stages
        self.moves = Shipments(send, recv)

    @staticmethod
    def number(line):
        return 3 if line is None else line

    def ship(self, source, target, index, to):
        self.moves.ship(source, target, lambda: index, lambda: self.at(*to))

    def landed(self, target, index):
        self.moves.landed(target, index, self.at(1, 0, None))

    def start(self, line):
        for far_p in (1, 0):
            index = self.number(line) * 2 + far_p
            self.ship(
                lambda far_p=far_p: self.pick(self.sent, self.at(far_p, 1, line)),
                lambda index=index: self.first.at[index],
                index,
                (0, 1, None),
            )

    def mine(self, *what):
        return self.pick(self.own, self.at(*what))[...].astype(HIGH)

    def side(self, line):
        number = self.number(line)
        index = number * 2 + 1
        self.landed(self.first.at[index], index)
        self.first[index] = (self.first[index].astype(HIGH) + self.mine(1, 0, line)).astype(LOW)
        self.ship(
            lambda: self.first.at[index], lambda: self.second.at[number], 8 + number, (1, 0, None)
        )

    def line(self, line):
        number = self.number(line)
        index = number * 2
        self.landed(self.first.at[index], index)
        self.landed(self.second.at[number], 8 + number)
        total = (
            self.first[index].astype(HIGH)
            + self.second[number].astype(HIGH)
            + self.mine(0, 0, line)
        )
        if line is None:
            return total
        self.first[index] = total.astype(LOW)
        ahead = lambda: lax.rem(lax.div(self.at(0, 0, None), 4) - lax.div(self.at(0, 0, line), 4) + 4, 4) - 1
        self.moves.ship(
            lambda: self.first.at[index],
            lambda: self.third_in.at[ahead()],
            lambda: 12 + ahead(),
            lambda: self.at(0, 0, line),
        )

    def finish(self, result):
        result[...] = self.line(None)
        for ahead in range(3):
            self.landed(self.third_in.at[ahead], 12 + ahead)
            result[...] += self.third_in[ahead].astype(HIGH)
        self.moves.all_sent(15)


class ReduceEarly(Reduce):
    PLANE = ((0, 0), (1, 0), (0, 1), (1, 1))

    def ahead(self, line):
        return lax.rem(lax.div(self.at(0, 0, None), 4) - lax.div(self.at(0, 0, line), 4) + 4, 4) - 1

    def start(self):
        for line in (2, 1, 0):
            for number, what in enumerate(self.PLANE):
                index = lambda number=number, line=line: self.ahead(line) * 4 + number
                self.moves.ship(
                    lambda what=what, line=line: self.pick(self.sent, self.at(*what, line)),
                    lambda index=index: self.first.at[index()],
                    index,
                    lambda line=line: self.at(0, 0, line),
                )

    def plane_sum(self, number):
        total = self.mine(*self.PLANE[number], None)
        for ahead in range(3):
            index = ahead * 4 + number
            self.landed(self.first.at[index], index)
            total += self.first[index].astype(HIGH)
        return total

    def third(self):
        for number, far_p in ((3, 1), (2, 0)):
            self.first[number] = self.plane_sum(number).astype(LOW)
            self.ship(
                lambda number=number: self.first.at[number],
                lambda far_p=far_p: self.second.at[far_p],
                12 + far_p,
                (0, 1, None),
            )

    def across(self):
        total = self.plane_sum(1)
        self.landed(self.second.at[1], 13)
        self.first[1] = (total + self.second[1].astype(HIGH)).astype(LOW)
        self.ship(lambda: self.first.at[1], lambda: self.third_in.at[0], 14, (1, 0, None))

    def finish(self, result):
        total = self.plane_sum(0)
        self.landed(self.second.at[0], 12)
        self.landed(self.third_in.at[0], 14)
        result[...] = total + self.second[0].astype(HIGH) + self.third_in[0].astype(HIGH)
        self.moves.all_sent(15)


def cube_of(order):
    core, chip = place()
    z, y, x = coordinates(chip)

    def at(*flips):
        far = dict(zip(order, flips))
        plane = z + 1 - 2 * lax.rem(z, 2) if far["z"] else z
        return plane * 4 + (1 - y if far["y"] else y) * 2 + (1 - x if far["x"] else x)

    return at


class CubeGather:
    def __init__(self, pick, send, recv, order):
        self.pick, self.at = pick, cube_of(order)
        self.moves = Shipments(send, recv)

    def ship(self, what, to):
        slot = lambda: lax.rem(self.at(*what), HALF)
        ref = lambda: self.pick(slot())
        self.moves.ship(ref, ref, slot, lambda: self.at(*to))

    def landed(self, *what):
        slot = lax.rem(self.at(*what), HALF)
        self.moves.landed(self.pick(slot), slot, self.at(1, 0, 0))

    def own(self):
        for to in ((1, 0, 0), (0, 1, 0), (0, 0, 1)):
            self.ship((0, 0, 0), to)

    def one(self):
        self.landed(1, 0, 0)
        self.ship((1, 0, 0), (0, 1, 0))
        self.ship((1, 0, 0), (0, 0, 1))

    def two(self):
        for what in ((0, 1, 0), (1, 1, 0)):
            self.landed(*what)
            self.ship(what, (0, 0, 1))

    def arrive(self):
        for what in ((0, 0, 1), (1, 0, 1), (0, 1, 1), (1, 1, 1)):
            self.landed(*what)

    def finish(self):
        self.moves.all_sent(7)


class CubeReduce:
    def __init__(self, pick, stage, send, recv, order):
        self.pick, self.stage, self.at = pick, stage, cube_of(order)
        self.moves = Shipments(send, recv)

    def ship(self, source, index, to):
        self.moves.ship(source, lambda: self.stage.at[index], lambda: index, lambda: self.at(*to))

    def mine(self, *what):
        return self.pick(lax.rem(self.at(*what), HALF))

    def term(self, index):
        self.moves.landed(self.stage.at[index], index, self.at(1, 0, 0))
        return self.stage[index].astype(HIGH)

    def own(self):
        for index, (one, two) in enumerate(((1, 1), (0, 1), (1, 0), (0, 0))):
            self.ship(lambda one=one, two=two: self.mine(one, two, 1), index, (0, 0, 1))

    def one(self):
        for index, one in ((0, 1), (1, 0)):
            total = self.mine(one, 1, 0)[...].astype(HIGH) + self.term(index)
            self.stage[index] = total.astype(LOW)
            self.ship(lambda index=index: self.stage.at[index], 4 + index, (0, 1, 0))

    def two(self):
        total = self.mine(1, 0, 0)[...].astype(HIGH) + self.term(2) + self.term(4)
        self.stage[2] = total.astype(LOW)
        self.ship(lambda: self.stage.at[2], 6, (1, 0, 0))

    def arrive(self):
        return self.mine(0, 0, 0)[...].astype(HIGH) + self.term(3) + self.term(5) + self.term(6)

    def finish(self):
        self.moves.all_sent(7)


def each(plans, act, *arguments):
    for plan in plans:
        act(plan, *arguments)


def unit():
    core, chip = place()
    return lax.div(chip, HALF), lax.rem(chip, HALF), core


def to_tokens(source, target, send, recv):
    core, chip = place()
    group, position, _ = unit()
    to_core = lax.div(position, 4)
    mine = group * HALF + 2 * lax.rem(position, 4) + core
    here = to_core == core

    def copy_to(ahead):
        chip_to = lax.rem(chip + ahead, CHIPS)
        return remote(
            source.at[chip_to], target.at[mine], send.at[ahead], recv.at[mine], (to_core, chip_to)
        )

    pl.when(here)(lambda: local(source.at[chip], target.at[mine], recv.at[mine]).start())
    pl.when(jnp.logical_not(here))(lambda: copy_to(0).start())
    for ahead in range(1, CHIPS):
        copy_to(ahead).start()

    def arrive():
        for slot in range(CHIPS):
            local(source.at[slot], target.at[slot], recv.at[slot]).wait()

    def finish():
        pl.when(jnp.logical_not(here))(lambda: copy_to(0).wait_send())
        for ahead in range(1, CHIPS):
            copy_to(ahead).wait_send()

    return arrive, finish


def to_heads(source, target, send, recv):
    core, chip = place()
    group, position, _ = unit()
    here = lax.div(position, 4) == core
    start = 2 * lax.rem(position, 4) + core

    def copy_to(turn_group, ahead):
        to_group = lax.rem(group + turn_group, 2)
        head = lax.rem(start + ahead, HALF)
        return remote(
            source.at[to_group * HALF + head],
            target.at[chip],
            send.at[turn_group * HALF + ahead],
            recv.at[chip],
            (lax.rem(head, 2), to_group * HALF + core * 4 + lax.div(head, 2)),
        )

    def every(act):
        pl.when(jnp.logical_not(here))(lambda: act(copy_to(0, 0)))
        for turn_group in range(2):
            for ahead in range(0 if turn_group else 1, HALF):
                act(copy_to(turn_group, ahead))

    pl.when(here)(
        lambda: local(source.at[group * HALF + start], target.at[chip], recv.at[chip]).start()
    )
    every(lambda copy: copy.start())

    def arrive():
        for slot in range(CHIPS):
            local(source.at[slot], target.at[slot], recv.at[slot]).wait()

    return arrive, lambda: every(lambda copy: copy.wait_send())


def lanes(rows, width=128):
    return lax.broadcasted_iota(jnp.int32, (rows, width), 1)


def turn(values):
    return pltpu.roll(values, HD, 1)


def fold(rows_in):
    half = rows_in.shape[0] // 2
    both = jnp.where(lanes(half) < HD, rows_in[:half], turn(rows_in[half:]))
    pad = -half % 16
    if pad:
        both = jnp.concatenate([both, jnp.zeros((pad, 128), HIGH)], axis=0)
    return both.astype(LOW)


def column_sums(v):
    return jnp.sum(v, axis=0, keepdims=True)


def gelu_parts(pre):
    cdf = 0.5 * (1.0 + lax.erf(pre * math.sqrt(0.5)))
    density = jnp.exp(-0.5 * pre * pre) * (1.0 / math.sqrt(2.0 * math.pi))
    return pre * cdf, cdf + pre * density


def normalize(v, gain, shift):
    center = v - jnp.mean(v, axis=1, keepdims=True)
    inverse = lax.rsqrt(jnp.mean(center * center, axis=1, keepdims=True) + EPSILON)
    normed = center * inverse
    return normed * gain + shift, normed, inverse


def normalize_back(c, normed, inverse, gain):
    scaled = c * gain
    inner = (
        scaled
        - jnp.mean(scaled, axis=1, keepdims=True)
        - normed * jnp.mean(scaled * normed, axis=1, keepdims=True)
    )
    return inner * inverse


def at_steps(index, steps):
    for number, acts in steps.items():

        def run(acts=acts):
            for act in acts:
                act()

        pl.when(index == number)(run)


def columns_of(half, width):
    return pl.ds(pl.multiple_of(half * width, 128), width)


GAIN_AT, SHIFT_AT, BIAS_AT = 128, 256, 384


def first_kernel(names, *refs):
    r = types.SimpleNamespace(**dict(zip(names, refs)))
    hidden, x_all, w_all, rel_all = r.hidden_in, r.x_all, r.w_all, r.rel_all
    token_rows, width = hidden.shape
    slot_rows = x_all.shape[1]
    total = CHIPS * slot_rows
    depth = r.out_weight.shape[0]
    w_in, w_down, w_out = r.w_in, r.w_down, r.w_out
    half_hidden = w_in.shape[3]
    half_width = width // 2
    core, chip = place()
    group, position, _ = unit()
    other = 1 - core
    me = core * CHIPS + chip
    keep = r.keep_sem

    greet_all()

    loads = [
        local(r.ffn_in.at[:, columns_of(core, half_hidden)], w_in.at[core, chip], keep.at[0]),
        local(r.ffn_out, w_down.at[chip], keep.at[1]),
        local(r.out_weight, w_out.at[chip, pl.ds(0, depth)], keep.at[2]),
    ]
    for copy in loads:
        copy.start()

    extra = r.extra
    extra[...] = jnp.zeros_like(extra)
    extra[0:1, 0:256] = jnp.full((1, 256), 4.0, HIGH)
    extra[0:1, 0:token_rows] = r.segment_ids[...].astype(HIGH)
    extra[1:2, 0:token_rows] = r.order_ids[...].astype(HIGH)
    extra[2:4, 0:token_rows] = r.box_ids[...].astype(HIGH)
    tail = token_rows - token_rows % 16
    x_own = r.x_own
    x_own[0:tail, :] = hidden[0:tail, :]
    x_own[tail:slot_rows, :] = jnp.concatenate(
        [hidden[tail:token_rows, :].astype(HIGH), extra[...]], axis=0
    ).astype(LOW)
    weight = r.qkv_weight
    rel_own = r.rel_own
    for kind in range(3):
        rel_own[:, kind * NB : (kind + 1) * NB] = r.rel_tables[kind]
    eye_depth = (
        lax.broadcasted_iota(jnp.int32, (depth, depth), 0)
        == lax.broadcasted_iota(jnp.int32, (depth, depth), 1)
    ).astype(LOW)
    bias_columns = dot(eye_depth, r.qkv_bias[...], NT)
    rel_own[:, 3 * NB : 4 * NB] = jnp.where(
        lanes(depth) == 0, bias_columns[:, 0:1], jnp.where(lanes(depth) == 1, bias_columns[:, 1:2], 0.0)
    ).astype(LOW)
    small_own = r.small_own
    small_own[...] = jnp.zeros_like(small_own)
    small_own[0:2, 0:depth] = r.branch_bias[...]
    small_own[0:2, GAIN_AT : GAIN_AT + depth] = r.norm_gains[...]
    small_own[0:2, SHIFT_AT : SHIFT_AT + depth] = r.norm_shifts[...]
    small_own[0:1, BIAS_AT : BIAS_AT + 128] = r.ffn_in_bias[...]
    loads += [
        local(small_own, w_out.at[chip, pl.ds(depth, 16)], keep.at[3]),
        local(weight.at[:, :, columns_of(position, 128)], w_all.at[:, core, chip], keep.at[4]),
    ]
    for copy in loads[3:]:
        copy.start()
    await_all()

    at_home = group == core
    away = lax.rem(chip + HALF, CHIPS)
    x_slot = x_all.at[position]
    home = lambda: local(x_own, x_slot, r.home_sem.at[1])
    abroad = lambda: remote(x_own, x_slot, r.home_sem.at[0], r.home_sem.at[1], (other, away))
    pl.when(at_home)(lambda: home().start())
    pl.when(jnp.logical_not(at_home))(lambda: abroad().start())

    rel_head = core * HALF + lax.div(chip, 2)
    parity = lax.rem(chip, 2)
    rel_slot = rel_all.at[pl.ds(parity * depth, depth)]

    def rel_each(act_remote, act_own):
        for to_group in range(2):
            to = (lax.rem(rel_head, 2), to_group * HALF + lax.div(rel_head, 2))
            itself = jnp.logical_and(to[0] == core, to[1] == chip)
            copy = lambda: remote(
                rel_own, rel_slot, r.rel_send.at[to_group], r.rel_recv.at[parity], to
            )
            pl.when(jnp.logical_not(itself))(lambda: act_remote(copy()))
            if act_own is not None:
                pl.when(itself)(act_own)

    rel_each(
        lambda copy: copy.start(), lambda: local(rel_own, rel_slot, r.rel_recv.at[parity]).start()
    )

    def w_copy(ahead):
        to = lax.rem(chip + ahead, CHIPS)
        return remote(
            weight.at[:, :, columns_of(lax.rem(to, HALF), 128)],
            w_all.at[:, core, chip],
            r.w_send.at[ahead],
            r.w_recv.at[chip],
            (core, to),
        )

    swap_in = remote(
        r.ffn_in.at[:, columns_of(other, half_hidden)],
        w_in.at[core, chip],
        r.pair_send.at[0],
        r.pair_recv.at[0],
        (other, chip),
    )
    swap_in.start()

    third = slot_rows // 3
    x_plans = [
        CubeGather(
            lambda slot, part=part: x_all.at[slot, pl.ds(part * third, third)],
            r.x_send.at[part],
            r.x_recv.at[part],
            order,
        )
        for part, order in enumerate(("xyz", "yzx", "zxy"))
    ]
    half = width // 2
    half_tile = half_hidden // 2
    plan_out = GatherLate(lambda slot: w_out.at[slot], r.out_send, r.out_recv, "x")

    def halves(ref, wide, sends, recvs):
        return [
            Gather(
                lambda slot, part=part: ref(slot, pl.ds(part * wide, wide)), sends.at[part], recvs.at[part], across
            )
            for part, across in enumerate("xy")
        ]

    plans_in = halves(lambda slot, columns: w_in.at[:, slot, :, columns], half_tile, r.in_send, r.in_recv)
    plans_down = halves(lambda slot, columns: w_down.at[slot, :, columns], half, r.down_send, r.down_recv)

    for ahead in range(1, CHIPS):
        w_copy(ahead).start()
    for copy in loads:
        copy.wait()
    each(plans_down, Gather.own_plane)
    swap_in.wait()
    each(plans_in, Gather.own_plane)
    plan_out.first()
    each(plans_in, Gather.own_line, 0)
    home().wait()
    each(x_plans, CubeGather.own)
    each(x_plans, CubeGather.one)
    each(plans_down, Gather.own_line, 1)
    plan_out.second()
    each(x_plans, CubeGather.two)
    each(plans_down, Gather.own_line, 0)
    plan_out.third()
    each(plans_in, Gather.line, 0)
    for ahead in range(1, CHIPS):
        came = lax.rem(chip + ahead, CHIPS)
        remote(
            weight.at[:, :, pl.ds(0, 128)], w_all.at[:, core, came], r.w_send.at[0], r.w_recv.at[came], (core, came)
        ).wait_recv()
    pair_w = remote(w_all.at[:, core], w_all.at[:, core], r.pair_send.at[1], r.pair_recv.at[1], (other, chip))
    pair_w.start()
    for slot in range(2):
        local(rel_own, rel_all.at[pl.ds(slot * depth, depth)], r.rel_recv.at[slot]).wait()
    pair_bias = remote(
        rel_all.at[:, pl.ds(3 * NB, NB)], r.bias_far, r.pair_send.at[2], r.pair_recv.at[2], (other, chip)
    )
    pair_bias.start()
    each(x_plans, CubeGather.arrive)

    labels = r.labels
    first_slot = core * HALF
    label_part = x_all.at[:, pl.ds(slot_rows - 16, 16), pl.ds(0, 256)]
    label_slots = labels.at[pl.ds(first_slot, HALF)]
    pair_label = remote(label_part, label_slots, r.pair_send.at[3], r.pair_recv.at[3], (other, chip))
    pair_label.start()
    own_label = local(label_part, label_slots, keep.at[5])
    own_label.start()
    keep_x = local(x_all, r.x_out, keep.at[6])
    keep_x.start()
    keep_rel = local(rel_all, r.rel_out, keep.at[7])
    keep_rel.start()
    pair_w.wait()
    pair_bias.wait()
    keep_w = local(w_all, r.w_all_out, keep.at[15])
    keep_w.start()

    head_rows = 2 * depth
    row_at = lax.broadcasted_iota(jnp.int32, (head_rows, 128), 0)
    column_at = lanes(head_rows)

    def bias_row(columns, number):
        column = columns[:, number : number + 1]
        return column_sums(jnp.where(row_at == column_at, column, 0.0))

    rel = rel_all[...]
    bias_near = rel[:, 3 * NB : 4 * NB].astype(HIGH)
    bias_far = r.bias_far[...].astype(HIGH)
    bias_query, bias_value = (
        bias_row(bias_near, number) + turn(bias_row(bias_far, number)) for number in range(2)
    )
    weights = [w_all[n].reshape(width, 128) for n in range(3)]
    near, far_part = r.near, r.far_part
    pair_rows = 2 * slot_rows
    pair_half = lanes(pair_rows) < HD

    for pair in range(HALF // 2):
        tokens = x_all[2 * pair : 2 * pair + 2].reshape(pair_rows, width)
        query, key, value_rows = (
            pltpu.roll(dot(tokens, weights[n]), core * HD, 1) for n in range(3)
        )
        query, value_rows = query + bias_query, value_rows + bias_value
        rows = pl.ds(pl.multiple_of(core * HALF * slot_rows, 16) + pair * pair_rows, pair_rows)
        near[rows, 0:128] = jnp.where(pair_half, query, turn(value_rows)).astype(LOW)
        near[rows, 128:256] = key.astype(LOW)
        far_rows = slice(pair * pair_rows, (pair + 1) * pair_rows)
        far_part[far_rows, 0:128] = jnp.where(pair_half, turn(query), value_rows).astype(LOW)
        far_part[far_rows, 128:256] = turn(key).astype(LOW)
    pair_qkv = remote(
        far_part,
        near.at[pl.ds(pl.multiple_of(core * HALF * slot_rows, 16), HALF * slot_rows)],
        r.pair_send.at[4],
        r.pair_recv.at[4],
        (other, chip),
    )
    pair_qkv.start()

    meta = r.meta
    eye = (
        lax.broadcasted_iota(jnp.int32, (slot_rows, 256), 0)
        == lax.broadcasted_iota(jnp.int32, (slot_rows, 256), 1)
    ).astype(LOW)
    pair_label.wait()
    own_label.wait()
    for slot in range(CHIPS):
        meta[slot * slot_rows : (slot + 1) * slot_rows, 0:16] = dot(eye, labels[slot], NT)
    table_t = rel[:, 0 : 3 * NB]
    lane = lanes(BLOCK)
    first_half = lane < HD
    scale = 1.0 / math.sqrt(4.0 * HD)
    left, right, right_t = r.left, r.right, r.right_t
    value, value_t, kept = r.value, r.value_t, r.kept
    pair_qkv.wait()
    each(plans_in, Gather.own_line, 1)
    each(plans_in, Gather.side, None)

    def prepare(index, carry):
        rows = pl.ds(pl.multiple_of(index * BLOCK, BLOCK), BLOCK)
        at_steps(
            index,
            {
                3: [lambda: each(plans_down, Gather.side, None), lambda: each(plans_down, Gather.line, 1)],
                4: [lambda: each(plans_in, Gather.side, 0), lambda: each(plans_down, Gather.line, 0)],
            },
        )
        query_value = near[rows, 0:128].astype(HIGH)
        key = near[rows, 128:256].astype(HIGH)
        tables = dot(near[rows, 0:128][:, 0:HD], table_t).astype(LOW).astype(HIGH)
        ids = meta[rows, 8:12].astype(jnp.int32)
        segment, order, box_x, box_y = ids[:, 0:1], ids[:, 1:2], ids[:, 2:3], ids[:, 3:4]

        def selected(column, ids_of, values):
            bucket = jnp.clip(ids_of - values, -(NB // 2), NB // 2 - 1) + NB // 2
            return jnp.take_along_axis(tables[:, column * NB : (column + 1) * NB], bucket, axis=1)

        wide = selected(0, order, lane)
        narrow = jnp.where(first_half, selected(1, box_x, lane), selected(2, box_y, lane - HD))
        label = lane - HD
        query_side = jnp.where(
            first_half,
            query_value * scale,
            jnp.where(jnp.logical_and(label != segment, label < 8), MASKED, 0.0),
        )
        key_side = jnp.where(first_half, key, (label == segment).astype(HIGH))
        left[rows, 0:128] = (wide * scale).astype(LOW)
        left[rows, 128:256] = (narrow * scale).astype(LOW)
        left[rows, 256:384] = query_side.astype(LOW)
        order_hot = (lane == order).astype(HIGH)
        box_hot = (jnp.where(first_half, box_x, box_y + HD) == lane).astype(HIGH)
        right[rows, 0:128] = order_hot.astype(LOW)
        right[rows, 128:256] = box_hot.astype(LOW)
        right[rows, 256:384] = key_side.astype(LOW)
        right_t[0:128, rows] = order_hot.T.astype(LOW)
        right_t[128:256, rows] = box_hot.T.astype(LOW)
        right_t[256:384, rows] = key_side.T.astype(LOW)
        held = jnp.where(first_half, turn(query_value), (label == 0).astype(HIGH))
        value[rows, :] = held.astype(LOW)
        value_t[:, rows] = held.T.astype(LOW)
        return carry

    lax.fori_loop(0, total // BLOCK, prepare, 0)
    stash = [
        local(held, out, keep.at[8 + k])
        for k, (held, out) in enumerate(
            (
                (left, r.left_out),
                (right, r.right_out),
                (right_t, r.right_t_out),
                (value_t, r.value_t_out),
            )
        )
    ]
    for copy in stash:
        copy.start()

    def attend(index, carry):
        rows = pl.ds(pl.multiple_of(index * BLOCK, BLOCK), BLOCK)
        at_steps(
            index,
            {
                1: [lambda: each(plans_in, Gather.line, 2)],
                5: [lambda: each(plans_in, Gather.line, 1)],
                6: [lambda: plan_out.late_line(0)],
            },
        )
        logits = dot(left[rows, :], right_t[...])
        top = jnp.max(logits, axis=1, keepdims=True)
        weights = jnp.exp(logits - top).astype(LOW)
        mixed = dot(weights, value[...])
        row_sum = mixed[:, HD : HD + 1]
        ids = meta[rows, 8:12]
        facts = jnp.where(lane == HD, top + jnp.log(row_sum), ids[:, 3:4])
        facts = jnp.where(lane == HD + 1, ids[:, 1:2], facts)
        facts = jnp.where(lane == HD + 2, ids[:, 2:3], facts)
        kept[rows, :] = jnp.where(first_half, mixed / row_sum, facts)
        return carry

    lax.fori_loop(0, total // BLOCK, attend, 0)
    keep_facts = local(kept, r.kept_out, keep.at[12])
    keep_facts.start()
    message, context_in = r.message, r.context_in
    for slot in range(CHIPS):
        message[slot] = fold(kept[slot * slot_rows : (slot + 1) * slot_rows, :])
    context_arrives, context_sent = to_tokens(message, context_in, r.msg_send, r.msg_recv)
    each(plans_down, Gather.side, 1)
    each(plans_down, Gather.line, 2)
    plan_out.late_line(1)
    each(plans_down, Gather.side, 0)
    each(plans_in, Gather.side, 1)
    plan_out.late_line(2)

    keep_out = local(w_out, r.w_out_out, keep.at[13])
    keep_out.start()
    shares, bias_in = r.shares, r.bias_in
    shares[core] = jnp.zeros(shares.shape[1:], HIGH)
    for slot in range(CHIPS):
        small = w_out[slot, depth : depth + 16, 0 : BIAS_AT + 128].astype(HIGH)[0:8]
        target = slice(slot * depth // 128 * 128, slot * depth // 128 * 128 + 128)
        for number in range(3):
            piece = jnp.where(lanes(8) < depth, small[:, number * 128 : number * 128 + 128], 0.0)
            if slot * depth % 128:
                piece = pltpu.roll(piece, slot * depth % 128, 1)
            shares[core, number, :, target] += piece
        bias_in[:, slot * 128 : slot * 128 + 128] = small[0:1, BIAS_AT : BIAS_AT + 128]
    pair_small = remote(
        shares.at[core], shares.at[core], r.pair_send.at[5], r.pair_recv.at[5], (other, chip)
    )
    pair_small.start()
    each(plans_in, Gather.side, 2)
    context_arrives()
    each(plans_down, Gather.side, 2)

    context_wide, context, low_first = r.context_wide, r.context, r.low_first
    act, slope = r.act, r.slope
    out_part, in_part, g_small = r.out_part, r.in_part, r.g_small
    own = pl.ds(pl.multiple_of(core * slot_rows, 16), slot_rows)
    far = pl.ds(pl.multiple_of(other * slot_rows, 16), slot_rows)
    tile = 512
    half_slot = slot_rows // 2
    count = [6]

    def swap(source, target):
        copy = remote(
            source, target, r.pair_send.at[count[0]], r.pair_recv.at[count[0]], (other, chip)
        )
        count[0] += 1
        copy.start()
        return copy

    left_half = lanes(half_slot) < HD
    for slot_group in range(2):
        for pair in range(HALF // 2):
            even = context_in[slot_group * HALF + 2 * pair].astype(HIGH)[:half_slot]
            odd = context_in[slot_group * HALF + 2 * pair + 1].astype(HIGH)[:half_slot]
            top = slot_group * slot_rows
            columns = slice(pair * 128, pair * 128 + 128)
            context_wide[top : top + half_slot, columns] = jnp.where(left_half, even, turn(odd))
            context_wide[top + half_slot : top + slot_rows, columns] = jnp.where(
                left_half, turn(even), odd
            )
    context[...] = context_wide[...].astype(LOW)
    keep_context = local(context, r.context_out, keep.at[14])
    keep_context.start()

    def product(index, lhs, rhs):
        out_part[index] = dot(lhs[far, :], rhs)
        copy = swap(out_part.at[index], in_part.at[index])
        mine = dot(lhs[own, :], rhs)
        copy.wait()
        return mine + in_part[index]

    pair_small.wait()
    branch_bias, gains, shifts = (
        [jnp.concatenate([shares[0, number, k : k + 1], shares[1, number, k : k + 1]], axis=1) for k in range(2)]
        for number in range(3)
    )
    for k in range(2):
        r.gains_out[k : k + 1, :] = gains[k]
    branch = product(0, context, w_out[:, 0:depth, :].reshape(half_width, width)) + branch_bias[0]
    row_index = lax.broadcasted_iota(jnp.int32, (slot_rows, 1), 0)
    x_mine = jnp.where(row_index < token_rows, x_own[...].astype(HIGH), 0.0)
    first, normed1, inverse1 = normalize(x_mine + branch, gains[0], shifts[0])
    low_first[own, :] = first.astype(LOW)
    copy = swap(low_first.at[own], low_first.at[own])
    r.normed1[...] = normed1
    r.inverse1[...] = jnp.broadcast_to(inverse1, r.inverse1.shape)
    each(plans_in, Gather.arrive)
    keep_in = local(w_in, r.w_in_out, keep.at[16])
    keep_in.start()
    copy.wait()
    keep_first = local(low_first, r.low_first_out, keep.at[17])
    keep_first.start()

    def widen(index, carry):
        columns = pl.ds(pl.multiple_of(index * tile, tile), tile)
        pre = dot(low_first[...], w_in[:, :, :, columns].reshape(width, tile)) + bias_in[:, columns]
        found, derivative = gelu_parts(pre)
        act[:, columns] = found.astype(LOW)
        slope[:, columns] = derivative
        return carry

    lax.fori_loop(0, half_hidden // tile, widen, 0)
    keep_act = local(act, r.act_out, keep.at[18])
    keep_act.start()
    keep_slope = local(slope, r.slope_out, keep.at[19])
    keep_slope.start()
    each(plans_down, Gather.arrive)
    keep_down = local(w_down, r.w_down_out, keep.at[20])
    keep_down.start()
    second = product(1, act, w_down[...].reshape(half_hidden, width)) + branch_bias[1]
    result, normed2, inverse2 = normalize(first + second, gains[1], shifts[1])
    r.hidden_out[...] = result[:token_rows].astype(LOW)
    upstream = jnp.concatenate(
        [r.out_grad[...].astype(HIGH), jnp.zeros((slot_rows - token_rows, width), HIGH)], axis=0
    )
    d_sum2 = normalize_back(upstream, normed2, inverse2, gains[1])
    r.d_sum2[...] = d_sum2
    low_second = d_sum2.astype(LOW)
    r.d_second_out[...] = low_second
    g_small[...] = jnp.zeros_like(g_small)
    g_small[1:2, :] = column_sums(low_second.astype(HIGH))
    g_small[3:4, :] = column_sums(upstream * normed2)
    g_small[5:6, :] = column_sums(upstream)

    for ahead in range(1, CHIPS):
        w_copy(ahead).wait_send()
    rel_each(lambda copy: copy.wait_send(), None)
    pl.when(jnp.logical_not(at_home))(lambda: abroad().wait_send())
    context_sent()
    each(x_plans, CubeGather.finish)
    each(plans_in + plans_down, Gather.finish)
    plan_out.finish()
    for copy in stash + [
        keep_x,
        keep_rel,
        keep_w,
        keep_facts,
        keep_out,
        keep_context,
        keep_in,
        keep_first,
        keep_act,
        keep_slope,
        keep_down,
    ]:
        copy.wait()


def second_kernel(names, *refs):
    r = types.SimpleNamespace(**dict(zip(names, refs)))
    core, chip = place()
    group, position, _ = unit()
    other = 1 - core
    left, right, right_t, value_t, kept = r.left, r.right, r.right_t, r.value_t, r.kept
    rel_all, x_all, w_all = r.rel_all, r.x_all, r.w_all
    w_in, w_down, w_out = r.w_in, r.w_down, r.w_out
    slot_rows, width = x_all.shape[1:]
    total = CHIPS * slot_rows
    half_total = HALF * slot_rows
    half_slot = slot_rows // 2
    half_hidden = w_in.shape[3]
    half_width = width // 2
    depth = r.g_out.shape[1]
    token_rows = r.hidden_grad.shape[0]
    scale = 1.0 / math.sqrt(4.0 * HD)
    keep = r.keep_sem
    loads = [
        local(there, held, keep.at[k])
        for k, (there, held) in enumerate(
            (
                (r.w_down_any, w_down),
                (r.act_any, r.act),
                (r.slope_any, r.slope),
                (r.w_in_any, w_in),
                (r.low_first_any, r.low_first),
                (r.w_out_any, w_out),
                (r.context_any, r.context),
                (r.left_any, left),
                (r.right_t_any, right_t),
                (r.value_t_any, value_t),
                (r.kept_any, kept),
                (r.right_any, right),
                (r.x_any, x_all),
                (r.w_all_any, w_all),
            )
        )
    ]
    for copy in loads:
        copy.start()
    greet_all()
    await_all()
    count = [0]

    def swap(source, target):
        copy = remote(
            source, target, r.pair_send.at[count[0]], r.pair_recv.at[count[0]], (other, chip)
        )
        count[0] += 1
        copy.start()
        return copy

    own = pl.ds(pl.multiple_of(core * slot_rows, 16), slot_rows)
    far = pl.ds(pl.multiple_of(other * slot_rows, 16), slot_rows)
    act, slope, low_first, context = r.act, r.slope, r.low_first, r.context
    d_second, d_branch, context_wide = r.d_second, r.d_branch, r.context_wide
    d_inner = act
    out_part, in_part, small_sum = r.out_part, r.in_part, r.small_sum
    plan_down = Reduce(
        w_down,
        w_down,
        lambda ref, slot: ref.at[slot],
        [r.down_1, r.down_2, r.down_3],
        r.down_send,
        r.down_recv,
        "y",
    )
    plan_in = Reduce(
        w_in,
        w_in,
        lambda ref, slot: ref.at[:, slot],
        [r.in_1, r.in_2, r.in_3],
        r.in_send,
        r.in_recv,
        "x",
    )
    plan_out = ReduceEarly(
        r.g_out,
        r.g_out,
        lambda ref, slot: ref.at[slot],
        [r.out_1, r.out_2, r.out_3],
        r.out_send,
        r.out_recv,
        "y",
    )

    d_second[own, :] = r.d_second_own[...]
    copy = swap(r.d_second_own, d_second.at[own])
    small_sum[...] = r.g_small[...]
    for load in loads[0:3]:
        load.wait()
    copy.wait()
    tile = 512
    slots = tile // w_down.shape[1]

    def narrow_back(index, carry):
        columns = pl.ds(pl.multiple_of(index * tile, tile), tile)
        rows = pl.ds(index * slots, slots)
        low = (dot(d_second[...], w_down[rows].reshape(tile, width), NT) * slope[:, columns]).astype(LOW)
        turns = width // tile
        bias_sums = column_sums(low.astype(HIGH))
        bias_columns = pl.ds(pl.multiple_of(lax.rem(index, turns) * tile, tile), tile)
        for row in range(half_hidden // width):

            @pl.when(lax.div(index, turns) == row)
            def _():
                small_sum[6 + row : 7 + row, bias_columns] = bias_sums

        w_down[rows] = (
            dot(act[:, columns], d_second[...], TN).astype(LOW).reshape(slots, tile // slots, width)
        )
        d_inner[:, columns] = low
        return carry

    lax.fori_loop(0, half_hidden // tile, narrow_back, 0)
    plan_down.start(2)
    for load in loads[3:5]:
        load.wait()
    w_in_all = w_in[...].reshape(width, half_hidden)
    out_part[...] = dot(d_inner[far, :], w_in_all, NT)
    copy = swap(out_part, in_part)
    mine = dot(d_inner[own, :], w_in_all, NT)
    slots_in = 256 // depth

    def widen_grad(index, carry):
        rows = pl.ds(pl.multiple_of(index * 256, 256), 256)
        parts = CHIPS // slots_in
        w_in[lax.div(index, parts), pl.ds(lax.rem(index, parts) * slots_in, slots_in)] = (
            dot(low_first[:, rows], d_inner[...], TN).astype(LOW).reshape(slots_in, depth, half_hidden)
        )
        return carry

    lax.fori_loop(0, width // 256, widen_grad, 0)
    copy.wait()
    d_sum2, gains = r.d_sum2, r.gains
    d_first = d_sum2[...] + mine + in_part[...]
    d_sum1 = normalize_back(d_first, r.normed1[...], r.inverse1[:, 0:1], gains[0:1])
    low_branch = d_sum1.astype(LOW)
    d_branch[own, :] = low_branch
    copy = swap(d_branch.at[own], d_branch.at[own])
    r.d_sum1[...] = d_sum1
    small_sum[0:1, :] = column_sums(low_branch.astype(HIGH))
    small_sum[2:3, :] = column_sums(d_first * r.normed1[...])
    small_sum[4:5, :] = column_sums(d_first)
    for load in loads[5:7]:
        load.wait()
    copy.wait()
    context_wide[...] = dot(d_branch[...], w_out[:, 0:depth, :].reshape(half_width, width), NT)
    for slot_group in range(2):
        for pair in range(HALF // 2):
            both = context_wide[
                slot_group * slot_rows : (slot_group + 1) * slot_rows, pair * 128 : pair * 128 + 128
            ]
            r.d_message[slot_group * HALF + 2 * pair] = fold(both)
            r.d_message[slot_group * HALF + 2 * pair + 1] = fold(turn(both))
    d_arrived = r.d_arrived
    grad_arrives, grad_sent = to_heads(r.d_message, d_arrived, r.d_send, r.d_recv)
    r.g_out[...] = dot(context[...], d_branch[...], TN).astype(LOW).reshape(r.g_out.shape)

    z, y, x = coordinates(chip)
    small_in = r.small_in

    def small_copy(index, to_core, to_chip):
        return remote(
            small_sum, small_in.at[index], r.small_send.at[index], r.small_recv.at[index], (to_core, to_chip)
        )

    def small_turn(index):
        if index == 0:
            return [small_copy(0, other, chip)]
        if index == 1:
            return [small_copy(1, core, z * 4 + (1 - y) * 2 + x)]
        if index == 2:
            return [small_copy(2, core, z * 4 + y * 2 + 1 - x)]
        return [
            small_copy(2 + ahead, core, lax.rem(z + ahead, 4) * 4 + y * 2 + x) for ahead in (1, 2, 3)
        ]

    def small_start(index):
        for copy in small_turn(index):
            copy.start()

    def small_end(index):
        for copy in small_turn(index):
            copy.wait()
        if index == 0:
            small_sum[0:6, :] += small_in[0, 0:6, :]
        elif index < 3:
            small_sum[...] += small_in[index]

    small_start(0)
    plan_down.side(2)
    plan_down.start(1)
    small_end(0)
    plan_in.start(2)
    left_half = lanes(half_slot) < HD
    d_context = r.d_context
    grad_arrives()
    plan_down.start(0)
    plan_out.start()
    small_start(1)
    plan_in.start(0)
    for slot in range(CHIPS):
        both = d_arrived[slot].astype(HIGH)[:half_slot]
        top = slot * slot_rows
        d_context[top : top + half_slot, :] = jnp.where(left_half, both, 0.0)
        d_context[top + half_slot : top + slot_rows, :] = jnp.where(left_half, turn(both), 0.0)
    table_t = rel_all[:, 0 : 3 * NB]
    lane = lanes(BLOCK)
    first_half = lane < HD
    d_heads, d_pair_t, rel_grad = r.d_heads, r.d_pair_t, r.rel_grad
    d_pair_t[...] = jnp.zeros_like(d_pair_t)
    rel_grad[...] = jnp.zeros_like(rel_grad)
    for load in loads[7:]:
        load.wait()

    def step(index, carry):
        rows = pl.ds(pl.multiple_of(index * BLOCK, BLOCK), BLOCK)
        at_steps(
            index,
            {
                1: [lambda: plan_in.side(2), lambda: plan_in.start(1)],
                2: [lambda: plan_down.line(2), lambda: small_end(1), lambda: plan_down.side(0)],
                3: [lambda: plan_in.side(0)],
                5: [lambda: plan_in.line(2)],
                6: [lambda: plan_in.line(0), lambda: plan_in.side(1)],
                7: [lambda: plan_down.start(None)],
                8: [lambda: plan_in.start(None)],
            },
        )
        facts = kept[rows, :]
        grad = d_context[rows, :]
        delta = jnp.sum(grad * facts, axis=1, keepdims=True)
        probs = jnp.exp(dot(left[rows, :], right_t[...]) - facts[:, HD : HD + 1])
        d_probs = dot(grad.astype(LOW), value_t[...])
        d_logits = (probs * (d_probs - delta)).astype(LOW)
        query_t = jnp.where(first_half, left[rows, 256:384].astype(HIGH), 0.0).T[0:HD]
        d_pair_t[0:HD, :] += dot(query_t.astype(LOW), d_logits)
        d_pair_t[HD : 2 * HD, :] += dot(grad.T[0:HD].astype(LOW), probs.astype(LOW))
        back = dot(d_logits, right[...]) * scale
        ids = facts.astype(jnp.int32)
        order, box_x, box_y = (ids[:, HD + k : HD + k + 1] for k in (1, 2, 3))

        def placed(column, ids_of, extent, start):
            found_at = ids_of + NB // 2 - lane
            found = jnp.take_along_axis(
                back[:, column * 128 : column * 128 + 128], jnp.clip(found_at, 0, extent - 1) + start, axis=1
            )
            return jnp.where(jnp.logical_and(found_at >= 0, found_at < extent), found, 0.0)

        wide = back[:, 0:128]
        low_end = jnp.sum(jnp.where(lane >= order + NB // 2, wide, 0.0), axis=1, keepdims=True)
        high_end = jnp.sum(jnp.where(lane <= order - (NB // 2 - 1), wide, 0.0), axis=1, keepdims=True)
        first = placed(0, order, ORDER_RANGE, 0)
        first = jnp.where(lane == 0, low_end, jnp.where(lane == NB - 1, high_end, first))
        d_tables = jnp.concatenate(
            [first, placed(1, box_x, BOX_RANGE, 0), placed(1, box_y, BOX_RANGE, BOX_RANGE)], axis=1
        ).astype(LOW)
        from_tables = dot(d_tables, table_t, NT)
        d_query = back[:, 256:384] + jnp.concatenate([from_tables, from_tables], axis=1)
        d_heads[0, :, rows] = d_query.T[0:HD].astype(LOW)
        rel_grad[:, 0 : 3 * NB] += dot((query_t / scale).astype(LOW), d_tables)
        return carry

    lax.fori_loop(0, total // BLOCK, step, 0)
    small_start(2)
    plan_in.line(1)
    plan_down.line(0)

    d_heads[1] = d_pair_t[0:HD, :].astype(LOW)
    d_heads[2] = d_pair_t[HD : 2 * HD, :].astype(LOW)
    d_both = r.d_both
    near_part = pl.ds(pl.multiple_of(core * half_total, 128), half_total)
    far_part = pl.ds(pl.multiple_of(other * half_total, 128), half_total)
    copy = swap(d_heads.at[:, :, far_part], d_both.at[:, core])
    d_both[:, core] = d_heads[:, :, near_part]
    sums = [jnp.sum(d_heads[n].astype(HIGH), axis=1, keepdims=True) for n in (0, 2)]
    rel_grad[:, 3 * NB : 4 * NB] = jnp.where(
        lanes(HD) == 0, sums[0], jnp.where(lanes(HD) == 1, sums[1], 0.0)
    )
    head = 2 * position + core
    rel_came = r.rel_came

    def rel_each(act_remote, act_own):
        for side in range(2):
            to = (lax.div(position, 4), lax.rem(2 * head + side, CHIPS))
            itself = jnp.logical_and(to[0] == core, to[1] == chip)
            source = rel_grad.at[pl.ds(side * depth, depth)]
            act = lambda: act_remote(
                remote(source, rel_came.at[group], r.rel_send.at[side], r.rel_recv.at[group], to)
            )
            pl.when(jnp.logical_not(itself))(act)
            if act_own:
                pl.when(itself)(lambda: local(source, rel_came.at[group], r.rel_recv.at[group]).start())

    rel_each(lambda copy: copy.start(), True)
    copy.wait()
    d_columns = d_both[...].reshape(6 * HD, half_total)

    w_heads = jnp.concatenate([w_all[n].reshape(width, 128) for n in range(3)], axis=1)
    d_rows = d_columns.T
    d_x = r.d_x
    pair_rows = 2 * slot_rows
    for pair in range(HALF // 2):
        d_x[2 * pair : 2 * pair + 2] = (
            dot(d_rows[pair * pair_rows : (pair + 1) * pair_rows], w_heads, NT)
            .astype(LOW)
            .reshape(2, slot_rows, width)
        )
    third = slot_rows // 3
    x_plans = [
        CubeReduce(
            lambda slot, part=part: d_x.at[slot, pl.ds(part * third, third)],
            r.x_stage.at[part],
            r.x_send.at[part],
            r.x_recv.at[part],
            order,
        )
        for part, order in enumerate(("xyz", "yzx", "zxy"))
    ]
    plan_down.side(1)
    each(x_plans, CubeReduce.own)
    small_end(2)
    plan_down.line(1)
    plan_out.third()
    plan_out.across()

    w_grad = dot(d_columns, x_all[...].reshape(half_total, width))
    w_mine, w_far, w_low, w_came = r.w_mine, r.w_far, r.w_low, r.w_came
    for part in range(2):
        w_mine[part] = w_grad[:, part * half_width : (part + 1) * half_width]
    copy = swap(w_mine.at[other], w_far)
    plan_in.side(None)
    each(x_plans, CubeReduce.one)
    plan_down.side(None)
    copy.wait()
    w_sum = (w_mine[core] + w_far[...]).T
    for slot in range(CHIPS):
        w_low[slot] = w_sum[slot * depth : (slot + 1) * depth].astype(LOW)

    def w_copy(ahead):
        to = lax.rem(chip + ahead, CHIPS)
        return remote(w_low.at[to], w_came.at[chip], r.w_send.at[ahead], r.w_recv.at[chip], (core, to))

    own_w = local(w_low.at[chip], w_came.at[chip], keep.at[14])
    own_w.start()
    for ahead in range(1, CHIPS):
        w_copy(ahead).start()
    each(x_plans, CubeReduce.two)
    plan_down.finish(r.down_grad)
    small_start(3)
    plan_out.finish(r.out_grad)
    in_total, in_far = r.in_total, r.in_far
    plan_in.finish(in_total)
    in_pair = swap(in_total.at[other], in_far)
    x_total, x_came = r.x_total, r.x_came
    for part, plan in enumerate(x_plans):
        x_total[part * third : (part + 1) * third] = plan.arrive().astype(LOW)
    at_home = group == core
    home = lambda: local(x_total, x_came, r.home_sem.at[1])
    abroad = lambda: remote(
        x_total, x_came, r.home_sem.at[0], r.home_sem.at[1], (other, lax.rem(chip + HALF, CHIPS))
    )
    pl.when(at_home)(lambda: home().start())
    pl.when(jnp.logical_not(at_home))(lambda: abroad().start())

    in_grad = r.in_grad
    in_grad[:, columns_of(core, half_hidden)] = in_total[core]
    small_end(3)
    me = core * CHIPS + chip
    small_all = lambda rows, columns: (
        small_sum[rows, columns] + small_in[3, rows, columns] + small_in[4, rows, columns] + small_in[5, rows, columns]
    )
    strip = columns_of(lax.div(me * depth, 128), 128)
    shares = pltpu.roll(small_all(pl.ds(0, 8), strip), 128 - lax.rem(me * depth, 128), 1)
    for number, result in enumerate((r.branch_grad, r.gain_grad, r.shift_grad)):
        result[...] = shares[2 * number : 2 * number + 2, 0:depth]
    bias_strip = small_all(pl.ds(0, 8), columns_of(position, 128))
    r.bias_grad[...] = jnp.where(group == 0, bias_strip[6:7], bias_strip[7:8])
    for slot in range(2):
        local(rel_grad.at[pl.ds(0, depth)], rel_came.at[slot], r.rel_recv.at[slot]).wait()
    rel_each(lambda copy: copy.wait_send(), False)
    rel_total = rel_came[0] + rel_came[1]
    for kind in range(3):
        r.rel_tables_grad[kind] = rel_total[:, kind * NB : (kind + 1) * NB]
    r.qkv_bias_grad[...] = rel_total[:, 3 * NB : 4 * NB].T[0:2]
    own_w.wait()
    for ahead in range(1, CHIPS):
        came = lax.rem(chip + ahead, CHIPS)
        remote(w_low.at[0], w_came.at[came], r.w_send.at[0], r.w_recv.at[came], (core, came)).wait_recv()
        w_copy(ahead).wait_send()
    for pair in range(HALF):
        both = w_came[pair].astype(HIGH) + w_came[HALF + pair].astype(HIGH)
        for n in range(3):
            r.qkv_grad[n, :, pair * 128 : pair * 128 + 128] = both[:, n * 128 : n * 128 + 128]
    home().wait()
    pl.when(jnp.logical_not(at_home))(lambda: abroad().wait_send())
    r.hidden_grad[...] = (r.d_sum1[...] + x_came[...].astype(HIGH))[:token_rows].astype(LOW)
    in_pair.wait()
    in_grad[:, columns_of(other, half_hidden)] = in_far[...]
    grad_sent()
    each(x_plans, CubeReduce.finish)


def hand_over(count, *refs):
    for source, target in zip(refs[:count], refs[count:]):
        target[...] = source[...]


def handed_over(arrays):
    return pl.pallas_call(
        functools.partial(hand_over, len(arrays)),
        out_shape=[jax.ShapeDtypeStruct(array.shape, array.dtype) for array in arrays],
        name="hand_over",
    )(*arrays)


def call(kernel, name, number, inputs, outputs, scratch):
    names = list(inputs) + list(outputs) + list(scratch)
    results = pl.pallas_call(
        functools.partial(kernel, names),
        out_shape=[jax.ShapeDtypeStruct(shape, dtype) for shape, dtype, _ in outputs.values()],
        in_specs=[pl.BlockSpec(memory_space=space) for _, space in inputs.values()],
        out_specs=[pl.BlockSpec(memory_space=space) for _, _, space in outputs.values()],
        scratch_shapes=list(scratch.values()),
        compiler_params=pltpu.CompilerParams(
            collective_id=number, has_side_effects=True, vmem_limit_bytes=VMEM_LIMIT
        ),
        name=name,
    )(*(array for array, _ in inputs.values()))
    return types.SimpleNamespace(**dict(zip(outputs, results)))


def head_shards(
    hidden_in,
    segment_ids,
    order_ids,
    box_ids,
    qkv_weight,
    qkv_bias,
    rel_tables,
    out_weight,
    branch_bias,
    norm_gains,
    norm_shifts,
    ffn_in,
    ffn_in_bias,
    ffn_out,
    out_grad,
):
    rows, width = hidden_in.shape
    slot_rows = -(-rows // 48) * 48
    total = CHIPS * slot_rows
    depth = qkv_weight.shape[1]
    hidden = ffn_in.shape[1]
    half_hidden, half_width = hidden // 2, width // 2
    down_rows = ffn_out.shape[0]
    both = 2 * slot_rows
    fold_rows = -(-(slot_rows // 2) // 16) * 16
    any_, vmem, dma = pl.ANY, pltpu.VMEM, pltpu.SemaphoreType.DMA
    message = (CHIPS, fold_rows, 128)
    x_block, w_block = (HALF, slot_rows, width), (3, 2, CHIPS, depth, 128)
    in_all, down_all = (2, CHIPS, depth, half_hidden), (CHIPS, down_rows, width)
    out_all = (CHIPS, depth + 16, width)
    made = call(
        first_kernel,
        "forward_pass",
        0,
        dict(
            hidden_in=(hidden_in, vmem),
            segment_ids=(segment_ids.reshape(1, rows), vmem),
            order_ids=(order_ids.reshape(1, rows), vmem),
            box_ids=(box_ids, vmem),
            qkv_weight=(qkv_weight, vmem),
            qkv_bias=(qkv_bias, vmem),
            rel_tables=(rel_tables.transpose(0, 2, 1), vmem),
            out_weight=(out_weight, any_),
            branch_bias=(branch_bias, vmem),
            norm_gains=(norm_gains, vmem),
            norm_shifts=(norm_shifts, vmem),
            ffn_in=(ffn_in, any_),
            ffn_in_bias=(ffn_in_bias.reshape(1, down_rows), vmem),
            ffn_out=(ffn_out, any_),
            out_grad=(out_grad, vmem),
        ),
        dict(
            hidden_out=((rows, width), LOW, vmem),
            x_out=(x_block, LOW, any_),
            w_all_out=(w_block, LOW, any_),
            rel_out=((2 * depth, 4 * NB), LOW, any_),
            left_out=((total, 384), LOW, any_),
            right_out=((total, 384), LOW, any_),
            right_t_out=((384, total), LOW, any_),
            value_t_out=((128, total), LOW, any_),
            kept_out=((total, 128), HIGH, any_),
            w_in_out=(in_all, LOW, any_),
            w_down_out=(down_all, LOW, any_),
            w_out_out=(out_all, LOW, any_),
            context_out=((both, half_width), LOW, any_),
            low_first_out=((both, width), LOW, any_),
            act_out=((both, half_hidden), LOW, any_),
            slope_out=((both, half_hidden), HIGH, any_),
            normed1=((slot_rows, width), HIGH, vmem),
            inverse1=((slot_rows, 128), HIGH, vmem),
            d_sum2=((slot_rows, width), HIGH, vmem),
            d_second_out=((slot_rows, width), LOW, vmem),
            gains_out=((2, width), HIGH, vmem),
            g_small=((8, width), HIGH, vmem),
        ),
        dict(
            x_own=vmem((slot_rows, width), LOW),
            x_all=vmem(x_block, LOW),
            extra=vmem((slot_rows - rows, width), HIGH),
            small_own=vmem((16, width), LOW),
            w_all=vmem(w_block, LOW),
            rel_own=vmem((depth, 4 * NB), LOW),
            rel_all=vmem((2 * depth, 4 * NB), LOW),
            bias_far=vmem((2 * depth, NB), LOW),
            labels=vmem((CHIPS, 16, 256), LOW),
            near=vmem((total, 256), LOW),
            far_part=vmem((total // 2, 256), LOW),
            w_in=vmem(in_all, LOW),
            w_down=vmem(down_all, LOW),
            w_out=vmem(out_all, LOW),
            meta=vmem((total, 128), HIGH),
            shares=vmem((2, 3, 8, half_width), HIGH),
            bias_in=vmem((1, half_hidden), HIGH),
            left=vmem((total, 384), LOW),
            right=vmem((total, 384), LOW),
            right_t=vmem((384, total), LOW),
            value=vmem((total, 128), LOW),
            value_t=vmem((128, total), LOW),
            kept=vmem((total, 128), HIGH),
            message=vmem(message, LOW),
            context_in=vmem(message, LOW),
            context_wide=vmem((both, half_width), HIGH),
            context=vmem((both, half_width), LOW),
            low_first=vmem((both, width), LOW),
            act=vmem((both, half_hidden), LOW),
            slope=vmem((both, half_hidden), HIGH),
            out_part=vmem((2, slot_rows, width), HIGH),
            in_part=vmem((2, slot_rows, width), HIGH),
            keep_sem=dma((21,)),
            home_sem=dma((2,)),
            x_send=dma((3, 8)),
            x_recv=dma((3, 8)),
            w_send=dma((16,)),
            w_recv=dma((16,)),
            rel_send=dma((2,)),
            rel_recv=dma((2,)),
            out_send=dma((24,)),
            out_recv=dma((16,)),
            in_send=dma((2, 18)),
            in_recv=dma((2, 16)),
            down_send=dma((2, 18)),
            down_recv=dma((2, 16)),
            msg_send=dma((16,)),
            msg_recv=dma((16,)),
            pair_send=dma((9,)),
            pair_recv=dma((9,)),
        ),
    )
    in_block, down_block, out_block = (2, depth, half_hidden), (down_rows, width), (depth, width)
    ended = call(
        second_kernel,
        "backward_pass",
        1,
        dict(
            left_any=(made.left_out, any_),
            right_any=(made.right_out, any_),
            right_t_any=(made.right_t_out, any_),
            value_t_any=(made.value_t_out, any_),
            kept_any=(made.kept_out, any_),
            rel_all=(made.rel_out, vmem),
            x_any=(made.x_out, any_),
            w_all_any=(made.w_all_out, any_),
            w_in_any=(made.w_in_out, any_),
            w_down_any=(made.w_down_out, any_),
            w_out_any=(made.w_out_out, any_),
            context_any=(made.context_out, any_),
            low_first_any=(made.low_first_out, any_),
            act_any=(made.act_out, any_),
            slope_any=(made.slope_out, any_),
            normed1=(made.normed1, vmem),
            inverse1=(made.inverse1, vmem),
            d_sum2=(made.d_sum2, vmem),
            d_second_own=(made.d_second_out, vmem),
            gains=(made.gains_out, vmem),
            g_small=(made.g_small, vmem),
        ),
        dict(
            hidden_grad=((rows, width), LOW, vmem),
            qkv_grad=((3, depth, width), HIGH, vmem),
            qkv_bias_grad=((2, depth), HIGH, vmem),
            rel_tables_grad=((3, depth, NB), HIGH, vmem),
            out_grad=((depth, width), HIGH, vmem),
            branch_grad=((2, depth), HIGH, vmem),
            gain_grad=((2, depth), HIGH, vmem),
            shift_grad=((2, depth), HIGH, vmem),
            in_grad=((depth, hidden), HIGH, vmem),
            bias_grad=((1, down_rows), HIGH, vmem),
            down_grad=((down_rows, width), HIGH, vmem),
        ),
        dict(
            left=vmem((total, 384), LOW),
            right=vmem((total, 384), LOW),
            right_t=vmem((384, total), LOW),
            value_t=vmem((128, total), LOW),
            kept=vmem((total, 128), HIGH),
            x_all=vmem(x_block, LOW),
            w_all=vmem(w_block, LOW),
            w_in=vmem(in_all, LOW),
            w_down=vmem(down_all, LOW),
            w_out=vmem(out_all, LOW),
            g_out=vmem((CHIPS,) + out_block, LOW),
            context=vmem((both, half_width), LOW),
            context_wide=vmem((both, half_width), HIGH),
            low_first=vmem((both, width), LOW),
            act=vmem((both, half_hidden), LOW),
            slope=vmem((both, half_hidden), HIGH),
            d_second=vmem((both, width), LOW),
            d_branch=vmem((both, width), LOW),
            d_sum1=vmem((slot_rows, width), HIGH),
            out_part=vmem((slot_rows, width), HIGH),
            in_part=vmem((slot_rows, width), HIGH),
            in_1=vmem((8,) + in_block, LOW),
            in_2=vmem((4,) + in_block, LOW),
            in_3=vmem((3,) + in_block, LOW),
            down_1=vmem((8,) + down_block, LOW),
            down_2=vmem((4,) + down_block, LOW),
            down_3=vmem((3,) + down_block, LOW),
            out_1=vmem((12,) + out_block, LOW),
            out_2=vmem((2,) + out_block, LOW),
            out_3=vmem((1,) + out_block, LOW),
            in_total=vmem(in_block, HIGH),
            in_far=vmem((depth, half_hidden), HIGH),
            small_sum=vmem((8, width), HIGH),
            small_in=vmem((6, 8, width), HIGH),
            d_message=vmem(message, LOW),
            d_arrived=vmem(message, LOW),
            d_context=vmem((total, 128), HIGH),
            d_heads=vmem((3, HD, total), LOW),
            d_pair_t=vmem((2 * HD, total), HIGH),
            d_both=vmem((3, 2, HD, total // 2), LOW),
            d_x=vmem(x_block, LOW),
            x_stage=vmem((3, 7, slot_rows // 3, width), LOW),
            x_total=vmem((slot_rows, width), LOW),
            x_came=vmem((slot_rows, width), LOW),
            rel_grad=vmem((2 * depth, 4 * NB), HIGH),
            rel_came=vmem((2, depth, 4 * NB), HIGH),
            w_mine=vmem((2, 6 * HD, half_width), HIGH),
            w_far=vmem((6 * HD, half_width), HIGH),
            w_low=vmem((CHIPS, depth, 6 * HD), LOW),
            w_came=vmem((CHIPS, depth, 6 * HD), LOW),
            keep_sem=dma((15,)),
            home_sem=dma((2,)),
            d_send=dma((16,)),
            d_recv=dma((16,)),
            in_send=dma((16,)),
            in_recv=dma((16,)),
            down_send=dma((16,)),
            down_recv=dma((16,)),
            out_send=dma((16,)),
            out_recv=dma((16,)),
            small_send=dma((6,)),
            small_recv=dma((6,)),
            x_send=dma((3, 8)),
            x_recv=dma((3, 8)),
            w_send=dma((16,)),
            w_recv=dma((16,)),
            rel_send=dma((2,)),
            rel_recv=dma((2,)),
            pair_send=dma((6,)),
            pair_recv=dma((6,)),
        ),
    )
    results = list(
        handed_over(
            [
                made.hidden_out,
                ended.hidden_grad,
                ended.qkv_grad,
                ended.qkv_bias_grad,
                ended.rel_tables_grad,
                ended.out_grad,
                ended.branch_grad,
                ended.gain_grad,
                ended.shift_grad,
                ended.in_grad,
                ended.bias_grad,
                ended.down_grad,
            ]
        )
    )
    results[4] = results[4].transpose(0, 2, 1)
    results[10] = results[10].reshape(down_rows)
    return tuple(results)


def solution(mesh):
    by_heads = mesh.shape["grp"] == 2 and mesh.shape["blk"] == CHIPS == H
    return jax.shard_map(
        head_shards if by_heads else shards,
        mesh=mesh,
        in_specs=(
            P(("grp", "blk"), None),
            P(("grp", "blk")),
            P(("grp", "blk")),
            P(None, ("grp", "blk")),
            P(None, ("grp", "blk"), None),
            P(None, ("grp", "blk")),
            P(None, None, ("grp", "blk")),
            P(("grp", "blk"), None),
            P(None, ("grp", "blk")),
            P(None, ("grp", "blk")),
            P(None, ("grp", "blk")),
            P(("grp", "blk"), None),
            P(("grp", "blk")),
            P(("grp", "blk"), None),
            P(("grp", "blk"), None),
        ),
        out_specs=(
            P(("grp", "blk"), None),
            P(("grp", "blk"), None),
            P(None, ("grp", "blk"), None),
            P(None, ("grp", "blk")),
            P(None, None, ("grp", "blk")),
            P(("grp", "blk"), None),
            P(None, ("grp", "blk")),
            P(None, ("grp", "blk")),
            P(None, ("grp", "blk")),
            P(("grp", "blk"), None),
            P(("grp", "blk")),
            P(("grp", "blk"), None),
        ),
        check_vma=False,
    )
```

```python
import functools
import math
import types

import jax
import jax.numpy as jnp
from jax import lax
from jax.experimental import pallas as pl
from jax.experimental.pallas import tpu as pltpu
from jax.sharding import PartitionSpec as P

H = 16
HD = 64
NB = 128
ORDER_RANGE = 128
BOX_RANGE = 64


NEGATIVE = -1e30
EPSILON = 1e-05


def shifted(x, axis, by):
    devices = lax.axis_size(axis)
    return lax.ppermute(x, axis, [(i, (i + by) % devices) for i in range(devices)])


def block_size(row_count):
    chosen = 1
    for option in range(1, min(row_count, 544) + 1):
        if row_count % option == 0:
            chosen = option
    return chosen


def kind_ranges():
    return (ORDER_RANGE, BOX_RANGE, BOX_RANGE)


def query_maps(layout_ids):
    maps_out = []
    for column, extent in enumerate(kind_ranges()):
        offsets = layout_ids[:, column][:, None] - jnp.arange(extent, dtype=jnp.int32)[None, :]
        bucket = jnp.clip(offsets, -(NB // 2), NB // 2 - 1) + NB // 2
        maps_out.append(bucket[:, :, None] == jnp.arange(NB, dtype=jnp.int32)[None, None, :])
    return maps_out


def key_onehot(key_ids):
    pieces_out = []
    for column, extent in enumerate(kind_ranges()):
        pieces_out.append(
            key_ids[:, column + 1][:, None] == jnp.arange(extent, dtype=jnp.int32)[None, :]
        )
    return jnp.concatenate(pieces_out, axis=1).astype(jnp.bfloat16)


def norm_forward(values_in, norm_gain, norm_shift):
    center = values_in - jnp.mean(values_in, axis=-1, keepdims=True)
    inverse = lax.rsqrt(jnp.mean(center * center, axis=-1, keepdims=True) + EPSILON)
    normed = center * inverse
    return (normed * norm_gain + norm_shift, normed, inverse)


def norm_backward(upstream, normed, inverse, norm_gain):
    scaled = upstream * norm_gain
    inner_part = (
        scaled
        - jnp.mean(scaled, axis=-1, keepdims=True)
        - normed * jnp.mean(scaled * normed, axis=-1, keepdims=True)
    )
    return (inner_part * inverse, jnp.sum(upstream * normed, axis=0), jnp.sum(upstream, axis=0))


def block_logits(query_heads, selector, query_seg, key_part, meta_part, scaling):
    key_ids = meta_part.astype(jnp.int32)
    row_count = key_part.shape[0]
    key_heads = key_part.reshape(row_count, H, HD)
    content = jnp.einsum("thd,khd->htk", query_heads, key_heads, preferred_element_type=jnp.float32)
    onehot = key_onehot(key_ids)
    rel_bias = jnp.einsum("thv,kv->htk", selector, onehot, preferred_element_type=jnp.float32)
    allowed = query_seg[:, None] == key_ids[None, :, 0]
    logits = jnp.where(allowed[None], (content + rel_bias) * scaling, NEGATIVE)
    return (logits, allowed, onehot, key_heads)


def over_blocks(advance, carry, piece, start):
    row_count = piece[0].shape[0]
    stride = block_size(row_count)

    def one_step(block_index, running):
        portion = tuple(
            (lax.dynamic_slice_in_dim(member, block_index * stride, stride, 0) for member in piece)
        )
        return advance(running, portion, start + block_index * stride)

    return lax.fori_loop(0, row_count // stride, one_step, carry)


def shards(
    hidden_in,
    segment_ids,
    order_ids,
    box_ids,
    qkv_weight,
    qkv_bias,
    rel_tables,
    out_weight,
    branch_bias,
    norm_gains,
    norm_shifts,
    ffn_in,
    ffn_in_bias,
    ffn_out,
    out_grad,
):
    gathered = (
        lax.all_gather(qkv_weight, ("grp", "blk"), axis=1, tiled=True),
        lax.all_gather(qkv_bias, ("grp", "blk"), axis=1, tiled=True),
        lax.all_gather(rel_tables, ("grp", "blk"), axis=2, tiled=True),
        lax.all_gather(out_weight, ("grp", "blk"), axis=0, tiled=True),
        lax.all_gather(branch_bias, ("grp", "blk"), axis=1, tiled=True),
        lax.all_gather(norm_gains, ("grp", "blk"), axis=1, tiled=True),
        lax.all_gather(norm_shifts, ("grp", "blk"), axis=1, tiled=True),
        lax.all_gather(ffn_in, ("grp", "blk"), axis=0, tiled=True),
        lax.all_gather(ffn_in_bias, ("grp", "blk"), axis=0, tiled=True),
        lax.all_gather(ffn_out, ("grp", "blk"), axis=0, tiled=True),
    )
    w_qkv, b_qkv, w_rel, w_out, b_branch, gains, shifts, w_in, b_in, w_down = gathered
    row_count = hidden_in.shape[0]
    width = hidden_in.shape[1]
    scaling = 1.0 / math.sqrt(4.0 * HD)
    select_width = ORDER_RANGE + 2 * BOX_RANGE
    projected = jnp.einsum("td,cde->cte", hidden_in, w_qkv, preferred_element_type=jnp.float32)
    bias_qkv = b_qkv.astype(jnp.float32)
    query_rows = (projected[0] + bias_qkv[0]).astype(jnp.bfloat16)
    key_rows = projected[1].astype(jnp.bfloat16)
    value_rows = (projected[2] + bias_qkv[1]).astype(jnp.bfloat16)
    layout_ids = jnp.stack([order_ids, box_ids[0], box_ids[1]], axis=1)
    key_meta = jnp.stack([segment_ids, order_ids, box_ids[0], box_ids[1]], axis=1).astype(
        jnp.bfloat16
    )
    query_heads = query_rows.reshape(row_count, H, HD)
    rel_heads = w_rel.reshape(3, NB, H, HD)
    tables = jnp.einsum(
        "thd,nbhd->thnb", query_heads, rel_heads, preferred_element_type=jnp.float32
    ).astype(jnp.bfloat16)
    maps_list = query_maps(layout_ids)
    selector = jnp.concatenate(
        [
            jnp.einsum(
                "thb,tvb->thv",
                tables[:, :, column],
                maps_list[column].astype(jnp.bfloat16),
                preferred_element_type=jnp.float32,
            )
            for column in range(3)
        ],
        axis=2,
    ).astype(jnp.bfloat16)

    def forward_step(running, portion, offset):
        row_top, row_total, weighted = running
        key_part, value_part, meta_part = portion
        logits, allowed, onehot, key_heads = block_logits(
            query_heads, selector, segment_ids, key_part, meta_part, scaling
        )
        new_top = jnp.maximum(row_top, jnp.max(logits, axis=2))
        rescale = jnp.exp(row_top - new_top)
        weights = jnp.where(allowed[None], jnp.exp(logits - new_top[:, :, None]), 0.0)
        value_heads = value_part.reshape(value_part.shape[0], H, HD)
        weighted = weighted * rescale.T[:, :, None] + jnp.einsum(
            "htk,khd->thd",
            weights.astype(jnp.bfloat16),
            value_heads,
            preferred_element_type=jnp.float32,
        )
        return (new_top, row_total * rescale + jnp.sum(weights, axis=2), weighted)

    start_state = (
        jnp.full((H, row_count), NEGATIVE, jnp.float32),
        jnp.zeros((H, row_count), jnp.float32),
        jnp.zeros((row_count, H, HD), jnp.float32),
    )
    row_top, row_total, weighted = over_blocks(
        forward_step,
        start_state,
        (
            lax.all_gather(key_rows, "blk", axis=0, tiled=True),
            lax.all_gather(value_rows, "blk", axis=0, tiled=True),
            lax.all_gather(key_meta, "blk", axis=0, tiled=True),
        ),
        jnp.int32(0),
    )
    context_full = weighted / row_total.T[:, :, None]
    log_total = row_top + jnp.log(row_total)
    context = context_full.reshape(row_count, width).astype(jnp.bfloat16)
    branch = jnp.dot(context, w_out, preferred_element_type=jnp.float32) + b_branch[0].astype(
        jnp.float32
    )
    first, normed_one, inverse_one = norm_forward(
        hidden_in.astype(jnp.float32) + branch,
        gains[0].astype(jnp.float32),
        shifts[0].astype(jnp.float32),
    )
    first_low = first.astype(jnp.bfloat16)
    inner_pre = jnp.dot(first_low, w_in, preferred_element_type=jnp.float32) + b_in.astype(
        jnp.float32
    )
    activated, gelu_pull = jax.vjp(
        lambda pre_act: jax.nn.gelu(pre_act, approximate=False), inner_pre
    )
    activated_low = activated.astype(jnp.bfloat16)
    second = jnp.dot(activated_low, w_down, preferred_element_type=jnp.float32) + b_branch[
        1
    ].astype(jnp.float32)
    result, normed_two, inverse_two = norm_forward(
        first + second, gains[1].astype(jnp.float32), shifts[1].astype(jnp.float32)
    )
    hidden_out = result.astype(jnp.bfloat16)
    grad_sum2, gain_grad2, shift_grad2 = norm_backward(
        out_grad.astype(jnp.float32), normed_two, inverse_two, gains[1].astype(jnp.float32)
    )
    grad_second = grad_sum2.astype(jnp.bfloat16)
    grad_w_down = jnp.einsum(
        "tf,td->fd", activated_low, grad_second, preferred_element_type=jnp.float32
    )
    grad_bias_two = jnp.sum(grad_second.astype(jnp.float32), axis=0)
    grad_act = jnp.einsum("td,fd->tf", grad_second, w_down, preferred_element_type=jnp.float32)
    grad_inner = gelu_pull(grad_act)[0].astype(jnp.bfloat16)
    grad_b_in = jnp.sum(grad_inner.astype(jnp.float32), axis=0)
    grad_w_in = jnp.einsum("td,tf->df", first_low, grad_inner, preferred_element_type=jnp.float32)
    grad_first = grad_sum2 + jnp.einsum(
        "tf,df->td", grad_inner, w_in, preferred_element_type=jnp.float32
    )
    grad_sum1, gain_grad1, shift_grad1 = norm_backward(
        grad_first, normed_one, inverse_one, gains[0].astype(jnp.float32)
    )
    grad_branch = grad_sum1.astype(jnp.bfloat16)
    grad_w_out = jnp.einsum("td,te->de", context, grad_branch, preferred_element_type=jnp.float32)
    grad_bias_one = jnp.sum(grad_branch.astype(jnp.float32), axis=0)
    grad_context = jnp.einsum(
        "te,de->td", grad_branch, w_out, preferred_element_type=jnp.float32
    ).astype(jnp.bfloat16)
    grad_heads = grad_context.reshape(row_count, H, HD)
    delta = jnp.einsum("thd,thd->ht", grad_heads.astype(jnp.float32), context_full)

    def backward_core(grad_query, grad_select, portion):
        key_part, value_part, meta_part = portion
        logits, allowed, onehot, key_heads = block_logits(
            query_heads, selector, segment_ids, key_part, meta_part, scaling
        )
        probs = jnp.where(allowed[None], jnp.exp(logits - log_total[:, :, None]), 0.0)
        part_rows = key_part.shape[0]
        value_heads = value_part.reshape(part_rows, H, HD)
        grad_probs = jnp.einsum(
            "thd,khd->htk", grad_heads, value_heads, preferred_element_type=jnp.float32
        )
        grad_logits = (probs * (grad_probs - delta[:, :, None])).astype(jnp.bfloat16)
        grad_query = grad_query + scaling * jnp.einsum(
            "htk,khd->thd", grad_logits, key_heads, preferred_element_type=jnp.float32
        )
        grad_select = grad_select + scaling * jnp.einsum(
            "htk,kv->thv", grad_logits, onehot, preferred_element_type=jnp.float32
        )
        grad_key = scaling * jnp.einsum(
            "htk,thd->khd", grad_logits, query_heads, preferred_element_type=jnp.float32
        )
        grad_value = jnp.einsum(
            "htk,thd->khd",
            probs.astype(jnp.bfloat16),
            grad_heads,
            preferred_element_type=jnp.float32,
        )
        update = jnp.concatenate(
            [grad_key.reshape(part_rows, width), grad_value.reshape(part_rows, width)], axis=1
        )
        return (grad_query, grad_select, update)

    query_zero = jnp.zeros((row_count, H, HD), jnp.float32)
    select_zero = jnp.zeros((row_count, H, select_width), jnp.float32)

    def cycle_turn(turn, carry):
        grad_query, grad_select, key_part, value_part, meta_part, carried = carry
        portion = (key_part, value_part, meta_part)
        grad_query, grad_select, update = backward_core(grad_query, grad_select, portion)
        carried = carried + update
        key_part, value_part, meta_part = shifted((key_part, value_part, meta_part), "blk", 1)
        carried = shifted(carried.astype(jnp.bfloat16), "blk", 1).astype(carried.dtype)
        return (grad_query, grad_select, key_part, value_part, meta_part, carried)

    cycle_start = (
        query_zero,
        select_zero,
        key_rows,
        value_rows,
        key_meta,
        jnp.zeros((row_count, 2 * width), jnp.float32),
    )
    cycle_end = lax.fori_loop(0, lax.axis_size("blk"), cycle_turn, cycle_start)
    grad_query, grad_select, own_pairs = (cycle_end[0], cycle_end[1], cycle_end[5])
    grad_key_rows = own_pairs[:, :width].astype(jnp.bfloat16)
    grad_value_rows = own_pairs[:, width:].astype(jnp.bfloat16)
    cursor = 0
    table_parts = []
    for column, extent in enumerate(kind_ranges()):
        table_parts.append(
            jnp.einsum(
                "thv,tvb->thb",
                grad_select[:, :, cursor : cursor + extent],
                maps_list[column].astype(jnp.float32),
                precision=lax.Precision.HIGHEST,
            )
        )
        cursor = cursor + extent
    grad_tables = jnp.stack(table_parts, axis=2).astype(jnp.bfloat16)
    grad_query_total = grad_query + jnp.einsum(
        "thnb,nbhd->thd", grad_tables, rel_heads, preferred_element_type=jnp.float32
    )
    grad_query_rows = grad_query_total.reshape(row_count, width).astype(jnp.bfloat16)
    grad_rel = jnp.einsum(
        "thnb,thd->nbhd", grad_tables, query_heads, preferred_element_type=jnp.float32
    ).reshape(3, NB, width)
    grad_stack = jnp.stack([grad_query_rows, grad_key_rows, grad_value_rows])
    grad_w_qkv = jnp.einsum(
        "td,cte->cde", hidden_in, grad_stack, preferred_element_type=jnp.float32
    )
    grad_b_qkv = jnp.stack(
        [
            jnp.sum(grad_query_rows.astype(jnp.float32), axis=0),
            jnp.sum(grad_value_rows.astype(jnp.float32), axis=0),
        ]
    )
    grad_input = grad_sum1 + jnp.einsum(
        "cte,cde->td", grad_stack, w_qkv, preferred_element_type=jnp.float32
    )
    summed = (
        lax.psum_scatter(grad_w_qkv, ("grp", "blk"), scatter_dimension=1, tiled=True),
        lax.psum_scatter(grad_b_qkv, ("grp", "blk"), scatter_dimension=1, tiled=True),
        lax.psum_scatter(grad_rel, ("grp", "blk"), scatter_dimension=2, tiled=True),
        lax.psum_scatter(grad_w_out, ("grp", "blk"), scatter_dimension=0, tiled=True),
        lax.psum_scatter(
            jnp.stack([grad_bias_one, grad_bias_two]),
            ("grp", "blk"),
            scatter_dimension=1,
            tiled=True,
        ),
        lax.psum_scatter(
            jnp.stack([gain_grad1, gain_grad2]), ("grp", "blk"), scatter_dimension=1, tiled=True
        ),
        lax.psum_scatter(
            jnp.stack([shift_grad1, shift_grad2]), ("grp", "blk"), scatter_dimension=1, tiled=True
        ),
        lax.psum_scatter(grad_w_in, ("grp", "blk"), scatter_dimension=0, tiled=True),
        lax.psum_scatter(grad_b_in, ("grp", "blk"), scatter_dimension=0, tiled=True),
        lax.psum_scatter(grad_w_down, ("grp", "blk"), scatter_dimension=0, tiled=True),
    )
    return (
        hidden_out,
        grad_input.astype(jnp.bfloat16),
        summed[0],
        summed[1],
        summed[2],
        summed[3],
        summed[4],
        summed[5],
        summed[6],
        summed[7],
        summed[8],
        summed[9],
    )


MESH = pl.DeviceIdType.MESH
LOW = jnp.bfloat16
HIGH = jnp.float32
CHIPS = 16
HALF = 8
BLOCK = 256
MASKED = -1e30
VMEM_LIMIT = 62 * 2**20
NT = ((1,), (1,))
TN = ((0,), (0,))


def dot(left, right, dims=((1,), (0,))):
    return lax.dot_general(left, right, (dims, ((), ())), preferred_element_type=HIGH)


def place():
    return lax.axis_index("grp"), lax.axis_index("blk")


def coordinates(chip):
    return lax.div(chip, 4), lax.rem(lax.div(chip, 2), 2), lax.rem(chip, 2)


def greet_all():
    core, chip = place()
    me = core * CHIPS + chip
    barrier = pltpu.get_barrier_semaphore()

    def greet(ahead, carry):
        other = lax.rem(me + ahead, 2 * CHIPS)
        pl.semaphore_signal(
            barrier,
            inc=1,
            device_id=(lax.div(other, CHIPS), lax.rem(other, CHIPS)),
            device_id_type=MESH,
        )
        return carry

    lax.fori_loop(1, 2 * CHIPS, greet, 0)


def await_all():
    pl.semaphore_wait(pltpu.get_barrier_semaphore(), 2 * CHIPS - 1)


def remote(source, target, send, recv, device):
    return pltpu.make_async_remote_copy(
        src_ref=source,
        dst_ref=target,
        send_sem=send,
        recv_sem=recv,
        device_id=device,
        device_id_type=MESH,
    )


def local(source, target, sem):
    return pltpu.make_async_copy(source, target, sem)


MIRROR = 3


def in_the_middle():
    z, _, _ = coordinates(lax.axis_index("blk"))
    return jnp.logical_and(z > 0, z < 3)


def neighbours(across):
    core, chip = place()
    z, y, x = coordinates(chip)
    planes = (z + 1 - 2 * lax.rem(z, 2), 2 - lax.div(z, 2), 3 - 3 * lax.div(z, 2), 3 - z)

    def slot(far_p, far_q, line):
        far_y, far_x = (far_q, far_p) if across == "x" else (far_p, far_q)
        plane = z if line is None else planes[line]
        return plane * 4 + (1 - y if far_y else y) * 2 + (1 - x if far_x else x)

    return slot


class Shipments:
    def __init__(self, send, recv):
        self.send, self.recv, self.made = send, recv, []
        self.core = lax.axis_index("grp")

    def ship(self, source, target, recv_index, to, when=None):
        index = len(self.made)

        def make():
            return remote(
                source(), target(), self.send.at[index], self.recv.at[recv_index()], (self.core, to())
            )

        self.made.append((make, when))
        self.on(when, lambda: make().start())

    @staticmethod
    def on(when, act):
        if when is None:
            act()
        else:
            pl.when(when)(act)

    def landed(self, target, recv_index, near):
        remote(target, target, self.send.at[0], self.recv.at[recv_index], (self.core, near)).wait_recv()

    def all_sent(self, count):
        assert len(self.made) == count
        for make, when in self.made:
            self.on(when, lambda make=make: make().wait_send())


class Gather:
    def __init__(self, pick, send, recv, across):
        self.pick, self.at = pick, neighbours(across)
        self.moves = Shipments(send, recv)
        self.middle = in_the_middle()

    def ship(self, what, to, when=None):
        slot = lambda: self.at(*what)
        ref = lambda: self.pick(slot())
        self.moves.ship(ref, ref, slot, lambda: self.at(*to), when)

    def landed(self, *what):
        slot = self.at(*what)
        self.moves.landed(self.pick(slot), slot, self.at(1, 0, None))

    def pass_on(self, what, line):
        self.ship(what, (0, 0, MIRROR if line == 0 else 0), self.middle)

    def own_line(self, number):
        if number == 0:
            self.ship((0, 0, None), (0, 0, 0))
        else:
            self.ship((0, 0, None), (0, 0, MIRROR), self.middle)

    def own_plane(self):
        self.ship((0, 0, None), (1, 0, None))
        self.ship((0, 0, None), (0, 1, None))

    def line(self, line):
        self.landed(0, 0, line)
        self.pass_on((0, 0, line), line)
        self.ship((0, 0, line), (1, 0, None))
        self.ship((0, 0, line), (0, 1, None))

    def side(self, line):
        self.landed(1, 0, line)
        self.ship((1, 0, line), (0, 1, None))

    def arrive(self):
        for line in (None, 0, 1, 2):
            for far_p in (0, 1):
                self.landed(far_p, 1, line)

    def finish(self):
        self.moves.all_sent(17)


class GatherLate(Gather):
    PLANE = ((0, 0), (1, 0), (0, 1), (1, 1))

    def first(self):
        self.own_plane()

    def second(self):
        self.landed(1, 0, None)
        self.ship((1, 0, None), (0, 1, None))

    def third(self):
        for far_p in (0, 1):
            self.landed(far_p, 1, None)
        for what in self.PLANE:
            self.ship(what + (None,), (0, 0, 0))
        for what in self.PLANE:
            self.ship(what + (None,), (0, 0, MIRROR), self.middle)

    def late_line(self, line):
        for what in self.PLANE:
            self.landed(*what, line)
            self.pass_on(what + (line,), line)

    def finish(self):
        self.moves.all_sent(23)


class Reduce:
    def __init__(self, sent, own, pick, stages, send, recv, across):
        self.sent, self.own, self.pick, self.at = sent, own, pick, neighbours(across)
        self.first, self.second, self.third_in = stages
        self.moves = Shipments(send, recv)

    @staticmethod
    def number(line):
        return 3 if line is None else line

    def ship(self, source, target, index, to):
        self.moves.ship(source, target, lambda: index, lambda: self.at(*to))

    def landed(self, target, index):
        self.moves.landed(target, index, self.at(1, 0, None))

    def start(self, line):
        for far_p in (1, 0):
            index = self.number(line) * 2 + far_p
            self.ship(
                lambda far_p=far_p: self.pick(self.sent, self.at(far_p, 1, line)),
                lambda index=index: self.first.at[index],
                index,
                (0, 1, None),
            )

    def mine(self, *what):
        return self.pick(self.own, self.at(*what))[...].astype(HIGH)

    def side(self, line):
        number = self.number(line)
        index = number * 2 + 1
        self.landed(self.first.at[index], index)
        self.first[index] = (self.first[index].astype(HIGH) + self.mine(1, 0, line)).astype(LOW)
        self.ship(
            lambda: self.first.at[index], lambda: self.second.at[number], 8 + number, (1, 0, None)
        )

    def line(self, line):
        number = self.number(line)
        index = number * 2
        self.landed(self.first.at[index], index)
        self.landed(self.second.at[number], 8 + number)
        total = (
            self.first[index].astype(HIGH)
            + self.second[number].astype(HIGH)
            + self.mine(0, 0, line)
        )
        if line is None:
            return total
        self.first[index] = total.astype(LOW)
        ahead = lambda: lax.rem(lax.div(self.at(0, 0, None), 4) - lax.div(self.at(0, 0, line), 4) + 4, 4) - 1
        self.moves.ship(
            lambda: self.first.at[index],
            lambda: self.third_in.at[ahead()],
            lambda: 12 + ahead(),
            lambda: self.at(0, 0, line),
        )

    def finish(self, result):
        result[...] = self.line(None)
        for ahead in range(3):
            self.landed(self.third_in.at[ahead], 12 + ahead)
            result[...] += self.third_in[ahead].astype(HIGH)
        self.moves.all_sent(15)


class ReduceEarly(Reduce):
    PLANE = ((0, 0), (1, 0), (0, 1), (1, 1))

    def ahead(self, line):
        return lax.rem(lax.div(self.at(0, 0, None), 4) - lax.div(self.at(0, 0, line), 4) + 4, 4) - 1

    def start(self):
        for line in (2, 1, 0):
            for number, what in enumerate(self.PLANE):
                index = lambda number=number, line=line: self.ahead(line) * 4 + number
                self.moves.ship(
                    lambda what=what, line=line: self.pick(self.sent, self.at(*what, line)),
                    lambda index=index: self.first.at[index()],
                    index,
                    lambda line=line: self.at(0, 0, line),
                )

    def plane_sum(self, number):
        total = self.mine(*self.PLANE[number], None)
        for ahead in range(3):
            index = ahead * 4 + number
            self.landed(self.first.at[index], index)
            total += self.first[index].astype(HIGH)
        return total

    def third(self):
        for number, far_p in ((3, 1), (2, 0)):
            self.first[number] = self.plane_sum(number).astype(LOW)
            self.ship(
                lambda number=number: self.first.at[number],
                lambda far_p=far_p: self.second.at[far_p],
                12 + far_p,
                (0, 1, None),
            )

    def across(self):
        total = self.plane_sum(1)
        self.landed(self.second.at[1], 13)
        self.first[1] = (total + self.second[1].astype(HIGH)).astype(LOW)
        self.ship(lambda: self.first.at[1], lambda: self.third_in.at[0], 14, (1, 0, None))

    def finish(self, result):
        total = self.plane_sum(0)
        self.landed(self.second.at[0], 12)
        self.landed(self.third_in.at[0], 14)
        result[...] = total + self.second[0].astype(HIGH) + self.third_in[0].astype(HIGH)
        self.moves.all_sent(15)


def cube_of(order):
    core, chip = place()
    z, y, x = coordinates(chip)

    def at(*flips):
        far = dict(zip(order, flips))
        plane = z + 1 - 2 * lax.rem(z, 2) if far["z"] else z
        return plane * 4 + (1 - y if far["y"] else y) * 2 + (1 - x if far["x"] else x)

    return at


class CubeGather:
    def __init__(self, pick, send, recv, order):
        self.pick, self.at = pick, cube_of(order)
        self.moves = Shipments(send, recv)

    def ship(self, what, to):
        slot = lambda: lax.rem(self.at(*what), HALF)
        ref = lambda: self.pick(slot())
        self.moves.ship(ref, ref, slot, lambda: self.at(*to))

    def landed(self, *what):
        slot = lax.rem(self.at(*what), HALF)
        self.moves.landed(self.pick(slot), slot, self.at(1, 0, 0))

    def own(self):
        for to in ((1, 0, 0), (0, 1, 0), (0, 0, 1)):
            self.ship((0, 0, 0), to)

    def one(self):
        self.landed(1, 0, 0)
        self.ship((1, 0, 0), (0, 1, 0))
        self.ship((1, 0, 0), (0, 0, 1))

    def two(self):
        for what in ((0, 1, 0), (1, 1, 0)):
            self.landed(*what)
            self.ship(what, (0, 0, 1))

    def arrive(self):
        for what in ((0, 0, 1), (1, 0, 1), (0, 1, 1), (1, 1, 1)):
            self.landed(*what)

    def finish(self):
        self.moves.all_sent(7)


class CubeReduce:
    def __init__(self, pick, stage, send, recv, order):
        self.pick, self.stage, self.at = pick, stage, cube_of(order)
        self.moves = Shipments(send, recv)

    def ship(self, source, index, to):
        self.moves.ship(source, lambda: self.stage.at[index], lambda: index, lambda: self.at(*to))

    def mine(self, *what):
        return self.pick(lax.rem(self.at(*what), HALF))

    def term(self, index):
        self.moves.landed(self.stage.at[index], index, self.at(1, 0, 0))
        return self.stage[index].astype(HIGH)

    def own(self):
        for index, (one, two) in enumerate(((1, 1), (0, 1), (1, 0), (0, 0))):
            self.ship(lambda one=one, two=two: self.mine(one, two, 1), index, (0, 0, 1))

    def one(self):
        for index, one in ((0, 1), (1, 0)):
            total = self.mine(one, 1, 0)[...].astype(HIGH) + self.term(index)
            self.stage[index] = total.astype(LOW)
            self.ship(lambda index=index: self.stage.at[index], 4 + index, (0, 1, 0))

    def two(self):
        total = self.mine(1, 0, 0)[...].astype(HIGH) + self.term(2) + self.term(4)
        self.stage[2] = total.astype(LOW)
        self.ship(lambda: self.stage.at[2], 6, (1, 0, 0))

    def arrive(self):
        return self.mine(0, 0, 0)[...].astype(HIGH) + self.term(3) + self.term(5) + self.term(6)

    def finish(self):
        self.moves.all_sent(7)


def each(plans, act, *arguments):
    for plan in plans:
        act(plan, *arguments)


def unit():
    core, chip = place()
    return lax.div(chip, HALF), lax.rem(chip, HALF), core


def to_tokens(source, target, send, recv):
    core, chip = place()
    group, position, _ = unit()
    to_core = lax.div(position, 4)
    mine = group * HALF + 2 * lax.rem(position, 4) + core
    here = to_core == core

    def copy_to(ahead):
        chip_to = lax.rem(chip + ahead, CHIPS)
        return remote(
            source.at[chip_to], target.at[mine], send.at[ahead], recv.at[mine], (to_core, chip_to)
        )

    pl.when(here)(lambda: local(source.at[chip], target.at[mine], recv.at[mine]).start())
    pl.when(jnp.logical_not(here))(lambda: copy_to(0).start())
    for ahead in range(1, CHIPS):
        copy_to(ahead).start()

    def arrive():
        for slot in range(CHIPS):
            local(source.at[slot], target.at[slot], recv.at[slot]).wait()

    def finish():
        pl.when(jnp.logical_not(here))(lambda: copy_to(0).wait_send())
        for ahead in range(1, CHIPS):
            copy_to(ahead).wait_send()

    return arrive, finish


def to_heads(source, target, send, recv):
    core, chip = place()
    group, position, _ = unit()
    here = lax.div(position, 4) == core
    start = 2 * lax.rem(position, 4) + core

    def copy_to(turn_group, ahead):
        to_group = lax.rem(group + turn_group, 2)
        head = lax.rem(start + ahead, HALF)
        return remote(
            source.at[to_group * HALF + head],
            target.at[chip],
            send.at[turn_group * HALF + ahead],
            recv.at[chip],
            (lax.rem(head, 2), to_group * HALF + core * 4 + lax.div(head, 2)),
        )

    def every(act):
        pl.when(jnp.logical_not(here))(lambda: act(copy_to(0, 0)))
        for turn_group in range(2):
            for ahead in range(0 if turn_group else 1, HALF):
                act(copy_to(turn_group, ahead))

    pl.when(here)(
        lambda: local(source.at[group * HALF + start], target.at[chip], recv.at[chip]).start()
    )
    every(lambda copy: copy.start())

    def arrive():
        for slot in range(CHIPS):
            local(source.at[slot], target.at[slot], recv.at[slot]).wait()

    return arrive, lambda: every(lambda copy: copy.wait_send())


def lanes(rows, width=128):
    return lax.broadcasted_iota(jnp.int32, (rows, width), 1)


def turn(values):
    return pltpu.roll(values, HD, 1)


def fold(rows_in):
    half = rows_in.shape[0] // 2
    both = jnp.where(lanes(half) < HD, rows_in[:half], turn(rows_in[half:]))
    pad = -half % 16
    if pad:
        both = jnp.concatenate([both, jnp.zeros((pad, 128), HIGH)], axis=0)
    return both.astype(LOW)


def column_sums(v):
    return jnp.sum(v, axis=0, keepdims=True)


def gelu_parts(pre):
    cdf = 0.5 * (1.0 + lax.erf(pre * math.sqrt(0.5)))
    density = jnp.exp(-0.5 * pre * pre) * (1.0 / math.sqrt(2.0 * math.pi))
    return pre * cdf, cdf + pre * density


def normalize(v, gain, shift):
    center = v - jnp.mean(v, axis=1, keepdims=True)
    inverse = lax.rsqrt(jnp.mean(center * center, axis=1, keepdims=True) + EPSILON)
    normed = center * inverse
    return normed * gain + shift, normed, inverse


def normalize_back(c, normed, inverse, gain):
    scaled = c * gain
    inner = (
        scaled
        - jnp.mean(scaled, axis=1, keepdims=True)
        - normed * jnp.mean(scaled * normed, axis=1, keepdims=True)
    )
    return inner * inverse


def at_steps(index, steps):
    for number, acts in steps.items():

        def run(acts=acts):
            for act in acts:
                act()

        pl.when(index == number)(run)


def columns_of(half, width):
    return pl.ds(pl.multiple_of(half * width, 128), width)


GAIN_AT, SHIFT_AT, BIAS_AT = 128, 256, 384


def layer_kernel(names, *refs):
    r = types.SimpleNamespace(**dict(zip(names, refs)))
    hidden, x_all, w_all, rel_all = r.hidden_in, r.x_all, r.w_all, r.rel_all
    token_rows, width = hidden.shape
    slot_rows = x_all.shape[1]
    total = CHIPS * slot_rows
    depth = r.out_weight.shape[0]
    w_in, w_down, w_out = r.w_in, r.w_down, r.w_out
    half_hidden = w_in.shape[3]
    half_width = width // 2
    core, chip = place()
    group, position, _ = unit()
    other = 1 - core
    me = core * CHIPS + chip
    keep = r.keep_sem

    greet_all()

    loads = [
        local(r.ffn_in.at[:, columns_of(core, half_hidden)], w_in.at[core, chip], keep.at[0]),
        local(r.ffn_out, w_down.at[chip], keep.at[1]),
        local(r.out_weight, w_out.at[chip, pl.ds(0, depth)], keep.at[2]),
    ]
    for copy in loads:
        copy.start()

    extra = r.extra
    extra[...] = jnp.zeros_like(extra)
    extra[0:1, 0:256] = jnp.full((1, 256), 4.0, HIGH)
    extra[0:1, 0:token_rows] = r.segment_ids[...].astype(HIGH)
    extra[1:2, 0:token_rows] = r.order_ids[...].astype(HIGH)
    extra[2:4, 0:token_rows] = r.box_ids[...].astype(HIGH)
    tail = token_rows - token_rows % 16
    x_own = r.x_own
    x_own[0:tail, :] = hidden[0:tail, :]
    x_own[tail:slot_rows, :] = jnp.concatenate(
        [hidden[tail:token_rows, :].astype(HIGH), extra[...]], axis=0
    ).astype(LOW)
    weight = r.qkv_weight
    rel_own = r.rel_own
    for kind in range(3):
        rel_own[:, kind * NB : (kind + 1) * NB] = r.rel_tables[kind]
    eye_depth = (
        lax.broadcasted_iota(jnp.int32, (depth, depth), 0)
        == lax.broadcasted_iota(jnp.int32, (depth, depth), 1)
    ).astype(LOW)
    bias_columns = dot(eye_depth, r.qkv_bias[...], NT)
    rel_own[:, 3 * NB : 4 * NB] = jnp.where(
        lanes(depth) == 0, bias_columns[:, 0:1], jnp.where(lanes(depth) == 1, bias_columns[:, 1:2], 0.0)
    ).astype(LOW)
    small_own = r.small_own
    small_own[...] = jnp.zeros_like(small_own)
    small_own[0:2, 0:depth] = r.branch_bias[...]
    small_own[0:2, GAIN_AT : GAIN_AT + depth] = r.norm_gains[...]
    small_own[0:2, SHIFT_AT : SHIFT_AT + depth] = r.norm_shifts[...]
    small_own[0:1, BIAS_AT : BIAS_AT + 128] = r.ffn_in_bias[...]
    loads += [
        local(small_own, w_out.at[chip, pl.ds(depth, 16)], keep.at[3]),
        local(weight.at[:, :, columns_of(position, 128)], w_all.at[:, core, chip], keep.at[4]),
    ]
    for copy in loads[3:]:
        copy.start()
    await_all()

    at_home = group == core
    away = lax.rem(chip + HALF, CHIPS)
    x_slot = x_all.at[position]
    home = lambda: local(x_own, x_slot, r.home_sem.at[1])
    abroad = lambda: remote(x_own, x_slot, r.home_sem.at[0], r.home_sem.at[1], (other, away))
    pl.when(at_home)(lambda: home().start())
    pl.when(jnp.logical_not(at_home))(lambda: abroad().start())

    rel_head = core * HALF + lax.div(chip, 2)
    parity = lax.rem(chip, 2)
    rel_slot = rel_all.at[pl.ds(parity * depth, depth)]

    def rel_each(act_remote, act_own):
        for to_group in range(2):
            to = (lax.rem(rel_head, 2), to_group * HALF + lax.div(rel_head, 2))
            itself = jnp.logical_and(to[0] == core, to[1] == chip)
            copy = lambda: remote(
                rel_own, rel_slot, r.rel_send.at[to_group], r.rel_recv.at[parity], to
            )
            pl.when(jnp.logical_not(itself))(lambda: act_remote(copy()))
            if act_own is not None:
                pl.when(itself)(act_own)

    rel_each(
        lambda copy: copy.start(), lambda: local(rel_own, rel_slot, r.rel_recv.at[parity]).start()
    )

    def w_copy(ahead):
        to = lax.rem(chip + ahead, CHIPS)
        return remote(
            weight.at[:, :, columns_of(lax.rem(to, HALF), 128)],
            w_all.at[:, core, chip],
            r.w_send.at[ahead],
            r.w_recv.at[chip],
            (core, to),
        )

    swap_in = remote(
        r.ffn_in.at[:, columns_of(other, half_hidden)],
        w_in.at[core, chip],
        r.pair_send.at[0],
        r.pair_recv.at[0],
        (other, chip),
    )
    swap_in.start()

    third = slot_rows // 3
    x_plans = [
        CubeGather(
            lambda slot, part=part: x_all.at[slot, pl.ds(part * third, third)],
            r.x_send.at[part],
            r.x_recv.at[part],
            order,
        )
        for part, order in enumerate(("xyz", "yzx", "zxy"))
    ]
    half = width // 2
    half_tile = half_hidden // 2
    plan_out = GatherLate(lambda slot: w_out.at[slot], r.out_send, r.out_recv, "x")

    def halves(ref, wide, sends, recvs):
        return [
            Gather(
                lambda slot, part=part: ref(slot, pl.ds(part * wide, wide)), sends.at[part], recvs.at[part], across
            )
            for part, across in enumerate("xy")
        ]

    plans_in = halves(lambda slot, columns: w_in.at[:, slot, :, columns], half_tile, r.in_send, r.in_recv)
    plans_down = halves(lambda slot, columns: w_down.at[slot, :, columns], half, r.down_send, r.down_recv)

    for ahead in range(1, CHIPS):
        w_copy(ahead).start()
    for copy in loads:
        copy.wait()
    each(plans_down, Gather.own_plane)
    swap_in.wait()
    each(plans_in, Gather.own_plane)
    plan_out.first()
    each(plans_in, Gather.own_line, 0)
    home().wait()
    each(x_plans, CubeGather.own)
    each(x_plans, CubeGather.one)
    each(plans_down, Gather.own_line, 1)
    plan_out.second()
    each(x_plans, CubeGather.two)
    each(plans_down, Gather.own_line, 0)
    plan_out.third()
    each(plans_in, Gather.line, 0)
    for ahead in range(1, CHIPS):
        came = lax.rem(chip + ahead, CHIPS)
        remote(
            weight.at[:, :, pl.ds(0, 128)], w_all.at[:, core, came], r.w_send.at[0], r.w_recv.at[came], (core, came)
        ).wait_recv()
    pair_w = remote(w_all.at[:, core], w_all.at[:, core], r.pair_send.at[1], r.pair_recv.at[1], (other, chip))
    pair_w.start()
    for slot in range(2):
        local(rel_own, rel_all.at[pl.ds(slot * depth, depth)], r.rel_recv.at[slot]).wait()
    pair_bias = remote(
        rel_all.at[:, pl.ds(3 * NB, NB)], r.bias_far, r.pair_send.at[2], r.pair_recv.at[2], (other, chip)
    )
    pair_bias.start()
    each(x_plans, CubeGather.arrive)
    pl.when(jnp.logical_not(at_home))(lambda: abroad().wait_send())

    labels = r.labels
    first_slot = core * HALF
    label_part = x_all.at[:, pl.ds(slot_rows - 16, 16), pl.ds(0, 256)]
    label_slots = labels.at[pl.ds(first_slot, HALF)]
    pair_label = remote(label_part, label_slots, r.pair_send.at[3], r.pair_recv.at[3], (other, chip))
    pair_label.start()
    own_label = local(label_part, label_slots, keep.at[5])
    own_label.start()
    pair_w.wait()
    pair_bias.wait()

    head_rows = 2 * depth
    row_at = lax.broadcasted_iota(jnp.int32, (head_rows, 128), 0)
    column_at = lanes(head_rows)

    def bias_row(columns, number):
        column = columns[:, number : number + 1]
        return column_sums(jnp.where(row_at == column_at, column, 0.0))

    rel = rel_all[...]
    bias_near = rel[:, 3 * NB : 4 * NB].astype(HIGH)
    bias_far = r.bias_far[...].astype(HIGH)
    bias_query, bias_value = (
        bias_row(bias_near, number) + turn(bias_row(bias_far, number)) for number in range(2)
    )
    weights = [w_all[n].reshape(width, 128) for n in range(3)]
    near, far_part = r.near, r.far_part
    pair_rows = 2 * slot_rows
    pair_half = lanes(pair_rows) < HD

    for pair in range(HALF // 2):
        tokens = x_all[2 * pair : 2 * pair + 2].reshape(pair_rows, width)
        query, key, value_rows = (
            pltpu.roll(dot(tokens, weights[n]), core * HD, 1) for n in range(3)
        )
        query, value_rows = query + bias_query, value_rows + bias_value
        rows = pl.ds(pl.multiple_of(core * HALF * slot_rows, 16) + pair * pair_rows, pair_rows)
        near[rows, 0:128] = jnp.where(pair_half, query, turn(value_rows)).astype(LOW)
        near[rows, 128:256] = key.astype(LOW)
        far_rows = slice(pair * pair_rows, (pair + 1) * pair_rows)
        far_part[far_rows, 0:128] = jnp.where(pair_half, turn(query), value_rows).astype(LOW)
        far_part[far_rows, 128:256] = turn(key).astype(LOW)
    pair_qkv = remote(
        far_part,
        near.at[pl.ds(pl.multiple_of(core * HALF * slot_rows, 16), HALF * slot_rows)],
        r.pair_send.at[4],
        r.pair_recv.at[4],
        (other, chip),
    )
    pair_qkv.start()

    meta = r.meta
    eye = (
        lax.broadcasted_iota(jnp.int32, (slot_rows, 256), 0)
        == lax.broadcasted_iota(jnp.int32, (slot_rows, 256), 1)
    ).astype(LOW)
    pair_label.wait()
    own_label.wait()
    for slot in range(CHIPS):
        meta[slot * slot_rows : (slot + 1) * slot_rows, 0:16] = dot(eye, labels[slot], NT)
    table_t = rel[:, 0 : 3 * NB]
    lane = lanes(BLOCK)
    first_half = lane < HD
    scale = 1.0 / math.sqrt(4.0 * HD)
    left, right, right_t = r.left, r.right, r.right_t
    value, value_t, kept = r.value, r.value_t, r.kept
    pair_qkv.wait()
    each(plans_in, Gather.own_line, 1)
    each(plans_in, Gather.side, None)

    def prepare(index, carry):
        rows = pl.ds(pl.multiple_of(index * BLOCK, BLOCK), BLOCK)
        at_steps(
            index,
            {
                3: [lambda: each(plans_down, Gather.side, None), lambda: each(plans_down, Gather.line, 1)],
                4: [lambda: each(plans_in, Gather.side, 0), lambda: each(plans_down, Gather.line, 0)],
            },
        )
        query_value = near[rows, 0:128].astype(HIGH)
        key = near[rows, 128:256].astype(HIGH)
        tables = dot(near[rows, 0:128][:, 0:HD], table_t).astype(LOW).astype(HIGH)
        ids = meta[rows, 8:12].astype(jnp.int32)
        segment, order, box_x, box_y = ids[:, 0:1], ids[:, 1:2], ids[:, 2:3], ids[:, 3:4]

        def selected(column, ids_of, values):
            bucket = jnp.clip(ids_of - values, -(NB // 2), NB // 2 - 1) + NB // 2
            return jnp.take_along_axis(tables[:, column * NB : (column + 1) * NB], bucket, axis=1)

        wide = selected(0, order, lane)
        narrow = jnp.where(first_half, selected(1, box_x, lane), selected(2, box_y, lane - HD))
        label = lane - HD
        query_side = jnp.where(
            first_half,
            query_value * scale,
            jnp.where(jnp.logical_and(label != segment, label < 8), MASKED, 0.0),
        )
        key_side = jnp.where(first_half, key, (label == segment).astype(HIGH))
        left[rows, 0:128] = (wide * scale).astype(LOW)
        left[rows, 128:256] = (narrow * scale).astype(LOW)
        left[rows, 256:384] = query_side.astype(LOW)
        order_hot = (lane == order).astype(HIGH)
        box_hot = (jnp.where(first_half, box_x, box_y + HD) == lane).astype(HIGH)
        right[rows, 0:128] = order_hot.astype(LOW)
        right[rows, 128:256] = box_hot.astype(LOW)
        right[rows, 256:384] = key_side.astype(LOW)
        right_t[0:128, rows] = order_hot.T.astype(LOW)
        right_t[128:256, rows] = box_hot.T.astype(LOW)
        right_t[256:384, rows] = key_side.T.astype(LOW)
        held = jnp.where(first_half, turn(query_value), (label == 0).astype(HIGH))
        value[rows, :] = held.astype(LOW)
        value_t[:, rows] = held.T.astype(LOW)
        return carry

    lax.fori_loop(0, total // BLOCK, prepare, 0)
    def attend(index, carry):
        rows = pl.ds(pl.multiple_of(index * BLOCK, BLOCK), BLOCK)
        at_steps(
            index,
            {
                1: [lambda: each(plans_in, Gather.line, 2)],
                5: [lambda: each(plans_in, Gather.line, 1)],
                6: [lambda: plan_out.late_line(0)],
            },
        )
        logits = dot(left[rows, :], right_t[...])
        top = jnp.max(logits, axis=1, keepdims=True)
        weights = jnp.exp(logits - top).astype(LOW)
        mixed = dot(weights, value[...])
        row_sum = mixed[:, HD : HD + 1]
        ids = meta[rows, 8:12]
        facts = jnp.where(lane == HD, top + jnp.log(row_sum), ids[:, 3:4])
        facts = jnp.where(lane == HD + 1, ids[:, 1:2], facts)
        facts = jnp.where(lane == HD + 2, ids[:, 2:3], facts)
        kept[rows, :] = jnp.where(first_half, mixed / row_sum, facts)
        return carry

    lax.fori_loop(0, total // BLOCK, attend, 0)
    message, context_in = r.message, r.context_in
    for slot in range(CHIPS):
        message[slot] = fold(kept[slot * slot_rows : (slot + 1) * slot_rows, :])
    context_arrives, context_sent = to_tokens(message, context_in, r.msg_send, r.msg_recv)
    each(plans_down, Gather.side, 1)
    each(plans_down, Gather.line, 2)
    plan_out.late_line(1)
    each(plans_down, Gather.side, 0)
    each(plans_in, Gather.side, 1)
    plan_out.late_line(2)

    shares, bias_in = r.shares, r.bias_in
    shares[core] = jnp.zeros(shares.shape[1:], HIGH)
    for slot in range(CHIPS):
        small = w_out[slot, depth : depth + 16, 0 : BIAS_AT + 128].astype(HIGH)[0:8]
        target = slice(slot * depth // 128 * 128, slot * depth // 128 * 128 + 128)
        for number in range(3):
            piece = jnp.where(lanes(8) < depth, small[:, number * 128 : number * 128 + 128], 0.0)
            if slot * depth % 128:
                piece = pltpu.roll(piece, slot * depth % 128, 1)
            shares[core, number, :, target] += piece
        bias_in[:, slot * 128 : slot * 128 + 128] = small[0:1, BIAS_AT : BIAS_AT + 128]
    pair_small = remote(
        shares.at[core], shares.at[core], r.pair_send.at[5], r.pair_recv.at[5], (other, chip)
    )
    pair_small.start()
    each(plans_in, Gather.side, 2)
    context_arrives()
    each(plans_down, Gather.side, 2)

    context_wide, context, low_first = r.context_wide, r.context, r.low_first
    act, slope = r.act, r.slope
    out_part, in_part = r.out_part, r.in_part
    own = pl.ds(pl.multiple_of(core * slot_rows, 16), slot_rows)
    far = pl.ds(pl.multiple_of(other * slot_rows, 16), slot_rows)
    tile = 512
    half_slot = slot_rows // 2
    count = [6]

    def swap(source, target):
        copy = remote(
            source, target, r.pair_send.at[count[0]], r.pair_recv.at[count[0]], (other, chip)
        )
        count[0] += 1
        copy.start()
        return copy

    left_half = lanes(half_slot) < HD
    for slot_group in range(2):
        for pair in range(HALF // 2):
            even = context_in[slot_group * HALF + 2 * pair].astype(HIGH)[:half_slot]
            odd = context_in[slot_group * HALF + 2 * pair + 1].astype(HIGH)[:half_slot]
            top = slot_group * slot_rows
            columns = slice(pair * 128, pair * 128 + 128)
            context_wide[top : top + half_slot, columns] = jnp.where(left_half, even, turn(odd))
            context_wide[top + half_slot : top + slot_rows, columns] = jnp.where(
                left_half, turn(even), odd
            )
    context[...] = context_wide[...].astype(LOW)

    def product(lhs, rhs):
        out_part[...] = dot(lhs[far, :], rhs)
        copy = swap(out_part, in_part)
        mine = dot(lhs[own, :], rhs)
        copy.wait()
        return mine + in_part[...]

    pair_small.wait()
    branch_bias, gains, shifts = (
        [jnp.concatenate([shares[0, number, k : k + 1], shares[1, number, k : k + 1]], axis=1) for k in range(2)]
        for number in range(3)
    )
    branch = product(context, w_out[:, 0:depth, :].reshape(half_width, width)) + branch_bias[0]
    row_index = lax.broadcasted_iota(jnp.int32, (slot_rows, 1), 0)
    x_mine = jnp.where(row_index < token_rows, x_own[...].astype(HIGH), 0.0)
    first, normed1, inverse1 = normalize(x_mine + branch, gains[0], shifts[0])
    low_first[own, :] = first.astype(LOW)
    copy = swap(low_first.at[own], low_first.at[own])
    each(plans_in, Gather.arrive)
    copy.wait()

    def widen(index, carry):
        columns = pl.ds(pl.multiple_of(index * tile, tile), tile)
        pre = dot(low_first[...], w_in[:, :, :, columns].reshape(width, tile)) + bias_in[:, columns]
        found, derivative = gelu_parts(pre)
        act[:, columns] = found.astype(LOW)
        slope[:, columns] = derivative
        return carry

    lax.fori_loop(0, half_hidden // tile, widen, 0)
    each(plans_down, Gather.arrive)
    second = product(act, w_down[...].reshape(half_hidden, width)) + branch_bias[1]
    result, normed2, inverse2 = normalize(first + second, gains[1], shifts[1])
    r.hidden_out[...] = result[:token_rows].astype(LOW)
    upstream = jnp.concatenate(
        [r.out_grad[...].astype(HIGH), jnp.zeros((slot_rows - token_rows, width), HIGH)], axis=0
    )
    d_sum2 = normalize_back(upstream, normed2, inverse2, gains[1])
    low_second = d_sum2.astype(LOW)
    d_second, small_sum = r.d_second, r.small_sum
    d_second[own, :] = low_second
    copy = swap(d_second.at[own], d_second.at[own])
    small_sum[...] = jnp.zeros_like(small_sum)
    small_sum[1:2, :] = column_sums(low_second.astype(HIGH))
    small_sum[3:4, :] = column_sums(upstream * normed2)
    small_sum[5:6, :] = column_sums(upstream)

    half_total = HALF * slot_rows
    sum_down = Reduce(
        w_down,
        w_down,
        lambda ref, slot: ref.at[slot],
        [r.down_1, r.down_2, r.down_3],
        r.g_down_send,
        r.g_down_recv,
        "y",
    )
    sum_in = Reduce(
        w_in,
        w_in,
        lambda ref, slot: ref.at[:, slot],
        [r.in_1, r.in_2, r.in_3],
        r.g_in_send,
        r.g_in_recv,
        "x",
    )
    sum_out = ReduceEarly(
        r.g_out,
        r.g_out,
        lambda ref, slot: ref.at[slot],
        [r.out_1, r.out_2, r.out_3],
        r.g_out_send,
        r.g_out_recv,
        "y",
    )

    d_inner = act
    each(plans_in + plans_down, Gather.finish)
    copy.wait()
    slots = tile // w_down.shape[1]

    def narrow_back(index, carry):
        columns = pl.ds(pl.multiple_of(index * tile, tile), tile)
        rows = pl.ds(index * slots, slots)
        low = (dot(d_second[...], w_down[rows].reshape(tile, width), NT) * slope[:, columns]).astype(LOW)
        turns = width // tile
        bias_sums = column_sums(low.astype(HIGH))
        bias_columns = pl.ds(pl.multiple_of(lax.rem(index, turns) * tile, tile), tile)
        for row in range(half_hidden // width):

            @pl.when(lax.div(index, turns) == row)
            def _():
                small_sum[6 + row : 7 + row, bias_columns] = bias_sums

        w_down[rows] = (
            dot(act[:, columns], d_second[...], TN).astype(LOW).reshape(slots, tile // slots, width)
        )
        d_inner[:, columns] = low
        return carry

    lax.fori_loop(0, half_hidden // tile, narrow_back, 0)
    sum_down.start(2)
    w_in_all = w_in[...].reshape(width, half_hidden)
    out_part[...] = dot(d_inner[far, :], w_in_all, NT)
    copy = swap(out_part, in_part)
    mine = dot(d_inner[own, :], w_in_all, NT)
    slots_in = 256 // depth

    def widen_grad(index, carry):
        rows = pl.ds(pl.multiple_of(index * 256, 256), 256)
        parts = CHIPS // slots_in
        w_in[lax.div(index, parts), pl.ds(lax.rem(index, parts) * slots_in, slots_in)] = (
            dot(low_first[:, rows], d_inner[...], TN).astype(LOW).reshape(slots_in, depth, half_hidden)
        )
        return carry

    lax.fori_loop(0, width // 256, widen_grad, 0)
    copy.wait()
    d_first = d_sum2 + mine + in_part[...]
    d_sum1 = normalize_back(d_first, normed1, inverse1, gains[0])
    low_branch = d_sum1.astype(LOW)
    d_branch = d_second
    d_branch[own, :] = low_branch
    copy = swap(d_branch.at[own], d_branch.at[own])
    out_part[...] = d_sum1
    small_sum[0:1, :] = column_sums(low_branch.astype(HIGH))
    small_sum[2:3, :] = column_sums(d_first * normed1)
    small_sum[4:5, :] = column_sums(d_first)
    copy.wait()
    context_wide[...] = dot(d_branch[...], w_out[:, 0:depth, :].reshape(half_width, width), NT)
    d_message, d_arrived = context_in, r.d_arrived
    for slot_group in range(2):
        for pair in range(HALF // 2):
            both = context_wide[
                slot_group * slot_rows : (slot_group + 1) * slot_rows, pair * 128 : pair * 128 + 128
            ]
            d_message[slot_group * HALF + 2 * pair] = fold(both)
            d_message[slot_group * HALF + 2 * pair + 1] = fold(turn(both))
    grad_arrives, grad_sent = to_heads(d_message, d_arrived, r.d_send, r.d_recv)
    r.g_out[...] = dot(context[...], d_branch[...], TN).astype(LOW).reshape(r.g_out.shape)

    z, y, x = coordinates(chip)
    small_in = r.small_in

    def small_copy(index, to_core, to_chip):
        return remote(
            small_sum, small_in.at[index], r.small_send.at[index], r.small_recv.at[index], (to_core, to_chip)
        )

    def small_turn(index):
        if index == 0:
            return [small_copy(0, other, chip)]
        if index == 1:
            return [small_copy(1, core, z * 4 + (1 - y) * 2 + x)]
        if index == 2:
            return [small_copy(2, core, z * 4 + y * 2 + 1 - x)]
        return [
            small_copy(2 + ahead, core, lax.rem(z + ahead, 4) * 4 + y * 2 + x) for ahead in (1, 2, 3)
        ]

    def small_start(index):
        for copy in small_turn(index):
            copy.start()

    def small_end(index):
        for copy in small_turn(index):
            copy.wait()
        if index == 0:
            small_sum[0:6, :] += small_in[0, 0:6, :]
        elif index < 3:
            small_sum[...] += small_in[index]

    small_start(0)
    sum_down.side(2)
    sum_down.start(1)
    small_end(0)
    sum_in.start(2)
    d_context = meta
    grad_arrives()
    sum_down.start(0)
    sum_out.start()
    small_start(1)
    sum_in.start(0)
    for slot in range(CHIPS):
        both = d_arrived[slot].astype(HIGH)[:half_slot]
        top = slot * slot_rows
        d_context[top : top + half_slot, :] = jnp.where(left_half, both, 0.0)
        d_context[top + half_slot : top + slot_rows, :] = jnp.where(left_half, turn(both), 0.0)
    d_heads, d_pair_t, rel_grad = r.d_heads, r.d_pair_t, r.rel_grad
    d_pair_t[...] = jnp.zeros_like(d_pair_t)
    rel_grad[...] = jnp.zeros_like(rel_grad)

    def step(index, carry):
        rows = pl.ds(pl.multiple_of(index * BLOCK, BLOCK), BLOCK)
        at_steps(
            index,
            {
                1: [lambda: sum_in.side(2), lambda: sum_in.start(1)],
                2: [lambda: sum_down.line(2), lambda: small_end(1), lambda: sum_down.side(0)],
                3: [lambda: sum_in.side(0)],
                5: [lambda: sum_in.line(2)],
                6: [lambda: sum_in.line(0), lambda: sum_in.side(1)],
                7: [lambda: sum_down.start(None)],
                8: [lambda: sum_in.start(None)],
            },
        )
        facts = kept[rows, :]
        grad = d_context[rows, :]
        delta = jnp.sum(grad * facts, axis=1, keepdims=True)
        probs = jnp.exp(dot(left[rows, :], right_t[...]) - facts[:, HD : HD + 1])
        d_probs = dot(grad.astype(LOW), value_t[...])
        d_logits = (probs * (d_probs - delta)).astype(LOW)
        query_t = jnp.where(first_half, left[rows, 256:384].astype(HIGH), 0.0).T[0:HD]
        d_pair_t[0:HD, :] += dot(query_t.astype(LOW), d_logits)
        d_pair_t[HD : 2 * HD, :] += dot(grad.T[0:HD].astype(LOW), probs.astype(LOW))
        back = dot(d_logits, right[...]) * scale
        ids = facts.astype(jnp.int32)
        order, box_x, box_y = (ids[:, HD + k : HD + k + 1] for k in (1, 2, 3))

        def placed(column, ids_of, extent, start):
            found_at = ids_of + NB // 2 - lane
            found = jnp.take_along_axis(
                back[:, column * 128 : column * 128 + 128], jnp.clip(found_at, 0, extent - 1) + start, axis=1
            )
            return jnp.where(jnp.logical_and(found_at >= 0, found_at < extent), found, 0.0)

        wide = back[:, 0:128]
        low_end = jnp.sum(jnp.where(lane >= order + NB // 2, wide, 0.0), axis=1, keepdims=True)
        high_end = jnp.sum(jnp.where(lane <= order - (NB // 2 - 1), wide, 0.0), axis=1, keepdims=True)
        first = placed(0, order, ORDER_RANGE, 0)
        first = jnp.where(lane == 0, low_end, jnp.where(lane == NB - 1, high_end, first))
        d_tables = jnp.concatenate(
            [first, placed(1, box_x, BOX_RANGE, 0), placed(1, box_y, BOX_RANGE, BOX_RANGE)], axis=1
        ).astype(LOW)
        from_tables = dot(d_tables, table_t, NT)
        d_query = back[:, 256:384] + jnp.concatenate([from_tables, from_tables], axis=1)
        d_heads[0, :, rows] = d_query.T[0:HD].astype(LOW)
        rel_grad[:, 0 : 3 * NB] += dot((query_t / scale).astype(LOW), d_tables)
        return carry

    lax.fori_loop(0, total // BLOCK, step, 0)
    small_start(2)
    sum_in.line(1)
    sum_down.line(0)

    d_heads[1] = d_pair_t[0:HD, :].astype(LOW)
    d_heads[2] = d_pair_t[HD : 2 * HD, :].astype(LOW)
    d_both = r.d_both
    near_part = pl.ds(pl.multiple_of(core * half_total, 128), half_total)
    far_part = pl.ds(pl.multiple_of(other * half_total, 128), half_total)
    copy = swap(d_heads.at[:, :, far_part], d_both.at[:, core])
    d_both[:, core] = d_heads[:, :, near_part]
    sums = [jnp.sum(d_heads[n].astype(HIGH), axis=1, keepdims=True) for n in (0, 2)]
    rel_grad[:, 3 * NB : 4 * NB] = jnp.where(
        lanes(HD) == 0, sums[0], jnp.where(lanes(HD) == 1, sums[1], 0.0)
    )
    head = 2 * position + core
    rel_came = r.rel_came

    def d_rel_each(act_remote, act_own):
        for side in range(2):
            to = (lax.div(position, 4), lax.rem(2 * head + side, CHIPS))
            itself = jnp.logical_and(to[0] == core, to[1] == chip)
            source = rel_grad.at[pl.ds(side * depth, depth)]
            act = lambda: act_remote(
                remote(source, rel_came.at[group], r.d_rel_send.at[side], r.d_rel_recv.at[group], to)
            )
            pl.when(jnp.logical_not(itself))(act)
            if act_own:
                pl.when(itself)(lambda: local(source, rel_came.at[group], r.d_rel_recv.at[group]).start())

    d_rel_each(lambda copy: copy.start(), True)
    copy.wait()
    d_columns = d_both[...].reshape(6 * HD, half_total)

    w_grad = dot(d_columns, x_all[...].reshape(half_total, width))

    w_heads = jnp.concatenate([w_all[n].reshape(width, 128) for n in range(3)], axis=1)
    d_rows = d_columns.T
    d_x = x_all
    each(x_plans, CubeGather.finish)
    for pair in range(HALF // 2):
        d_x[2 * pair : 2 * pair + 2] = (
            dot(d_rows[pair * pair_rows : (pair + 1) * pair_rows], w_heads, NT)
            .astype(LOW)
            .reshape(2, slot_rows, width)
        )
    d_x_plans = [
        CubeReduce(
            lambda slot, part=part: d_x.at[slot, pl.ds(part * third, third)],
            r.x_stage.at[part],
            r.d_x_send.at[part],
            r.d_x_recv.at[part],
            order,
        )
        for part, order in enumerate(("xyz", "yzx", "zxy"))
    ]
    sum_down.side(1)
    each(d_x_plans, CubeReduce.own)
    small_end(2)
    sum_down.line(1)
    sum_out.third()
    sum_out.across()

    w_mine, w_far, w_low, w_came = slope, r.w_far, r.w_low, r.w_came
    w_rows = 3 * HD
    for part in range(2):
        w_mine[0:w_rows, part * width : (part + 1) * width] = w_grad[part * w_rows : (part + 1) * w_rows]

    def w_columns(part, half):
        return pl.ds(pl.multiple_of(part * width + half * half_width, 128), half_width)

    w_swaps = [
        swap(w_mine.at[pl.ds(0, w_rows), w_columns(part, other)], w_far.at[part]) for part in range(2)
    ]
    sum_in.side(None)
    each(d_x_plans, CubeReduce.one)
    sum_down.side(None)
    for copy in w_swaps:
        copy.wait()
    w_sum = jnp.concatenate(
        [(w_mine[0:w_rows, w_columns(part, core)] + w_far[part]).T for part in range(2)], axis=1
    )
    for slot in range(CHIPS):
        w_low[slot] = w_sum[slot * depth : (slot + 1) * depth].astype(LOW)

    def d_w_copy(ahead):
        to = lax.rem(chip + ahead, CHIPS)
        return remote(w_low.at[to], w_came.at[chip], r.d_w_send.at[ahead], r.d_w_recv.at[chip], (core, to))

    own_d_w = local(w_low.at[chip], w_came.at[chip], keep.at[6])
    own_d_w.start()
    for ahead in range(1, CHIPS):
        d_w_copy(ahead).start()
    each(d_x_plans, CubeReduce.two)
    sum_down.finish(r.down_grad)
    small_start(3)
    sum_out.finish(r.out_w_grad)
    in_total, in_far = r.in_total, r.in_far
    sum_in.finish(in_total)
    in_pair = swap(in_total.at[other], in_far)
    x_total, x_came = x_own, r.x_came
    for part, plan in enumerate(d_x_plans):
        x_total[part * third : (part + 1) * third] = plan.arrive().astype(LOW)
    back = lambda: local(x_total, x_came, r.back_sem.at[1])
    back_abroad = lambda: remote(
        x_total, x_came, r.back_sem.at[0], r.back_sem.at[1], (other, lax.rem(chip + HALF, CHIPS))
    )
    pl.when(at_home)(lambda: back().start())
    pl.when(jnp.logical_not(at_home))(lambda: back_abroad().start())

    in_grad = r.in_grad
    in_grad[:, columns_of(core, half_hidden)] = in_total[core]
    small_end(3)
    me = core * CHIPS + chip
    small_all = lambda rows, columns: (
        small_sum[rows, columns] + small_in[3, rows, columns] + small_in[4, rows, columns] + small_in[5, rows, columns]
    )
    strip = columns_of(lax.div(me * depth, 128), 128)
    shares = pltpu.roll(small_all(pl.ds(0, 8), strip), 128 - lax.rem(me * depth, 128), 1)
    for number, result in enumerate((r.branch_grad, r.gain_grad, r.shift_grad)):
        result[...] = shares[2 * number : 2 * number + 2, 0:depth]
    bias_strip = small_all(pl.ds(0, 8), columns_of(position, 128))
    r.bias_grad[...] = jnp.where(group == 0, bias_strip[6:7], bias_strip[7:8])
    for slot in range(2):
        local(rel_grad.at[pl.ds(0, depth)], rel_came.at[slot], r.d_rel_recv.at[slot]).wait()
    d_rel_each(lambda copy: copy.wait_send(), False)
    rel_total = rel_came[0] + rel_came[1]
    for kind in range(3):
        r.rel_tables_grad[kind] = rel_total[:, kind * NB : (kind + 1) * NB]
    r.qkv_bias_grad[...] = rel_total[:, 3 * NB : 4 * NB].T[0:2]
    own_d_w.wait()
    for ahead in range(1, CHIPS):
        came = lax.rem(chip + ahead, CHIPS)
        remote(w_low.at[0], w_came.at[came], r.d_w_send.at[0], r.d_w_recv.at[came], (core, came)).wait_recv()
        d_w_copy(ahead).wait_send()
    for pair in range(HALF):
        both = w_came[pair].astype(HIGH) + w_came[HALF + pair].astype(HIGH)
        for n in range(3):
            r.qkv_grad[n, :, pair * 128 : pair * 128 + 128] = both[:, n * 128 : n * 128 + 128]
    back().wait()
    pl.when(jnp.logical_not(at_home))(lambda: back_abroad().wait_send())
    r.hidden_grad[...] = (out_part[...] + x_came[...].astype(HIGH))[:token_rows].astype(LOW)
    in_pair.wait()
    in_grad[:, columns_of(other, half_hidden)] = in_far[...]
    grad_sent()
    each(d_x_plans, CubeReduce.finish)
    for ahead in range(1, CHIPS):
        w_copy(ahead).wait_send()
    rel_each(lambda copy: copy.wait_send(), None)
    context_sent()
    plan_out.finish()


def hand_over(count, *refs):
    for source, target in zip(refs[:count], refs[count:]):
        target[...] = source[...]


def handed_over(arrays):
    return pl.pallas_call(
        functools.partial(hand_over, len(arrays)),
        out_shape=[jax.ShapeDtypeStruct(array.shape, array.dtype) for array in arrays],
        name="hand_over",
    )(*arrays)


def call(kernel, name, number, inputs, outputs, scratch):
    names = list(inputs) + list(outputs) + list(scratch)
    results = pl.pallas_call(
        functools.partial(kernel, names),
        out_shape=[jax.ShapeDtypeStruct(shape, dtype) for shape, dtype, _ in outputs.values()],
        in_specs=[pl.BlockSpec(memory_space=space) for _, space in inputs.values()],
        out_specs=[pl.BlockSpec(memory_space=space) for _, _, space in outputs.values()],
        scratch_shapes=list(scratch.values()),
        compiler_params=pltpu.CompilerParams(
            collective_id=number, has_side_effects=True, vmem_limit_bytes=VMEM_LIMIT
        ),
        name=name,
    )(*(array for array, _ in inputs.values()))
    return types.SimpleNamespace(**dict(zip(outputs, results)))


def head_shards(
    hidden_in,
    segment_ids,
    order_ids,
    box_ids,
    qkv_weight,
    qkv_bias,
    rel_tables,
    out_weight,
    branch_bias,
    norm_gains,
    norm_shifts,
    ffn_in,
    ffn_in_bias,
    ffn_out,
    out_grad,
):
    rows, width = hidden_in.shape
    slot_rows = -(-rows // 48) * 48
    total = CHIPS * slot_rows
    depth = qkv_weight.shape[1]
    hidden = ffn_in.shape[1]
    half_hidden, half_width = hidden // 2, width // 2
    down_rows = ffn_out.shape[0]
    both = 2 * slot_rows
    fold_rows = -(-(slot_rows // 2) // 16) * 16
    any_, vmem, dma = pl.ANY, pltpu.VMEM, pltpu.SemaphoreType.DMA
    message = (CHIPS, fold_rows, 128)
    x_block, w_block = (HALF, slot_rows, width), (3, 2, CHIPS, depth, 128)
    in_all, down_all = (2, CHIPS, depth, half_hidden), (CHIPS, down_rows, width)
    out_all = (CHIPS, depth + 16, width)
    in_block, down_block, out_block = (2, depth, half_hidden), (down_rows, width), (depth, width)
    made = call(
        layer_kernel,
        "layer",
        0,
        dict(
            hidden_in=(hidden_in, vmem),
            segment_ids=(segment_ids.reshape(1, rows), vmem),
            order_ids=(order_ids.reshape(1, rows), vmem),
            box_ids=(box_ids, vmem),
            qkv_weight=(qkv_weight, vmem),
            qkv_bias=(qkv_bias, vmem),
            rel_tables=(rel_tables.transpose(0, 2, 1), vmem),
            out_weight=(out_weight, any_),
            branch_bias=(branch_bias, vmem),
            norm_gains=(norm_gains, vmem),
            norm_shifts=(norm_shifts, vmem),
            ffn_in=(ffn_in, any_),
            ffn_in_bias=(ffn_in_bias.reshape(1, down_rows), vmem),
            ffn_out=(ffn_out, any_),
            out_grad=(out_grad, vmem),
        ),
        dict(
            hidden_out=((rows, width), LOW, vmem),
            hidden_grad=((rows, width), LOW, vmem),
            qkv_grad=((3, depth, width), HIGH, vmem),
            qkv_bias_grad=((2, depth), HIGH, vmem),
            rel_tables_grad=((3, depth, NB), HIGH, vmem),
            out_w_grad=((depth, width), HIGH, vmem),
            branch_grad=((2, depth), HIGH, vmem),
            gain_grad=((2, depth), HIGH, vmem),
            shift_grad=((2, depth), HIGH, vmem),
            in_grad=((depth, hidden), HIGH, vmem),
            bias_grad=((1, down_rows), HIGH, vmem),
            down_grad=((down_rows, width), HIGH, vmem),
        ),
        dict(
            x_own=vmem((slot_rows, width), LOW),
            x_all=vmem(x_block, LOW),
            extra=vmem((slot_rows - rows, width), HIGH),
            small_own=vmem((16, width), LOW),
            w_all=vmem(w_block, LOW),
            rel_own=vmem((depth, 4 * NB), LOW),
            rel_all=vmem((2 * depth, 4 * NB), LOW),
            bias_far=vmem((2 * depth, NB), LOW),
            labels=vmem((CHIPS, 16, 256), LOW),
            near=vmem((total, 256), LOW),
            far_part=vmem((total // 2, 256), LOW),
            w_in=vmem(in_all, LOW),
            w_down=vmem(down_all, LOW),
            w_out=vmem(out_all, LOW),
            meta=vmem((total, 128), HIGH),
            shares=vmem((2, 3, 8, half_width), HIGH),
            bias_in=vmem((1, half_hidden), HIGH),
            left=vmem((total, 384), LOW),
            right=vmem((total, 384), LOW),
            right_t=vmem((384, total), LOW),
            value=vmem((total, 128), LOW),
            value_t=vmem((128, total), LOW),
            kept=vmem((total, 128), HIGH),
            message=vmem(message, LOW),
            context_in=vmem(message, LOW),
            context_wide=vmem((both, half_width), HIGH),
            context=vmem((both, half_width), LOW),
            low_first=vmem((both, width), LOW),
            act=vmem((both, half_hidden), LOW),
            slope=vmem((both, half_hidden), HIGH),
            out_part=vmem((slot_rows, width), HIGH),
            in_part=vmem((slot_rows, width), HIGH),
            d_second=vmem((both, width), LOW),
            g_out=vmem((CHIPS,) + out_block, LOW),
            in_1=vmem((8,) + in_block, LOW),
            in_2=vmem((4,) + in_block, LOW),
            in_3=vmem((3,) + in_block, LOW),
            down_1=vmem((8,) + down_block, LOW),
            down_2=vmem((4,) + down_block, LOW),
            down_3=vmem((3,) + down_block, LOW),
            out_1=vmem((12,) + out_block, LOW),
            out_2=vmem((2,) + out_block, LOW),
            out_3=vmem((1,) + out_block, LOW),
            in_total=vmem(in_block, HIGH),
            in_far=vmem((depth, half_hidden), HIGH),
            small_sum=vmem((8, width), HIGH),
            small_in=vmem((6, 8, width), HIGH),
            d_arrived=vmem(message, LOW),
            d_heads=vmem((3, HD, total), LOW),
            d_pair_t=vmem((2 * HD, total), HIGH),
            d_both=vmem((3, 2, HD, total // 2), LOW),
            x_stage=vmem((3, 7, slot_rows // 3, width), LOW),
            x_came=vmem((slot_rows, width), LOW),
            rel_grad=vmem((2 * depth, 4 * NB), HIGH),
            rel_came=vmem((2, depth, 4 * NB), HIGH),
            w_far=vmem((2, 3 * HD, half_width), HIGH),
            w_low=vmem((CHIPS, depth, 6 * HD), LOW),
            w_came=vmem((CHIPS, depth, 6 * HD), LOW),
            keep_sem=dma((7,)),
            home_sem=dma((2,)),
            back_sem=dma((2,)),
            x_send=dma((3, 8)),
            x_recv=dma((3, 8)),
            w_send=dma((16,)),
            w_recv=dma((16,)),
            rel_send=dma((2,)),
            rel_recv=dma((2,)),
            out_send=dma((24,)),
            out_recv=dma((16,)),
            in_send=dma((2, 18)),
            in_recv=dma((2, 16)),
            down_send=dma((2, 18)),
            down_recv=dma((2, 16)),
            msg_send=dma((16,)),
            msg_recv=dma((16,)),
            d_send=dma((16,)),
            d_recv=dma((16,)),
            g_in_send=dma((16,)),
            g_in_recv=dma((16,)),
            g_down_send=dma((16,)),
            g_down_recv=dma((16,)),
            g_out_send=dma((16,)),
            g_out_recv=dma((16,)),
            small_send=dma((6,)),
            small_recv=dma((6,)),
            d_x_send=dma((3, 8)),
            d_x_recv=dma((3, 8)),
            d_w_send=dma((16,)),
            d_w_recv=dma((16,)),
            d_rel_send=dma((2,)),
            d_rel_recv=dma((2,)),
            pair_send=dma((16,)),
            pair_recv=dma((16,)),
        ),
    )
    results = list(
        handed_over(
            [
                made.hidden_out,
                made.hidden_grad,
                made.qkv_grad,
                made.qkv_bias_grad,
                made.rel_tables_grad,
                made.out_w_grad,
                made.branch_grad,
                made.gain_grad,
                made.shift_grad,
                made.in_grad,
                made.bias_grad,
                made.down_grad,
            ]
        )
    )
    results[4] = results[4].transpose(0, 2, 1)
    results[10] = results[10].reshape(down_rows)
    return tuple(results)


def solution(mesh):
    by_heads = mesh.shape["grp"] == 2 and mesh.shape["blk"] == CHIPS == H
    return jax.shard_map(
        head_shards if by_heads else shards,
        mesh=mesh,
        in_specs=(
            P(("grp", "blk"), None),
            P(("grp", "blk")),
            P(("grp", "blk")),
            P(None, ("grp", "blk")),
            P(None, ("grp", "blk"), None),
            P(None, ("grp", "blk")),
            P(None, None, ("grp", "blk")),
            P(("grp", "blk"), None),
            P(None, ("grp", "blk")),
            P(None, ("grp", "blk")),
            P(None, ("grp", "blk")),
            P(("grp", "blk"), None),
            P(("grp", "blk")),
            P(("grp", "blk"), None),
            P(("grp", "blk"), None),
        ),
        out_specs=(
            P(("grp", "blk"), None),
            P(("grp", "blk"), None),
            P(None, ("grp", "blk"), None),
            P(None, ("grp", "blk")),
            P(None, None, ("grp", "blk")),
            P(("grp", "blk"), None),
            P(None, ("grp", "blk")),
            P(None, ("grp", "blk")),
            P(None, ("grp", "blk")),
            P(("grp", "blk"), None),
            P(("grp", "blk")),
            P(("grp", "blk"), None),
        ),
        check_vma=False,
    )
```

```python
import functools
import math
import types

import jax
import jax.numpy as jnp
from jax import lax
from jax.experimental import pallas as pl
from jax.experimental.pallas import tpu as pltpu
from jax.sharding import PartitionSpec as P

H = 16
HD = 64
NB = 128
ORDER_RANGE = 128
BOX_RANGE = 64


NEGATIVE = -1e30
EPSILON = 1e-05


def shifted(x, axis, by):
    devices = lax.axis_size(axis)
    return lax.ppermute(x, axis, [(i, (i + by) % devices) for i in range(devices)])


def block_size(row_count):
    chosen = 1
    for option in range(1, min(row_count, 544) + 1):
        if row_count % option == 0:
            chosen = option
    return chosen


def kind_ranges():
    return (ORDER_RANGE, BOX_RANGE, BOX_RANGE)


def query_maps(layout_ids):
    maps_out = []
    for column, extent in enumerate(kind_ranges()):
        offsets = layout_ids[:, column][:, None] - jnp.arange(extent, dtype=jnp.int32)[None, :]
        bucket = jnp.clip(offsets, -(NB // 2), NB // 2 - 1) + NB // 2
        maps_out.append(bucket[:, :, None] == jnp.arange(NB, dtype=jnp.int32)[None, None, :])
    return maps_out


def key_onehot(key_ids):
    pieces_out = []
    for column, extent in enumerate(kind_ranges()):
        pieces_out.append(
            key_ids[:, column + 1][:, None] == jnp.arange(extent, dtype=jnp.int32)[None, :]
        )
    return jnp.concatenate(pieces_out, axis=1).astype(jnp.bfloat16)


def norm_forward(values_in, norm_gain, norm_shift):
    center = values_in - jnp.mean(values_in, axis=-1, keepdims=True)
    inverse = lax.rsqrt(jnp.mean(center * center, axis=-1, keepdims=True) + EPSILON)
    normed = center * inverse
    return (normed * norm_gain + norm_shift, normed, inverse)


def norm_backward(upstream, normed, inverse, norm_gain):
    scaled = upstream * norm_gain
    inner_part = (
        scaled
        - jnp.mean(scaled, axis=-1, keepdims=True)
        - normed * jnp.mean(scaled * normed, axis=-1, keepdims=True)
    )
    return (inner_part * inverse, jnp.sum(upstream * normed, axis=0), jnp.sum(upstream, axis=0))


def block_logits(query_heads, selector, query_seg, key_part, meta_part, scaling):
    key_ids = meta_part.astype(jnp.int32)
    row_count = key_part.shape[0]
    key_heads = key_part.reshape(row_count, H, HD)
    content = jnp.einsum("thd,khd->htk", query_heads, key_heads, preferred_element_type=jnp.float32)
    onehot = key_onehot(key_ids)
    rel_bias = jnp.einsum("thv,kv->htk", selector, onehot, preferred_element_type=jnp.float32)
    allowed = query_seg[:, None] == key_ids[None, :, 0]
    logits = jnp.where(allowed[None], (content + rel_bias) * scaling, NEGATIVE)
    return (logits, allowed, onehot, key_heads)


def over_blocks(advance, carry, piece, start):
    row_count = piece[0].shape[0]
    stride = block_size(row_count)

    def one_step(block_index, running):
        portion = tuple(
            (lax.dynamic_slice_in_dim(member, block_index * stride, stride, 0) for member in piece)
        )
        return advance(running, portion, start + block_index * stride)

    return lax.fori_loop(0, row_count // stride, one_step, carry)


def shards(
    hidden_in,
    segment_ids,
    order_ids,
    box_ids,
    qkv_weight,
    qkv_bias,
    rel_tables,
    out_weight,
    branch_bias,
    norm_gains,
    norm_shifts,
    ffn_in,
    ffn_in_bias,
    ffn_out,
    out_grad,
):
    gathered = (
        lax.all_gather(qkv_weight, ("grp", "blk"), axis=1, tiled=True),
        lax.all_gather(qkv_bias, ("grp", "blk"), axis=1, tiled=True),
        lax.all_gather(rel_tables, ("grp", "blk"), axis=2, tiled=True),
        lax.all_gather(out_weight, ("grp", "blk"), axis=0, tiled=True),
        lax.all_gather(branch_bias, ("grp", "blk"), axis=1, tiled=True),
        lax.all_gather(norm_gains, ("grp", "blk"), axis=1, tiled=True),
        lax.all_gather(norm_shifts, ("grp", "blk"), axis=1, tiled=True),
        lax.all_gather(ffn_in, ("grp", "blk"), axis=0, tiled=True),
        lax.all_gather(ffn_in_bias, ("grp", "blk"), axis=0, tiled=True),
        lax.all_gather(ffn_out, ("grp", "blk"), axis=0, tiled=True),
    )
    w_qkv, b_qkv, w_rel, w_out, b_branch, gains, shifts, w_in, b_in, w_down = gathered
    row_count = hidden_in.shape[0]
    width = hidden_in.shape[1]
    scaling = 1.0 / math.sqrt(4.0 * HD)
    select_width = ORDER_RANGE + 2 * BOX_RANGE
    projected = jnp.einsum("td,cde->cte", hidden_in, w_qkv, preferred_element_type=jnp.float32)
    bias_qkv = b_qkv.astype(jnp.float32)
    query_rows = (projected[0] + bias_qkv[0]).astype(jnp.bfloat16)
    key_rows = projected[1].astype(jnp.bfloat16)
    value_rows = (projected[2] + bias_qkv[1]).astype(jnp.bfloat16)
    layout_ids = jnp.stack([order_ids, box_ids[0], box_ids[1]], axis=1)
    key_meta = jnp.stack([segment_ids, order_ids, box_ids[0], box_ids[1]], axis=1).astype(
        jnp.bfloat16
    )
    query_heads = query_rows.reshape(row_count, H, HD)
    rel_heads = w_rel.reshape(3, NB, H, HD)
    tables = jnp.einsum(
        "thd,nbhd->thnb", query_heads, rel_heads, preferred_element_type=jnp.float32
    ).astype(jnp.bfloat16)
    maps_list = query_maps(layout_ids)
    selector = jnp.concatenate(
        [
            jnp.einsum(
                "thb,tvb->thv",
                tables[:, :, column],
                maps_list[column].astype(jnp.bfloat16),
                preferred_element_type=jnp.float32,
            )
            for column in range(3)
        ],
        axis=2,
    ).astype(jnp.bfloat16)

    def forward_step(running, portion, offset):
        row_top, row_total, weighted = running
        key_part, value_part, meta_part = portion
        logits, allowed, onehot, key_heads = block_logits(
            query_heads, selector, segment_ids, key_part, meta_part, scaling
        )
        new_top = jnp.maximum(row_top, jnp.max(logits, axis=2))
        rescale = jnp.exp(row_top - new_top)
        weights = jnp.where(allowed[None], jnp.exp(logits - new_top[:, :, None]), 0.0)
        value_heads = value_part.reshape(value_part.shape[0], H, HD)
        weighted = weighted * rescale.T[:, :, None] + jnp.einsum(
            "htk,khd->thd",
            weights.astype(jnp.bfloat16),
            value_heads,
            preferred_element_type=jnp.float32,
        )
        return (new_top, row_total * rescale + jnp.sum(weights, axis=2), weighted)

    start_state = (
        jnp.full((H, row_count), NEGATIVE, jnp.float32),
        jnp.zeros((H, row_count), jnp.float32),
        jnp.zeros((row_count, H, HD), jnp.float32),
    )
    row_top, row_total, weighted = over_blocks(
        forward_step,
        start_state,
        (
            lax.all_gather(key_rows, "blk", axis=0, tiled=True),
            lax.all_gather(value_rows, "blk", axis=0, tiled=True),
            lax.all_gather(key_meta, "blk", axis=0, tiled=True),
        ),
        jnp.int32(0),
    )
    context_full = weighted / row_total.T[:, :, None]
    log_total = row_top + jnp.log(row_total)
    context = context_full.reshape(row_count, width).astype(jnp.bfloat16)
    branch = jnp.dot(context, w_out, preferred_element_type=jnp.float32) + b_branch[0].astype(
        jnp.float32
    )
    first, normed_one, inverse_one = norm_forward(
        hidden_in.astype(jnp.float32) + branch,
        gains[0].astype(jnp.float32),
        shifts[0].astype(jnp.float32),
    )
    first_low = first.astype(jnp.bfloat16)
    inner_pre = jnp.dot(first_low, w_in, preferred_element_type=jnp.float32) + b_in.astype(
        jnp.float32
    )
    activated, gelu_pull = jax.vjp(
        lambda pre_act: jax.nn.gelu(pre_act, approximate=False), inner_pre
    )
    activated_low = activated.astype(jnp.bfloat16)
    second = jnp.dot(activated_low, w_down, preferred_element_type=jnp.float32) + b_branch[
        1
    ].astype(jnp.float32)
    result, normed_two, inverse_two = norm_forward(
        first + second, gains[1].astype(jnp.float32), shifts[1].astype(jnp.float32)
    )
    hidden_out = result.astype(jnp.bfloat16)
    grad_sum2, gain_grad2, shift_grad2 = norm_backward(
        out_grad.astype(jnp.float32), normed_two, inverse_two, gains[1].astype(jnp.float32)
    )
    grad_second = grad_sum2.astype(jnp.bfloat16)
    grad_w_down = jnp.einsum(
        "tf,td->fd", activated_low, grad_second, preferred_element_type=jnp.float32
    )
    grad_bias_two = jnp.sum(grad_second.astype(jnp.float32), axis=0)
    grad_act = jnp.einsum("td,fd->tf", grad_second, w_down, preferred_element_type=jnp.float32)
    grad_inner = gelu_pull(grad_act)[0].astype(jnp.bfloat16)
    grad_b_in = jnp.sum(grad_inner.astype(jnp.float32), axis=0)
    grad_w_in = jnp.einsum("td,tf->df", first_low, grad_inner, preferred_element_type=jnp.float32)
    grad_first = grad_sum2 + jnp.einsum(
        "tf,df->td", grad_inner, w_in, preferred_element_type=jnp.float32
    )
    grad_sum1, gain_grad1, shift_grad1 = norm_backward(
        grad_first, normed_one, inverse_one, gains[0].astype(jnp.float32)
    )
    grad_branch = grad_sum1.astype(jnp.bfloat16)
    grad_w_out = jnp.einsum("td,te->de", context, grad_branch, preferred_element_type=jnp.float32)
    grad_bias_one = jnp.sum(grad_branch.astype(jnp.float32), axis=0)
    grad_context = jnp.einsum(
        "te,de->td", grad_branch, w_out, preferred_element_type=jnp.float32
    ).astype(jnp.bfloat16)
    grad_heads = grad_context.reshape(row_count, H, HD)
    delta = jnp.einsum("thd,thd->ht", grad_heads.astype(jnp.float32), context_full)

    def backward_core(grad_query, grad_select, portion):
        key_part, value_part, meta_part = portion
        logits, allowed, onehot, key_heads = block_logits(
            query_heads, selector, segment_ids, key_part, meta_part, scaling
        )
        probs = jnp.where(allowed[None], jnp.exp(logits - log_total[:, :, None]), 0.0)
        part_rows = key_part.shape[0]
        value_heads = value_part.reshape(part_rows, H, HD)
        grad_probs = jnp.einsum(
            "thd,khd->htk", grad_heads, value_heads, preferred_element_type=jnp.float32
        )
        grad_logits = (probs * (grad_probs - delta[:, :, None])).astype(jnp.bfloat16)
        grad_query = grad_query + scaling * jnp.einsum(
            "htk,khd->thd", grad_logits, key_heads, preferred_element_type=jnp.float32
        )
        grad_select = grad_select + scaling * jnp.einsum(
            "htk,kv->thv", grad_logits, onehot, preferred_element_type=jnp.float32
        )
        grad_key = scaling * jnp.einsum(
            "htk,thd->khd", grad_logits, query_heads, preferred_element_type=jnp.float32
        )
        grad_value = jnp.einsum(
            "htk,thd->khd",
            probs.astype(jnp.bfloat16),
            grad_heads,
            preferred_element_type=jnp.float32,
        )
        update = jnp.concatenate(
            [grad_key.reshape(part_rows, width), grad_value.reshape(part_rows, width)], axis=1
        )
        return (grad_query, grad_select, update)

    query_zero = jnp.zeros((row_count, H, HD), jnp.float32)
    select_zero = jnp.zeros((row_count, H, select_width), jnp.float32)

    def cycle_turn(turn, carry):
        grad_query, grad_select, key_part, value_part, meta_part, carried = carry
        portion = (key_part, value_part, meta_part)
        grad_query, grad_select, update = backward_core(grad_query, grad_select, portion)
        carried = carried + update
        key_part, value_part, meta_part = shifted((key_part, value_part, meta_part), "blk", 1)
        carried = shifted(carried.astype(jnp.bfloat16), "blk", 1).astype(carried.dtype)
        return (grad_query, grad_select, key_part, value_part, meta_part, carried)

    cycle_start = (
        query_zero,
        select_zero,
        key_rows,
        value_rows,
        key_meta,
        jnp.zeros((row_count, 2 * width), jnp.float32),
    )
    cycle_end = lax.fori_loop(0, lax.axis_size("blk"), cycle_turn, cycle_start)
    grad_query, grad_select, own_pairs = (cycle_end[0], cycle_end[1], cycle_end[5])
    grad_key_rows = own_pairs[:, :width].astype(jnp.bfloat16)
    grad_value_rows = own_pairs[:, width:].astype(jnp.bfloat16)
    cursor = 0
    table_parts = []
    for column, extent in enumerate(kind_ranges()):
        table_parts.append(
            jnp.einsum(
                "thv,tvb->thb",
                grad_select[:, :, cursor : cursor + extent],
                maps_list[column].astype(jnp.float32),
                precision=lax.Precision.HIGHEST,
            )
        )
        cursor = cursor + extent
    grad_tables = jnp.stack(table_parts, axis=2).astype(jnp.bfloat16)
    grad_query_total = grad_query + jnp.einsum(
        "thnb,nbhd->thd", grad_tables, rel_heads, preferred_element_type=jnp.float32
    )
    grad_query_rows = grad_query_total.reshape(row_count, width).astype(jnp.bfloat16)
    grad_rel = jnp.einsum(
        "thnb,thd->nbhd", grad_tables, query_heads, preferred_element_type=jnp.float32
    ).reshape(3, NB, width)
    grad_stack = jnp.stack([grad_query_rows, grad_key_rows, grad_value_rows])
    grad_w_qkv = jnp.einsum(
        "td,cte->cde", hidden_in, grad_stack, preferred_element_type=jnp.float32
    )
    grad_b_qkv = jnp.stack(
        [
            jnp.sum(grad_query_rows.astype(jnp.float32), axis=0),
            jnp.sum(grad_value_rows.astype(jnp.float32), axis=0),
        ]
    )
    grad_input = grad_sum1 + jnp.einsum(
        "cte,cde->td", grad_stack, w_qkv, preferred_element_type=jnp.float32
    )
    summed = (
        lax.psum_scatter(grad_w_qkv, ("grp", "blk"), scatter_dimension=1, tiled=True),
        lax.psum_scatter(grad_b_qkv, ("grp", "blk"), scatter_dimension=1, tiled=True),
        lax.psum_scatter(grad_rel, ("grp", "blk"), scatter_dimension=2, tiled=True),
        lax.psum_scatter(grad_w_out, ("grp", "blk"), scatter_dimension=0, tiled=True),
        lax.psum_scatter(
            jnp.stack([grad_bias_one, grad_bias_two]),
            ("grp", "blk"),
            scatter_dimension=1,
            tiled=True,
        ),
        lax.psum_scatter(
            jnp.stack([gain_grad1, gain_grad2]), ("grp", "blk"), scatter_dimension=1, tiled=True
        ),
        lax.psum_scatter(
            jnp.stack([shift_grad1, shift_grad2]), ("grp", "blk"), scatter_dimension=1, tiled=True
        ),
        lax.psum_scatter(grad_w_in, ("grp", "blk"), scatter_dimension=0, tiled=True),
        lax.psum_scatter(grad_b_in, ("grp", "blk"), scatter_dimension=0, tiled=True),
        lax.psum_scatter(grad_w_down, ("grp", "blk"), scatter_dimension=0, tiled=True),
    )
    return (
        hidden_out,
        grad_input.astype(jnp.bfloat16),
        summed[0],
        summed[1],
        summed[2],
        summed[3],
        summed[4],
        summed[5],
        summed[6],
        summed[7],
        summed[8],
        summed[9],
    )


MESH = pl.DeviceIdType.MESH
LOW = jnp.bfloat16
HIGH = jnp.float32
CHIPS = 16
HALF = 8
BLOCK = 256
MASKED = -1e30
VMEM_LIMIT = 62 * 2**20
NT = ((1,), (1,))
TN = ((0,), (0,))


def dot(left, right, dims=((1,), (0,))):
    return lax.dot_general(left, right, (dims, ((), ())), preferred_element_type=HIGH)


def place():
    return lax.axis_index("grp"), lax.axis_index("blk")


def coordinates(chip):
    return lax.div(chip, 4), lax.rem(lax.div(chip, 2), 2), lax.rem(chip, 2)


def greet_all():
    core, chip = place()
    me = core * CHIPS + chip
    barrier = pltpu.get_barrier_semaphore()

    def greet(ahead, carry):
        other = lax.rem(me + ahead, 2 * CHIPS)
        pl.semaphore_signal(
            barrier,
            inc=1,
            device_id=(lax.div(other, CHIPS), lax.rem(other, CHIPS)),
            device_id_type=MESH,
        )
        return carry

    lax.fori_loop(1, 2 * CHIPS, greet, 0)


def await_all():
    pl.semaphore_wait(pltpu.get_barrier_semaphore(), 2 * CHIPS - 1)


def remote(source, target, send, recv, device):
    return pltpu.make_async_remote_copy(
        src_ref=source,
        dst_ref=target,
        send_sem=send,
        recv_sem=recv,
        device_id=device,
        device_id_type=MESH,
    )


def local(source, target, sem):
    return pltpu.make_async_copy(source, target, sem)


MIRROR = 3


def in_the_middle():
    z, _, _ = coordinates(lax.axis_index("blk"))
    return jnp.logical_and(z > 0, z < 3)


def neighbours(across):
    core, chip = place()
    z, y, x = coordinates(chip)
    planes = (z + 1 - 2 * lax.rem(z, 2), 2 - lax.div(z, 2), 3 - 3 * lax.div(z, 2), 3 - z)

    def slot(far_p, far_q, line):
        far_y, far_x = (far_q, far_p) if across == "x" else (far_p, far_q)
        plane = z if line is None else planes[line]
        return plane * 4 + (1 - y if far_y else y) * 2 + (1 - x if far_x else x)

    return slot


class Shipments:
    def __init__(self, send, recv):
        self.send, self.recv = send, recv
        self.core = lax.axis_index("grp")

    def ship(self, source, target, kind, recv_index, to, when=None):
        start = lambda: remote(
            source, target, self.send.at[kind], self.recv.at[recv_index], (self.core, to)
        ).start()
        if when is None:
            start()
        else:
            pl.when(when)(start)

    def landed(self, target, recv_index):
        local(target, target, self.recv.at[recv_index]).wait()

    def all_sent(self, bytes_of, kind):
        local(bytes_of, bytes_of, self.send.at[kind]).wait()


class Gather:
    SENDS, RECEIVES = 2, 9

    def __init__(self, pick, send, recv, across):
        self.pick, self.at = pick, neighbours(across)
        self.moves = Shipments(send, recv)
        self.middle = in_the_middle()

    def ship(self, what, kind, recv_index, to, when=None):
        ref = self.pick(self.at(*what))
        self.moves.ship(ref, ref, kind, recv_index, self.at(*to), when)

    def plane(self, line):
        return lax.div(self.at(0, 0, line), 4)

    def along_z(self, line, to, when=None):
        self.ship((0, 0, line), 0, self.plane(line), (0, 0, to), when)

    def along_p(self, line):
        self.ship((0, 0, line), 1, 4 + self.plane(line), (1, 0, None))

    def along_q(self, far_p, line):
        self.ship((far_p, 0, line), 1, 8, (0, 1, None))

    def own_line(self, number):
        if number == 0:
            self.along_z(None, 0)
        else:
            self.along_z(None, MIRROR, self.middle)

    def own_plane(self):
        self.along_p(None)
        self.along_q(0, None)

    def line(self, line):
        self.moves.landed(self.pick(self.at(0, 0, line)), self.plane(line))
        self.along_z(line, MIRROR if line == 0 else 0, self.middle)
        self.along_p(line)
        self.along_q(0, line)

    def side(self, line):
        self.moves.landed(self.pick(self.at(1, 0, line)), 4 + self.plane(line))
        self.along_q(1, line)

    def arrive(self):
        self.moves.landed(self.pick(pl.ds(0, 8)), 8)

    def finish(self):
        self.moves.all_sent(self.pick(pl.ds(0, 12)), 1)
        pl.when(self.middle)(lambda: self.moves.all_sent(self.pick(pl.ds(0, 5)), 0))
        pl.when(jnp.logical_not(self.middle))(lambda: self.moves.all_sent(self.pick(pl.ds(0, 1)), 0))


class GatherLate(Gather):
    SENDS, RECEIVES = 3, 6

    def plane_slots(self, line):
        return self.pick(pl.ds(self.plane(line) * 4, 4))

    def first(self):
        self.ship((0, 0, None), 0, 4, (1, 0, None))
        self.ship((0, 0, None), 0, 5, (0, 1, None))

    def second(self):
        self.moves.landed(self.pick(self.at(1, 0, None)), 4)
        self.ship((1, 0, None), 0, 5, (0, 1, None))

    def pass_plane(self, line, kind, to, when=None):
        slots = self.plane_slots(line)
        self.moves.ship(slots, slots, kind, self.plane(line), self.at(0, 0, to), when)

    def third(self):
        self.moves.landed(self.pick(pl.ds(0, 2)), 5)
        self.pass_plane(None, 1, 0)
        self.pass_plane(None, 2, MIRROR, self.middle)

    def late_line(self, line):
        self.moves.landed(self.plane_slots(line), self.plane(line))
        self.pass_plane(line, 2, MIRROR if line == 0 else 0, self.middle)

    def finish(self):
        self.moves.all_sent(self.pick(pl.ds(0, 3)), 0)
        self.moves.all_sent(self.pick(pl.ds(0, 4)), 1)
        pl.when(self.middle)(lambda: self.moves.all_sent(self.pick(pl.ds(0, 16)), 2))


class Reduce:
    SENDS, RECEIVES = 1, 15

    def __init__(self, held, pick, stages, send, recv, across):
        self.held, self.pick, self.at = held, pick, neighbours(across)
        self.first, self.second, self.third_in = stages
        self.moves = Shipments(send, recv)

    @staticmethod
    def number(line):
        return 3 if line is None else line

    def mine(self, *what):
        return self.pick(self.held, self.at(*what))

    def term(self, stage, index, recv_index):
        self.moves.landed(stage.at[index], recv_index)
        return stage[index].astype(HIGH)

    def start(self, line):
        for far_p in (1, 0):
            index = self.number(line) * 2 + far_p
            self.moves.ship(
                self.mine(far_p, 1, line), self.first.at[index], 0, index, self.at(0, 1, None)
            )

    def side(self, line):
        number = self.number(line)
        index = number * 2 + 1
        total = self.term(self.first, index, index) + self.mine(1, 0, line)[...].astype(HIGH)
        self.first[index] = total.astype(LOW)
        self.moves.ship(
            self.first.at[index], self.second.at[number], 0, 8 + number, self.at(1, 0, None)
        )

    def line(self, line):
        number = self.number(line)
        index = number * 2
        total = (
            self.term(self.first, index, index)
            + self.term(self.second, number, 8 + number)
            + self.mine(0, 0, line)[...].astype(HIGH)
        )
        if line is None:
            return total
        self.first[index] = total.astype(LOW)
        ahead = self.ahead(line)
        self.moves.ship(
            self.first.at[index], self.third_in.at[ahead], 0, 12 + ahead, self.at(0, 0, line)
        )

    def ahead(self, line):
        return lax.rem(lax.div(self.at(0, 0, None), 4) - lax.div(self.at(0, 0, line), 4) + 4, 4) - 1

    def finish(self, result):
        total = self.line(None)
        for ahead in range(3):
            total += self.term(self.third_in, ahead, 12 + ahead)
        result[...] = total
        self.moves.all_sent(self.pick(self.held, pl.ds(0, 15)), 0)


class ReduceEarly(Reduce):
    SENDS, RECEIVES = 1, 6

    def start(self):
        for line in (2, 1, 0):
            plane = lax.div(self.at(0, 0, line), 4)
            ahead = self.ahead(line)
            self.moves.ship(
                self.pick(self.held, pl.ds(plane * 4, 4)),
                self.first.at[ahead],
                0,
                ahead,
                self.at(0, 0, line),
            )

    def plane_sum(self, *what):
        slot = self.at(*what, None)
        total = self.pick(self.held, slot)[...].astype(HIGH)
        for ahead in range(3):
            total += self.first[ahead, lax.rem(slot, 4)].astype(HIGH)
        return total

    def plane_ref(self, *what):
        return self.first.at[0, lax.rem(self.at(*what, None), 4)]

    def third(self):
        for ahead in range(3):
            self.moves.landed(self.first.at[ahead], ahead)
        for far_p in (1, 0):
            ref = self.plane_ref(far_p, 1)
            ref[...] = self.plane_sum(far_p, 1).astype(LOW)
            self.moves.ship(ref, self.second.at[far_p], 0, 3 + far_p, self.at(0, 1, None))

    def across(self):
        ref = self.plane_ref(1, 0)
        ref[...] = (self.plane_sum(1, 0) + self.term(self.second, 1, 4)).astype(LOW)
        self.moves.ship(ref, self.third_in.at[0], 0, 5, self.at(1, 0, None))

    def finish(self, result):
        result[...] = (
            self.plane_sum(0, 0) + self.term(self.second, 0, 3) + self.term(self.third_in, 0, 5)
        )
        self.moves.all_sent(self.pick(self.held, pl.ds(0, 15)), 0)


def cube_of(order):
    core, chip = place()
    z, y, x = coordinates(chip)

    def at(*flips):
        far = dict(zip(order, flips))
        plane = z + 1 - 2 * lax.rem(z, 2) if far["z"] else z
        return plane * 4 + (1 - y if far["y"] else y) * 2 + (1 - x if far["x"] else x)

    return at


class CubeGather:
    SENDS, RECEIVES = 1, 4

    def __init__(self, pick, send, recv, order):
        self.pick, self.at = pick, cube_of(order)
        self.moves = Shipments(send, recv)

    def ref(self, *what):
        return self.pick(lax.rem(self.at(*what), HALF))

    def ship(self, what, recv_index, to):
        self.moves.ship(self.ref(*what), self.ref(*what), 0, recv_index, self.at(*to))

    def own(self):
        self.ship((0, 0, 0), 0, (1, 0, 0))
        self.ship((0, 0, 0), 1, (0, 1, 0))
        self.ship((0, 0, 0), 3, (0, 0, 1))

    def one(self):
        self.moves.landed(self.ref(1, 0, 0), 0)
        self.ship((1, 0, 0), 2, (0, 1, 0))
        self.ship((1, 0, 0), 3, (0, 0, 1))

    def two(self):
        for one in range(2):
            self.moves.landed(self.ref(one, 1, 0), 1 + one)
            self.ship((one, 1, 0), 3, (0, 0, 1))

    def arrive(self):
        self.moves.landed(self.pick(pl.ds(0, 4)), 3)

    def finish(self):
        self.moves.all_sent(self.pick(pl.ds(0, 7)), 0)


class CubeReduce:
    SENDS, RECEIVES = 1, 7

    def __init__(self, pick, stage, send, recv, order):
        self.pick, self.stage, self.at = pick, stage, cube_of(order)
        self.moves = Shipments(send, recv)

    def ship(self, source, index, to):
        self.moves.ship(source, self.stage.at[index], 0, index, self.at(*to))

    def mine(self, *what):
        return self.pick(lax.rem(self.at(*what), HALF))

    def term(self, index):
        self.moves.landed(self.stage.at[index], index)
        return self.stage[index].astype(HIGH)

    def own(self):
        for index, (one, two) in enumerate(((1, 1), (0, 1), (1, 0), (0, 0))):
            self.ship(self.mine(one, two, 1), index, (0, 0, 1))

    def one(self):
        for index, one in ((0, 1), (1, 0)):
            total = self.mine(one, 1, 0)[...].astype(HIGH) + self.term(index)
            self.stage[index] = total.astype(LOW)
            self.ship(self.stage.at[index], 4 + index, (0, 1, 0))

    def two(self):
        total = self.mine(1, 0, 0)[...].astype(HIGH) + self.term(2) + self.term(4)
        self.stage[2] = total.astype(LOW)
        self.ship(self.stage.at[2], 6, (1, 0, 0))

    def arrive(self):
        return self.mine(0, 0, 0)[...].astype(HIGH) + self.term(3) + self.term(5) + self.term(6)

    def finish(self):
        self.moves.all_sent(self.stage, 0)


def each(plans, act, *arguments):
    for plan in plans:
        act(plan, *arguments)


def unit():
    core, chip = place()
    return lax.div(chip, HALF), lax.rem(chip, HALF), core


def all_but_one(source, send, itself):
    most = source.at[pl.ds(0, CHIPS - 1)]
    pl.when(itself)(lambda: local(most, most, send.at[0]).wait())
    pl.when(jnp.logical_not(itself))(lambda: local(source, source, send.at[0]).wait())


def to_tokens(source, target, send, recv):
    core, chip = place()
    group, position, _ = unit()
    to_core = lax.div(position, 4)
    mine = group * HALF + 2 * lax.rem(position, 4) + core
    here = to_core == core

    def copy_to(ahead):
        chip_to = lax.rem(chip + ahead, CHIPS)
        return remote(
            source.at[chip_to], target.at[mine], send.at[0], recv.at[0], (to_core, chip_to)
        )

    pl.when(here)(lambda: local(source.at[chip], target.at[mine], recv.at[0]).start())
    pl.when(jnp.logical_not(here))(lambda: copy_to(0).start())
    for ahead in range(1, CHIPS):
        copy_to(ahead).start()
    arrive = lambda: local(target, target, recv.at[0]).wait()
    return arrive, lambda: all_but_one(source, send, here)


def to_heads(source, target, send, recv):
    core, chip = place()
    group, position, _ = unit()
    here = lax.div(position, 4) == core
    start = 2 * lax.rem(position, 4) + core

    def copy_to(turn_group, ahead):
        to_group = lax.rem(group + turn_group, 2)
        head = lax.rem(start + ahead, HALF)
        return remote(
            source.at[to_group * HALF + head],
            target.at[chip],
            send.at[0],
            recv.at[0],
            (lax.rem(head, 2), to_group * HALF + core * 4 + lax.div(head, 2)),
        )

    pl.when(here)(lambda: local(source.at[group * HALF + start], target.at[chip], recv.at[0]).start())
    pl.when(jnp.logical_not(here))(lambda: copy_to(0, 0).start())
    for turn_group in range(2):
        for ahead in range(0 if turn_group else 1, HALF):
            copy_to(turn_group, ahead).start()
    arrive = lambda: local(target, target, recv.at[0]).wait()
    return arrive, lambda: all_but_one(source, send, here)


def lanes(rows, width=128):
    return lax.broadcasted_iota(jnp.int32, (rows, width), 1)


def turn(values):
    return pltpu.roll(values, HD, 1)


def fold(rows_in):
    half = rows_in.shape[0] // 2
    both = jnp.where(lanes(half) < HD, rows_in[:half], turn(rows_in[half:]))
    pad = -half % 16
    if pad:
        both = jnp.concatenate([both, jnp.zeros((pad, 128), HIGH)], axis=0)
    return both.astype(LOW)


def column_sums(v):
    return jnp.sum(v, axis=0, keepdims=True)


def gelu_parts(pre):
    cdf = 0.5 * (1.0 + lax.erf(pre * math.sqrt(0.5)))
    density = jnp.exp(-0.5 * pre * pre) * (1.0 / math.sqrt(2.0 * math.pi))
    return pre * cdf, cdf + pre * density


def normalize(v, gain, shift):
    center = v - jnp.mean(v, axis=1, keepdims=True)
    inverse = lax.rsqrt(jnp.mean(center * center, axis=1, keepdims=True) + EPSILON)
    normed = center * inverse
    return normed * gain + shift, normed, inverse


def normalize_back(c, normed, inverse, gain):
    scaled = c * gain
    inner = (
        scaled
        - jnp.mean(scaled, axis=1, keepdims=True)
        - normed * jnp.mean(scaled * normed, axis=1, keepdims=True)
    )
    return inner * inverse


def at_steps(index, steps):
    for number, acts in steps.items():

        def run(acts=acts):
            for act in acts:
                act()

        pl.when(index == number)(run)


def columns_of(half, width):
    return pl.ds(pl.multiple_of(half * width, 128), width)


GAIN_AT, SHIFT_AT, BIAS_AT = 128, 256, 384


def layer_kernel(names, *refs):
    r = types.SimpleNamespace(**dict(zip(names, refs)))
    hidden, x_all, w_all, rel_all = r.hidden_in, r.x_all, r.w_all, r.rel_all
    token_rows, width = hidden.shape
    slot_rows = x_all.shape[1]
    total = CHIPS * slot_rows
    depth = r.out_weight.shape[0]
    w_in, w_down, w_out = r.w_in, r.w_down, r.w_out
    half_hidden = w_in.shape[3]
    half_width = width // 2
    core, chip = place()
    group, position, _ = unit()
    other = 1 - core
    me = core * CHIPS + chip
    keep = r.keep_sem

    greet_all()

    loads = [
        local(r.ffn_in.at[:, columns_of(core, half_hidden)], w_in.at[core, chip], keep.at[0]),
        local(r.ffn_out, w_down.at[chip], keep.at[1]),
        local(r.out_weight, w_out.at[chip, pl.ds(0, depth)], keep.at[2]),
    ]
    for copy in loads:
        copy.start()

    extra = r.extra
    extra[...] = jnp.zeros_like(extra)
    extra[0:1, 0:256] = jnp.full((1, 256), 4.0, HIGH)
    extra[0:1, 0:token_rows] = r.segment_ids[...].astype(HIGH)
    extra[1:2, 0:token_rows] = r.order_ids[...].astype(HIGH)
    extra[2:4, 0:token_rows] = r.box_ids[...].astype(HIGH)
    tail = token_rows - token_rows % 16
    x_own = r.x_own
    x_own[0:tail, :] = hidden[0:tail, :]
    x_own[tail:slot_rows, :] = jnp.concatenate(
        [hidden[tail:token_rows, :].astype(HIGH), extra[...]], axis=0
    ).astype(LOW)
    weight = r.qkv_weight
    rel_own = r.rel_own
    for kind in range(3):
        rel_own[:, kind * NB : (kind + 1) * NB] = r.rel_tables[kind]
    eye_depth = (
        lax.broadcasted_iota(jnp.int32, (depth, depth), 0)
        == lax.broadcasted_iota(jnp.int32, (depth, depth), 1)
    ).astype(LOW)
    bias_columns = dot(eye_depth, r.qkv_bias[...], NT)
    rel_own[:, 3 * NB : 4 * NB] = jnp.where(
        lanes(depth) == 0, bias_columns[:, 0:1], jnp.where(lanes(depth) == 1, bias_columns[:, 1:2], 0.0)
    ).astype(LOW)
    small_own = r.small_own
    small_own[...] = jnp.zeros_like(small_own)
    small_own[0:2, 0:depth] = r.branch_bias[...]
    small_own[0:2, GAIN_AT : GAIN_AT + depth] = r.norm_gains[...]
    small_own[0:2, SHIFT_AT : SHIFT_AT + depth] = r.norm_shifts[...]
    small_own[0:1, BIAS_AT : BIAS_AT + 128] = r.ffn_in_bias[...]
    loads += [
        local(small_own, w_out.at[chip, pl.ds(depth, 16)], keep.at[3]),
        local(weight.at[:, :, columns_of(position, 128)], w_all.at[:, core, chip], keep.at[4]),
    ]
    for copy in loads[3:]:
        copy.start()
    await_all()

    at_home = group == core
    away = lax.rem(chip + HALF, CHIPS)
    x_slot = x_all.at[position]
    home = lambda: local(x_own, x_slot, r.home_sem.at[1])
    abroad = lambda: remote(x_own, x_slot, r.home_sem.at[0], r.home_sem.at[1], (other, away))
    pl.when(at_home)(lambda: home().start())
    pl.when(jnp.logical_not(at_home))(lambda: abroad().start())

    rel_head = core * HALF + lax.div(chip, 2)
    parity = lax.rem(chip, 2)
    rel_slot = rel_all.at[pl.ds(parity * depth, depth)]

    def rel_each(act_remote, act_own):
        for to_group in range(2):
            to = (lax.rem(rel_head, 2), to_group * HALF + lax.div(rel_head, 2))
            itself = jnp.logical_and(to[0] == core, to[1] == chip)
            copy = lambda: remote(
                rel_own, rel_slot, r.rel_send.at[to_group], r.rel_recv.at[parity], to
            )
            pl.when(jnp.logical_not(itself))(lambda: act_remote(copy()))
            if act_own is not None:
                pl.when(itself)(act_own)

    rel_each(
        lambda copy: copy.start(), lambda: local(rel_own, rel_slot, r.rel_recv.at[parity]).start()
    )

    def w_copy(ahead):
        to = lax.rem(chip + ahead, CHIPS)
        return remote(
            weight.at[:, :, columns_of(lax.rem(to, HALF), 128)],
            w_all.at[:, core, chip],
            r.w_send.at[0],
            r.w_recv.at[0],
            (core, to),
        )

    swap_in = remote(
        r.ffn_in.at[:, columns_of(other, half_hidden)],
        w_in.at[core, chip],
        r.pair_send.at[0],
        r.pair_recv.at[0],
        (other, chip),
    )
    swap_in.start()

    third = slot_rows // 3
    x_plans = [
        CubeGather(
            lambda slot, part=part: x_all.at[slot, pl.ds(part * third, third)],
            r.x_send.at[part],
            r.x_recv.at[part],
            order,
        )
        for part, order in enumerate(("xyz", "yzx", "zxy"))
    ]
    half = width // 2
    half_tile = half_hidden // 2
    plan_out = GatherLate(lambda slot: w_out.at[slot], r.out_send, r.out_recv, "x")

    def halves(ref, wide, sends, recvs):
        return [
            Gather(
                lambda slot, part=part: ref(slot, pl.ds(part * wide, wide)), sends.at[part], recvs.at[part], across
            )
            for part, across in enumerate("xy")
        ]

    plans_in = halves(lambda slot, columns: w_in.at[:, slot, :, columns], half_tile, r.in_send, r.in_recv)
    plans_down = halves(lambda slot, columns: w_down.at[slot, :, columns], half, r.down_send, r.down_recv)

    for ahead in range(1, CHIPS):
        w_copy(ahead).start()
    for copy in loads:
        copy.wait()
    each(plans_down, Gather.own_plane)
    swap_in.wait()
    each(plans_in, Gather.own_plane)
    plan_out.first()
    each(plans_in, Gather.own_line, 0)
    home().wait()
    each(x_plans, CubeGather.own)
    each(x_plans, CubeGather.one)
    each(plans_down, Gather.own_line, 1)
    plan_out.second()
    each(x_plans, CubeGather.two)
    each(plans_down, Gather.own_line, 0)
    plan_out.third()
    each(plans_in, Gather.line, 0)
    w_most = w_all.at[:, core, pl.ds(0, CHIPS - 1)]
    local(w_most, w_most, r.w_recv.at[0]).wait()
    pair_w = remote(w_all.at[:, core], w_all.at[:, core], r.pair_send.at[1], r.pair_recv.at[1], (other, chip))
    pair_w.start()
    for slot in range(2):
        local(rel_own, rel_all.at[pl.ds(slot * depth, depth)], r.rel_recv.at[slot]).wait()
    pair_bias = remote(
        rel_all.at[:, pl.ds(3 * NB, NB)], r.bias_far, r.pair_send.at[2], r.pair_recv.at[2], (other, chip)
    )
    pair_bias.start()
    each(x_plans, CubeGather.arrive)
    pl.when(jnp.logical_not(at_home))(lambda: abroad().wait_send())

    labels = r.labels
    first_slot = core * HALF
    label_part = x_all.at[:, pl.ds(slot_rows - 16, 16), pl.ds(0, 256)]
    label_slots = labels.at[pl.ds(first_slot, HALF)]
    pair_label = remote(label_part, label_slots, r.pair_send.at[3], r.pair_recv.at[3], (other, chip))
    pair_label.start()
    own_label = local(label_part, label_slots, keep.at[5])
    own_label.start()
    pair_w.wait()
    pair_bias.wait()

    head_rows = 2 * depth
    row_at = lax.broadcasted_iota(jnp.int32, (head_rows, 128), 0)
    column_at = lanes(head_rows)

    def bias_row(columns, number):
        column = columns[:, number : number + 1]
        return column_sums(jnp.where(row_at == column_at, column, 0.0))

    rel = rel_all[...]
    bias_near = rel[:, 3 * NB : 4 * NB].astype(HIGH)
    bias_far = r.bias_far[...].astype(HIGH)
    bias_query, bias_value = (
        bias_row(bias_near, number) + turn(bias_row(bias_far, number)) for number in range(2)
    )
    weights = [w_all[n].reshape(width, 128) for n in range(3)]
    near, far_part = r.near, r.far_part
    pair_rows = 2 * slot_rows
    pair_half = lanes(pair_rows) < HD

    for pair in range(HALF // 2):
        tokens = x_all[2 * pair : 2 * pair + 2].reshape(pair_rows, width)
        query, key, value_rows = (
            pltpu.roll(dot(tokens, weights[n]), core * HD, 1) for n in range(3)
        )
        query, value_rows = query + bias_query, value_rows + bias_value
        rows = pl.ds(pl.multiple_of(core * HALF * slot_rows, 16) + pair * pair_rows, pair_rows)
        near[rows, 0:128] = jnp.where(pair_half, query, turn(value_rows)).astype(LOW)
        near[rows, 128:256] = key.astype(LOW)
        far_rows = slice(pair * pair_rows, (pair + 1) * pair_rows)
        far_part[far_rows, 0:128] = jnp.where(pair_half, turn(query), value_rows).astype(LOW)
        far_part[far_rows, 128:256] = turn(key).astype(LOW)
    pair_qkv = remote(
        far_part,
        near.at[pl.ds(pl.multiple_of(core * HALF * slot_rows, 16), HALF * slot_rows)],
        r.pair_send.at[4],
        r.pair_recv.at[4],
        (other, chip),
    )
    pair_qkv.start()

    meta = r.meta
    eye = (
        lax.broadcasted_iota(jnp.int32, (slot_rows, 256), 0)
        == lax.broadcasted_iota(jnp.int32, (slot_rows, 256), 1)
    ).astype(LOW)
    pair_label.wait()
    own_label.wait()
    for slot in range(CHIPS):
        meta[slot * slot_rows : (slot + 1) * slot_rows, 0:16] = dot(eye, labels[slot], NT)
    table_t = rel[:, 0 : 3 * NB]
    lane = lanes(BLOCK)
    first_half = lane < HD
    scale = 1.0 / math.sqrt(4.0 * HD)
    left, right, right_t = r.left, r.right, r.right_t
    value, value_t, kept = r.value, r.value_t, r.kept
    pair_qkv.wait()
    each(plans_in, Gather.own_line, 1)
    each(plans_in, Gather.side, None)

    def prepare(index, carry):
        rows = pl.ds(pl.multiple_of(index * BLOCK, BLOCK), BLOCK)
        at_steps(
            index,
            {
                3: [lambda: each(plans_down, Gather.side, None), lambda: each(plans_down, Gather.line, 1)],
                4: [lambda: each(plans_in, Gather.side, 0), lambda: each(plans_down, Gather.line, 0)],
            },
        )
        query_value = near[rows, 0:128].astype(HIGH)
        key = near[rows, 128:256].astype(HIGH)
        tables = dot(near[rows, 0:128][:, 0:HD], table_t).astype(LOW).astype(HIGH)
        ids = meta[rows, 8:12].astype(jnp.int32)
        segment, order, box_x, box_y = ids[:, 0:1], ids[:, 1:2], ids[:, 2:3], ids[:, 3:4]

        def selected(column, ids_of, values):
            bucket = jnp.clip(ids_of - values, -(NB // 2), NB // 2 - 1) + NB // 2
            return jnp.take_along_axis(tables[:, column * NB : (column + 1) * NB], bucket, axis=1)

        wide = selected(0, order, lane)
        narrow = jnp.where(first_half, selected(1, box_x, lane), selected(2, box_y, lane - HD))
        label = lane - HD
        query_side = jnp.where(
            first_half,
            query_value * scale,
            jnp.where(jnp.logical_and(label != segment, label < 8), MASKED, 0.0),
        )
        key_side = jnp.where(first_half, key, (label == segment).astype(HIGH))
        left[rows, 0:128] = (wide * scale).astype(LOW)
        left[rows, 128:256] = (narrow * scale).astype(LOW)
        left[rows, 256:384] = query_side.astype(LOW)
        order_hot = (lane == order).astype(HIGH)
        box_hot = (jnp.where(first_half, box_x, box_y + HD) == lane).astype(HIGH)
        right[rows, 0:128] = order_hot.astype(LOW)
        right[rows, 128:256] = box_hot.astype(LOW)
        right[rows, 256:384] = key_side.astype(LOW)
        right_t[0:128, rows] = order_hot.T.astype(LOW)
        right_t[128:256, rows] = box_hot.T.astype(LOW)
        right_t[256:384, rows] = key_side.T.astype(LOW)
        held = jnp.where(first_half, turn(query_value), (label == 0).astype(HIGH))
        value[rows, :] = held.astype(LOW)
        value_t[:, rows] = held.T.astype(LOW)
        return carry

    lax.fori_loop(0, total // BLOCK, prepare, 0)
    def attend(index, carry):
        rows = pl.ds(pl.multiple_of(index * BLOCK, BLOCK), BLOCK)
        at_steps(
            index,
            {
                1: [lambda: each(plans_in, Gather.line, 2)],
                5: [lambda: each(plans_in, Gather.line, 1)],
                6: [lambda: plan_out.late_line(0)],
            },
        )
        logits = dot(left[rows, :], right_t[...])
        top = jnp.max(logits, axis=1, keepdims=True)
        weights = jnp.exp(logits - top).astype(LOW)
        mixed = dot(weights, value[...])
        row_sum = mixed[:, HD : HD + 1]
        ids = meta[rows, 8:12]
        facts = jnp.where(lane == HD, top + jnp.log(row_sum), ids[:, 3:4])
        facts = jnp.where(lane == HD + 1, ids[:, 1:2], facts)
        facts = jnp.where(lane == HD + 2, ids[:, 2:3], facts)
        kept[rows, :] = jnp.where(first_half, mixed / row_sum, facts)
        return carry

    lax.fori_loop(0, total // BLOCK, attend, 0)
    message, context_in = r.message, r.context_in
    for slot in range(CHIPS):
        message[slot] = fold(kept[slot * slot_rows : (slot + 1) * slot_rows, :])
    context_arrives, context_sent = to_tokens(message, context_in, r.msg_send, r.msg_recv)
    each(plans_down, Gather.side, 1)
    each(plans_down, Gather.line, 2)
    plan_out.late_line(1)
    each(plans_down, Gather.side, 0)
    each(plans_in, Gather.side, 1)
    plan_out.late_line(2)

    shares, bias_in = r.shares, r.bias_in
    shares[core] = jnp.zeros(shares.shape[1:], HIGH)
    for slot in range(CHIPS):
        small = w_out[slot, depth : depth + 16, 0 : BIAS_AT + 128].astype(HIGH)[0:8]
        target = slice(slot * depth // 128 * 128, slot * depth // 128 * 128 + 128)
        for number in range(3):
            piece = jnp.where(lanes(8) < depth, small[:, number * 128 : number * 128 + 128], 0.0)
            if slot * depth % 128:
                piece = pltpu.roll(piece, slot * depth % 128, 1)
            shares[core, number, :, target] += piece
        bias_in[:, slot * 128 : slot * 128 + 128] = small[0:1, BIAS_AT : BIAS_AT + 128]
    pair_small = remote(
        shares.at[core], shares.at[core], r.pair_send.at[5], r.pair_recv.at[5], (other, chip)
    )
    pair_small.start()
    each(plans_in, Gather.side, 2)
    context_arrives()
    each(plans_down, Gather.side, 2)

    context_wide, context, low_first = r.context_wide, r.context, r.low_first
    act, slope = r.act, r.slope
    out_part, in_part = r.out_part, r.in_part
    own = pl.ds(pl.multiple_of(core * slot_rows, 16), slot_rows)
    far = pl.ds(pl.multiple_of(other * slot_rows, 16), slot_rows)
    tile = 512
    half_slot = slot_rows // 2
    count = [6]

    def swap(source, target):
        copy = remote(
            source, target, r.pair_send.at[count[0]], r.pair_recv.at[count[0]], (other, chip)
        )
        count[0] += 1
        copy.start()
        return copy

    left_half = lanes(half_slot) < HD
    for slot_group in range(2):
        for pair in range(HALF // 2):
            even = context_in[slot_group * HALF + 2 * pair].astype(HIGH)[:half_slot]
            odd = context_in[slot_group * HALF + 2 * pair + 1].astype(HIGH)[:half_slot]
            top = slot_group * slot_rows
            columns = slice(pair * 128, pair * 128 + 128)
            context_wide[top : top + half_slot, columns] = jnp.where(left_half, even, turn(odd))
            context_wide[top + half_slot : top + slot_rows, columns] = jnp.where(
                left_half, turn(even), odd
            )
    context[...] = context_wide[...].astype(LOW)

    def product(lhs, rhs):
        out_part[...] = dot(lhs[far, :], rhs)
        copy = swap(out_part, in_part)
        mine = dot(lhs[own, :], rhs)
        copy.wait()
        return mine + in_part[...]

    pair_small.wait()
    branch_bias, gains, shifts = (
        [jnp.concatenate([shares[0, number, k : k + 1], shares[1, number, k : k + 1]], axis=1) for k in range(2)]
        for number in range(3)
    )
    branch = product(context, w_out[:, 0:depth, :].reshape(half_width, width)) + branch_bias[0]
    row_index = lax.broadcasted_iota(jnp.int32, (slot_rows, 1), 0)
    x_mine = jnp.where(row_index < token_rows, x_own[...].astype(HIGH), 0.0)
    first, normed1, inverse1 = normalize(x_mine + branch, gains[0], shifts[0])
    low_first[own, :] = first.astype(LOW)
    copy = swap(low_first.at[own], low_first.at[own])
    each(plans_in, Gather.arrive)
    copy.wait()

    def widen(index, carry):
        columns = pl.ds(pl.multiple_of(index * tile, tile), tile)
        pre = dot(low_first[...], w_in[:, :, :, columns].reshape(width, tile)) + bias_in[:, columns]
        found, derivative = gelu_parts(pre)
        act[:, columns] = found.astype(LOW)
        slope[:, columns] = derivative
        return carry

    lax.fori_loop(0, half_hidden // tile, widen, 0)
    each(plans_down, Gather.arrive)
    second = product(act, w_down[...].reshape(half_hidden, width)) + branch_bias[1]
    result, normed2, inverse2 = normalize(first + second, gains[1], shifts[1])
    r.hidden_out[...] = result[:token_rows].astype(LOW)
    upstream = jnp.concatenate(
        [r.out_grad[...].astype(HIGH), jnp.zeros((slot_rows - token_rows, width), HIGH)], axis=0
    )
    d_sum2 = normalize_back(upstream, normed2, inverse2, gains[1])
    low_second = d_sum2.astype(LOW)
    d_second, small_sum = r.d_second, r.small_sum
    d_second[own, :] = low_second
    copy = swap(d_second.at[own], d_second.at[own])
    small_sum[...] = jnp.zeros_like(small_sum)
    small_sum[1:2, :] = column_sums(low_second.astype(HIGH))
    small_sum[3:4, :] = column_sums(upstream * normed2)
    small_sum[5:6, :] = column_sums(upstream)

    half_total = HALF * slot_rows
    def half_sums(ref, pick, wide, stages, sends, recvs):
        return [
            Reduce(
                ref,
                lambda held, slot, part=part: pick(held, slot, pl.ds(part * wide, wide)),
                [stage.at[part] for stage in stages],
                sends.at[part],
                recvs.at[part],
                across,
            )
            for part, across in enumerate("xy")
        ]

    sums_down = half_sums(
        w_down,
        lambda held, slot, columns: held.at[slot, :, columns],
        half,
        (r.down_1, r.down_2, r.down_3),
        r.g_down_send,
        r.g_down_recv,
    )
    sums_in = half_sums(
        w_in,
        lambda held, slot, columns: held.at[:, slot, :, columns],
        half_tile,
        (r.in_1, r.in_2, r.in_3),
        r.g_in_send,
        r.g_in_recv,
    )
    sum_out = ReduceEarly(
        r.g_out,
        lambda ref, slot: ref.at[slot],
        [r.out_1, r.out_2, r.out_3],
        r.g_out_send,
        r.g_out_recv,
        "y",
    )

    d_inner = act
    each(plans_in + plans_down, Gather.finish)
    copy.wait()
    slots = tile // w_down.shape[1]

    def narrow_back(index, carry):
        columns = pl.ds(pl.multiple_of(index * tile, tile), tile)
        rows = pl.ds(index * slots, slots)
        low = (dot(d_second[...], w_down[rows].reshape(tile, width), NT) * slope[:, columns]).astype(LOW)
        turns = width // tile
        bias_sums = column_sums(low.astype(HIGH))
        bias_columns = pl.ds(pl.multiple_of(lax.rem(index, turns) * tile, tile), tile)
        for row in range(half_hidden // width):

            @pl.when(lax.div(index, turns) == row)
            def _():
                small_sum[6 + row : 7 + row, bias_columns] = bias_sums

        w_down[rows] = (
            dot(act[:, columns], d_second[...], TN).astype(LOW).reshape(slots, tile // slots, width)
        )
        d_inner[:, columns] = low
        return carry

    lax.fori_loop(0, half_hidden // tile, narrow_back, 0)
    each(sums_down, Reduce.start, 1)
    w_in_all = w_in[...].reshape(width, half_hidden)
    out_part[...] = dot(d_inner[far, :], w_in_all, NT)
    copy = swap(out_part, in_part)
    mine = dot(d_inner[own, :], w_in_all, NT)
    slots_in = 256 // depth

    def widen_grad(index, carry):
        rows = pl.ds(pl.multiple_of(index * 256, 256), 256)
        parts = CHIPS // slots_in
        w_in[lax.div(index, parts), pl.ds(lax.rem(index, parts) * slots_in, slots_in)] = (
            dot(low_first[:, rows], d_inner[...], TN).astype(LOW).reshape(slots_in, depth, half_hidden)
        )
        return carry

    lax.fori_loop(0, width // 256, widen_grad, 0)
    copy.wait()
    d_first = d_sum2 + mine + in_part[...]
    d_sum1 = normalize_back(d_first, normed1, inverse1, gains[0])
    low_branch = d_sum1.astype(LOW)
    d_branch = d_second
    d_branch[own, :] = low_branch
    copy = swap(d_branch.at[own], d_branch.at[own])
    out_part[...] = d_sum1
    small_sum[0:1, :] = column_sums(low_branch.astype(HIGH))
    small_sum[2:3, :] = column_sums(d_first * normed1)
    small_sum[4:5, :] = column_sums(d_first)
    copy.wait()
    context_wide[...] = dot(d_branch[...], w_out[:, 0:depth, :].reshape(half_width, width), NT)
    d_message, d_arrived = context_in, r.d_arrived
    for slot_group in range(2):
        for pair in range(HALF // 2):
            both = context_wide[
                slot_group * slot_rows : (slot_group + 1) * slot_rows, pair * 128 : pair * 128 + 128
            ]
            d_message[slot_group * HALF + 2 * pair] = fold(both)
            d_message[slot_group * HALF + 2 * pair + 1] = fold(turn(both))
    grad_arrives, grad_sent = to_heads(d_message, d_arrived, r.d_send, r.d_recv)
    r.g_out[...] = dot(context[...], d_branch[...], TN).astype(LOW).reshape(r.g_out.shape)

    z, y, x = coordinates(chip)
    small_in = r.small_in

    def small_copy(index, to_core, to_chip):
        return remote(
            small_sum, small_in.at[index], r.small_send.at[index], r.small_recv.at[index], (to_core, to_chip)
        )

    def small_turn(index):
        if index == 0:
            return [small_copy(0, other, chip)]
        if index == 1:
            return [small_copy(1, core, z * 4 + (1 - y) * 2 + x)]
        if index == 2:
            return [small_copy(2, core, z * 4 + y * 2 + 1 - x)]
        return [
            small_copy(2 + ahead, core, lax.rem(z + ahead, 4) * 4 + y * 2 + x) for ahead in (1, 2, 3)
        ]

    def small_start(index):
        for copy in small_turn(index):
            copy.start()

    def small_end(index):
        for copy in small_turn(index):
            copy.wait()
        if index == 0:
            small_sum[0:6, :] += small_in[0, 0:6, :]
        elif index < 3:
            small_sum[...] += small_in[index]

    each(sums_down, Reduce.start, None)
    each(sums_in, Reduce.start, 2)
    each(sums_down, Reduce.side, 1)
    small_start(0)
    each(sums_down, Reduce.start, 2)
    small_end(0)
    small_start(1)
    sum_out.start()
    each(sums_down, Reduce.side, 2)
    each(sums_down, Reduce.start, 0)
    each(sums_in, Reduce.side, 2)
    d_context = meta
    grad_arrives()
    for slot in range(CHIPS):
        both = d_arrived[slot].astype(HIGH)[:half_slot]
        top = slot * slot_rows
        d_context[top : top + half_slot, :] = jnp.where(left_half, both, 0.0)
        d_context[top + half_slot : top + slot_rows, :] = jnp.where(left_half, turn(both), 0.0)
    d_heads, d_pair_t, rel_grad = r.d_heads, r.d_pair_t, r.rel_grad
    d_pair_t[...] = jnp.zeros_like(d_pair_t)
    rel_grad[...] = jnp.zeros_like(rel_grad)

    def step(index, carry):
        rows = pl.ds(pl.multiple_of(index * BLOCK, BLOCK), BLOCK)
        at_steps(
            index,
            {
                1: [lambda: small_end(1)],
                2: [
                    lambda: small_start(2),
                    lambda: each(sums_in, Reduce.start, None),
                    lambda: each(sums_down, Reduce.line, 2),
                ],
                3: [
                    lambda: each(sums_down, Reduce.side, 0),
                    lambda: each(sums_in, Reduce.start, 1),
                    lambda: small_end(2),
                    lambda: each(sums_in, Reduce.line, 2),
                ],
                4: [lambda: small_start(3)],
                6: [lambda: each(sums_down, Reduce.line, 0), lambda: each(sums_in, Reduce.side, 1)],
                7: [
                    lambda: each(sums_in, Reduce.start, 0),
                    lambda: each(sums_down, Reduce.line, 1),
                    sum_out.third,
                ],
                8: [lambda: each(sums_in, Reduce.line, 1)],
            },
        )
        facts = kept[rows, :]
        grad = d_context[rows, :]
        delta = jnp.sum(grad * facts, axis=1, keepdims=True)
        probs = jnp.exp(dot(left[rows, :], right_t[...]) - facts[:, HD : HD + 1])
        d_probs = dot(grad.astype(LOW), value_t[...])
        d_logits = (probs * (d_probs - delta)).astype(LOW)
        query_t = jnp.where(first_half, left[rows, 256:384].astype(HIGH), 0.0).T[0:HD]
        d_pair_t[0:HD, :] += dot(query_t.astype(LOW), d_logits)
        d_pair_t[HD : 2 * HD, :] += dot(grad.T[0:HD].astype(LOW), probs.astype(LOW))
        back = dot(d_logits, right[...]) * scale
        ids = facts.astype(jnp.int32)
        order, box_x, box_y = (ids[:, HD + k : HD + k + 1] for k in (1, 2, 3))

        def placed(column, ids_of, extent, start):
            found_at = ids_of + NB // 2 - lane
            found = jnp.take_along_axis(
                back[:, column * 128 : column * 128 + 128], jnp.clip(found_at, 0, extent - 1) + start, axis=1
            )
            return jnp.where(jnp.logical_and(found_at >= 0, found_at < extent), found, 0.0)

        wide = back[:, 0:128]
        low_end = jnp.sum(jnp.where(lane >= order + NB // 2, wide, 0.0), axis=1, keepdims=True)
        high_end = jnp.sum(jnp.where(lane <= order - (NB // 2 - 1), wide, 0.0), axis=1, keepdims=True)
        first = placed(0, order, ORDER_RANGE, 0)
        first = jnp.where(lane == 0, low_end, jnp.where(lane == NB - 1, high_end, first))
        d_tables = jnp.concatenate(
            [first, placed(1, box_x, BOX_RANGE, 0), placed(1, box_y, BOX_RANGE, BOX_RANGE)], axis=1
        ).astype(LOW)
        from_tables = dot(d_tables, table_t, NT)
        d_query = back[:, 256:384] + jnp.concatenate([from_tables, from_tables], axis=1)
        d_heads[0, :, rows] = d_query.T[0:HD].astype(LOW)
        rel_grad[:, 0 : 3 * NB] += dot((query_t / scale).astype(LOW), d_tables)
        return carry

    lax.fori_loop(0, total // BLOCK, step, 0)

    d_heads[1] = d_pair_t[0:HD, :].astype(LOW)
    d_heads[2] = d_pair_t[HD : 2 * HD, :].astype(LOW)
    d_both = r.d_both
    near_part = pl.ds(pl.multiple_of(core * half_total, 128), half_total)
    far_part = pl.ds(pl.multiple_of(other * half_total, 128), half_total)
    copy = swap(d_heads.at[:, :, far_part], d_both.at[:, core])
    d_both[:, core] = d_heads[:, :, near_part]
    sums = [jnp.sum(d_heads[n].astype(HIGH), axis=1, keepdims=True) for n in (0, 2)]
    rel_grad[:, 3 * NB : 4 * NB] = jnp.where(
        lanes(HD) == 0, sums[0], jnp.where(lanes(HD) == 1, sums[1], 0.0)
    )
    head = 2 * position + core
    rel_came = r.rel_came

    def d_rel_each(act_remote, act_own):
        for side in range(2):
            to = (lax.div(position, 4), lax.rem(2 * head + side, CHIPS))
            itself = jnp.logical_and(to[0] == core, to[1] == chip)
            source = rel_grad.at[pl.ds(side * depth, depth)]
            act = lambda: act_remote(
                remote(source, rel_came.at[group], r.d_rel_send.at[side], r.d_rel_recv.at[group], to)
            )
            pl.when(jnp.logical_not(itself))(act)
            if act_own:
                pl.when(itself)(lambda: local(source, rel_came.at[group], r.d_rel_recv.at[group]).start())

    d_rel_each(lambda copy: copy.start(), True)
    copy.wait()
    d_columns = d_both[...].reshape(6 * HD, half_total)

    w_grad = dot(d_columns, x_all[...].reshape(half_total, width))

    w_heads = jnp.concatenate([w_all[n].reshape(width, 128) for n in range(3)], axis=1)
    d_rows = d_columns.T
    d_x = x_all
    each(x_plans, CubeGather.finish)
    for pair in range(HALF // 2):
        d_x[2 * pair : 2 * pair + 2] = (
            dot(d_rows[pair * pair_rows : (pair + 1) * pair_rows], w_heads, NT)
            .astype(LOW)
            .reshape(2, slot_rows, width)
        )
    d_x_plans = [
        CubeReduce(
            lambda slot, part=part: d_x.at[slot, pl.ds(part * third, third)],
            r.x_stage.at[part],
            r.d_x_send.at[part],
            r.d_x_recv.at[part],
            order,
        )
        for part, order in enumerate(("xyz", "yzx", "zxy"))
    ]
    each(d_x_plans, CubeReduce.own)
    small_end(3)

    w_mine, w_far, w_low, w_came = slope, r.w_far, r.w_low, r.w_came
    w_rows = 3 * HD
    for part in range(2):
        w_mine[0:w_rows, part * width : (part + 1) * width] = w_grad[part * w_rows : (part + 1) * w_rows]

    def w_columns(part, half):
        return pl.ds(pl.multiple_of(part * width + half * half_width, 128), half_width)

    w_swaps = [
        swap(w_mine.at[pl.ds(0, w_rows), w_columns(part, other)], w_far.at[part]) for part in range(2)
    ]
    each(sums_in, Reduce.side, 0)
    each(d_x_plans, CubeReduce.one)
    for copy in w_swaps:
        copy.wait()
    w_sum = jnp.concatenate(
        [(w_mine[0:w_rows, w_columns(part, core)] + w_far[part]).T for part in range(2)], axis=1
    )
    for slot in range(CHIPS):
        w_low[slot] = w_sum[slot * depth : (slot + 1) * depth].astype(LOW)

    def d_w_copy(ahead):
        to = lax.rem(chip + ahead, CHIPS)
        return remote(w_low.at[to], w_came.at[chip], r.d_w_send.at[0], r.d_w_recv.at[0], (core, to))

    own_d_w = local(w_low.at[chip], w_came.at[chip], keep.at[6])
    own_d_w.start()
    for ahead in range(1, CHIPS):
        d_w_copy(ahead).start()
    sum_out.across()
    each(d_x_plans, CubeReduce.two)
    each(sums_in, Reduce.line, 0)
    each(sums_down, Reduce.side, None)
    each(sums_in, Reduce.side, None)
    x_total, x_came = x_own, r.x_came
    back_part = lambda part: pl.ds(part * third, third)
    back = lambda part: local(
        x_total.at[back_part(part)], x_came.at[back_part(part)], r.back_recv.at[part]
    )
    back_abroad = lambda part: remote(
        x_total.at[back_part(part)],
        x_came.at[back_part(part)],
        r.back_send.at[part],
        r.back_recv.at[part],
        (other, away),
    )
    for part, plan in enumerate(d_x_plans):
        x_total[part * third : (part + 1) * third] = plan.arrive().astype(LOW)
        pl.when(at_home)(lambda: back(part).start())
        pl.when(jnp.logical_not(at_home))(lambda: back_abroad(part).start())
    for part, plan in enumerate(sums_down):
        plan.finish(r.down_grad.at[:, pl.ds(part * half, half)])
    sum_out.finish(r.out_w_grad)
    in_total, in_far = r.in_total, r.in_far
    for part, plan in enumerate(sums_in):
        plan.finish(in_total.at[:, :, pl.ds(part * half_tile, half_tile)])
    in_pair = swap(in_total.at[other], in_far)

    in_grad = r.in_grad
    in_grad[:, columns_of(core, half_hidden)] = in_total[core]
    me = core * CHIPS + chip
    small_all = lambda rows, columns: (
        small_sum[rows, columns] + small_in[3, rows, columns] + small_in[4, rows, columns] + small_in[5, rows, columns]
    )
    strip = columns_of(lax.div(me * depth, 128), 128)
    shares = pltpu.roll(small_all(pl.ds(0, 8), strip), 128 - lax.rem(me * depth, 128), 1)
    for number, result in enumerate((r.branch_grad, r.gain_grad, r.shift_grad)):
        result[...] = shares[2 * number : 2 * number + 2, 0:depth]
    bias_strip = small_all(pl.ds(0, 8), columns_of(position, 128))
    r.bias_grad[...] = jnp.where(group == 0, bias_strip[6:7], bias_strip[7:8])
    for slot in range(2):
        local(rel_grad.at[pl.ds(0, depth)], rel_came.at[slot], r.d_rel_recv.at[slot]).wait()
    d_rel_each(lambda copy: copy.wait_send(), False)
    rel_total = rel_came[0] + rel_came[1]
    for kind in range(3):
        r.rel_tables_grad[kind] = rel_total[:, kind * NB : (kind + 1) * NB]
    r.qkv_bias_grad[...] = rel_total[:, 3 * NB : 4 * NB].T[0:2]
    own_d_w.wait()
    w_came_most = w_came.at[pl.ds(0, CHIPS - 1)]
    local(w_came_most, w_came_most, r.d_w_recv.at[0]).wait()
    local(w_came_most, w_came_most, r.d_w_send.at[0]).wait()
    for pair in range(HALF):
        both = w_came[pair].astype(HIGH) + w_came[HALF + pair].astype(HIGH)
        for n in range(3):
            r.qkv_grad[n, :, pair * 128 : pair * 128 + 128] = both[:, n * 128 : n * 128 + 128]
    for part in range(3):
        back(part).wait()
        pl.when(jnp.logical_not(at_home))(lambda: back_abroad(part).wait_send())
    r.hidden_grad[...] = (out_part[...] + x_came[...].astype(HIGH))[:token_rows].astype(LOW)
    in_pair.wait()
    in_grad[:, columns_of(other, half_hidden)] = in_far[...]
    grad_sent()
    each(d_x_plans, CubeReduce.finish)
    local(w_most, w_most, r.w_send.at[0]).wait()
    rel_each(lambda copy: copy.wait_send(), None)
    context_sent()
    plan_out.finish()


def hand_over(count, *refs):
    for source, target in zip(refs[:count], refs[count:]):
        target[...] = source[...]


def handed_over(arrays):
    return pl.pallas_call(
        functools.partial(hand_over, len(arrays)),
        out_shape=[jax.ShapeDtypeStruct(array.shape, array.dtype) for array in arrays],
        name="hand_over",
    )(*arrays)


def call(kernel, name, number, inputs, outputs, scratch):
    names = list(inputs) + list(outputs) + list(scratch)
    results = pl.pallas_call(
        functools.partial(kernel, names),
        out_shape=[jax.ShapeDtypeStruct(shape, dtype) for shape, dtype, _ in outputs.values()],
        in_specs=[pl.BlockSpec(memory_space=space) for _, space in inputs.values()],
        out_specs=[pl.BlockSpec(memory_space=space) for _, _, space in outputs.values()],
        scratch_shapes=list(scratch.values()),
        compiler_params=pltpu.CompilerParams(
            collective_id=number, has_side_effects=True, vmem_limit_bytes=VMEM_LIMIT
        ),
        name=name,
    )(*(array for array, _ in inputs.values()))
    return types.SimpleNamespace(**dict(zip(outputs, results)))


def head_shards(
    hidden_in,
    segment_ids,
    order_ids,
    box_ids,
    qkv_weight,
    qkv_bias,
    rel_tables,
    out_weight,
    branch_bias,
    norm_gains,
    norm_shifts,
    ffn_in,
    ffn_in_bias,
    ffn_out,
    out_grad,
):
    rows, width = hidden_in.shape
    slot_rows = -(-rows // 48) * 48
    total = CHIPS * slot_rows
    depth = qkv_weight.shape[1]
    hidden = ffn_in.shape[1]
    half_hidden, half_width = hidden // 2, width // 2
    down_rows = ffn_out.shape[0]
    both = 2 * slot_rows
    fold_rows = -(-(slot_rows // 2) // 16) * 16
    any_, vmem, dma = pl.ANY, pltpu.VMEM, pltpu.SemaphoreType.DMA
    message = (CHIPS, fold_rows, 128)
    x_block, w_block = (HALF, slot_rows, width), (3, 2, CHIPS, depth, 128)
    in_all, down_all = (2, CHIPS, depth, half_hidden), (CHIPS, down_rows, width)
    out_all = (CHIPS, depth + 16, width)
    in_half, down_half = (2, depth, half_hidden // 2), (down_rows, half_width)
    in_block, out_block = (2, depth, half_hidden), (depth, width)
    made = call(
        layer_kernel,
        "layer",
        0,
        dict(
            hidden_in=(hidden_in, vmem),
            segment_ids=(segment_ids.reshape(1, rows), vmem),
            order_ids=(order_ids.reshape(1, rows), vmem),
            box_ids=(box_ids, vmem),
            qkv_weight=(qkv_weight, vmem),
            qkv_bias=(qkv_bias, vmem),
            rel_tables=(rel_tables.transpose(0, 2, 1), vmem),
            out_weight=(out_weight, any_),
            branch_bias=(branch_bias, vmem),
            norm_gains=(norm_gains, vmem),
            norm_shifts=(norm_shifts, vmem),
            ffn_in=(ffn_in, any_),
            ffn_in_bias=(ffn_in_bias.reshape(1, down_rows), vmem),
            ffn_out=(ffn_out, any_),
            out_grad=(out_grad, vmem),
        ),
        dict(
            hidden_out=((rows, width), LOW, vmem),
            hidden_grad=((rows, width), LOW, vmem),
            qkv_grad=((3, depth, width), HIGH, vmem),
            qkv_bias_grad=((2, depth), HIGH, vmem),
            rel_tables_grad=((3, depth, NB), HIGH, vmem),
            out_w_grad=((depth, width), HIGH, vmem),
            branch_grad=((2, depth), HIGH, vmem),
            gain_grad=((2, depth), HIGH, vmem),
            shift_grad=((2, depth), HIGH, vmem),
            in_grad=((depth, hidden), HIGH, vmem),
            bias_grad=((1, down_rows), HIGH, vmem),
            down_grad=((down_rows, width), HIGH, vmem),
        ),
        dict(
            x_own=vmem((slot_rows, width), LOW),
            x_all=vmem(x_block, LOW),
            extra=vmem((slot_rows - rows, width), HIGH),
            small_own=vmem((16, width), LOW),
            w_all=vmem(w_block, LOW),
            rel_own=vmem((depth, 4 * NB), LOW),
            rel_all=vmem((2 * depth, 4 * NB), LOW),
            bias_far=vmem((2 * depth, NB), LOW),
            labels=vmem((CHIPS, 16, 256), LOW),
            near=vmem((total, 256), LOW),
            far_part=vmem((total // 2, 256), LOW),
            w_in=vmem(in_all, LOW),
            w_down=vmem(down_all, LOW),
            w_out=vmem(out_all, LOW),
            meta=vmem((total, 128), HIGH),
            shares=vmem((2, 3, 8, half_width), HIGH),
            bias_in=vmem((1, half_hidden), HIGH),
            left=vmem((total, 384), LOW),
            right=vmem((total, 384), LOW),
            right_t=vmem((384, total), LOW),
            value=vmem((total, 128), LOW),
            value_t=vmem((128, total), LOW),
            kept=vmem((total, 128), HIGH),
            message=vmem(message, LOW),
            context_in=vmem(message, LOW),
            context_wide=vmem((both, half_width), HIGH),
            context=vmem((both, half_width), LOW),
            low_first=vmem((both, width), LOW),
            act=vmem((both, half_hidden), LOW),
            slope=vmem((both, half_hidden), HIGH),
            out_part=vmem((slot_rows, width), HIGH),
            in_part=vmem((slot_rows, width), HIGH),
            d_second=vmem((both, width), LOW),
            g_out=vmem((CHIPS,) + out_block, LOW),
            in_1=vmem((2, 8) + in_half, LOW),
            in_2=vmem((2, 4) + in_half, LOW),
            in_3=vmem((2, 3) + in_half, LOW),
            down_1=vmem((2, 8) + down_half, LOW),
            down_2=vmem((2, 4) + down_half, LOW),
            down_3=vmem((2, 3) + down_half, LOW),
            out_1=vmem((3, 4) + out_block, LOW),
            out_2=vmem((2,) + out_block, LOW),
            out_3=vmem((1,) + out_block, LOW),
            in_total=vmem(in_block, HIGH),
            in_far=vmem((depth, half_hidden), HIGH),
            small_sum=vmem((8, width), HIGH),
            small_in=vmem((6, 8, width), HIGH),
            d_arrived=vmem(message, LOW),
            d_heads=vmem((3, HD, total), LOW),
            d_pair_t=vmem((2 * HD, total), HIGH),
            d_both=vmem((3, 2, HD, total // 2), LOW),
            x_stage=vmem((3, 7, slot_rows // 3, width), LOW),
            x_came=vmem((slot_rows, width), LOW),
            rel_grad=vmem((2 * depth, 4 * NB), HIGH),
            rel_came=vmem((2, depth, 4 * NB), HIGH),
            w_far=vmem((2, 3 * HD, half_width), HIGH),
            w_low=vmem((CHIPS, depth, 6 * HD), LOW),
            w_came=vmem((CHIPS, depth, 6 * HD), LOW),
            keep_sem=dma((7,)),
            home_sem=dma((2,)),
            back_send=dma((3,)),
            back_recv=dma((3,)),
            x_send=dma((3, CubeGather.SENDS)),
            x_recv=dma((3, CubeGather.RECEIVES)),
            w_send=dma((1,)),
            w_recv=dma((1,)),
            rel_send=dma((2,)),
            rel_recv=dma((2,)),
            out_send=dma((GatherLate.SENDS,)),
            out_recv=dma((GatherLate.RECEIVES,)),
            in_send=dma((2, Gather.SENDS)),
            in_recv=dma((2, Gather.RECEIVES)),
            down_send=dma((2, Gather.SENDS)),
            down_recv=dma((2, Gather.RECEIVES)),
            msg_send=dma((1,)),
            msg_recv=dma((1,)),
            d_send=dma((1,)),
            d_recv=dma((1,)),
            g_in_send=dma((2, Reduce.SENDS)),
            g_in_recv=dma((2, Reduce.RECEIVES)),
            g_down_send=dma((2, Reduce.SENDS)),
            g_down_recv=dma((2, Reduce.RECEIVES)),
            g_out_send=dma((ReduceEarly.SENDS,)),
            g_out_recv=dma((ReduceEarly.RECEIVES,)),
            small_send=dma((6,)),
            small_recv=dma((6,)),
            d_x_send=dma((3, CubeReduce.SENDS)),
            d_x_recv=dma((3, CubeReduce.RECEIVES)),
            d_w_send=dma((1,)),
            d_w_recv=dma((1,)),
            d_rel_send=dma((2,)),
            d_rel_recv=dma((2,)),
            pair_send=dma((16,)),
            pair_recv=dma((16,)),
        ),
    )
    results = list(
        handed_over(
            [
                made.hidden_out,
                made.hidden_grad,
                made.qkv_grad,
                made.qkv_bias_grad,
                made.rel_tables_grad,
                made.out_w_grad,
                made.branch_grad,
                made.gain_grad,
                made.shift_grad,
                made.in_grad,
                made.bias_grad,
                made.down_grad,
            ]
        )
    )
    results[4] = results[4].transpose(0, 2, 1)
    results[10] = results[10].reshape(down_rows)
    return tuple(results)


def solution(mesh):
    by_heads = mesh.shape["grp"] == 2 and mesh.shape["blk"] == CHIPS == H
    return jax.shard_map(
        head_shards if by_heads else shards,
        mesh=mesh,
        in_specs=(
            P(("grp", "blk"), None),
            P(("grp", "blk")),
            P(("grp", "blk")),
            P(None, ("grp", "blk")),
            P(None, ("grp", "blk"), None),
            P(None, ("grp", "blk")),
            P(None, None, ("grp", "blk")),
            P(("grp", "blk"), None),
            P(None, ("grp", "blk")),
            P(None, ("grp", "blk")),
            P(None, ("grp", "blk")),
            P(("grp", "blk"), None),
            P(("grp", "blk")),
            P(("grp", "blk"), None),
            P(("grp", "blk"), None),
        ),
        out_specs=(
            P(("grp", "blk"), None),
            P(("grp", "blk"), None),
            P(None, ("grp", "blk"), None),
            P(None, ("grp", "blk")),
            P(None, None, ("grp", "blk")),
            P(("grp", "blk"), None),
            P(None, ("grp", "blk")),
            P(None, ("grp", "blk")),
            P(None, ("grp", "blk")),
            P(("grp", "blk"), None),
            P(("grp", "blk")),
            P(("grp", "blk"), None),
        ),
        check_vma=False,
    )
```

```python
import functools
import math
import types

import jax
import jax.numpy as jnp
from jax import lax
from jax.experimental import pallas as pl
from jax.experimental.pallas import tpu as pltpu
from jax.sharding import PartitionSpec as P

H = 16
HD = 64
NB = 128
ORDER_RANGE = 128
BOX_RANGE = 64


NEGATIVE = -1e30
EPSILON = 1e-05


def shifted(x, axis, by):
    devices = lax.axis_size(axis)
    return lax.ppermute(x, axis, [(i, (i + by) % devices) for i in range(devices)])


def block_size(row_count):
    chosen = 1
    for option in range(1, min(row_count, 544) + 1):
        if row_count % option == 0:
            chosen = option
    return chosen


def kind_ranges():
    return (ORDER_RANGE, BOX_RANGE, BOX_RANGE)


def query_maps(layout_ids):
    maps_out = []
    for column, extent in enumerate(kind_ranges()):
        offsets = layout_ids[:, column][:, None] - jnp.arange(extent, dtype=jnp.int32)[None, :]
        bucket = jnp.clip(offsets, -(NB // 2), NB // 2 - 1) + NB // 2
        maps_out.append(bucket[:, :, None] == jnp.arange(NB, dtype=jnp.int32)[None, None, :])
    return maps_out


def key_onehot(key_ids):
    pieces_out = []
    for column, extent in enumerate(kind_ranges()):
        pieces_out.append(
            key_ids[:, column + 1][:, None] == jnp.arange(extent, dtype=jnp.int32)[None, :]
        )
    return jnp.concatenate(pieces_out, axis=1).astype(jnp.bfloat16)


def norm_forward(values_in, norm_gain, norm_shift):
    center = values_in - jnp.mean(values_in, axis=-1, keepdims=True)
    inverse = lax.rsqrt(jnp.mean(center * center, axis=-1, keepdims=True) + EPSILON)
    normed = center * inverse
    return (normed * norm_gain + norm_shift, normed, inverse)


def norm_backward(upstream, normed, inverse, norm_gain):
    scaled = upstream * norm_gain
    inner_part = (
        scaled
        - jnp.mean(scaled, axis=-1, keepdims=True)
        - normed * jnp.mean(scaled * normed, axis=-1, keepdims=True)
    )
    return (inner_part * inverse, jnp.sum(upstream * normed, axis=0), jnp.sum(upstream, axis=0))


def block_logits(query_heads, selector, query_seg, key_part, meta_part, scaling):
    key_ids = meta_part.astype(jnp.int32)
    row_count = key_part.shape[0]
    key_heads = key_part.reshape(row_count, H, HD)
    content = jnp.einsum("thd,khd->htk", query_heads, key_heads, preferred_element_type=jnp.float32)
    onehot = key_onehot(key_ids)
    rel_bias = jnp.einsum("thv,kv->htk", selector, onehot, preferred_element_type=jnp.float32)
    allowed = query_seg[:, None] == key_ids[None, :, 0]
    logits = jnp.where(allowed[None], (content + rel_bias) * scaling, NEGATIVE)
    return (logits, allowed, onehot, key_heads)


def over_blocks(advance, carry, piece, start):
    row_count = piece[0].shape[0]
    stride = block_size(row_count)

    def one_step(block_index, running):
        portion = tuple(
            (lax.dynamic_slice_in_dim(member, block_index * stride, stride, 0) for member in piece)
        )
        return advance(running, portion, start + block_index * stride)

    return lax.fori_loop(0, row_count // stride, one_step, carry)


def shards(
    hidden_in,
    segment_ids,
    order_ids,
    box_ids,
    qkv_weight,
    qkv_bias,
    rel_tables,
    out_weight,
    branch_bias,
    norm_gains,
    norm_shifts,
    ffn_in,
    ffn_in_bias,
    ffn_out,
    out_grad,
):
    gathered = (
        lax.all_gather(qkv_weight, ("grp", "blk"), axis=1, tiled=True),
        lax.all_gather(qkv_bias, ("grp", "blk"), axis=1, tiled=True),
        lax.all_gather(rel_tables, ("grp", "blk"), axis=2, tiled=True),
        lax.all_gather(out_weight, ("grp", "blk"), axis=0, tiled=True),
        lax.all_gather(branch_bias, ("grp", "blk"), axis=1, tiled=True),
        lax.all_gather(norm_gains, ("grp", "blk"), axis=1, tiled=True),
        lax.all_gather(norm_shifts, ("grp", "blk"), axis=1, tiled=True),
        lax.all_gather(ffn_in, ("grp", "blk"), axis=0, tiled=True),
        lax.all_gather(ffn_in_bias, ("grp", "blk"), axis=0, tiled=True),
        lax.all_gather(ffn_out, ("grp", "blk"), axis=0, tiled=True),
    )
    w_qkv, b_qkv, w_rel, w_out, b_branch, gains, shifts, w_in, b_in, w_down = gathered
    row_count = hidden_in.shape[0]
    width = hidden_in.shape[1]
    scaling = 1.0 / math.sqrt(4.0 * HD)
    select_width = ORDER_RANGE + 2 * BOX_RANGE
    projected = jnp.einsum("td,cde->cte", hidden_in, w_qkv, preferred_element_type=jnp.float32)
    bias_qkv = b_qkv.astype(jnp.float32)
    query_rows = (projected[0] + bias_qkv[0]).astype(jnp.bfloat16)
    key_rows = projected[1].astype(jnp.bfloat16)
    value_rows = (projected[2] + bias_qkv[1]).astype(jnp.bfloat16)
    layout_ids = jnp.stack([order_ids, box_ids[0], box_ids[1]], axis=1)
    key_meta = jnp.stack([segment_ids, order_ids, box_ids[0], box_ids[1]], axis=1).astype(
        jnp.bfloat16
    )
    query_heads = query_rows.reshape(row_count, H, HD)
    rel_heads = w_rel.reshape(3, NB, H, HD)
    tables = jnp.einsum(
        "thd,nbhd->thnb", query_heads, rel_heads, preferred_element_type=jnp.float32
    ).astype(jnp.bfloat16)
    maps_list = query_maps(layout_ids)
    selector = jnp.concatenate(
        [
            jnp.einsum(
                "thb,tvb->thv",
                tables[:, :, column],
                maps_list[column].astype(jnp.bfloat16),
                preferred_element_type=jnp.float32,
            )
            for column in range(3)
        ],
        axis=2,
    ).astype(jnp.bfloat16)

    def forward_step(running, portion, offset):
        row_top, row_total, weighted = running
        key_part, value_part, meta_part = portion
        logits, allowed, onehot, key_heads = block_logits(
            query_heads, selector, segment_ids, key_part, meta_part, scaling
        )
        new_top = jnp.maximum(row_top, jnp.max(logits, axis=2))
        rescale = jnp.exp(row_top - new_top)
        weights = jnp.where(allowed[None], jnp.exp(logits - new_top[:, :, None]), 0.0)
        value_heads = value_part.reshape(value_part.shape[0], H, HD)
        weighted = weighted * rescale.T[:, :, None] + jnp.einsum(
            "htk,khd->thd",
            weights.astype(jnp.bfloat16),
            value_heads,
            preferred_element_type=jnp.float32,
        )
        return (new_top, row_total * rescale + jnp.sum(weights, axis=2), weighted)

    start_state = (
        jnp.full((H, row_count), NEGATIVE, jnp.float32),
        jnp.zeros((H, row_count), jnp.float32),
        jnp.zeros((row_count, H, HD), jnp.float32),
    )
    row_top, row_total, weighted = over_blocks(
        forward_step,
        start_state,
        (
            lax.all_gather(key_rows, "blk", axis=0, tiled=True),
            lax.all_gather(value_rows, "blk", axis=0, tiled=True),
            lax.all_gather(key_meta, "blk", axis=0, tiled=True),
        ),
        jnp.int32(0),
    )
    context_full = weighted / row_total.T[:, :, None]
    log_total = row_top + jnp.log(row_total)
    context = context_full.reshape(row_count, width).astype(jnp.bfloat16)
    branch = jnp.dot(context, w_out, preferred_element_type=jnp.float32) + b_branch[0].astype(
        jnp.float32
    )
    first, normed_one, inverse_one = norm_forward(
        hidden_in.astype(jnp.float32) + branch,
        gains[0].astype(jnp.float32),
        shifts[0].astype(jnp.float32),
    )
    first_low = first.astype(jnp.bfloat16)
    inner_pre = jnp.dot(first_low, w_in, preferred_element_type=jnp.float32) + b_in.astype(
        jnp.float32
    )
    activated, gelu_pull = jax.vjp(
        lambda pre_act: jax.nn.gelu(pre_act, approximate=False), inner_pre
    )
    activated_low = activated.astype(jnp.bfloat16)
    second = jnp.dot(activated_low, w_down, preferred_element_type=jnp.float32) + b_branch[
        1
    ].astype(jnp.float32)
    result, normed_two, inverse_two = norm_forward(
        first + second, gains[1].astype(jnp.float32), shifts[1].astype(jnp.float32)
    )
    hidden_out = result.astype(jnp.bfloat16)
    grad_sum2, gain_grad2, shift_grad2 = norm_backward(
        out_grad.astype(jnp.float32), normed_two, inverse_two, gains[1].astype(jnp.float32)
    )
    grad_second = grad_sum2.astype(jnp.bfloat16)
    grad_w_down = jnp.einsum(
        "tf,td->fd", activated_low, grad_second, preferred_element_type=jnp.float32
    )
    grad_bias_two = jnp.sum(grad_second.astype(jnp.float32), axis=0)
    grad_act = jnp.einsum("td,fd->tf", grad_second, w_down, preferred_element_type=jnp.float32)
    grad_inner = gelu_pull(grad_act)[0].astype(jnp.bfloat16)
    grad_b_in = jnp.sum(grad_inner.astype(jnp.float32), axis=0)
    grad_w_in = jnp.einsum("td,tf->df", first_low, grad_inner, preferred_element_type=jnp.float32)
    grad_first = grad_sum2 + jnp.einsum(
        "tf,df->td", grad_inner, w_in, preferred_element_type=jnp.float32
    )
    grad_sum1, gain_grad1, shift_grad1 = norm_backward(
        grad_first, normed_one, inverse_one, gains[0].astype(jnp.float32)
    )
    grad_branch = grad_sum1.astype(jnp.bfloat16)
    grad_w_out = jnp.einsum("td,te->de", context, grad_branch, preferred_element_type=jnp.float32)
    grad_bias_one = jnp.sum(grad_branch.astype(jnp.float32), axis=0)
    grad_context = jnp.einsum(
        "te,de->td", grad_branch, w_out, preferred_element_type=jnp.float32
    ).astype(jnp.bfloat16)
    grad_heads = grad_context.reshape(row_count, H, HD)
    delta = jnp.einsum("thd,thd->ht", grad_heads.astype(jnp.float32), context_full)

    def backward_core(grad_query, grad_select, portion):
        key_part, value_part, meta_part = portion
        logits, allowed, onehot, key_heads = block_logits(
            query_heads, selector, segment_ids, key_part, meta_part, scaling
        )
        probs = jnp.where(allowed[None], jnp.exp(logits - log_total[:, :, None]), 0.0)
        part_rows = key_part.shape[0]
        value_heads = value_part.reshape(part_rows, H, HD)
        grad_probs = jnp.einsum(
            "thd,khd->htk", grad_heads, value_heads, preferred_element_type=jnp.float32
        )
        grad_logits = (probs * (grad_probs - delta[:, :, None])).astype(jnp.bfloat16)
        grad_query = grad_query + scaling * jnp.einsum(
            "htk,khd->thd", grad_logits, key_heads, preferred_element_type=jnp.float32
        )
        grad_select = grad_select + scaling * jnp.einsum(
            "htk,kv->thv", grad_logits, onehot, preferred_element_type=jnp.float32
        )
        grad_key = scaling * jnp.einsum(
            "htk,thd->khd", grad_logits, query_heads, preferred_element_type=jnp.float32
        )
        grad_value = jnp.einsum(
            "htk,thd->khd",
            probs.astype(jnp.bfloat16),
            grad_heads,
            preferred_element_type=jnp.float32,
        )
        update = jnp.concatenate(
            [grad_key.reshape(part_rows, width), grad_value.reshape(part_rows, width)], axis=1
        )
        return (grad_query, grad_select, update)

    query_zero = jnp.zeros((row_count, H, HD), jnp.float32)
    select_zero = jnp.zeros((row_count, H, select_width), jnp.float32)

    def cycle_turn(turn, carry):
        grad_query, grad_select, key_part, value_part, meta_part, carried = carry
        portion = (key_part, value_part, meta_part)
        grad_query, grad_select, update = backward_core(grad_query, grad_select, portion)
        carried = carried + update
        key_part, value_part, meta_part = shifted((key_part, value_part, meta_part), "blk", 1)
        carried = shifted(carried.astype(jnp.bfloat16), "blk", 1).astype(carried.dtype)
        return (grad_query, grad_select, key_part, value_part, meta_part, carried)

    cycle_start = (
        query_zero,
        select_zero,
        key_rows,
        value_rows,
        key_meta,
        jnp.zeros((row_count, 2 * width), jnp.float32),
    )
    cycle_end = lax.fori_loop(0, lax.axis_size("blk"), cycle_turn, cycle_start)
    grad_query, grad_select, own_pairs = (cycle_end[0], cycle_end[1], cycle_end[5])
    grad_key_rows = own_pairs[:, :width].astype(jnp.bfloat16)
    grad_value_rows = own_pairs[:, width:].astype(jnp.bfloat16)
    cursor = 0
    table_parts = []
    for column, extent in enumerate(kind_ranges()):
        table_parts.append(
            jnp.einsum(
                "thv,tvb->thb",
                grad_select[:, :, cursor : cursor + extent],
                maps_list[column].astype(jnp.float32),
                precision=lax.Precision.HIGHEST,
            )
        )
        cursor = cursor + extent
    grad_tables = jnp.stack(table_parts, axis=2).astype(jnp.bfloat16)
    grad_query_total = grad_query + jnp.einsum(
        "thnb,nbhd->thd", grad_tables, rel_heads, preferred_element_type=jnp.float32
    )
    grad_query_rows = grad_query_total.reshape(row_count, width).astype(jnp.bfloat16)
    grad_rel = jnp.einsum(
        "thnb,thd->nbhd", grad_tables, query_heads, preferred_element_type=jnp.float32
    ).reshape(3, NB, width)
    grad_stack = jnp.stack([grad_query_rows, grad_key_rows, grad_value_rows])
    grad_w_qkv = jnp.einsum(
        "td,cte->cde", hidden_in, grad_stack, preferred_element_type=jnp.float32
    )
    grad_b_qkv = jnp.stack(
        [
            jnp.sum(grad_query_rows.astype(jnp.float32), axis=0),
            jnp.sum(grad_value_rows.astype(jnp.float32), axis=0),
        ]
    )
    grad_input = grad_sum1 + jnp.einsum(
        "cte,cde->td", grad_stack, w_qkv, preferred_element_type=jnp.float32
    )
    summed = (
        lax.psum_scatter(grad_w_qkv, ("grp", "blk"), scatter_dimension=1, tiled=True),
        lax.psum_scatter(grad_b_qkv, ("grp", "blk"), scatter_dimension=1, tiled=True),
        lax.psum_scatter(grad_rel, ("grp", "blk"), scatter_dimension=2, tiled=True),
        lax.psum_scatter(grad_w_out, ("grp", "blk"), scatter_dimension=0, tiled=True),
        lax.psum_scatter(
            jnp.stack([grad_bias_one, grad_bias_two]),
            ("grp", "blk"),
            scatter_dimension=1,
            tiled=True,
        ),
        lax.psum_scatter(
            jnp.stack([gain_grad1, gain_grad2]), ("grp", "blk"), scatter_dimension=1, tiled=True
        ),
        lax.psum_scatter(
            jnp.stack([shift_grad1, shift_grad2]), ("grp", "blk"), scatter_dimension=1, tiled=True
        ),
        lax.psum_scatter(grad_w_in, ("grp", "blk"), scatter_dimension=0, tiled=True),
        lax.psum_scatter(grad_b_in, ("grp", "blk"), scatter_dimension=0, tiled=True),
        lax.psum_scatter(grad_w_down, ("grp", "blk"), scatter_dimension=0, tiled=True),
    )
    return (
        hidden_out,
        grad_input.astype(jnp.bfloat16),
        summed[0],
        summed[1],
        summed[2],
        summed[3],
        summed[4],
        summed[5],
        summed[6],
        summed[7],
        summed[8],
        summed[9],
    )


MESH = pl.DeviceIdType.MESH
LOW = jnp.bfloat16
HIGH = jnp.float32
CHIPS = 16
HALF = 8
BLOCK = 256
MASKED = -1e30
VMEM_LIMIT = 62 * 2**20
NT = ((1,), (1,))
TN = ((0,), (0,))


def dot(left, right, dims=((1,), (0,))):
    return lax.dot_general(left, right, (dims, ((), ())), preferred_element_type=HIGH)


def place():
    return lax.axis_index("grp"), lax.axis_index("blk")


def coordinates(chip):
    return lax.div(chip, 4), lax.rem(lax.div(chip, 2), 2), lax.rem(chip, 2)


def greet_all():
    core, chip = place()
    me = core * CHIPS + chip
    barrier = pltpu.get_barrier_semaphore()

    def greet(ahead, carry):
        other = lax.rem(me + ahead, 2 * CHIPS)
        pl.semaphore_signal(
            barrier,
            inc=1,
            device_id=(lax.div(other, CHIPS), lax.rem(other, CHIPS)),
            device_id_type=MESH,
        )
        return carry

    lax.fori_loop(1, 2 * CHIPS, greet, 0)


def await_all():
    pl.semaphore_wait(pltpu.get_barrier_semaphore(), 2 * CHIPS - 1)


def remote(source, target, send, recv, device):
    return pltpu.make_async_remote_copy(
        src_ref=source,
        dst_ref=target,
        send_sem=send,
        recv_sem=recv,
        device_id=device,
        device_id_type=MESH,
    )


def local(source, target, sem):
    return pltpu.make_async_copy(source, target, sem)


MIRROR = 3


def in_the_middle():
    z, _, _ = coordinates(lax.axis_index("blk"))
    return jnp.logical_and(z > 0, z < 3)


def neighbours(across):
    core, chip = place()
    z, y, x = coordinates(chip)
    planes = (z + 1 - 2 * lax.rem(z, 2), 2 - lax.div(z, 2), 3 - 3 * lax.div(z, 2), 3 - z)

    def slot(far_p, far_q, line):
        far_y, far_x = (far_q, far_p) if across == "x" else (far_p, far_q)
        plane = z if line is None else planes[line]
        return plane * 4 + (1 - y if far_y else y) * 2 + (1 - x if far_x else x)

    return slot


class Shipments:
    def __init__(self, send, recv):
        self.send, self.recv = send, recv
        self.core = lax.axis_index("grp")

    def ship(self, source, target, kind, recv_index, to, when=None):
        start = lambda: remote(
            source, target, self.send.at[kind], self.recv.at[recv_index], (self.core, to)
        ).start()
        if when is None:
            start()
        else:
            pl.when(when)(start)

    def landed(self, target, recv_index):
        local(target, target, self.recv.at[recv_index]).wait()

    def all_sent(self, bytes_of, kind):
        local(bytes_of, bytes_of, self.send.at[kind]).wait()


class Gather:
    SENDS, RECEIVES = 2, 9

    def __init__(self, pick, send, recv, across):
        self.pick, self.at = pick, neighbours(across)
        self.moves = Shipments(send, recv)
        self.middle = in_the_middle()

    def ship(self, what, kind, recv_index, to, when=None):
        ref = self.pick(self.at(*what))
        self.moves.ship(ref, ref, kind, recv_index, self.at(*to), when)

    def plane(self, line):
        return lax.div(self.at(0, 0, line), 4)

    def along_z(self, line, to, when=None):
        self.ship((0, 0, line), 0, self.plane(line), (0, 0, to), when)

    def along_p(self, line):
        self.ship((0, 0, line), 1, 4 + self.plane(line), (1, 0, None))

    def along_q(self, far_p, line):
        self.ship((far_p, 0, line), 1, 8, (0, 1, None))

    def own_line(self, number):
        if number == 0:
            self.along_z(None, 0)
        else:
            self.along_z(None, MIRROR, self.middle)

    def own_plane(self):
        self.along_p(None)
        self.along_q(0, None)

    def line(self, line):
        self.moves.landed(self.pick(self.at(0, 0, line)), self.plane(line))
        self.along_z(line, MIRROR if line == 0 else 0, self.middle)
        self.along_p(line)
        self.along_q(0, line)

    def side(self, line):
        self.moves.landed(self.pick(self.at(1, 0, line)), 4 + self.plane(line))
        self.along_q(1, line)

    def arrive(self):
        self.moves.landed(self.pick(pl.ds(0, 8)), 8)

    def finish(self):
        self.moves.all_sent(self.pick(pl.ds(0, 12)), 1)
        pl.when(self.middle)(lambda: self.moves.all_sent(self.pick(pl.ds(0, 5)), 0))
        pl.when(jnp.logical_not(self.middle))(lambda: self.moves.all_sent(self.pick(pl.ds(0, 1)), 0))


class GatherLate(Gather):
    SENDS, RECEIVES = 3, 6

    def plane_slots(self, line):
        return self.pick(pl.ds(self.plane(line) * 4, 4))

    def first(self):
        self.ship((0, 0, None), 0, 4, (1, 0, None))
        self.ship((0, 0, None), 0, 5, (0, 1, None))

    def second(self):
        self.moves.landed(self.pick(self.at(1, 0, None)), 4)
        self.ship((1, 0, None), 0, 5, (0, 1, None))

    def pass_plane(self, line, kind, to, when=None):
        slots = self.plane_slots(line)
        self.moves.ship(slots, slots, kind, self.plane(line), self.at(0, 0, to), when)

    def third(self):
        self.moves.landed(self.pick(pl.ds(0, 2)), 5)
        self.pass_plane(None, 1, 0)
        self.pass_plane(None, 2, MIRROR, self.middle)

    def late_line(self, line):
        self.moves.landed(self.plane_slots(line), self.plane(line))
        self.pass_plane(line, 2, MIRROR if line == 0 else 0, self.middle)

    def finish(self):
        self.moves.all_sent(self.pick(pl.ds(0, 3)), 0)
        self.moves.all_sent(self.pick(pl.ds(0, 4)), 1)
        pl.when(self.middle)(lambda: self.moves.all_sent(self.pick(pl.ds(0, 16)), 2))


class Reduce:
    SENDS, RECEIVES = 1, 15

    def __init__(self, held, pick, stages, send, recv, across):
        self.held, self.pick, self.at = held, pick, neighbours(across)
        self.first, self.second, self.third_in = stages
        self.moves = Shipments(send, recv)

    @staticmethod
    def number(line):
        return 3 if line is None else line

    def plane(self, line):
        return lax.div(self.at(0, 0, line), 4)

    def mine(self, *what):
        return self.pick(self.held, self.at(*what))

    def term(self, stage, index, recv_index):
        self.moves.landed(stage.at[index], recv_index)
        return stage[index].astype(HIGH)

    def start(self, line):
        for far_p in (1, 0):
            index = self.number(line) * 2 + far_p
            self.moves.ship(
                self.mine(far_p, 1, line), self.first.at[index], 0, index, self.at(0, 1, None)
            )

    def side(self, line):
        number = self.number(line)
        index = number * 2 + 1
        total = self.term(self.first, index, index) + self.mine(1, 0, line)[...].astype(HIGH)
        self.first[index] = total.astype(LOW)
        self.moves.ship(
            self.first.at[index], self.second.at[number], 0, 8 + number, self.at(1, 0, None)
        )

    def line(self, line):
        number = self.number(line)
        index = number * 2
        total = (
            self.term(self.first, index, index)
            + self.term(self.second, number, 8 + number)
            + self.mine(0, 0, line)[...].astype(HIGH)
        )
        if line is None:
            return total
        self.first[index] = total.astype(LOW)
        ahead = self.ahead(line)
        self.moves.ship(
            self.first.at[index], self.third_in.at[ahead], 0, 12 + ahead, self.at(0, 0, line)
        )

    def ahead(self, line):
        return lax.rem(self.plane(None) - self.plane(line) + 4, 4) - 1

    def finish(self, result):
        total = self.line(None)
        for ahead in range(3):
            total += self.term(self.third_in, ahead, 12 + ahead)
        result[...] = total
        self.moves.all_sent(self.pick(self.held, pl.ds(0, 15)), 0)


class ReduceEarly(Reduce):
    SENDS, RECEIVES = 1, 6

    def start(self):
        for line in (2, 1, 0):
            ahead = self.ahead(line)
            self.moves.ship(
                self.pick(self.held, pl.ds(self.plane(line) * 4, 4)),
                self.first.at[ahead],
                0,
                ahead,
                self.at(0, 0, line),
            )

    def plane_sum(self, *what):
        slot = self.at(*what, None)
        total = self.pick(self.held, slot)[...].astype(HIGH)
        for ahead in range(3):
            total += self.first[ahead, lax.rem(slot, 4)].astype(HIGH)
        return total

    def plane_ref(self, *what):
        return self.first.at[0, lax.rem(self.at(*what, None), 4)]

    def third(self):
        for ahead in range(3):
            self.moves.landed(self.first.at[ahead], ahead)
        for far_p in (1, 0):
            ref = self.plane_ref(far_p, 1)
            ref[...] = self.plane_sum(far_p, 1).astype(LOW)
            self.moves.ship(ref, self.second.at[far_p], 0, 3 + far_p, self.at(0, 1, None))

    def across(self):
        ref = self.plane_ref(1, 0)
        ref[...] = (self.plane_sum(1, 0) + self.term(self.second, 1, 4)).astype(LOW)
        self.moves.ship(ref, self.third_in.at[0], 0, 5, self.at(1, 0, None))

    def finish(self, result):
        result[...] = (
            self.plane_sum(0, 0) + self.term(self.second, 0, 3) + self.term(self.third_in, 0, 5)
        )
        self.moves.all_sent(self.pick(self.held, pl.ds(0, 15)), 0)


def cube_of(order):
    core, chip = place()
    z, y, x = coordinates(chip)

    def at(*flips):
        far = dict(zip(order, flips))
        plane = z + 1 - 2 * lax.rem(z, 2) if far["z"] else z
        return plane * 4 + (1 - y if far["y"] else y) * 2 + (1 - x if far["x"] else x)

    return at


class CubeGather:
    SENDS, RECEIVES = 1, 4

    def __init__(self, pick, send, recv, order):
        self.pick, self.at = pick, cube_of(order)
        self.moves = Shipments(send, recv)

    def ref(self, *what):
        return self.pick(lax.rem(self.at(*what), HALF))

    def ship(self, what, recv_index, to):
        self.moves.ship(self.ref(*what), self.ref(*what), 0, recv_index, self.at(*to))

    def own(self):
        self.ship((0, 0, 0), 0, (1, 0, 0))
        self.ship((0, 0, 0), 1, (0, 1, 0))
        self.ship((0, 0, 0), 3, (0, 0, 1))

    def one(self):
        self.moves.landed(self.ref(1, 0, 0), 0)
        self.ship((1, 0, 0), 2, (0, 1, 0))
        self.ship((1, 0, 0), 3, (0, 0, 1))

    def two(self):
        for one in range(2):
            self.moves.landed(self.ref(one, 1, 0), 1 + one)
            self.ship((one, 1, 0), 3, (0, 0, 1))

    def arrive(self):
        self.moves.landed(self.pick(pl.ds(0, 4)), 3)

    def finish(self):
        self.moves.all_sent(self.pick(pl.ds(0, 7)), 0)


class CubeReduce:
    SENDS, RECEIVES = 1, 7

    def __init__(self, pick, stage, send, recv, order):
        self.pick, self.stage, self.at = pick, stage, cube_of(order)
        self.moves = Shipments(send, recv)

    def ship(self, source, index, to):
        self.moves.ship(source, self.stage.at[index], 0, index, self.at(*to))

    def mine(self, *what):
        return self.pick(lax.rem(self.at(*what), HALF))

    def term(self, index):
        self.moves.landed(self.stage.at[index], index)
        return self.stage[index].astype(HIGH)

    def own(self):
        for index, (one, two) in enumerate(((1, 1), (0, 1), (1, 0), (0, 0))):
            self.ship(self.mine(one, two, 1), index, (0, 0, 1))

    def one(self):
        for index, one in ((0, 1), (1, 0)):
            total = self.mine(one, 1, 0)[...].astype(HIGH) + self.term(index)
            self.stage[index] = total.astype(LOW)
            self.ship(self.stage.at[index], 4 + index, (0, 1, 0))

    def two(self):
        total = self.mine(1, 0, 0)[...].astype(HIGH) + self.term(2) + self.term(4)
        self.stage[2] = total.astype(LOW)
        self.ship(self.stage.at[2], 6, (1, 0, 0))

    def arrive(self):
        return self.mine(0, 0, 0)[...].astype(HIGH) + self.term(3) + self.term(5) + self.term(6)

    def finish(self):
        self.moves.all_sent(self.stage, 0)


def each(plans, act, *arguments):
    for plan in plans:
        act(plan, *arguments)


def unit():
    core, chip = place()
    return lax.div(chip, HALF), lax.rem(chip, HALF), core


def all_but_one(source, send, itself):
    most = source.at[pl.ds(0, CHIPS - 1)]
    pl.when(itself)(lambda: local(most, most, send.at[0]).wait())
    pl.when(jnp.logical_not(itself))(lambda: local(source, source, send.at[0]).wait())


def to_tokens(source, target, send, recv):
    core, chip = place()
    group, position, _ = unit()
    to_core = lax.div(position, 4)
    mine = group * HALF + 2 * lax.rem(position, 4) + core
    here = to_core == core

    def copy_to(ahead):
        chip_to = lax.rem(chip + ahead, CHIPS)
        return remote(
            source.at[chip_to], target.at[mine], send.at[0], recv.at[0], (to_core, chip_to)
        )

    pl.when(here)(lambda: local(source.at[chip], target.at[mine], recv.at[0]).start())
    pl.when(jnp.logical_not(here))(lambda: copy_to(0).start())
    for ahead in range(1, CHIPS):
        copy_to(ahead).start()
    arrive = lambda: local(target, target, recv.at[0]).wait()
    return arrive, lambda: all_but_one(source, send, here)


def to_heads(source, target, send, recv):
    core, chip = place()
    group, position, _ = unit()
    here = lax.div(position, 4) == core
    start = 2 * lax.rem(position, 4) + core

    def copy_to(turn_group, ahead):
        to_group = lax.rem(group + turn_group, 2)
        head = lax.rem(start + ahead, HALF)
        return remote(
            source.at[to_group * HALF + head],
            target.at[chip],
            send.at[0],
            recv.at[0],
            (lax.rem(head, 2), to_group * HALF + core * 4 + lax.div(head, 2)),
        )

    pl.when(here)(lambda: local(source.at[group * HALF + start], target.at[chip], recv.at[0]).start())
    pl.when(jnp.logical_not(here))(lambda: copy_to(0, 0).start())
    for turn_group in range(2):
        for ahead in range(0 if turn_group else 1, HALF):
            copy_to(turn_group, ahead).start()
    arrive = lambda: local(target, target, recv.at[0]).wait()
    return arrive, lambda: all_but_one(source, send, here)


def lanes(rows, width=128):
    return lax.broadcasted_iota(jnp.int32, (rows, width), 1)


def turn(values):
    return pltpu.roll(values, HD, 1)


def fold(rows_in):
    half = rows_in.shape[0] // 2
    both = jnp.where(lanes(half) < HD, rows_in[:half], turn(rows_in[half:]))
    pad = -half % 16
    if pad:
        both = jnp.concatenate([both, jnp.zeros((pad, 128), HIGH)], axis=0)
    return both.astype(LOW)


def column_sums(v):
    return jnp.sum(v, axis=0, keepdims=True)


def gelu_parts(pre):
    cdf = 0.5 * (1.0 + lax.erf(pre * math.sqrt(0.5)))
    density = jnp.exp(-0.5 * pre * pre) * (1.0 / math.sqrt(2.0 * math.pi))
    return pre * cdf, cdf + pre * density


def normalize(v, gain, shift):
    center = v - jnp.mean(v, axis=1, keepdims=True)
    inverse = lax.rsqrt(jnp.mean(center * center, axis=1, keepdims=True) + EPSILON)
    normed = center * inverse
    return normed * gain + shift, normed, inverse


def normalize_back(c, normed, inverse, gain):
    scaled = c * gain
    inner = (
        scaled
        - jnp.mean(scaled, axis=1, keepdims=True)
        - normed * jnp.mean(scaled * normed, axis=1, keepdims=True)
    )
    return inner * inverse


def at_steps(index, steps):
    for number, acts in steps.items():

        def run(acts=acts):
            for act in acts:
                act()

        pl.when(index == number)(run)


def columns_of(half, width):
    return pl.ds(pl.multiple_of(half * width, 128), width)


def layer_kernel(names, *refs):
    r = types.SimpleNamespace(**dict(zip(names, refs)))
    hidden, x_all, w_all, rel_all = r.hidden_in, r.x_all, r.w_all, r.rel_all
    token_rows, width = hidden.shape
    slot_rows = x_all.shape[1]
    total = CHIPS * slot_rows
    depth = r.out_weight.shape[0]
    w_in, w_down, w_out = r.w_in, r.w_down, r.w_out
    half_hidden = w_in.shape[3]
    half_width = width // 2
    core, chip = place()
    group, position, _ = unit()
    other = 1 - core
    me = core * CHIPS + chip
    keep = r.keep_sem

    greet_all()

    loads = [
        local(r.ffn_in.at[:, columns_of(core, half_hidden)], w_in.at[core, chip], keep.at[0]),
        local(r.ffn_out, w_down.at[chip], keep.at[1]),
        local(r.out_weight, w_out.at[chip], keep.at[2]),
    ]
    for copy in loads:
        copy.start()

    extra = r.extra
    extra[...] = jnp.zeros_like(extra)
    extra[0:1, 0:256] = jnp.full((1, 256), 4.0, HIGH)
    extra[0:1, 0:token_rows] = r.segment_ids[...].astype(HIGH)
    extra[1:2, 0:token_rows] = r.order_ids[...].astype(HIGH)
    extra[2:4, 0:token_rows] = r.box_ids[...].astype(HIGH)
    tail = token_rows - token_rows % 16
    x_own = r.x_own
    x_own[0:tail, :] = hidden[0:tail, :]
    x_own[tail:slot_rows, :] = jnp.concatenate(
        [hidden[tail:token_rows, :].astype(HIGH), extra[...]], axis=0
    ).astype(LOW)
    weight = r.qkv_weight
    rel_own = r.rel_own
    for kind in range(3):
        rel_own[:, kind * NB : (kind + 1) * NB] = r.rel_tables[kind]
    eye_depth = (
        lax.broadcasted_iota(jnp.int32, (depth, depth), 0)
        == lax.broadcasted_iota(jnp.int32, (depth, depth), 1)
    ).astype(LOW)
    bias_columns = dot(eye_depth, r.qkv_bias[...], NT)
    rel_own[:, 3 * NB : 4 * NB] = jnp.where(
        lanes(depth) == 0, bias_columns[:, 0:1], jnp.where(lanes(depth) == 1, bias_columns[:, 1:2], 0.0)
    ).astype(LOW)
    small_wide, small_own, small_all = r.small_wide, r.small_own, r.small_all
    small_wide[...] = jnp.zeros_like(small_wide)
    for number, pair in enumerate((r.branch_bias, r.norm_gains, r.norm_shifts)):
        small_wide[2 * number : 2 * number + 2, 0:depth] = pair[...].astype(HIGH)
    small_wide[6:7, :] = r.ffn_in_bias[...].astype(HIGH)
    small_own[...] = small_wide[...].astype(LOW)
    loads += [
        local(small_own, small_all.at[chip], keep.at[3]),
        local(weight.at[:, :, columns_of(position, 128)], w_all.at[:, core, chip], keep.at[4]),
    ]
    for copy in loads[3:]:
        copy.start()
    await_all()

    at_home = group == core
    away = lax.rem(chip + HALF, CHIPS)
    x_slot = x_all.at[position]
    home = lambda: local(x_own, x_slot, r.home_sem.at[1])
    abroad = lambda: remote(x_own, x_slot, r.home_sem.at[0], r.home_sem.at[1], (other, away))
    pl.when(at_home)(lambda: home().start())
    pl.when(jnp.logical_not(at_home))(lambda: abroad().start())

    rel_head = core * HALF + lax.div(chip, 2)
    parity = lax.rem(chip, 2)
    rel_slot = rel_all.at[pl.ds(parity * depth, depth)]

    def rel_each(act_remote, act_own):
        for to_group in range(2):
            to = (lax.rem(rel_head, 2), to_group * HALF + lax.div(rel_head, 2))
            itself = jnp.logical_and(to[0] == core, to[1] == chip)
            copy = lambda: remote(
                rel_own, rel_slot, r.rel_send.at[to_group], r.rel_recv.at[parity], to
            )
            pl.when(jnp.logical_not(itself))(lambda: act_remote(copy()))
            if act_own is not None:
                pl.when(itself)(act_own)

    rel_each(
        lambda copy: copy.start(), lambda: local(rel_own, rel_slot, r.rel_recv.at[parity]).start()
    )

    def w_copy(ahead):
        to = lax.rem(chip + ahead, CHIPS)
        return remote(
            weight.at[:, :, columns_of(lax.rem(to, HALF), 128)],
            w_all.at[:, core, chip],
            r.w_send.at[0],
            r.w_recv.at[0],
            (core, to),
        )

    swap_in = remote(
        r.ffn_in.at[:, columns_of(other, half_hidden)],
        w_in.at[core, chip],
        r.pair_send.at[0],
        r.pair_recv.at[0],
        (other, chip),
    )
    swap_in.start()

    third = slot_rows // 3
    x_plans = [
        CubeGather(
            lambda slot, part=part: x_all.at[slot, pl.ds(part * third, third)],
            r.x_send.at[part],
            r.x_recv.at[part],
            order,
        )
        for part, order in enumerate(("xyz", "yzx", "zxy"))
    ]
    half = width // 2
    half_tile = half_hidden // 2
    plans_out = [
        GatherLate(lambda slot: w_out.at[slot], r.out_send.at[0], r.out_recv.at[0], "x"),
        GatherLate(lambda slot: small_all.at[slot], r.out_send.at[1], r.out_recv.at[1], "y"),
    ]

    def halves(ref, wide, sends, recvs):
        return [
            Gather(
                lambda slot, part=part: ref(slot, pl.ds(part * wide, wide)), sends.at[part], recvs.at[part], across
            )
            for part, across in enumerate("xy")
        ]

    plans_in = halves(lambda slot, columns: w_in.at[:, slot, :, columns], half_tile, r.in_send, r.in_recv)
    plans_down = halves(lambda slot, columns: w_down.at[slot, :, columns], half, r.down_send, r.down_recv)

    for copy in loads:
        copy.wait()
    each(plans_down, Gather.own_plane)
    each(plans_out, GatherLate.first)
    swap_in.wait()
    each(plans_in, Gather.own_plane)
    each(plans_in, Gather.own_line, 0)
    for ahead in range(1, CHIPS):
        w_copy(ahead).start()
    each(plans_out, GatherLate.second)
    each(plans_in, Gather.own_line, 1)
    home().wait()
    each(x_plans, CubeGather.own)
    each(x_plans, CubeGather.one)
    each(x_plans, CubeGather.two)
    each(plans_down, Gather.own_line, 0)
    w_most = w_all.at[:, core, pl.ds(0, CHIPS - 1)]
    local(w_most, w_most, r.w_recv.at[0]).wait()
    pair_w = remote(w_all.at[:, core], w_all.at[:, core], r.pair_send.at[1], r.pair_recv.at[1], (other, chip))
    pair_w.start()
    for slot in range(2):
        local(rel_own, rel_all.at[pl.ds(slot * depth, depth)], r.rel_recv.at[slot]).wait()
    pair_bias = remote(
        rel_all.at[:, pl.ds(3 * NB, NB)], r.bias_far, r.pair_send.at[2], r.pair_recv.at[2], (other, chip)
    )
    pair_bias.start()
    each(plans_down, Gather.side, None)
    each(plans_out, GatherLate.third)
    each(plans_in, Gather.line, 0)
    each(x_plans, CubeGather.arrive)
    pl.when(jnp.logical_not(at_home))(lambda: abroad().wait_send())

    labels = r.labels
    first_slot = core * HALF
    label_part = x_all.at[:, pl.ds(slot_rows - 16, 16), pl.ds(0, 256)]
    label_slots = labels.at[pl.ds(first_slot, HALF)]
    pair_label = remote(label_part, label_slots, r.pair_send.at[3], r.pair_recv.at[3], (other, chip))
    pair_label.start()
    own_label = local(label_part, label_slots, keep.at[5])
    own_label.start()
    pair_w.wait()
    pair_bias.wait()

    head_rows = 2 * depth
    row_at = lax.broadcasted_iota(jnp.int32, (head_rows, 128), 0)
    column_at = lanes(head_rows)

    def bias_row(columns, number):
        column = columns[:, number : number + 1]
        return column_sums(jnp.where(row_at == column_at, column, 0.0))

    rel = rel_all[...]
    bias_near = rel[:, 3 * NB : 4 * NB].astype(HIGH)
    bias_far = r.bias_far[...].astype(HIGH)
    bias_query, bias_value = (
        bias_row(bias_near, number) + turn(bias_row(bias_far, number)) for number in range(2)
    )
    weights = [w_all[n].reshape(width, 128) for n in range(3)]
    near, far_part = r.near, r.far_part
    pair_rows = 2 * slot_rows
    pair_half = lanes(pair_rows) < HD

    for pair in range(HALF // 2):
        tokens = x_all[2 * pair : 2 * pair + 2].reshape(pair_rows, width)
        query, key, value_rows = (
            pltpu.roll(dot(tokens, weights[n]), core * HD, 1) for n in range(3)
        )
        query, value_rows = query + bias_query, value_rows + bias_value
        rows = pl.ds(pl.multiple_of(core * HALF * slot_rows, 16) + pair * pair_rows, pair_rows)
        near[rows, 0:128] = jnp.where(pair_half, query, turn(value_rows)).astype(LOW)
        near[rows, 128:256] = key.astype(LOW)
        far_rows = slice(pair * pair_rows, (pair + 1) * pair_rows)
        far_part[far_rows, 0:128] = jnp.where(pair_half, turn(query), value_rows).astype(LOW)
        far_part[far_rows, 128:256] = turn(key).astype(LOW)
    pair_qkv = remote(
        far_part,
        near.at[pl.ds(pl.multiple_of(core * HALF * slot_rows, 16), HALF * slot_rows)],
        r.pair_send.at[4],
        r.pair_recv.at[4],
        (other, chip),
    )
    pair_qkv.start()

    meta = r.meta
    eye = (
        lax.broadcasted_iota(jnp.int32, (slot_rows, 256), 0)
        == lax.broadcasted_iota(jnp.int32, (slot_rows, 256), 1)
    ).astype(LOW)
    pair_label.wait()
    own_label.wait()
    for slot in range(CHIPS):
        meta[slot * slot_rows : (slot + 1) * slot_rows, 0:16] = dot(eye, labels[slot], NT)
    table_t = rel[:, 0 : 3 * NB]
    lane = lanes(BLOCK)
    first_half = lane < HD
    scale = 1.0 / math.sqrt(4.0 * HD)
    left, right, right_t = r.left, r.right, r.right_t
    value, value_t, kept = r.value, r.value_t, r.kept
    pair_qkv.wait()

    def prepare(index, carry):
        rows = pl.ds(pl.multiple_of(index * BLOCK, BLOCK), BLOCK)
        at_steps(
            index,
            {
                1: [lambda: each(plans_down, Gather.own_line, 1), lambda: each(plans_down, Gather.line, 0)],
                3: [lambda: each(plans_in, Gather.line, 1)],
                8: [lambda: each(plans_in, Gather.line, 2)],
            },
        )
        query_value = near[rows, 0:128].astype(HIGH)
        key = near[rows, 128:256].astype(HIGH)
        tables = dot(near[rows, 0:128][:, 0:HD], table_t).astype(LOW).astype(HIGH)
        ids = meta[rows, 8:12].astype(jnp.int32)
        segment, order, box_x, box_y = ids[:, 0:1], ids[:, 1:2], ids[:, 2:3], ids[:, 3:4]

        def selected(column, ids_of, values):
            bucket = jnp.clip(ids_of - values, -(NB // 2), NB // 2 - 1) + NB // 2
            return jnp.take_along_axis(tables[:, column * NB : (column + 1) * NB], bucket, axis=1)

        wide = selected(0, order, lane)
        narrow = jnp.where(first_half, selected(1, box_x, lane), selected(2, box_y, lane - HD))
        label = lane - HD
        query_side = jnp.where(
            first_half,
            query_value * scale,
            jnp.where(jnp.logical_and(label != segment, label < 8), MASKED, 0.0),
        )
        key_side = jnp.where(first_half, key, (label == segment).astype(HIGH))
        left[rows, 0:128] = (wide * scale).astype(LOW)
        left[rows, 128:256] = (narrow * scale).astype(LOW)
        left[rows, 256:384] = query_side.astype(LOW)
        order_hot = (lane == order).astype(HIGH)
        box_hot = (jnp.where(first_half, box_x, box_y + HD) == lane).astype(HIGH)
        right[rows, 0:128] = order_hot.astype(LOW)
        right[rows, 128:256] = box_hot.astype(LOW)
        right[rows, 256:384] = key_side.astype(LOW)
        right_t[0:128, rows] = order_hot.T.astype(LOW)
        right_t[128:256, rows] = box_hot.T.astype(LOW)
        right_t[256:384, rows] = key_side.T.astype(LOW)
        held = jnp.where(first_half, turn(query_value), (label == 0).astype(HIGH))
        value[rows, :] = held.astype(LOW)
        value_t[:, rows] = held.T.astype(LOW)
        return carry

    lax.fori_loop(0, total // BLOCK, prepare, 0)
    def attend(index, carry):
        rows = pl.ds(pl.multiple_of(index * BLOCK, BLOCK), BLOCK)
        at_steps(
            index,
            {
                2: [lambda: each(plans_in, Gather.side, None)],
                4: [lambda: each(plans_down, Gather.line, 1)],
                8: [lambda: each(plans_down, Gather.line, 2)],
            },
        )
        logits = dot(left[rows, :], right_t[...])
        top = jnp.max(logits, axis=1, keepdims=True)
        weights = jnp.exp(logits - top).astype(LOW)
        mixed = dot(weights, value[...])
        row_sum = mixed[:, HD : HD + 1]
        ids = meta[rows, 8:12]
        facts = jnp.where(lane == HD, top + jnp.log(row_sum), ids[:, 3:4])
        facts = jnp.where(lane == HD + 1, ids[:, 1:2], facts)
        facts = jnp.where(lane == HD + 2, ids[:, 2:3], facts)
        kept[rows, :] = jnp.where(first_half, mixed / row_sum, facts)
        return carry

    lax.fori_loop(0, total // BLOCK, attend, 0)
    each(plans_out, GatherLate.late_line, 0)
    message, context_in = r.message, r.context_in
    for slot in range(CHIPS):
        message[slot] = fold(kept[slot * slot_rows : (slot + 1) * slot_rows, :])
    context_arrives, context_sent = to_tokens(message, context_in, r.msg_send, r.msg_recv)
    each(plans_in, Gather.side, 1)
    each(plans_in, Gather.side, 2)
    each(plans_out, GatherLate.late_line, 1)
    each(plans_in, Gather.side, 0)
    each(plans_down, Gather.side, 1)
    each(plans_down, Gather.side, 0)
    each(plans_out, GatherLate.late_line, 2)
    each(plans_down, Gather.side, 2)

    shares, bias_in = r.shares, r.bias_in
    shares[core] = jnp.zeros(shares.shape[1:], HIGH)
    share = jnp.logical_and(lanes(8) < depth, lax.broadcasted_iota(jnp.int32, (8, 128), 0) < 6)
    for slot in range(CHIPS):
        small = small_all[slot].astype(HIGH)[0:8]
        target = slice(slot * depth // 128 * 128, slot * depth // 128 * 128 + 128)
        piece = jnp.where(share, small, 0.0)
        if slot * depth % 128:
            piece = pltpu.roll(piece, slot * depth % 128, 1)
        shares[core, :, target] += piece
        bias_in[:, slot * 128 : slot * 128 + 128] = small[6:7]
    pair_small = remote(
        shares.at[core], shares.at[core], r.pair_send.at[5], r.pair_recv.at[5], (other, chip)
    )
    pair_small.start()
    context_arrives()

    context_wide, context, low_first = r.context_wide, r.context, r.low_first
    act, slope = r.act, r.slope
    out_part, in_part = r.out_part, r.in_part
    own = pl.ds(pl.multiple_of(core * slot_rows, 16), slot_rows)
    far = pl.ds(pl.multiple_of(other * slot_rows, 16), slot_rows)
    tile = 512
    half_slot = slot_rows // 2
    count = [6]

    def swap(source, target):
        copy = remote(
            source, target, r.pair_send.at[count[0]], r.pair_recv.at[count[0]], (other, chip)
        )
        count[0] += 1
        copy.start()
        return copy

    left_half = lanes(half_slot) < HD
    for slot_group in range(2):
        for pair in range(HALF // 2):
            even = context_in[slot_group * HALF + 2 * pair].astype(HIGH)[:half_slot]
            odd = context_in[slot_group * HALF + 2 * pair + 1].astype(HIGH)[:half_slot]
            top = slot_group * slot_rows
            columns = slice(pair * 128, pair * 128 + 128)
            context_wide[top : top + half_slot, columns] = jnp.where(left_half, even, turn(odd))
            context_wide[top + half_slot : top + slot_rows, columns] = jnp.where(
                left_half, turn(even), odd
            )
    context[...] = context_wide[...].astype(LOW)

    def product(lhs, rhs):
        out_part[...] = dot(lhs[far, :], rhs).astype(LOW)
        copy = swap(out_part, in_part)
        mine = dot(lhs[own, :], rhs)
        copy.wait()
        return mine + in_part[...].astype(HIGH)

    pair_small.wait()
    branch_bias, gains, shifts = (
        [jnp.concatenate([shares[g, row : row + 1] for g in range(2)], axis=1) for row in (first_row, first_row + 1)]
        for first_row in (0, 2, 4)
    )
    branch = product(context, w_out[...].reshape(half_width, width)) + branch_bias[0]
    row_index = lax.broadcasted_iota(jnp.int32, (slot_rows, 1), 0)
    x_mine = jnp.where(row_index < token_rows, x_own[...].astype(HIGH), 0.0)
    first, normed1, inverse1 = normalize(x_mine + branch, gains[0], shifts[0])
    low_first[own, :] = first.astype(LOW)
    copy = swap(low_first.at[own], low_first.at[own])
    each(plans_in, Gather.arrive)
    copy.wait()

    def widen(index, carry):
        columns = pl.ds(pl.multiple_of(index * tile, tile), tile)
        pre = dot(low_first[...], w_in[:, :, :, columns].reshape(width, tile)) + bias_in[:, columns]
        found, derivative = gelu_parts(pre)
        act[:, columns] = found.astype(LOW)
        slope[:, columns] = derivative
        return carry

    lax.fori_loop(0, half_hidden // tile, widen, 0)
    each(plans_down, Gather.arrive)
    second = product(act, w_down[...].reshape(half_hidden, width)) + branch_bias[1]
    result, normed2, inverse2 = normalize(first + second, gains[1], shifts[1])
    r.hidden_out[...] = result[:token_rows].astype(LOW)
    upstream = jnp.concatenate(
        [r.out_grad[...].astype(HIGH), jnp.zeros((slot_rows - token_rows, width), HIGH)], axis=0
    )
    d_sum2 = normalize_back(upstream, normed2, inverse2, gains[1])
    low_second = d_sum2.astype(LOW)
    d_second, small_sum = r.d_second, r.small_sum
    d_second[own, :] = low_second
    copy = swap(d_second.at[own], d_second.at[own])
    small_sum[...] = jnp.zeros_like(small_sum)
    small_sum[1:2, :] = column_sums(low_second.astype(HIGH))
    small_sum[3:4, :] = column_sums(upstream * normed2)
    small_sum[5:6, :] = column_sums(upstream)

    half_total = HALF * slot_rows
    def half_sums(ref, pick, wide, stages, sends, recvs):
        return [
            Reduce(
                ref,
                lambda held, slot, part=part: pick(held, slot, pl.ds(part * wide, wide)),
                [stage.at[part] for stage in stages],
                sends.at[part],
                recvs.at[part],
                across,
            )
            for part, across in enumerate("xy")
        ]

    sums_down = half_sums(
        w_down,
        lambda held, slot, columns: held.at[slot, :, columns],
        half,
        (r.down_1, r.down_2, r.down_3),
        r.g_down_send,
        r.g_down_recv,
    )
    sums_in = half_sums(
        w_in,
        lambda held, slot, columns: held.at[:, slot, :, columns],
        half_tile,
        (r.in_1, r.in_2, r.in_3),
        r.g_in_send,
        r.g_in_recv,
    )
    sum_out = ReduceEarly(
        r.g_out,
        lambda ref, slot: ref.at[slot],
        [r.out_1, r.out_2, r.out_3],
        r.g_out_send,
        r.g_out_recv,
        "y",
    )

    d_inner = act
    each(plans_in + plans_down, Gather.finish)
    copy.wait()
    slots = tile // w_down.shape[1]

    turns = width // tile
    z, y, x = coordinates(chip)
    assert slots == 4
    for line in (1, None, 2, 0):
        plane = sums_down[0].plane(line)
        columns = pl.ds(pl.multiple_of(plane * tile, tile), tile)
        rows = pl.ds(plane * slots, slots)
        low = (dot(d_second[...], w_down[rows].reshape(tile, width), NT) * slope[:, columns]).astype(LOW)
        bias_sums = column_sums(low.astype(HIGH))
        bias_columns = pl.ds(pl.multiple_of(lax.rem(plane, turns) * tile, tile), tile)
        for row in range(half_hidden // width):

            @pl.when(lax.div(plane, turns) == row)
            def _():
                small_sum[6 + row : 7 + row, bias_columns] = bias_sums

        w_down[rows] = (
            dot(act[:, columns], d_second[...], TN).astype(LOW).reshape(slots, tile // slots, width)
        )
        d_inner[:, columns] = low
        if line == 1:
            each(sums_down, Reduce.start, 1)
    each(sums_down, Reduce.start, None)
    w_in_all = w_in[...].reshape(width, half_hidden)
    out_part[...] = dot(d_inner[far, :], w_in_all, NT).astype(LOW)
    copy = swap(out_part, in_part)
    mine = dot(d_inner[own, :], w_in_all, NT)
    slots_in = 256 // depth

    def widen_grad(index, carry):
        rows = pl.ds(pl.multiple_of(index * 256, 256), 256)
        parts = CHIPS // slots_in
        w_in[lax.div(index, parts), pl.ds(lax.rem(index, parts) * slots_in, slots_in)] = (
            dot(low_first[:, rows], d_inner[...], TN).astype(LOW).reshape(slots_in, depth, half_hidden)
        )
        return carry

    lax.fori_loop(0, width // 256, widen_grad, 0)
    copy.wait()
    d_first = d_sum2 + mine + in_part[...].astype(HIGH)
    d_sum1 = normalize_back(d_first, normed1, inverse1, gains[0])
    low_branch = d_sum1.astype(LOW)
    d_branch = d_second
    d_branch[own, :] = low_branch
    copy = swap(d_branch.at[own], d_branch.at[own])
    r.d_sum1[...] = d_sum1
    small_sum[0:1, :] = column_sums(low_branch.astype(HIGH))
    small_sum[2:3, :] = column_sums(d_first * normed1)
    small_sum[4:5, :] = column_sums(d_first)
    copy.wait()
    context_wide[...] = dot(d_branch[...], w_out[...].reshape(half_width, width), NT)
    d_message, d_arrived = context_in, r.d_arrived
    for slot_group in range(2):
        for pair in range(HALF // 2):
            both = context_wide[
                slot_group * slot_rows : (slot_group + 1) * slot_rows, pair * 128 : pair * 128 + 128
            ]
            d_message[slot_group * HALF + 2 * pair] = fold(both)
            d_message[slot_group * HALF + 2 * pair + 1] = fold(turn(both))
    grad_arrives, grad_sent = to_heads(d_message, d_arrived, r.d_send, r.d_recv)
    r.g_out[...] = dot(context[...], d_branch[...], TN).astype(LOW).reshape(r.g_out.shape)

    small_in = r.small_in

    def small_copy(index, to_core, to_chip):
        return remote(
            small_sum, small_in.at[index], r.small_send.at[index], r.small_recv.at[index], (to_core, to_chip)
        )

    def small_turn(index):
        if index == 0:
            return [small_copy(0, other, chip)]
        if index == 1:
            return [small_copy(1, core, z * 4 + (1 - y) * 2 + x)]
        if index == 2:
            return [small_copy(2, core, z * 4 + y * 2 + 1 - x)]
        return [
            small_copy(2 + ahead, core, lax.rem(z + ahead, 4) * 4 + y * 2 + x) for ahead in (1, 2, 3)
        ]

    def small_start(index):
        for copy in small_turn(index):
            copy.start()

    def small_end(index):
        for copy in small_turn(index):
            copy.wait()
        if index == 0:
            small_sum[0:6, :] += small_in[0, 0:6, :]
        elif index < 3:
            small_sum[...] += small_in[index]

    each(sums_down, Reduce.side, 1)
    small_start(0)
    small_end(0)
    each(sums_down, Reduce.start, 2)
    sum_out.start()
    each(sums_in, Reduce.start, 2)
    small_start(1)
    each(sums_down, Reduce.side, 2)
    each(sums_in, Reduce.side, 2)
    each(sums_down, Reduce.start, 0)
    d_context = meta
    grad_arrives()
    for slot in range(CHIPS):
        both = d_arrived[slot].astype(HIGH)[:half_slot]
        top = slot * slot_rows
        d_context[top : top + half_slot, :] = jnp.where(left_half, both, 0.0)
        d_context[top + half_slot : top + slot_rows, :] = jnp.where(left_half, turn(both), 0.0)
    d_heads, d_pair_t, rel_grad = r.d_heads, r.d_pair_t, r.rel_grad
    d_pair_t[...] = jnp.zeros_like(d_pair_t)
    rel_grad[...] = jnp.zeros_like(rel_grad)

    def step(index, carry):
        rows = pl.ds(pl.multiple_of(index * BLOCK, BLOCK), BLOCK)
        at_steps(
            index,
            {
                1: [
                    lambda: small_end(1),
                    lambda: each(sums_in, Reduce.start, 1),
                    lambda: each(sums_down, Reduce.side, None),
                    lambda: each(sums_down, Reduce.side, 0),
                    lambda: each(sums_down, Reduce.line, 2),
                    lambda: small_start(2),
                ],
                2: [lambda: each(sums_in, Reduce.line, 2)],
                4: [
                    lambda: each(sums_in, Reduce.start, None),
                    sum_out.third,
                    lambda: each(sums_down, Reduce.line, 1),
                ],
                5: [
                    lambda: small_end(2),
                    lambda: each(sums_in, Reduce.side, 1),
                    lambda: each(sums_down, Reduce.line, 0),
                ],
                8: [
                    lambda: each(sums_in, Reduce.start, 0),
                    lambda: small_start(3),
                    lambda: each(sums_in, Reduce.line, 1),
                ],
            },
        )
        facts = kept[rows, :]
        grad = d_context[rows, :]
        delta = jnp.sum(grad * facts, axis=1, keepdims=True)
        probs = jnp.exp(dot(left[rows, :], right_t[...]) - facts[:, HD : HD + 1])
        d_probs = dot(grad.astype(LOW), value_t[...])
        d_logits = (probs * (d_probs - delta)).astype(LOW)
        query_t = jnp.where(first_half, left[rows, 256:384].astype(HIGH), 0.0).T[0:HD]
        d_pair_t[0:HD, :] += dot(query_t.astype(LOW), d_logits)
        d_pair_t[HD : 2 * HD, :] += dot(grad.T[0:HD].astype(LOW), probs.astype(LOW))
        back = dot(d_logits, right[...]) * scale
        ids = facts.astype(jnp.int32)
        order, box_x, box_y = (ids[:, HD + k : HD + k + 1] for k in (1, 2, 3))

        def placed(column, ids_of, extent, start):
            found_at = ids_of + NB // 2 - lane
            found = jnp.take_along_axis(
                back[:, column * 128 : column * 128 + 128], jnp.clip(found_at, 0, extent - 1) + start, axis=1
            )
            return jnp.where(jnp.logical_and(found_at >= 0, found_at < extent), found, 0.0)

        wide = back[:, 0:128]
        low_end = jnp.sum(jnp.where(lane >= order + NB // 2, wide, 0.0), axis=1, keepdims=True)
        high_end = jnp.sum(jnp.where(lane <= order - (NB // 2 - 1), wide, 0.0), axis=1, keepdims=True)
        first = placed(0, order, ORDER_RANGE, 0)
        first = jnp.where(lane == 0, low_end, jnp.where(lane == NB - 1, high_end, first))
        d_tables = jnp.concatenate(
            [first, placed(1, box_x, BOX_RANGE, 0), placed(1, box_y, BOX_RANGE, BOX_RANGE)], axis=1
        ).astype(LOW)
        from_tables = dot(d_tables, table_t, NT)
        d_query = back[:, 256:384] + jnp.concatenate([from_tables, from_tables], axis=1)
        d_heads[0, :, rows] = d_query.T[0:HD].astype(LOW)
        rel_grad[:, 0 : 3 * NB] += dot((query_t / scale).astype(LOW), d_tables)
        return carry

    lax.fori_loop(0, total // BLOCK, step, 0)

    d_heads[1] = d_pair_t[0:HD, :].astype(LOW)
    d_heads[2] = d_pair_t[HD : 2 * HD, :].astype(LOW)
    d_both = r.d_both
    near_part = pl.ds(pl.multiple_of(core * half_total, 128), half_total)
    far_part = pl.ds(pl.multiple_of(other * half_total, 128), half_total)
    copy = swap(d_heads.at[:, :, far_part], d_both.at[:, core])
    d_both[:, core] = d_heads[:, :, near_part]
    sums = [jnp.sum(d_heads[n].astype(HIGH), axis=1, keepdims=True) for n in (0, 2)]
    rel_grad[:, 3 * NB : 4 * NB] = jnp.where(
        lanes(HD) == 0, sums[0], jnp.where(lanes(HD) == 1, sums[1], 0.0)
    )
    rel_low = r.rel_low
    rel_low[...] = rel_grad[...].astype(LOW)
    head = 2 * position + core
    rel_came = r.rel_came

    def d_rel_each(act_remote, act_own):
        for side in range(2):
            to = (lax.div(position, 4), lax.rem(2 * head + side, CHIPS))
            itself = jnp.logical_and(to[0] == core, to[1] == chip)
            source = rel_low.at[pl.ds(side * depth, depth)]
            act = lambda: act_remote(
                remote(source, rel_came.at[group], r.d_rel_send.at[side], r.d_rel_recv.at[group], to)
            )
            pl.when(jnp.logical_not(itself))(act)
            if act_own:
                pl.when(itself)(lambda: local(source, rel_came.at[group], r.d_rel_recv.at[group]).start())

    d_rel_each(lambda copy: copy.start(), True)
    copy.wait()
    d_columns = d_both[...].reshape(6 * HD, half_total)

    w_grad = dot(d_columns, x_all[...].reshape(half_total, width))

    w_heads = jnp.concatenate([w_all[n].reshape(width, 128) for n in range(3)], axis=1)
    d_rows = d_columns.T
    d_x = x_all
    each(x_plans, CubeGather.finish)
    for pair in range(HALF // 2):
        d_x[2 * pair : 2 * pair + 2] = (
            dot(d_rows[pair * pair_rows : (pair + 1) * pair_rows], w_heads, NT)
            .astype(LOW)
            .reshape(2, slot_rows, width)
        )
    d_x_plans = [
        CubeReduce(
            lambda slot, part=part: d_x.at[slot, pl.ds(part * third, third)],
            r.x_stage.at[part],
            r.d_x_send.at[part],
            r.d_x_recv.at[part],
            order,
        )
        for part, order in enumerate(("xyz", "yzx", "zxy"))
    ]
    each(d_x_plans, CubeReduce.own)

    w_mine, w_far, w_low, w_came = slope, r.w_far, r.w_low, r.w_came
    w_rows = 3 * HD
    for part in range(2):
        w_mine[0:w_rows, part * width : (part + 1) * width] = w_grad[part * w_rows : (part + 1) * w_rows]

    def w_columns(part, half):
        return pl.ds(pl.multiple_of(part * width + half * half_width, 128), half_width)

    w_swaps = [
        swap(w_mine.at[pl.ds(0, w_rows), w_columns(part, other)], w_far.at[part]) for part in range(2)
    ]
    sum_out.across()
    each(d_x_plans, CubeReduce.one)
    for copy in w_swaps:
        copy.wait()
    w_sum = jnp.concatenate(
        [(w_mine[0:w_rows, w_columns(part, core)] + w_far[part]).T for part in range(2)], axis=1
    )
    for slot in range(CHIPS):
        w_low[slot] = w_sum[slot * depth : (slot + 1) * depth].astype(LOW)

    def d_w_copy(ahead):
        to = lax.rem(chip + ahead, CHIPS)
        return remote(w_low.at[to], w_came.at[chip], r.d_w_send.at[0], r.d_w_recv.at[0], (core, to))

    own_d_w = local(w_low.at[chip], w_came.at[chip], keep.at[6])
    own_d_w.start()
    for ahead in range(1, CHIPS):
        d_w_copy(ahead).start()
    sum_out.finish(r.out_w_grad)
    each(sums_in, Reduce.side, 0)
    for part, plan in enumerate(sums_down):
        plan.finish(r.down_grad.at[:, pl.ds(part * half, half)])
    each(d_x_plans, CubeReduce.two)
    each(sums_in, Reduce.line, 0)
    each(sums_in, Reduce.side, None)
    small_end(3)
    x_total, x_came = x_own, r.x_came
    back_part = lambda part: pl.ds(part * third, third)
    back = lambda part: local(
        x_total.at[back_part(part)], x_came.at[back_part(part)], r.back_recv.at[part]
    )
    back_abroad = lambda part: remote(
        x_total.at[back_part(part)],
        x_came.at[back_part(part)],
        r.back_send.at[part],
        r.back_recv.at[part],
        (other, away),
    )
    for part, plan in enumerate(d_x_plans):
        x_total[part * third : (part + 1) * third] = plan.arrive().astype(LOW)
        pl.when(at_home)(lambda: back(part).start())
        pl.when(jnp.logical_not(at_home))(lambda: back_abroad(part).start())
    in_total, in_far = r.in_total, r.in_far
    for part, plan in enumerate(sums_in):
        plan.finish(in_total.at[:, :, pl.ds(part * half_tile, half_tile)])
    in_pair = swap(in_total.at[other], in_far)

    in_grad = r.in_grad
    in_grad[:, columns_of(core, half_hidden)] = in_total[core]
    me = core * CHIPS + chip
    small_total = lambda rows, columns: (
        small_sum[rows, columns] + small_in[3, rows, columns] + small_in[4, rows, columns] + small_in[5, rows, columns]
    )
    strip = columns_of(lax.div(me * depth, 128), 128)
    shares = pltpu.roll(small_total(pl.ds(0, 8), strip), 128 - lax.rem(me * depth, 128), 1)
    for number, result in enumerate((r.branch_grad, r.gain_grad, r.shift_grad)):
        result[...] = shares[2 * number : 2 * number + 2, 0:depth]
    bias_strip = small_total(pl.ds(0, 8), columns_of(position, 128))
    r.bias_grad[...] = jnp.where(group == 0, bias_strip[6:7], bias_strip[7:8])
    for slot in range(2):
        local(rel_low.at[pl.ds(0, depth)], rel_came.at[slot], r.d_rel_recv.at[slot]).wait()
    d_rel_each(lambda copy: copy.wait_send(), False)
    rel_total = rel_came[0].astype(HIGH) + rel_came[1].astype(HIGH)
    for kind in range(3):
        r.rel_tables_grad[kind] = rel_total[:, kind * NB : (kind + 1) * NB]
    r.qkv_bias_grad[...] = rel_total[:, 3 * NB : 4 * NB].T[0:2]
    own_d_w.wait()
    w_came_most = w_came.at[pl.ds(0, CHIPS - 1)]
    local(w_came_most, w_came_most, r.d_w_recv.at[0]).wait()
    local(w_came_most, w_came_most, r.d_w_send.at[0]).wait()
    for pair in range(HALF):
        both = w_came[pair].astype(HIGH) + w_came[HALF + pair].astype(HIGH)
        for n in range(3):
            r.qkv_grad[n, :, pair * 128 : pair * 128 + 128] = both[:, n * 128 : n * 128 + 128]
    for part in range(3):
        back(part).wait()
        pl.when(jnp.logical_not(at_home))(lambda: back_abroad(part).wait_send())
    r.hidden_grad[...] = (r.d_sum1[...] + x_came[...].astype(HIGH))[:token_rows].astype(LOW)
    in_pair.wait()
    in_grad[:, columns_of(other, half_hidden)] = in_far[...]
    grad_sent()
    each(d_x_plans, CubeReduce.finish)
    local(w_most, w_most, r.w_send.at[0]).wait()
    rel_each(lambda copy: copy.wait_send(), None)
    context_sent()
    each(plans_out, GatherLate.finish)


def hand_over(count, *refs):
    for source, target in zip(refs[:count], refs[count:]):
        target[...] = source[...]


def handed_over(arrays):
    return pl.pallas_call(
        functools.partial(hand_over, len(arrays)),
        out_shape=[jax.ShapeDtypeStruct(array.shape, array.dtype) for array in arrays],
        name="hand_over",
    )(*arrays)


def call(kernel, name, number, inputs, outputs, scratch):
    names = list(inputs) + list(outputs) + list(scratch)
    results = pl.pallas_call(
        functools.partial(kernel, names),
        out_shape=[jax.ShapeDtypeStruct(shape, dtype) for shape, dtype, _ in outputs.values()],
        in_specs=[pl.BlockSpec(memory_space=space) for _, space in inputs.values()],
        out_specs=[pl.BlockSpec(memory_space=space) for _, _, space in outputs.values()],
        scratch_shapes=list(scratch.values()),
        compiler_params=pltpu.CompilerParams(
            collective_id=number, has_side_effects=True, vmem_limit_bytes=VMEM_LIMIT
        ),
        name=name,
    )(*(array for array, _ in inputs.values()))
    return types.SimpleNamespace(**dict(zip(outputs, results)))


def head_shards(
    hidden_in,
    segment_ids,
    order_ids,
    box_ids,
    qkv_weight,
    qkv_bias,
    rel_tables,
    out_weight,
    branch_bias,
    norm_gains,
    norm_shifts,
    ffn_in,
    ffn_in_bias,
    ffn_out,
    out_grad,
):
    rows, width = hidden_in.shape
    slot_rows = -(-rows // 48) * 48
    total = CHIPS * slot_rows
    depth = qkv_weight.shape[1]
    hidden = ffn_in.shape[1]
    half_hidden, half_width = hidden // 2, width // 2
    down_rows = ffn_out.shape[0]
    both = 2 * slot_rows
    fold_rows = -(-(slot_rows // 2) // 16) * 16
    any_, vmem, dma = pl.ANY, pltpu.VMEM, pltpu.SemaphoreType.DMA
    message = (CHIPS, fold_rows, 128)
    x_block, w_block = (HALF, slot_rows, width), (3, 2, CHIPS, depth, 128)
    in_all, down_all = (2, CHIPS, depth, half_hidden), (CHIPS, down_rows, width)
    out_all = (CHIPS, depth, width)
    in_half, down_half = (2, depth, half_hidden // 2), (down_rows, half_width)
    in_block, out_block = (2, depth, half_hidden), (depth, width)
    made = call(
        layer_kernel,
        "layer",
        0,
        dict(
            hidden_in=(hidden_in, vmem),
            segment_ids=(segment_ids.reshape(1, rows), vmem),
            order_ids=(order_ids.reshape(1, rows), vmem),
            box_ids=(box_ids, vmem),
            qkv_weight=(qkv_weight, vmem),
            qkv_bias=(qkv_bias, vmem),
            rel_tables=(rel_tables.transpose(0, 2, 1), vmem),
            out_weight=(out_weight, any_),
            branch_bias=(branch_bias, vmem),
            norm_gains=(norm_gains, vmem),
            norm_shifts=(norm_shifts, vmem),
            ffn_in=(ffn_in, any_),
            ffn_in_bias=(ffn_in_bias.reshape(1, down_rows), vmem),
            ffn_out=(ffn_out, any_),
            out_grad=(out_grad, vmem),
        ),
        dict(
            hidden_out=((rows, width), LOW, vmem),
            hidden_grad=((rows, width), LOW, vmem),
            qkv_grad=((3, depth, width), HIGH, vmem),
            qkv_bias_grad=((2, depth), HIGH, vmem),
            rel_tables_grad=((3, depth, NB), HIGH, vmem),
            out_w_grad=((depth, width), HIGH, vmem),
            branch_grad=((2, depth), HIGH, vmem),
            gain_grad=((2, depth), HIGH, vmem),
            shift_grad=((2, depth), HIGH, vmem),
            in_grad=((depth, hidden), HIGH, vmem),
            bias_grad=((1, down_rows), HIGH, vmem),
            down_grad=((down_rows, width), HIGH, vmem),
        ),
        dict(
            x_own=vmem((slot_rows, width), LOW),
            x_all=vmem(x_block, LOW),
            extra=vmem((slot_rows - rows, width), HIGH),
            small_wide=vmem((16, 128), HIGH),
            small_own=vmem((16, 128), LOW),
            small_all=vmem((CHIPS, 16, 128), LOW),
            w_all=vmem(w_block, LOW),
            rel_own=vmem((depth, 4 * NB), LOW),
            rel_all=vmem((2 * depth, 4 * NB), LOW),
            bias_far=vmem((2 * depth, NB), LOW),
            labels=vmem((CHIPS, 16, 256), LOW),
            near=vmem((total, 256), LOW),
            far_part=vmem((total // 2, 256), LOW),
            w_in=vmem(in_all, LOW),
            w_down=vmem(down_all, LOW),
            w_out=vmem(out_all, LOW),
            meta=vmem((total, 128), HIGH),
            shares=vmem((2, 8, half_width), HIGH),
            bias_in=vmem((1, half_hidden), HIGH),
            left=vmem((total, 384), LOW),
            right=vmem((total, 384), LOW),
            right_t=vmem((384, total), LOW),
            value=vmem((total, 128), LOW),
            value_t=vmem((128, total), LOW),
            kept=vmem((total, 128), HIGH),
            message=vmem(message, LOW),
            context_in=vmem(message, LOW),
            context_wide=vmem((both, half_width), HIGH),
            context=vmem((both, half_width), LOW),
            low_first=vmem((both, width), LOW),
            act=vmem((both, half_hidden), LOW),
            slope=vmem((both, half_hidden), HIGH),
            out_part=vmem((slot_rows, width), LOW),
            in_part=vmem((slot_rows, width), LOW),
            d_sum1=vmem((slot_rows, width), HIGH),
            d_second=vmem((both, width), LOW),
            g_out=vmem((CHIPS,) + out_block, LOW),
            in_1=vmem((2, 8) + in_half, LOW),
            in_2=vmem((2, 4) + in_half, LOW),
            in_3=vmem((2, 3) + in_half, LOW),
            down_1=vmem((2, 8) + down_half, LOW),
            down_2=vmem((2, 4) + down_half, LOW),
            down_3=vmem((2, 3) + down_half, LOW),
            out_1=vmem((3, 4) + out_block, LOW),
            out_2=vmem((2,) + out_block, LOW),
            out_3=vmem((1,) + out_block, LOW),
            in_total=vmem(in_block, HIGH),
            in_far=vmem((depth, half_hidden), HIGH),
            small_sum=vmem((8, width), HIGH),
            small_in=vmem((6, 8, width), HIGH),
            d_arrived=vmem(message, LOW),
            d_heads=vmem((3, HD, total), LOW),
            d_pair_t=vmem((2 * HD, total), HIGH),
            d_both=vmem((3, 2, HD, total // 2), LOW),
            x_stage=vmem((3, 7, slot_rows // 3, width), LOW),
            x_came=vmem((slot_rows, width), LOW),
            rel_grad=vmem((2 * depth, 4 * NB), HIGH),
            rel_low=vmem((2 * depth, 4 * NB), LOW),
            rel_came=vmem((2, depth, 4 * NB), LOW),
            w_far=vmem((2, 3 * HD, half_width), HIGH),
            w_low=vmem((CHIPS, depth, 6 * HD), LOW),
            w_came=vmem((CHIPS, depth, 6 * HD), LOW),
            keep_sem=dma((7,)),
            home_sem=dma((2,)),
            back_send=dma((3,)),
            back_recv=dma((3,)),
            x_send=dma((3, CubeGather.SENDS)),
            x_recv=dma((3, CubeGather.RECEIVES)),
            w_send=dma((1,)),
            w_recv=dma((1,)),
            rel_send=dma((2,)),
            rel_recv=dma((2,)),
            out_send=dma((2, GatherLate.SENDS)),
            out_recv=dma((2, GatherLate.RECEIVES)),
            in_send=dma((2, Gather.SENDS)),
            in_recv=dma((2, Gather.RECEIVES)),
            down_send=dma((2, Gather.SENDS)),
            down_recv=dma((2, Gather.RECEIVES)),
            msg_send=dma((1,)),
            msg_recv=dma((1,)),
            d_send=dma((1,)),
            d_recv=dma((1,)),
            g_in_send=dma((2, Reduce.SENDS)),
            g_in_recv=dma((2, Reduce.RECEIVES)),
            g_down_send=dma((2, Reduce.SENDS)),
            g_down_recv=dma((2, Reduce.RECEIVES)),
            g_out_send=dma((ReduceEarly.SENDS,)),
            g_out_recv=dma((ReduceEarly.RECEIVES,)),
            small_send=dma((6,)),
            small_recv=dma((6,)),
            d_x_send=dma((3, CubeReduce.SENDS)),
            d_x_recv=dma((3, CubeReduce.RECEIVES)),
            d_w_send=dma((1,)),
            d_w_recv=dma((1,)),
            d_rel_send=dma((2,)),
            d_rel_recv=dma((2,)),
            pair_send=dma((16,)),
            pair_recv=dma((16,)),
        ),
    )
    results = list(
        handed_over(
            [
                made.hidden_out,
                made.hidden_grad,
                made.qkv_grad,
                made.qkv_bias_grad,
                made.rel_tables_grad,
                made.out_w_grad,
                made.branch_grad,
                made.gain_grad,
                made.shift_grad,
                made.in_grad,
                made.bias_grad,
                made.down_grad,
            ]
        )
    )
    results[4] = results[4].transpose(0, 2, 1)
    results[10] = results[10].reshape(down_rows)
    return tuple(results)


def solution(mesh):
    by_heads = mesh.shape["grp"] == 2 and mesh.shape["blk"] == CHIPS == H
    return jax.shard_map(
        head_shards if by_heads else shards,
        mesh=mesh,
        in_specs=(
            P(("grp", "blk"), None),
            P(("grp", "blk")),
            P(("grp", "blk")),
            P(None, ("grp", "blk")),
            P(None, ("grp", "blk"), None),
            P(None, ("grp", "blk")),
            P(None, None, ("grp", "blk")),
            P(("grp", "blk"), None),
            P(None, ("grp", "blk")),
            P(None, ("grp", "blk")),
            P(None, ("grp", "blk")),
            P(("grp", "blk"), None),
            P(("grp", "blk")),
            P(("grp", "blk"), None),
            P(("grp", "blk"), None),
        ),
        out_specs=(
            P(("grp", "blk"), None),
            P(("grp", "blk"), None),
            P(None, ("grp", "blk"), None),
            P(None, ("grp", "blk")),
            P(None, None, ("grp", "blk")),
            P(("grp", "blk"), None),
            P(None, ("grp", "blk")),
            P(None, ("grp", "blk")),
            P(None, ("grp", "blk")),
            P(("grp", "blk"), None),
            P(("grp", "blk")),
            P(("grp", "blk"), None),
        ),
        check_vma=False,
    )
```

```python
import functools
import math
import types

import jax
import jax.numpy as jnp
from jax import lax
from jax.experimental import pallas as pl
from jax.experimental.pallas import tpu as pltpu
from jax.sharding import PartitionSpec as P

H = 16
HD = 64
NB = 128
ORDER_RANGE = 128
BOX_RANGE = 64


NEGATIVE = -1e30
EPSILON = 1e-05


def shifted(x, axis, by):
    devices = lax.axis_size(axis)
    return lax.ppermute(x, axis, [(i, (i + by) % devices) for i in range(devices)])


def block_size(row_count):
    chosen = 1
    for option in range(1, min(row_count, 544) + 1):
        if row_count % option == 0:
            chosen = option
    return chosen


def kind_ranges():
    return (ORDER_RANGE, BOX_RANGE, BOX_RANGE)


def query_maps(layout_ids):
    maps_out = []
    for column, extent in enumerate(kind_ranges()):
        offsets = layout_ids[:, column][:, None] - jnp.arange(extent, dtype=jnp.int32)[None, :]
        bucket = jnp.clip(offsets, -(NB // 2), NB // 2 - 1) + NB // 2
        maps_out.append(bucket[:, :, None] == jnp.arange(NB, dtype=jnp.int32)[None, None, :])
    return maps_out


def key_onehot(key_ids):
    pieces_out = []
    for column, extent in enumerate(kind_ranges()):
        pieces_out.append(
            key_ids[:, column + 1][:, None] == jnp.arange(extent, dtype=jnp.int32)[None, :]
        )
    return jnp.concatenate(pieces_out, axis=1).astype(jnp.bfloat16)


def norm_forward(values_in, norm_gain, norm_shift):
    center = values_in - jnp.mean(values_in, axis=-1, keepdims=True)
    inverse = lax.rsqrt(jnp.mean(center * center, axis=-1, keepdims=True) + EPSILON)
    normed = center * inverse
    return (normed * norm_gain + norm_shift, normed, inverse)


def norm_backward(upstream, normed, inverse, norm_gain):
    scaled = upstream * norm_gain
    inner_part = (
        scaled
        - jnp.mean(scaled, axis=-1, keepdims=True)
        - normed * jnp.mean(scaled * normed, axis=-1, keepdims=True)
    )
    return (inner_part * inverse, jnp.sum(upstream * normed, axis=0), jnp.sum(upstream, axis=0))


def block_logits(query_heads, selector, query_seg, key_part, meta_part, scaling):
    key_ids = meta_part.astype(jnp.int32)
    row_count = key_part.shape[0]
    key_heads = key_part.reshape(row_count, H, HD)
    content = jnp.einsum("thd,khd->htk", query_heads, key_heads, preferred_element_type=jnp.float32)
    onehot = key_onehot(key_ids)
    rel_bias = jnp.einsum("thv,kv->htk", selector, onehot, preferred_element_type=jnp.float32)
    allowed = query_seg[:, None] == key_ids[None, :, 0]
    logits = jnp.where(allowed[None], (content + rel_bias) * scaling, NEGATIVE)
    return (logits, allowed, onehot, key_heads)


def over_blocks(advance, carry, piece, start):
    row_count = piece[0].shape[0]
    stride = block_size(row_count)

    def one_step(block_index, running):
        portion = tuple(
            (lax.dynamic_slice_in_dim(member, block_index * stride, stride, 0) for member in piece)
        )
        return advance(running, portion, start + block_index * stride)

    return lax.fori_loop(0, row_count // stride, one_step, carry)


def shards(
    hidden_in,
    segment_ids,
    order_ids,
    box_ids,
    qkv_weight,
    qkv_bias,
    rel_tables,
    out_weight,
    branch_bias,
    norm_gains,
    norm_shifts,
    ffn_in,
    ffn_in_bias,
    ffn_out,
    out_grad,
):
    gathered = (
        lax.all_gather(qkv_weight, ("grp", "blk"), axis=1, tiled=True),
        lax.all_gather(qkv_bias, ("grp", "blk"), axis=1, tiled=True),
        lax.all_gather(rel_tables, ("grp", "blk"), axis=2, tiled=True),
        lax.all_gather(out_weight, ("grp", "blk"), axis=0, tiled=True),
        lax.all_gather(branch_bias, ("grp", "blk"), axis=1, tiled=True),
        lax.all_gather(norm_gains, ("grp", "blk"), axis=1, tiled=True),
        lax.all_gather(norm_shifts, ("grp", "blk"), axis=1, tiled=True),
        lax.all_gather(ffn_in, ("grp", "blk"), axis=0, tiled=True),
        lax.all_gather(ffn_in_bias, ("grp", "blk"), axis=0, tiled=True),
        lax.all_gather(ffn_out, ("grp", "blk"), axis=0, tiled=True),
    )
    w_qkv, b_qkv, w_rel, w_out, b_branch, gains, shifts, w_in, b_in, w_down = gathered
    row_count = hidden_in.shape[0]
    width = hidden_in.shape[1]
    scaling = 1.0 / math.sqrt(4.0 * HD)
    select_width = ORDER_RANGE + 2 * BOX_RANGE
    projected = jnp.einsum("td,cde->cte", hidden_in, w_qkv, preferred_element_type=jnp.float32)
    bias_qkv = b_qkv.astype(jnp.float32)
    query_rows = (projected[0] + bias_qkv[0]).astype(jnp.bfloat16)
    key_rows = projected[1].astype(jnp.bfloat16)
    value_rows = (projected[2] + bias_qkv[1]).astype(jnp.bfloat16)
    layout_ids = jnp.stack([order_ids, box_ids[0], box_ids[1]], axis=1)
    key_meta = jnp.stack([segment_ids, order_ids, box_ids[0], box_ids[1]], axis=1).astype(
        jnp.bfloat16
    )
    query_heads = query_rows.reshape(row_count, H, HD)
    rel_heads = w_rel.reshape(3, NB, H, HD)
    tables = jnp.einsum(
        "thd,nbhd->thnb", query_heads, rel_heads, preferred_element_type=jnp.float32
    ).astype(jnp.bfloat16)
    maps_list = query_maps(layout_ids)
    selector = jnp.concatenate(
        [
            jnp.einsum(
                "thb,tvb->thv",
                tables[:, :, column],
                maps_list[column].astype(jnp.bfloat16),
                preferred_element_type=jnp.float32,
            )
            for column in range(3)
        ],
        axis=2,
    ).astype(jnp.bfloat16)

    def forward_step(running, portion, offset):
        row_top, row_total, weighted = running
        key_part, value_part, meta_part = portion
        logits, allowed, onehot, key_heads = block_logits(
            query_heads, selector, segment_ids, key_part, meta_part, scaling
        )
        new_top = jnp.maximum(row_top, jnp.max(logits, axis=2))
        rescale = jnp.exp(row_top - new_top)
        weights = jnp.where(allowed[None], jnp.exp(logits - new_top[:, :, None]), 0.0)
        value_heads = value_part.reshape(value_part.shape[0], H, HD)
        weighted = weighted * rescale.T[:, :, None] + jnp.einsum(
            "htk,khd->thd",
            weights.astype(jnp.bfloat16),
            value_heads,
            preferred_element_type=jnp.float32,
        )
        return (new_top, row_total * rescale + jnp.sum(weights, axis=2), weighted)

    start_state = (
        jnp.full((H, row_count), NEGATIVE, jnp.float32),
        jnp.zeros((H, row_count), jnp.float32),
        jnp.zeros((row_count, H, HD), jnp.float32),
    )
    row_top, row_total, weighted = over_blocks(
        forward_step,
        start_state,
        (
            lax.all_gather(key_rows, "blk", axis=0, tiled=True),
            lax.all_gather(value_rows, "blk", axis=0, tiled=True),
            lax.all_gather(key_meta, "blk", axis=0, tiled=True),
        ),
        jnp.int32(0),
    )
    context_full = weighted / row_total.T[:, :, None]
    log_total = row_top + jnp.log(row_total)
    context = context_full.reshape(row_count, width).astype(jnp.bfloat16)
    branch = jnp.dot(context, w_out, preferred_element_type=jnp.float32) + b_branch[0].astype(
        jnp.float32
    )
    first, normed_one, inverse_one = norm_forward(
        hidden_in.astype(jnp.float32) + branch,
        gains[0].astype(jnp.float32),
        shifts[0].astype(jnp.float32),
    )
    first_low = first.astype(jnp.bfloat16)
    inner_pre = jnp.dot(first_low, w_in, preferred_element_type=jnp.float32) + b_in.astype(
        jnp.float32
    )
    activated, gelu_pull = jax.vjp(
        lambda pre_act: jax.nn.gelu(pre_act, approximate=False), inner_pre
    )
    activated_low = activated.astype(jnp.bfloat16)
    second = jnp.dot(activated_low, w_down, preferred_element_type=jnp.float32) + b_branch[
        1
    ].astype(jnp.float32)
    result, normed_two, inverse_two = norm_forward(
        first + second, gains[1].astype(jnp.float32), shifts[1].astype(jnp.float32)
    )
    hidden_out = result.astype(jnp.bfloat16)
    grad_sum2, gain_grad2, shift_grad2 = norm_backward(
        out_grad.astype(jnp.float32), normed_two, inverse_two, gains[1].astype(jnp.float32)
    )
    grad_second = grad_sum2.astype(jnp.bfloat16)
    grad_w_down = jnp.einsum(
        "tf,td->fd", activated_low, grad_second, preferred_element_type=jnp.float32
    )
    grad_bias_two = jnp.sum(grad_second.astype(jnp.float32), axis=0)
    grad_act = jnp.einsum("td,fd->tf", grad_second, w_down, preferred_element_type=jnp.float32)
    grad_inner = gelu_pull(grad_act)[0].astype(jnp.bfloat16)
    grad_b_in = jnp.sum(grad_inner.astype(jnp.float32), axis=0)
    grad_w_in = jnp.einsum("td,tf->df", first_low, grad_inner, preferred_element_type=jnp.float32)
    grad_first = grad_sum2 + jnp.einsum(
        "tf,df->td", grad_inner, w_in, preferred_element_type=jnp.float32
    )
    grad_sum1, gain_grad1, shift_grad1 = norm_backward(
        grad_first, normed_one, inverse_one, gains[0].astype(jnp.float32)
    )
    grad_branch = grad_sum1.astype(jnp.bfloat16)
    grad_w_out = jnp.einsum("td,te->de", context, grad_branch, preferred_element_type=jnp.float32)
    grad_bias_one = jnp.sum(grad_branch.astype(jnp.float32), axis=0)
    grad_context = jnp.einsum(
        "te,de->td", grad_branch, w_out, preferred_element_type=jnp.float32
    ).astype(jnp.bfloat16)
    grad_heads = grad_context.reshape(row_count, H, HD)
    delta = jnp.einsum("thd,thd->ht", grad_heads.astype(jnp.float32), context_full)

    def backward_core(grad_query, grad_select, portion):
        key_part, value_part, meta_part = portion
        logits, allowed, onehot, key_heads = block_logits(
            query_heads, selector, segment_ids, key_part, meta_part, scaling
        )
        probs = jnp.where(allowed[None], jnp.exp(logits - log_total[:, :, None]), 0.0)
        part_rows = key_part.shape[0]
        value_heads = value_part.reshape(part_rows, H, HD)
        grad_probs = jnp.einsum(
            "thd,khd->htk", grad_heads, value_heads, preferred_element_type=jnp.float32
        )
        grad_logits = (probs * (grad_probs - delta[:, :, None])).astype(jnp.bfloat16)
        grad_query = grad_query + scaling * jnp.einsum(
            "htk,khd->thd", grad_logits, key_heads, preferred_element_type=jnp.float32
        )
        grad_select = grad_select + scaling * jnp.einsum(
            "htk,kv->thv", grad_logits, onehot, preferred_element_type=jnp.float32
        )
        grad_key = scaling * jnp.einsum(
            "htk,thd->khd", grad_logits, query_heads, preferred_element_type=jnp.float32
        )
        grad_value = jnp.einsum(
            "htk,thd->khd",
            probs.astype(jnp.bfloat16),
            grad_heads,
            preferred_element_type=jnp.float32,
        )
        update = jnp.concatenate(
            [grad_key.reshape(part_rows, width), grad_value.reshape(part_rows, width)], axis=1
        )
        return (grad_query, grad_select, update)

    query_zero = jnp.zeros((row_count, H, HD), jnp.float32)
    select_zero = jnp.zeros((row_count, H, select_width), jnp.float32)

    def cycle_turn(turn, carry):
        grad_query, grad_select, key_part, value_part, meta_part, carried = carry
        portion = (key_part, value_part, meta_part)
        grad_query, grad_select, update = backward_core(grad_query, grad_select, portion)
        carried = carried + update
        key_part, value_part, meta_part = shifted((key_part, value_part, meta_part), "blk", 1)
        carried = shifted(carried.astype(jnp.bfloat16), "blk", 1).astype(carried.dtype)
        return (grad_query, grad_select, key_part, value_part, meta_part, carried)

    cycle_start = (
        query_zero,
        select_zero,
        key_rows,
        value_rows,
        key_meta,
        jnp.zeros((row_count, 2 * width), jnp.float32),
    )
    cycle_end = lax.fori_loop(0, lax.axis_size("blk"), cycle_turn, cycle_start)
    grad_query, grad_select, own_pairs = (cycle_end[0], cycle_end[1], cycle_end[5])
    grad_key_rows = own_pairs[:, :width].astype(jnp.bfloat16)
    grad_value_rows = own_pairs[:, width:].astype(jnp.bfloat16)
    cursor = 0
    table_parts = []
    for column, extent in enumerate(kind_ranges()):
        table_parts.append(
            jnp.einsum(
                "thv,tvb->thb",
                grad_select[:, :, cursor : cursor + extent],
                maps_list[column].astype(jnp.float32),
                precision=lax.Precision.HIGHEST,
            )
        )
        cursor = cursor + extent
    grad_tables = jnp.stack(table_parts, axis=2).astype(jnp.bfloat16)
    grad_query_total = grad_query + jnp.einsum(
        "thnb,nbhd->thd", grad_tables, rel_heads, preferred_element_type=jnp.float32
    )
    grad_query_rows = grad_query_total.reshape(row_count, width).astype(jnp.bfloat16)
    grad_rel = jnp.einsum(
        "thnb,thd->nbhd", grad_tables, query_heads, preferred_element_type=jnp.float32
    ).reshape(3, NB, width)
    grad_stack = jnp.stack([grad_query_rows, grad_key_rows, grad_value_rows])
    grad_w_qkv = jnp.einsum(
        "td,cte->cde", hidden_in, grad_stack, preferred_element_type=jnp.float32
    )
    grad_b_qkv = jnp.stack(
        [
            jnp.sum(grad_query_rows.astype(jnp.float32), axis=0),
            jnp.sum(grad_value_rows.astype(jnp.float32), axis=0),
        ]
    )
    grad_input = grad_sum1 + jnp.einsum(
        "cte,cde->td", grad_stack, w_qkv, preferred_element_type=jnp.float32
    )
    summed = (
        lax.psum_scatter(grad_w_qkv, ("grp", "blk"), scatter_dimension=1, tiled=True),
        lax.psum_scatter(grad_b_qkv, ("grp", "blk"), scatter_dimension=1, tiled=True),
        lax.psum_scatter(grad_rel, ("grp", "blk"), scatter_dimension=2, tiled=True),
        lax.psum_scatter(grad_w_out, ("grp", "blk"), scatter_dimension=0, tiled=True),
        lax.psum_scatter(
            jnp.stack([grad_bias_one, grad_bias_two]),
            ("grp", "blk"),
            scatter_dimension=1,
            tiled=True,
        ),
        lax.psum_scatter(
            jnp.stack([gain_grad1, gain_grad2]), ("grp", "blk"), scatter_dimension=1, tiled=True
        ),
        lax.psum_scatter(
            jnp.stack([shift_grad1, shift_grad2]), ("grp", "blk"), scatter_dimension=1, tiled=True
        ),
        lax.psum_scatter(grad_w_in, ("grp", "blk"), scatter_dimension=0, tiled=True),
        lax.psum_scatter(grad_b_in, ("grp", "blk"), scatter_dimension=0, tiled=True),
        lax.psum_scatter(grad_w_down, ("grp", "blk"), scatter_dimension=0, tiled=True),
    )
    return (
        hidden_out,
        grad_input.astype(jnp.bfloat16),
        summed[0],
        summed[1],
        summed[2],
        summed[3],
        summed[4],
        summed[5],
        summed[6],
        summed[7],
        summed[8],
        summed[9],
    )


MESH = pl.DeviceIdType.MESH
LOW = jnp.bfloat16
HIGH = jnp.float32
CHIPS = 16
HALF = 8
BLOCK = 256
MASKED = -1e30
VMEM_LIMIT = 62 * 2**20
NT = ((1,), (1,))
TN = ((0,), (0,))


def dot(left, right, dims=((1,), (0,))):
    return lax.dot_general(left, right, (dims, ((), ())), preferred_element_type=HIGH)


def place():
    return lax.axis_index("grp"), lax.axis_index("blk")


def coordinates(chip):
    return lax.div(chip, 4), lax.rem(lax.div(chip, 2), 2), lax.rem(chip, 2)


def greet_all():
    core, chip = place()
    me = core * CHIPS + chip
    barrier = pltpu.get_barrier_semaphore()

    def greet(ahead, carry):
        other = lax.rem(me + ahead, 2 * CHIPS)
        pl.semaphore_signal(
            barrier,
            inc=1,
            device_id=(lax.div(other, CHIPS), lax.rem(other, CHIPS)),
            device_id_type=MESH,
        )
        return carry

    lax.fori_loop(1, 2 * CHIPS, greet, 0)


def await_all():
    pl.semaphore_wait(pltpu.get_barrier_semaphore(), 2 * CHIPS - 1)


def remote(source, target, send, recv, device):
    return pltpu.make_async_remote_copy(
        src_ref=source,
        dst_ref=target,
        send_sem=send,
        recv_sem=recv,
        device_id=device,
        device_id_type=MESH,
    )


def local(source, target, sem):
    return pltpu.make_async_copy(source, target, sem)


MIRROR = 3


def in_the_middle():
    z, _, _ = coordinates(lax.axis_index("blk"))
    return jnp.logical_and(z > 0, z < 3)


def neighbours(across):
    core, chip = place()
    z, y, x = coordinates(chip)
    planes = (z + 1 - 2 * lax.rem(z, 2), 2 - lax.div(z, 2), 3 - 3 * lax.div(z, 2), 3 - z)

    def slot(far_p, far_q, line):
        far_y, far_x = (far_q, far_p) if across == "x" else (far_p, far_q)
        plane = z if line is None else planes[line]
        return plane * 4 + (1 - y if far_y else y) * 2 + (1 - x if far_x else x)

    return slot


class Shipments:
    def __init__(self, send, recv):
        self.send, self.recv = send, recv
        self.core = lax.axis_index("grp")

    def ship(self, source, target, kind, recv_index, to, when=None):
        start = lambda: remote(
            source, target, self.send.at[kind], self.recv.at[recv_index], (self.core, to)
        ).start()
        if when is None:
            start()
        else:
            pl.when(when)(start)

    def landed(self, target, recv_index):
        local(target, target, self.recv.at[recv_index]).wait()

    def all_sent(self, bytes_of, kind):
        local(bytes_of, bytes_of, self.send.at[kind]).wait()


class Gather:
    SENDS, RECEIVES = 2, 9

    def __init__(self, pick, send, recv, across):
        self.pick, self.at = pick, neighbours(across)
        self.moves = Shipments(send, recv)
        self.middle = in_the_middle()

    def ship(self, what, kind, recv_index, to, when=None):
        ref = self.pick(self.at(*what))
        self.moves.ship(ref, ref, kind, recv_index, self.at(*to), when)

    def plane(self, line):
        return lax.div(self.at(0, 0, line), 4)

    def along_z(self, line, to, when=None):
        self.ship((0, 0, line), 0, self.plane(line), (0, 0, to), when)

    def along_p(self, line):
        self.ship((0, 0, line), 1, 4 + self.plane(line), (1, 0, None))

    def along_q(self, far_p, line):
        self.ship((far_p, 0, line), 1, 8, (0, 1, None))

    def own_line(self, number):
        if number == 0:
            self.along_z(None, 0)
        else:
            self.along_z(None, MIRROR, self.middle)

    def own_plane(self):
        self.along_p(None)
        self.along_q(0, None)

    def line(self, line):
        self.moves.landed(self.pick(self.at(0, 0, line)), self.plane(line))
        self.along_z(line, MIRROR if line == 0 else 0, self.middle)
        self.along_p(line)
        self.along_q(0, line)

    def side(self, line):
        self.moves.landed(self.pick(self.at(1, 0, line)), 4 + self.plane(line))
        self.along_q(1, line)

    def arrive(self):
        self.moves.landed(self.pick(pl.ds(0, 8)), 8)

    def finish(self):
        self.moves.all_sent(self.pick(pl.ds(0, 12)), 1)
        pl.when(self.middle)(lambda: self.moves.all_sent(self.pick(pl.ds(0, 5)), 0))
        pl.when(jnp.logical_not(self.middle))(lambda: self.moves.all_sent(self.pick(pl.ds(0, 1)), 0))


class GatherLate(Gather):
    SENDS, RECEIVES = 3, 6

    def plane_slots(self, line):
        return self.pick(pl.ds(self.plane(line) * 4, 4))

    def first(self):
        self.ship((0, 0, None), 0, 4, (1, 0, None))
        self.ship((0, 0, None), 0, 5, (0, 1, None))

    def second(self):
        self.moves.landed(self.pick(self.at(1, 0, None)), 4)
        self.ship((1, 0, None), 0, 5, (0, 1, None))

    def pass_plane(self, line, kind, to, when=None):
        slots = self.plane_slots(line)
        self.moves.ship(slots, slots, kind, self.plane(line), self.at(0, 0, to), when)

    def third(self):
        self.moves.landed(self.pick(pl.ds(0, 2)), 5)
        self.pass_plane(None, 1, 0)
        self.pass_plane(None, 2, MIRROR, self.middle)

    def late_line(self, line):
        self.moves.landed(self.plane_slots(line), self.plane(line))
        self.pass_plane(line, 2, MIRROR if line == 0 else 0, self.middle)

    def finish(self):
        self.moves.all_sent(self.pick(pl.ds(0, 3)), 0)
        self.moves.all_sent(self.pick(pl.ds(0, 4)), 1)
        pl.when(self.middle)(lambda: self.moves.all_sent(self.pick(pl.ds(0, 16)), 2))


class Reduce:
    SENDS, RECEIVES = 1, 15

    def __init__(self, pick, stages, send, recv, across):
        self.pick, self.at = pick, neighbours(across)
        self.first, self.second, self.third_in = stages
        self.moves = Shipments(send, recv)

    @staticmethod
    def number(line):
        return 3 if line is None else line

    def plane(self, line):
        return lax.div(self.at(0, 0, line), 4)

    def mine(self, *what):
        return self.pick(self.at(*what))

    def term(self, stage, index, recv_index):
        self.moves.landed(stage.at[index], recv_index)
        return stage[index].astype(HIGH)

    def start(self, line):
        for far_p in (1, 0):
            index = self.number(line) * 2 + far_p
            self.moves.ship(
                self.mine(far_p, 1, line), self.first.at[index], 0, index, self.at(0, 1, None)
            )

    def side(self, line):
        number = self.number(line)
        index = number * 2 + 1
        total = self.term(self.first, index, index) + self.mine(1, 0, line)[...].astype(HIGH)
        self.first[index] = total.astype(LOW)
        self.moves.ship(
            self.first.at[index], self.second.at[number], 0, 8 + number, self.at(1, 0, None)
        )

    def line(self, line):
        number = self.number(line)
        index = number * 2
        total = (
            self.term(self.first, index, index)
            + self.term(self.second, number, 8 + number)
            + self.mine(0, 0, line)[...].astype(HIGH)
        )
        if line is None:
            return total
        self.first[index] = total.astype(LOW)
        ahead = self.ahead(line)
        self.moves.ship(
            self.first.at[index], self.third_in.at[ahead], 0, 12 + ahead, self.at(0, 0, line)
        )

    def ahead(self, line):
        return lax.rem(self.plane(None) - self.plane(line) + 4, 4) - 1

    def finish(self, result):
        total = self.line(None)
        for ahead in range(3):
            total += self.term(self.third_in, ahead, 12 + ahead)
        result[...] = total
        self.moves.all_sent(self.pick(pl.ds(0, 15)), 0)


class ReduceEarly(Reduce):
    SENDS, RECEIVES = 1, 6

    def start(self):
        for line in (2, 1, 0):
            ahead = self.ahead(line)
            self.moves.ship(
                self.pick(pl.ds(self.plane(line) * 4, 4)),
                self.first.at[ahead],
                0,
                ahead,
                self.at(0, 0, line),
            )

    def plane_sum(self, *what):
        slot = self.at(*what, None)
        total = self.pick(slot)[...].astype(HIGH)
        for ahead in range(3):
            total += self.first[ahead, lax.rem(slot, 4)].astype(HIGH)
        return total

    def plane_ref(self, *what):
        return self.first.at[0, lax.rem(self.at(*what, None), 4)]

    def third(self):
        for ahead in range(3):
            self.moves.landed(self.first.at[ahead], ahead)
        for far_p in (1, 0):
            ref = self.plane_ref(far_p, 1)
            ref[...] = self.plane_sum(far_p, 1).astype(LOW)
            self.moves.ship(ref, self.second.at[far_p], 0, 3 + far_p, self.at(0, 1, None))

    def across(self):
        ref = self.plane_ref(1, 0)
        ref[...] = (self.plane_sum(1, 0) + self.term(self.second, 1, 4)).astype(LOW)
        self.moves.ship(ref, self.third_in.at[0], 0, 5, self.at(1, 0, None))

    def finish(self, result):
        result[...] = (
            self.plane_sum(0, 0) + self.term(self.second, 0, 3) + self.term(self.third_in, 0, 5)
        )
        self.moves.all_sent(self.pick(pl.ds(0, 15)), 0)


def cube_of(order):
    core, chip = place()
    z, y, x = coordinates(chip)

    def at(*flips):
        far = dict(zip(order, flips))
        plane = z + 1 - 2 * lax.rem(z, 2) if far["z"] else z
        return plane * 4 + (1 - y if far["y"] else y) * 2 + (1 - x if far["x"] else x)

    return at


class CubeGather:
    SENDS, RECEIVES = 1, 4

    def __init__(self, pick, send, recv, order):
        self.pick, self.at = pick, cube_of(order)
        self.moves = Shipments(send, recv)

    def ref(self, *what):
        return self.pick(lax.rem(self.at(*what), HALF))

    def ship(self, what, recv_index, to):
        self.moves.ship(self.ref(*what), self.ref(*what), 0, recv_index, self.at(*to))

    def own(self):
        self.ship((0, 0, 0), 0, (1, 0, 0))
        self.ship((0, 0, 0), 1, (0, 1, 0))
        self.ship((0, 0, 0), 3, (0, 0, 1))

    def one(self):
        self.moves.landed(self.ref(1, 0, 0), 0)
        self.ship((1, 0, 0), 2, (0, 1, 0))
        self.ship((1, 0, 0), 3, (0, 0, 1))

    def two(self):
        for one in range(2):
            self.moves.landed(self.ref(one, 1, 0), 1 + one)
            self.ship((one, 1, 0), 3, (0, 0, 1))

    def arrive(self):
        self.moves.landed(self.pick(pl.ds(0, 4)), 3)

    def finish(self):
        self.moves.all_sent(self.pick(pl.ds(0, 7)), 0)


class CubeReduce:
    SENDS, RECEIVES = 1, 7

    def __init__(self, pick, stage, send, recv, order):
        self.pick, self.stage, self.at = pick, stage, cube_of(order)
        self.moves = Shipments(send, recv)

    def ship(self, source, index, to):
        self.moves.ship(source, self.stage.at[index], 0, index, self.at(*to))

    def mine(self, *what):
        return self.pick(lax.rem(self.at(*what), HALF))

    def term(self, index):
        self.moves.landed(self.stage.at[index], index)
        return self.stage[index].astype(HIGH)

    def own(self):
        for index, (one, two) in enumerate(((1, 1), (0, 1), (1, 0), (0, 0))):
            self.ship(self.mine(one, two, 1), index, (0, 0, 1))

    def one(self):
        for index, one in ((0, 1), (1, 0)):
            total = self.mine(one, 1, 0)[...].astype(HIGH) + self.term(index)
            self.stage[index] = total.astype(LOW)
            self.ship(self.stage.at[index], 4 + index, (0, 1, 0))

    def two(self):
        total = self.mine(1, 0, 0)[...].astype(HIGH) + self.term(2) + self.term(4)
        self.stage[2] = total.astype(LOW)
        self.ship(self.stage.at[2], 6, (1, 0, 0))

    def arrive(self):
        return self.mine(0, 0, 0)[...].astype(HIGH) + self.term(3) + self.term(5) + self.term(6)

    def finish(self):
        self.moves.all_sent(self.stage, 0)


def each(plans, act, *arguments):
    for plan in plans:
        act(plan, *arguments)


def unit():
    core, chip = place()
    return lax.div(chip, HALF), lax.rem(chip, HALF), core


def all_but_one(source, send, itself):
    most = source.at[pl.ds(0, CHIPS - 1)]
    pl.when(itself)(lambda: local(most, most, send.at[0]).wait())
    pl.when(jnp.logical_not(itself))(lambda: local(source, source, send.at[0]).wait())


def to_tokens(source, target, send, recv):
    core, chip = place()
    group, position, _ = unit()
    to_core = lax.div(position, 4)
    mine = group * HALF + 2 * lax.rem(position, 4) + core
    here = to_core == core

    def copy_to(ahead):
        chip_to = lax.rem(chip + ahead, CHIPS)
        return remote(
            source.at[chip_to], target.at[mine], send.at[0], recv.at[0], (to_core, chip_to)
        )

    pl.when(here)(lambda: local(source.at[chip], target.at[mine], recv.at[0]).start())
    pl.when(jnp.logical_not(here))(lambda: copy_to(0).start())
    for ahead in range(1, CHIPS):
        copy_to(ahead).start()
    arrive = lambda: local(target, target, recv.at[0]).wait()
    return arrive, lambda: all_but_one(source, send, here)


def to_heads(source, target, send, recv):
    core, chip = place()
    group, position, _ = unit()
    here = lax.div(position, 4) == core
    start = 2 * lax.rem(position, 4) + core

    def copy_to(turn_group, ahead):
        to_group = lax.rem(group + turn_group, 2)
        head = lax.rem(start + ahead, HALF)
        return remote(
            source.at[to_group * HALF + head],
            target.at[chip],
            send.at[0],
            recv.at[0],
            (lax.rem(head, 2), to_group * HALF + core * 4 + lax.div(head, 2)),
        )

    pl.when(here)(lambda: local(source.at[group * HALF + start], target.at[chip], recv.at[0]).start())
    pl.when(jnp.logical_not(here))(lambda: copy_to(0, 0).start())
    for turn_group in range(2):
        for ahead in range(0 if turn_group else 1, HALF):
            copy_to(turn_group, ahead).start()
    arrive = lambda: local(target, target, recv.at[0]).wait()
    return arrive, lambda: all_but_one(source, send, here)


def lanes(rows, width=128):
    return lax.broadcasted_iota(jnp.int32, (rows, width), 1)


def turn(values):
    return pltpu.roll(values, HD, 1)


def fold(rows_in):
    half = rows_in.shape[0] // 2
    both = jnp.where(lanes(half) < HD, rows_in[:half], turn(rows_in[half:]))
    pad = -half % 16
    if pad:
        both = jnp.concatenate([both, jnp.zeros((pad, 128), HIGH)], axis=0)
    return both.astype(LOW)


def column_sums(v):
    return jnp.sum(v, axis=0, keepdims=True)


def gelu_parts(pre):
    cdf = 0.5 * (1.0 + lax.erf(pre * math.sqrt(0.5)))
    density = jnp.exp(-0.5 * pre * pre) * (1.0 / math.sqrt(2.0 * math.pi))
    return pre * cdf, cdf + pre * density


def normalize(v, gain, shift):
    center = v - jnp.mean(v, axis=1, keepdims=True)
    inverse = lax.rsqrt(jnp.mean(center * center, axis=1, keepdims=True) + EPSILON)
    normed = center * inverse
    return normed * gain + shift, normed, inverse


def normalize_back(c, normed, inverse, gain):
    scaled = c * gain
    inner = (
        scaled
        - jnp.mean(scaled, axis=1, keepdims=True)
        - normed * jnp.mean(scaled * normed, axis=1, keepdims=True)
    )
    return inner * inverse


def at_steps(index, steps):
    for number, acts in steps.items():

        def run(acts=acts):
            for act in acts:
                act()

        pl.when(index == number)(run)


def columns_of(half, width):
    return pl.ds(pl.multiple_of(half * width, 128), width)


def layer_kernel(names, *refs):
    r = types.SimpleNamespace(**dict(zip(names, refs)))
    hidden, x_all, w_all, rel_all = r.hidden_in, r.x_all, r.w_all, r.rel_all
    token_rows, width = hidden.shape
    slot_rows = x_all.shape[1]
    total = CHIPS * slot_rows
    depth = r.out_weight.shape[0]
    w_in, w_down, w_out = r.w_in, r.w_down, r.w_out
    half_hidden = w_in.shape[3]
    half_width = width // 2
    core, chip = place()
    group, position, _ = unit()
    other = 1 - core
    me = core * CHIPS + chip
    keep = r.keep_sem

    greet_all()

    loads = [
        local(r.ffn_in.at[:, columns_of(core, half_hidden)], w_in.at[core, chip], keep.at[0]),
        local(r.ffn_out, w_down.at[chip], keep.at[1]),
        local(r.out_weight, w_out.at[chip], keep.at[2]),
    ]
    for copy in loads:
        copy.start()

    extra = r.extra
    extra[...] = jnp.zeros_like(extra)
    extra[0:1, 0:256] = jnp.full((1, 256), 4.0, HIGH)
    extra[0:1, 0:token_rows] = r.segment_ids[...].astype(HIGH)
    extra[1:2, 0:token_rows] = r.order_ids[...].astype(HIGH)
    extra[2:4, 0:token_rows] = r.box_ids[...].astype(HIGH)
    tail = token_rows - token_rows % 16
    x_own = r.x_own
    x_own[0:tail, :] = hidden[0:tail, :]
    x_own[tail:slot_rows, :] = jnp.concatenate(
        [hidden[tail:token_rows, :].astype(HIGH), extra[...]], axis=0
    ).astype(LOW)
    weight = r.qkv_weight
    rel_own = r.rel_own
    for kind in range(3):
        rel_own[:, kind * NB : (kind + 1) * NB] = r.rel_tables[kind]
    eye_depth = (
        lax.broadcasted_iota(jnp.int32, (depth, depth), 0)
        == lax.broadcasted_iota(jnp.int32, (depth, depth), 1)
    ).astype(LOW)
    bias_columns = dot(eye_depth, r.qkv_bias[...], NT)
    rel_own[:, 3 * NB : 4 * NB] = jnp.where(
        lanes(depth) == 0, bias_columns[:, 0:1], jnp.where(lanes(depth) == 1, bias_columns[:, 1:2], 0.0)
    ).astype(LOW)
    small_wide, small_own, small_all = r.small_wide, r.small_own, r.small_all
    small_wide[...] = jnp.zeros_like(small_wide)
    for number, pair in enumerate((r.branch_bias, r.norm_gains, r.norm_shifts)):
        small_wide[2 * number : 2 * number + 2, 0:depth] = pair[...].astype(HIGH)
    small_wide[6:7, :] = r.ffn_in_bias[...].astype(HIGH)
    small_own[...] = small_wide[...].astype(LOW)
    loads += [
        local(small_own, small_all.at[chip], keep.at[3]),
        local(weight.at[:, :, columns_of(position, 128)], w_all.at[:, core, chip], keep.at[4]),
    ]
    for copy in loads[3:]:
        copy.start()
    await_all()

    at_home = group == core
    away = lax.rem(chip + HALF, CHIPS)
    x_slot = x_all.at[position]
    home = lambda: local(x_own, x_slot, r.home_sem.at[1])
    abroad = lambda: remote(x_own, x_slot, r.home_sem.at[0], r.home_sem.at[1], (other, away))
    pl.when(at_home)(lambda: home().start())
    pl.when(jnp.logical_not(at_home))(lambda: abroad().start())

    rel_head = core * HALF + lax.div(chip, 2)
    parity = lax.rem(chip, 2)
    rel_slot = rel_all.at[pl.ds(parity * depth, depth)]

    def rel_each(act_remote, act_own):
        for to_group in range(2):
            to = (lax.rem(rel_head, 2), to_group * HALF + lax.div(rel_head, 2))
            itself = jnp.logical_and(to[0] == core, to[1] == chip)
            copy = lambda: remote(
                rel_own, rel_slot, r.rel_send.at[to_group], r.rel_recv.at[parity], to
            )
            pl.when(jnp.logical_not(itself))(lambda: act_remote(copy()))
            if act_own is not None:
                pl.when(itself)(act_own)

    rel_each(
        lambda copy: copy.start(), lambda: local(rel_own, rel_slot, r.rel_recv.at[parity]).start()
    )

    def w_copy(ahead):
        to = lax.rem(chip + ahead, CHIPS)
        return remote(
            weight.at[:, :, columns_of(lax.rem(to, HALF), 128)],
            w_all.at[:, core, chip],
            r.w_send.at[0],
            r.w_recv.at[0],
            (core, to),
        )

    swap_in = remote(
        r.ffn_in.at[:, columns_of(other, half_hidden)],
        w_in.at[core, chip],
        r.pair_send.at[0],
        r.pair_recv.at[0],
        (other, chip),
    )
    swap_in.start()

    third = slot_rows // 3
    x_plans = [
        CubeGather(
            lambda slot, part=part: x_all.at[slot, pl.ds(part * third, third)],
            r.x_send.at[part],
            r.x_recv.at[part],
            order,
        )
        for part, order in enumerate(("xyz", "yzx", "zxy"))
    ]
    half_down = w_down.shape[1] // 2
    plans_out = [
        GatherLate(lambda slot: w_out.at[slot], r.out_send.at[0], r.out_recv.at[0], "x"),
        GatherLate(lambda slot: small_all.at[slot], r.out_send.at[1], r.out_recv.at[1], "y"),
    ]

    def in_half(slot, part):
        return w_in.at[part, slot]

    def down_half(slot, part):
        return w_down.at[slot, pl.ds(part * half_down, half_down)]

    def halves(pick, sends, recvs):
        return [
            Gather(functools.partial(pick, part=part), sends.at[part], recvs.at[part], across)
            for part, across in enumerate("xy")
        ]

    plans_in = halves(in_half, r.in_send, r.in_recv)
    plans_down = halves(down_half, r.down_send, r.down_recv)

    for copy in loads:
        copy.wait()
    each(plans_down, Gather.own_plane)
    each(plans_out, GatherLate.first)
    swap_in.wait()
    each(plans_in, Gather.own_plane)
    each(plans_in, Gather.own_line, 0)
    for ahead in range(1, CHIPS):
        w_copy(ahead).start()
    each(plans_out, GatherLate.second)
    each(plans_in, Gather.own_line, 1)
    home().wait()
    each(x_plans, CubeGather.own)
    each(x_plans, CubeGather.one)
    each(x_plans, CubeGather.two)
    each(plans_down, Gather.own_line, 0)
    w_most = w_all.at[:, core, pl.ds(0, CHIPS - 1)]
    local(w_most, w_most, r.w_recv.at[0]).wait()
    pair_w = remote(w_all.at[:, core], w_all.at[:, core], r.pair_send.at[1], r.pair_recv.at[1], (other, chip))
    pair_w.start()
    for slot in range(2):
        local(rel_own, rel_all.at[pl.ds(slot * depth, depth)], r.rel_recv.at[slot]).wait()
    pair_bias = remote(
        rel_all.at[:, pl.ds(3 * NB, NB)], r.bias_far, r.pair_send.at[2], r.pair_recv.at[2], (other, chip)
    )
    pair_bias.start()
    each(plans_down, Gather.side, None)
    each(plans_out, GatherLate.third)
    each(plans_in, Gather.line, 0)
    each(x_plans, CubeGather.arrive)
    pl.when(jnp.logical_not(at_home))(lambda: abroad().wait_send())

    labels = r.labels
    first_slot = core * HALF
    label_part = x_all.at[:, pl.ds(slot_rows - 16, 16), pl.ds(0, 256)]
    label_slots = labels.at[pl.ds(first_slot, HALF)]
    pair_label = remote(label_part, label_slots, r.pair_send.at[3], r.pair_recv.at[3], (other, chip))
    pair_label.start()
    own_label = local(label_part, label_slots, keep.at[5])
    own_label.start()
    pair_w.wait()
    pair_bias.wait()

    head_rows = 2 * depth
    row_at = lax.broadcasted_iota(jnp.int32, (head_rows, 128), 0)
    column_at = lanes(head_rows)

    def bias_row(columns, number):
        column = columns[:, number : number + 1]
        return column_sums(jnp.where(row_at == column_at, column, 0.0))

    rel = rel_all[...]
    bias_near = rel[:, 3 * NB : 4 * NB].astype(HIGH)
    bias_far = r.bias_far[...].astype(HIGH)
    bias_query, bias_value = (
        bias_row(bias_near, number) + turn(bias_row(bias_far, number)) for number in range(2)
    )
    weights = [w_all[n].reshape(width, 128) for n in range(3)]
    near, far_part = r.near, r.far_part
    pair_rows = 2 * slot_rows
    pair_half = lanes(pair_rows) < HD

    for pair in range(HALF // 2):
        tokens = x_all[2 * pair : 2 * pair + 2].reshape(pair_rows, width)
        query, key, value_rows = (
            pltpu.roll(dot(tokens, weights[n]), core * HD, 1) for n in range(3)
        )
        query, value_rows = query + bias_query, value_rows + bias_value
        rows = pl.ds(pl.multiple_of(core * HALF * slot_rows, 16) + pair * pair_rows, pair_rows)
        near[rows, 0:128] = jnp.where(pair_half, query, turn(value_rows)).astype(LOW)
        near[rows, 128:256] = key.astype(LOW)
        far_rows = slice(pair * pair_rows, (pair + 1) * pair_rows)
        far_part[far_rows, 0:128] = jnp.where(pair_half, turn(query), value_rows).astype(LOW)
        far_part[far_rows, 128:256] = turn(key).astype(LOW)
    pair_qkv = remote(
        far_part,
        near.at[pl.ds(pl.multiple_of(core * HALF * slot_rows, 16), HALF * slot_rows)],
        r.pair_send.at[4],
        r.pair_recv.at[4],
        (other, chip),
    )
    pair_qkv.start()

    meta = r.meta
    eye = (
        lax.broadcasted_iota(jnp.int32, (slot_rows, 256), 0)
        == lax.broadcasted_iota(jnp.int32, (slot_rows, 256), 1)
    ).astype(LOW)
    pair_label.wait()
    own_label.wait()
    for slot in range(CHIPS):
        meta[slot * slot_rows : (slot + 1) * slot_rows, 0:16] = dot(eye, labels[slot], NT)
    table_t = rel[:, 0 : 3 * NB]
    lane = lanes(BLOCK)
    first_half = lane < HD
    scale = 1.0 / math.sqrt(4.0 * HD)
    left, right, right_t = r.left, r.right, r.right_t
    value, value_t, kept = r.value, r.value_t, r.kept
    pair_qkv.wait()

    def prepare(index, carry):
        rows = pl.ds(pl.multiple_of(index * BLOCK, BLOCK), BLOCK)
        at_steps(
            index,
            {
                1: [lambda: each(plans_down, Gather.own_line, 1), lambda: each(plans_down, Gather.line, 0)],
                3: [lambda: each(plans_in, Gather.line, 1)],
                8: [lambda: each(plans_in, Gather.line, 2)],
            },
        )
        query_value = near[rows, 0:128].astype(HIGH)
        key = near[rows, 128:256].astype(HIGH)
        tables = dot(near[rows, 0:128][:, 0:HD], table_t).astype(LOW).astype(HIGH)
        ids = meta[rows, 8:12].astype(jnp.int32)
        segment, order, box_x, box_y = ids[:, 0:1], ids[:, 1:2], ids[:, 2:3], ids[:, 3:4]

        def selected(column, ids_of, values):
            bucket = jnp.clip(ids_of - values, -(NB // 2), NB // 2 - 1) + NB // 2
            return jnp.take_along_axis(tables[:, column * NB : (column + 1) * NB], bucket, axis=1)

        wide = selected(0, order, lane)
        narrow = jnp.where(first_half, selected(1, box_x, lane), selected(2, box_y, lane - HD))
        label = lane - HD
        query_side = jnp.where(
            first_half,
            query_value * scale,
            jnp.where(jnp.logical_and(label != segment, label < 8), MASKED, 0.0),
        )
        key_side = jnp.where(first_half, key, (label == segment).astype(HIGH))
        left[rows, 0:128] = (wide * scale).astype(LOW)
        left[rows, 128:256] = (narrow * scale).astype(LOW)
        left[rows, 256:384] = query_side.astype(LOW)
        order_hot = (lane == order).astype(HIGH)
        box_hot = (jnp.where(first_half, box_x, box_y + HD) == lane).astype(HIGH)
        right[rows, 0:128] = order_hot.astype(LOW)
        right[rows, 128:256] = box_hot.astype(LOW)
        right[rows, 256:384] = key_side.astype(LOW)
        right_t[0:128, rows] = order_hot.T.astype(LOW)
        right_t[128:256, rows] = box_hot.T.astype(LOW)
        right_t[256:384, rows] = key_side.T.astype(LOW)
        held = jnp.where(first_half, turn(query_value), (label == 0).astype(HIGH))
        value[rows, :] = held.astype(LOW)
        value_t[:, rows] = held.T.astype(LOW)
        return carry

    lax.fori_loop(0, total // BLOCK, prepare, 0)
    def attend(index, carry):
        rows = pl.ds(pl.multiple_of(index * BLOCK, BLOCK), BLOCK)
        at_steps(
            index,
            {
                2: [lambda: each(plans_in, Gather.side, None)],
                4: [lambda: each(plans_down, Gather.line, 1)],
                8: [lambda: each(plans_down, Gather.line, 2)],
            },
        )
        logits = dot(left[rows, :], right_t[...])
        top = jnp.max(logits, axis=1, keepdims=True)
        weights = jnp.exp(logits - top).astype(LOW)
        mixed = dot(weights, value[...])
        row_sum = mixed[:, HD : HD + 1]
        ids = meta[rows, 8:12]
        facts = jnp.where(lane == HD, top + jnp.log(row_sum), ids[:, 3:4])
        facts = jnp.where(lane == HD + 1, ids[:, 1:2], facts)
        facts = jnp.where(lane == HD + 2, ids[:, 2:3], facts)
        kept[rows, :] = jnp.where(first_half, mixed / row_sum, facts)
        return carry

    lax.fori_loop(0, total // BLOCK, attend, 0)
    each(plans_out, GatherLate.late_line, 0)
    message, context_in = r.message, r.context_in
    for slot in range(CHIPS):
        message[slot] = fold(kept[slot * slot_rows : (slot + 1) * slot_rows, :])
    context_arrives, context_sent = to_tokens(message, context_in, r.msg_send, r.msg_recv)
    each(plans_in, Gather.side, 1)
    each(plans_in, Gather.side, 2)
    each(plans_out, GatherLate.late_line, 1)
    each(plans_in, Gather.side, 0)
    each(plans_down, Gather.side, 1)
    each(plans_down, Gather.side, 0)
    each(plans_out, GatherLate.late_line, 2)
    each(plans_down, Gather.side, 2)

    shares, bias_in = r.shares, r.bias_in
    shares[core] = jnp.zeros(shares.shape[1:], HIGH)
    share = jnp.logical_and(lanes(8) < depth, lax.broadcasted_iota(jnp.int32, (8, 128), 0) < 6)
    for slot in range(CHIPS):
        small = small_all[slot].astype(HIGH)[0:8]
        target = slice(slot * depth // 128 * 128, slot * depth // 128 * 128 + 128)
        piece = jnp.where(share, small, 0.0)
        if slot * depth % 128:
            piece = pltpu.roll(piece, slot * depth % 128, 1)
        shares[core, :, target] += piece
        bias_in[:, slot * 128 : slot * 128 + 128] = small[6:7]
    pair_small = remote(
        shares.at[core], shares.at[core], r.pair_send.at[5], r.pair_recv.at[5], (other, chip)
    )
    pair_small.start()
    context_arrives()

    context_wide, context, low_first = r.context_wide, r.context, r.low_first
    act, slope = r.act, r.slope
    out_part, in_part = r.out_part, r.in_part
    own = pl.ds(pl.multiple_of(core * slot_rows, 16), slot_rows)
    far = pl.ds(pl.multiple_of(other * slot_rows, 16), slot_rows)
    tile = 512
    half_slot = slot_rows // 2
    count = [6]

    def swap(source, target):
        copy = remote(
            source, target, r.pair_send.at[count[0]], r.pair_recv.at[count[0]], (other, chip)
        )
        count[0] += 1
        copy.start()
        return copy

    left_half = lanes(half_slot) < HD
    for slot_group in range(2):
        for pair in range(HALF // 2):
            even = context_in[slot_group * HALF + 2 * pair].astype(HIGH)[:half_slot]
            odd = context_in[slot_group * HALF + 2 * pair + 1].astype(HIGH)[:half_slot]
            top = slot_group * slot_rows
            columns = slice(pair * 128, pair * 128 + 128)
            context_wide[top : top + half_slot, columns] = jnp.where(left_half, even, turn(odd))
            context_wide[top + half_slot : top + slot_rows, columns] = jnp.where(
                left_half, turn(even), odd
            )
    context[...] = context_wide[...].astype(LOW)

    def product(lhs, rhs):
        out_part[...] = dot(lhs[far, :], rhs).astype(LOW)
        copy = swap(out_part, in_part)
        mine = dot(lhs[own, :], rhs)
        copy.wait()
        return mine + in_part[...].astype(HIGH)

    pair_small.wait()
    branch_bias, gains, shifts = (
        [jnp.concatenate([shares[g, row : row + 1] for g in range(2)], axis=1) for row in (first_row, first_row + 1)]
        for first_row in (0, 2, 4)
    )
    branch = product(context, w_out[...].reshape(half_width, width)) + branch_bias[0]
    row_index = lax.broadcasted_iota(jnp.int32, (slot_rows, 1), 0)
    x_mine = jnp.where(row_index < token_rows, x_own[...].astype(HIGH), 0.0)
    first, normed1, inverse1 = normalize(x_mine + branch, gains[0], shifts[0])
    low_first[own, :] = first.astype(LOW)
    copy = swap(low_first.at[own], low_first.at[own])
    each(plans_in, Gather.arrive)
    copy.wait()

    def widen(index, carry):
        columns = pl.ds(pl.multiple_of(index * tile, tile), tile)
        pre = dot(low_first[...], w_in[:, :, :, columns].reshape(width, tile)) + bias_in[:, columns]
        found, derivative = gelu_parts(pre)
        act[:, columns] = found.astype(LOW)
        slope[:, columns] = derivative
        return carry

    lax.fori_loop(0, half_hidden // tile, widen, 0)
    each(plans_down, Gather.arrive)
    second = product(act, w_down[...].reshape(half_hidden, width)) + branch_bias[1]
    result, normed2, inverse2 = normalize(first + second, gains[1], shifts[1])
    r.hidden_out[...] = result[:token_rows].astype(LOW)
    upstream = jnp.concatenate(
        [r.out_grad[...].astype(HIGH), jnp.zeros((slot_rows - token_rows, width), HIGH)], axis=0
    )
    d_sum2 = normalize_back(upstream, normed2, inverse2, gains[1])
    low_second = d_sum2.astype(LOW)
    d_second, small_sum = r.d_second, r.small_sum
    d_second[own, :] = low_second
    copy = swap(d_second.at[own], d_second.at[own])
    small_sum[...] = jnp.zeros_like(small_sum)
    small_sum[1:2, :] = column_sums(low_second.astype(HIGH))
    small_sum[3:4, :] = column_sums(upstream * normed2)
    small_sum[5:6, :] = column_sums(upstream)

    half_total = HALF * slot_rows
    def half_sums(pick, stages, sends, recvs):
        return [
            Reduce(
                functools.partial(pick, part=part),
                [stage.at[part] for stage in stages],
                sends.at[part],
                recvs.at[part],
                across,
            )
            for part, across in enumerate("xy")
        ]

    sums_down = half_sums(down_half, (r.down_1, r.down_2, r.down_3), r.g_down_send, r.g_down_recv)
    sums_in = half_sums(in_half, (r.in_1, r.in_2, r.in_3), r.g_in_send, r.g_in_recv)
    sum_out = ReduceEarly(
        lambda slot: r.g_out.at[slot],
        [r.out_1, r.out_2, r.out_3],
        r.g_out_send,
        r.g_out_recv,
        "y",
    )

    d_inner = act
    each(plans_in + plans_down, Gather.finish)
    copy.wait()
    slots = tile // w_down.shape[1]

    turns = width // tile
    z, y, x = coordinates(chip)
    assert slots == 4
    for line in (1, None, 2, 0):
        plane = sums_down[0].plane(line)
        columns = pl.ds(pl.multiple_of(plane * tile, tile), tile)
        rows = pl.ds(plane * slots, slots)
        low = (dot(d_second[...], w_down[rows].reshape(tile, width), NT) * slope[:, columns]).astype(LOW)
        bias_sums = column_sums(low.astype(HIGH))
        bias_columns = pl.ds(pl.multiple_of(lax.rem(plane, turns) * tile, tile), tile)
        for row in range(half_hidden // width):

            @pl.when(lax.div(plane, turns) == row)
            def _():
                small_sum[6 + row : 7 + row, bias_columns] = bias_sums

        w_down[rows] = (
            dot(act[:, columns], d_second[...], TN).astype(LOW).reshape(slots, tile // slots, width)
        )
        d_inner[:, columns] = low
        if line == 1:
            each(sums_down, Reduce.start, 1)
    each(sums_down, Reduce.start, None)
    w_in_all = w_in[...].reshape(width, half_hidden)
    out_part[...] = dot(d_inner[far, :], w_in_all, NT).astype(LOW)
    copy = swap(out_part, in_part)
    mine = dot(d_inner[own, :], w_in_all, NT)
    slots_in = 256 // depth

    def widen_grad(index, carry):
        rows = pl.ds(pl.multiple_of(index * 256, 256), 256)
        parts = CHIPS // slots_in
        w_in[lax.div(index, parts), pl.ds(lax.rem(index, parts) * slots_in, slots_in)] = (
            dot(low_first[:, rows], d_inner[...], TN).astype(LOW).reshape(slots_in, depth, half_hidden)
        )
        return carry

    lax.fori_loop(0, width // 256, widen_grad, 0)
    copy.wait()
    d_first = d_sum2 + mine + in_part[...].astype(HIGH)
    d_sum1 = normalize_back(d_first, normed1, inverse1, gains[0])
    low_branch = d_sum1.astype(LOW)
    d_branch = d_second
    d_branch[own, :] = low_branch
    copy = swap(d_branch.at[own], d_branch.at[own])
    r.d_sum1[...] = d_sum1
    small_sum[0:1, :] = column_sums(low_branch.astype(HIGH))
    small_sum[2:3, :] = column_sums(d_first * normed1)
    small_sum[4:5, :] = column_sums(d_first)
    copy.wait()
    context_wide[...] = dot(d_branch[...], w_out[...].reshape(half_width, width), NT)
    d_message, d_arrived = context_in, r.d_arrived
    for slot_group in range(2):
        for pair in range(HALF // 2):
            both = context_wide[
                slot_group * slot_rows : (slot_group + 1) * slot_rows, pair * 128 : pair * 128 + 128
            ]
            d_message[slot_group * HALF + 2 * pair] = fold(both)
            d_message[slot_group * HALF + 2 * pair + 1] = fold(turn(both))
    grad_arrives, grad_sent = to_heads(d_message, d_arrived, r.d_send, r.d_recv)
    r.g_out[...] = dot(context[...], d_branch[...], TN).astype(LOW).reshape(r.g_out.shape)

    small_in = r.small_in

    def small_copy(index, to_core, to_chip):
        return remote(
            small_sum, small_in.at[index], r.small_send.at[index], r.small_recv.at[index], (to_core, to_chip)
        )

    def small_turn(index):
        if index == 0:
            return [small_copy(0, other, chip)]
        if index == 1:
            return [small_copy(1, core, z * 4 + (1 - y) * 2 + x)]
        if index == 2:
            return [small_copy(2, core, z * 4 + y * 2 + 1 - x)]
        return [
            small_copy(2 + ahead, core, lax.rem(z + ahead, 4) * 4 + y * 2 + x) for ahead in (1, 2, 3)
        ]

    def small_start(index):
        for copy in small_turn(index):
            copy.start()

    def small_end(index):
        for copy in small_turn(index):
            copy.wait()
        if index == 0:
            small_sum[0:6, :] += small_in[0, 0:6, :]
        elif index < 3:
            small_sum[...] += small_in[index]

    each(sums_down, Reduce.side, 1)
    small_start(0)
    small_end(0)
    each(sums_down, Reduce.start, 2)
    sum_out.start()
    each(sums_in, Reduce.start, 2)
    small_start(1)
    each(sums_down, Reduce.side, 2)
    each(sums_in, Reduce.side, 2)
    each(sums_down, Reduce.start, 0)
    d_context = meta
    grad_arrives()
    for slot in range(CHIPS):
        both = d_arrived[slot].astype(HIGH)[:half_slot]
        top = slot * slot_rows
        d_context[top : top + half_slot, :] = jnp.where(left_half, both, 0.0)
        d_context[top + half_slot : top + slot_rows, :] = jnp.where(left_half, turn(both), 0.0)
    d_heads, d_pair_t, rel_grad = r.d_heads, r.d_pair_t, r.rel_grad
    d_pair_t[...] = jnp.zeros_like(d_pair_t)
    rel_grad[...] = jnp.zeros_like(rel_grad)

    def step(index, carry):
        rows = pl.ds(pl.multiple_of(index * BLOCK, BLOCK), BLOCK)
        at_steps(
            index,
            {
                1: [
                    lambda: small_end(1),
                    lambda: each(sums_in, Reduce.start, 1),
                    lambda: each(sums_down, Reduce.side, None),
                    lambda: each(sums_down, Reduce.side, 0),
                    lambda: each(sums_down, Reduce.line, 2),
                    lambda: small_start(2),
                ],
                2: [lambda: each(sums_in, Reduce.line, 2)],
                4: [
                    lambda: each(sums_in, Reduce.start, None),
                    sum_out.third,
                    lambda: each(sums_down, Reduce.line, 1),
                ],
                5: [
                    lambda: small_end(2),
                    lambda: each(sums_in, Reduce.side, 1),
                    lambda: each(sums_down, Reduce.line, 0),
                ],
                8: [
                    lambda: each(sums_in, Reduce.start, 0),
                    lambda: small_start(3),
                    lambda: each(sums_in, Reduce.line, 1),
                ],
            },
        )
        facts = kept[rows, :]
        grad = d_context[rows, :]
        delta = jnp.sum(grad * facts, axis=1, keepdims=True)
        probs = jnp.exp(dot(left[rows, :], right_t[...]) - facts[:, HD : HD + 1])
        d_probs = dot(grad.astype(LOW), value_t[...])
        d_logits = (probs * (d_probs - delta)).astype(LOW)
        query_t = jnp.where(first_half, left[rows, 256:384].astype(HIGH), 0.0).T[0:HD]
        d_pair_t[0:HD, :] += dot(query_t.astype(LOW), d_logits)
        d_pair_t[HD : 2 * HD, :] += dot(grad.T[0:HD].astype(LOW), probs.astype(LOW))
        back = dot(d_logits, right[...]) * scale
        ids = facts.astype(jnp.int32)
        order, box_x, box_y = (ids[:, HD + k : HD + k + 1] for k in (1, 2, 3))

        def placed(column, ids_of, extent, start):
            found_at = ids_of + NB // 2 - lane
            found = jnp.take_along_axis(
                back[:, column * 128 : column * 128 + 128], jnp.clip(found_at, 0, extent - 1) + start, axis=1
            )
            return jnp.where(jnp.logical_and(found_at >= 0, found_at < extent), found, 0.0)

        wide = back[:, 0:128]
        low_end = jnp.sum(jnp.where(lane >= order + NB // 2, wide, 0.0), axis=1, keepdims=True)
        high_end = jnp.sum(jnp.where(lane <= order - (NB // 2 - 1), wide, 0.0), axis=1, keepdims=True)
        first = placed(0, order, ORDER_RANGE, 0)
        first = jnp.where(lane == 0, low_end, jnp.where(lane == NB - 1, high_end, first))
        d_tables = jnp.concatenate(
            [first, placed(1, box_x, BOX_RANGE, 0), placed(1, box_y, BOX_RANGE, BOX_RANGE)], axis=1
        ).astype(LOW)
        from_tables = dot(d_tables, table_t, NT)
        d_query = back[:, 256:384] + jnp.concatenate([from_tables, from_tables], axis=1)
        d_heads[0, :, rows] = d_query.T[0:HD].astype(LOW)
        rel_grad[:, 0 : 3 * NB] += dot((query_t / scale).astype(LOW), d_tables)
        return carry

    lax.fori_loop(0, total // BLOCK, step, 0)

    d_heads[1] = d_pair_t[0:HD, :].astype(LOW)
    d_heads[2] = d_pair_t[HD : 2 * HD, :].astype(LOW)
    d_both = r.d_both
    near_part = pl.ds(pl.multiple_of(core * half_total, 128), half_total)
    far_part = pl.ds(pl.multiple_of(other * half_total, 128), half_total)
    copy = swap(d_heads.at[:, :, far_part], d_both.at[:, core])
    d_both[:, core] = d_heads[:, :, near_part]
    sums = [jnp.sum(d_heads[n].astype(HIGH), axis=1, keepdims=True) for n in (0, 2)]
    rel_grad[:, 3 * NB : 4 * NB] = jnp.where(
        lanes(HD) == 0, sums[0], jnp.where(lanes(HD) == 1, sums[1], 0.0)
    )
    rel_low = r.rel_low
    rel_low[...] = rel_grad[...].astype(LOW)
    head = 2 * position + core
    rel_came = r.rel_came

    def d_rel_each(act_remote, act_own):
        for side in range(2):
            to = (lax.div(position, 4), lax.rem(2 * head + side, CHIPS))
            itself = jnp.logical_and(to[0] == core, to[1] == chip)
            source = rel_low.at[pl.ds(side * depth, depth)]
            act = lambda: act_remote(
                remote(source, rel_came.at[group], r.d_rel_send.at[side], r.d_rel_recv.at[group], to)
            )
            pl.when(jnp.logical_not(itself))(act)
            if act_own:
                pl.when(itself)(lambda: local(source, rel_came.at[group], r.d_rel_recv.at[group]).start())

    d_rel_each(lambda copy: copy.start(), True)
    copy.wait()
    d_columns = d_both[...].reshape(6 * HD, half_total)

    w_grad = dot(d_columns, x_all[...].reshape(half_total, width))

    w_heads = jnp.concatenate([w_all[n].reshape(width, 128) for n in range(3)], axis=1)
    d_rows = d_columns.T
    d_x = x_all
    each(x_plans, CubeGather.finish)
    for pair in range(HALF // 2):
        d_x[2 * pair : 2 * pair + 2] = (
            dot(d_rows[pair * pair_rows : (pair + 1) * pair_rows], w_heads, NT)
            .astype(LOW)
            .reshape(2, slot_rows, width)
        )
    d_x_plans = [
        CubeReduce(
            lambda slot, part=part: d_x.at[slot, pl.ds(part * third, third)],
            r.x_stage.at[part],
            r.d_x_send.at[part],
            r.d_x_recv.at[part],
            order,
        )
        for part, order in enumerate(("xyz", "yzx", "zxy"))
    ]
    each(d_x_plans, CubeReduce.own)

    w_mine, w_far, w_low, w_came = slope, r.w_far, r.w_low, r.w_came
    w_rows = 3 * HD
    for part in range(2):
        w_mine[0:w_rows, part * width : (part + 1) * width] = w_grad[part * w_rows : (part + 1) * w_rows]

    def w_columns(part, half):
        return pl.ds(pl.multiple_of(part * width + half * half_width, 128), half_width)

    w_swaps = [
        swap(w_mine.at[pl.ds(0, w_rows), w_columns(part, other)], w_far.at[part]) for part in range(2)
    ]
    sum_out.across()
    each(d_x_plans, CubeReduce.one)
    for copy in w_swaps:
        copy.wait()
    w_sum = jnp.concatenate(
        [(w_mine[0:w_rows, w_columns(part, core)] + w_far[part]).T for part in range(2)], axis=1
    )
    for slot in range(CHIPS):
        w_low[slot] = w_sum[slot * depth : (slot + 1) * depth].astype(LOW)

    def d_w_copy(ahead):
        to = lax.rem(chip + ahead, CHIPS)
        return remote(w_low.at[to], w_came.at[chip], r.d_w_send.at[0], r.d_w_recv.at[0], (core, to))

    own_d_w = local(w_low.at[chip], w_came.at[chip], keep.at[6])
    own_d_w.start()
    for ahead in range(1, CHIPS):
        d_w_copy(ahead).start()
    sum_out.finish(r.out_w_grad)
    each(sums_in, Reduce.side, 0)
    for part, plan in enumerate(sums_down):
        plan.finish(r.down_grad.at[pl.ds(part * half_down, half_down)])
    each(d_x_plans, CubeReduce.two)
    each(sums_in, Reduce.line, 0)
    each(sums_in, Reduce.side, None)
    small_end(3)
    x_total, x_came = x_own, r.x_came
    back_part = lambda part: pl.ds(part * third, third)
    back = lambda part: local(
        x_total.at[back_part(part)], x_came.at[back_part(part)], r.back_recv.at[part]
    )
    back_abroad = lambda part: remote(
        x_total.at[back_part(part)],
        x_came.at[back_part(part)],
        r.back_send.at[part],
        r.back_recv.at[part],
        (other, away),
    )
    for part, plan in enumerate(d_x_plans):
        x_total[part * third : (part + 1) * third] = plan.arrive().astype(LOW)
        pl.when(at_home)(lambda: back(part).start())
        pl.when(jnp.logical_not(at_home))(lambda: back_abroad(part).start())
    in_total, in_far = r.in_total, r.in_far
    for part, plan in enumerate(sums_in):
        plan.finish(in_total.at[part])
    in_pair = swap(in_total.at[other], in_far)

    in_grad = r.in_grad
    in_grad[:, columns_of(core, half_hidden)] = in_total[core]
    me = core * CHIPS + chip
    small_total = lambda rows, columns: (
        small_sum[rows, columns] + small_in[3, rows, columns] + small_in[4, rows, columns] + small_in[5, rows, columns]
    )
    strip = columns_of(lax.div(me * depth, 128), 128)
    shares = pltpu.roll(small_total(pl.ds(0, 8), strip), 128 - lax.rem(me * depth, 128), 1)
    for number, result in enumerate((r.branch_grad, r.gain_grad, r.shift_grad)):
        result[...] = shares[2 * number : 2 * number + 2, 0:depth]
    bias_strip = small_total(pl.ds(0, 8), columns_of(position, 128))
    r.bias_grad[...] = jnp.where(group == 0, bias_strip[6:7], bias_strip[7:8])
    for slot in range(2):
        local(rel_low.at[pl.ds(0, depth)], rel_came.at[slot], r.d_rel_recv.at[slot]).wait()
    d_rel_each(lambda copy: copy.wait_send(), False)
    rel_total = rel_came[0].astype(HIGH) + rel_came[1].astype(HIGH)
    for kind in range(3):
        r.rel_tables_grad[kind] = rel_total[:, kind * NB : (kind + 1) * NB]
    r.qkv_bias_grad[...] = rel_total[:, 3 * NB : 4 * NB].T[0:2]
    own_d_w.wait()
    w_came_most = w_came.at[pl.ds(0, CHIPS - 1)]
    local(w_came_most, w_came_most, r.d_w_recv.at[0]).wait()
    local(w_came_most, w_came_most, r.d_w_send.at[0]).wait()
    for pair in range(HALF):
        both = w_came[pair].astype(HIGH) + w_came[HALF + pair].astype(HIGH)
        for n in range(3):
            r.qkv_grad[n, :, pair * 128 : pair * 128 + 128] = both[:, n * 128 : n * 128 + 128]
    for part in range(3):
        back(part).wait()
        pl.when(jnp.logical_not(at_home))(lambda: back_abroad(part).wait_send())
    r.hidden_grad[...] = (r.d_sum1[...] + x_came[...].astype(HIGH))[:token_rows].astype(LOW)
    in_pair.wait()
    in_grad[:, columns_of(other, half_hidden)] = in_far[...]
    grad_sent()
    each(d_x_plans, CubeReduce.finish)
    local(w_most, w_most, r.w_send.at[0]).wait()
    rel_each(lambda copy: copy.wait_send(), None)
    context_sent()
    each(plans_out, GatherLate.finish)


def hand_over(count, *refs):
    sources, targets, held, sem = refs[:count], refs[count : 2 * count], refs[2 * count : 3 * count], refs[3 * count]
    loads = [local(source, here, sem.at[0, k]) for k, (source, here) in enumerate(zip(sources, held))]
    stores = [local(here, target, sem.at[1, k]) for k, (here, target) in enumerate(zip(held, targets))]
    for copy in loads:
        copy.start()
    for load, store in zip(loads, stores):
        load.wait()
        store.start()
    for copy in stores:
        copy.wait()


def handed_over(arrays):
    count = len(arrays)
    return pl.pallas_call(
        functools.partial(hand_over, count),
        out_shape=[jax.ShapeDtypeStruct(array.shape, array.dtype) for array in arrays],
        in_specs=[pl.BlockSpec(memory_space=pl.ANY)] * count,
        out_specs=[pl.BlockSpec(memory_space=pl.ANY)] * count,
        scratch_shapes=[pltpu.VMEM(array.shape, array.dtype) for array in arrays]
        + [pltpu.SemaphoreType.DMA((2, count))],
        name="hand_over",
    )(*arrays)


def call(kernel, name, number, inputs, outputs, scratch):
    names = list(inputs) + list(outputs) + list(scratch)
    results = pl.pallas_call(
        functools.partial(kernel, names),
        out_shape=[jax.ShapeDtypeStruct(shape, dtype) for shape, dtype, _ in outputs.values()],
        in_specs=[pl.BlockSpec(memory_space=space) for _, space in inputs.values()],
        out_specs=[pl.BlockSpec(memory_space=space) for _, _, space in outputs.values()],
        scratch_shapes=list(scratch.values()),
        compiler_params=pltpu.CompilerParams(
            collective_id=number, has_side_effects=True, vmem_limit_bytes=VMEM_LIMIT
        ),
        name=name,
    )(*(array for array, _ in inputs.values()))
    return types.SimpleNamespace(**dict(zip(outputs, results)))


def head_shards(
    hidden_in,
    segment_ids,
    order_ids,
    box_ids,
    qkv_weight,
    qkv_bias,
    rel_tables,
    out_weight,
    branch_bias,
    norm_gains,
    norm_shifts,
    ffn_in,
    ffn_in_bias,
    ffn_out,
    out_grad,
):
    rows, width = hidden_in.shape
    slot_rows = -(-rows // 48) * 48
    total = CHIPS * slot_rows
    depth = qkv_weight.shape[1]
    hidden = ffn_in.shape[1]
    half_hidden, half_width = hidden // 2, width // 2
    down_rows = ffn_out.shape[0]
    both = 2 * slot_rows
    fold_rows = -(-(slot_rows // 2) // 16) * 16
    any_, vmem, dma = pl.ANY, pltpu.VMEM, pltpu.SemaphoreType.DMA
    message = (CHIPS, fold_rows, 128)
    x_block, w_block = (HALF, slot_rows, width), (3, 2, CHIPS, depth, 128)
    in_all, down_all = (2, CHIPS, depth, half_hidden), (CHIPS, down_rows, width)
    out_all = (CHIPS, depth, width)
    in_half, down_half = (depth, half_hidden), (down_rows // 2, width)
    in_block, out_block = (2, depth, half_hidden), (depth, width)
    made = call(
        layer_kernel,
        "layer",
        0,
        dict(
            hidden_in=(hidden_in, vmem),
            segment_ids=(segment_ids.reshape(1, rows), vmem),
            order_ids=(order_ids.reshape(1, rows), vmem),
            box_ids=(box_ids, vmem),
            qkv_weight=(qkv_weight, vmem),
            qkv_bias=(qkv_bias, vmem),
            rel_tables=(rel_tables.transpose(0, 2, 1), vmem),
            out_weight=(out_weight, any_),
            branch_bias=(branch_bias, vmem),
            norm_gains=(norm_gains, vmem),
            norm_shifts=(norm_shifts, vmem),
            ffn_in=(ffn_in, any_),
            ffn_in_bias=(ffn_in_bias.reshape(1, down_rows), vmem),
            ffn_out=(ffn_out, any_),
            out_grad=(out_grad, vmem),
        ),
        dict(
            hidden_out=((rows, width), LOW, vmem),
            hidden_grad=((rows, width), LOW, vmem),
            qkv_grad=((3, depth, width), HIGH, vmem),
            qkv_bias_grad=((2, depth), HIGH, vmem),
            rel_tables_grad=((3, depth, NB), HIGH, vmem),
            out_w_grad=((depth, width), HIGH, vmem),
            branch_grad=((2, depth), HIGH, vmem),
            gain_grad=((2, depth), HIGH, vmem),
            shift_grad=((2, depth), HIGH, vmem),
            in_grad=((depth, hidden), HIGH, vmem),
            bias_grad=((1, down_rows), HIGH, vmem),
            down_grad=((down_rows, width), HIGH, vmem),
        ),
        dict(
            x_own=vmem((slot_rows, width), LOW),
            x_all=vmem(x_block, LOW),
            extra=vmem((slot_rows - rows, width), HIGH),
            small_wide=vmem((16, 128), HIGH),
            small_own=vmem((16, 128), LOW),
            small_all=vmem((CHIPS, 16, 128), LOW),
            w_all=vmem(w_block, LOW),
            rel_own=vmem((depth, 4 * NB), LOW),
            rel_all=vmem((2 * depth, 4 * NB), LOW),
            bias_far=vmem((2 * depth, NB), LOW),
            labels=vmem((CHIPS, 16, 256), LOW),
            near=vmem((total, 256), LOW),
            far_part=vmem((total // 2, 256), LOW),
            w_in=vmem(in_all, LOW),
            w_down=vmem(down_all, LOW),
            w_out=vmem(out_all, LOW),
            meta=vmem((total, 128), HIGH),
            shares=vmem((2, 8, half_width), HIGH),
            bias_in=vmem((1, half_hidden), HIGH),
            left=vmem((total, 384), LOW),
            right=vmem((total, 384), LOW),
            right_t=vmem((384, total), LOW),
            value=vmem((total, 128), LOW),
            value_t=vmem((128, total), LOW),
            kept=vmem((total, 128), HIGH),
            message=vmem(message, LOW),
            context_in=vmem(message, LOW),
            context_wide=vmem((both, half_width), HIGH),
            context=vmem((both, half_width), LOW),
            low_first=vmem((both, width), LOW),
            act=vmem((both, half_hidden), LOW),
            slope=vmem((both, half_hidden), HIGH),
            out_part=vmem((slot_rows, width), LOW),
            in_part=vmem((slot_rows, width), LOW),
            d_sum1=vmem((slot_rows, width), HIGH),
            d_second=vmem((both, width), LOW),
            g_out=vmem((CHIPS,) + out_block, LOW),
            in_1=vmem((2, 8) + in_half, LOW),
            in_2=vmem((2, 4) + in_half, LOW),
            in_3=vmem((2, 3) + in_half, LOW),
            down_1=vmem((2, 8) + down_half, LOW),
            down_2=vmem((2, 4) + down_half, LOW),
            down_3=vmem((2, 3) + down_half, LOW),
            out_1=vmem((3, 4) + out_block, LOW),
            out_2=vmem((2,) + out_block, LOW),
            out_3=vmem((1,) + out_block, LOW),
            in_total=vmem(in_block, HIGH),
            in_far=vmem((depth, half_hidden), HIGH),
            small_sum=vmem((8, width), HIGH),
            small_in=vmem((6, 8, width), HIGH),
            d_arrived=vmem(message, LOW),
            d_heads=vmem((3, HD, total), LOW),
            d_pair_t=vmem((2 * HD, total), HIGH),
            d_both=vmem((3, 2, HD, total // 2), LOW),
            x_stage=vmem((3, 7, slot_rows // 3, width), LOW),
            x_came=vmem((slot_rows, width), LOW),
            rel_grad=vmem((2 * depth, 4 * NB), HIGH),
            rel_low=vmem((2 * depth, 4 * NB), LOW),
            rel_came=vmem((2, depth, 4 * NB), LOW),
            w_far=vmem((2, 3 * HD, half_width), HIGH),
            w_low=vmem((CHIPS, depth, 6 * HD), LOW),
            w_came=vmem((CHIPS, depth, 6 * HD), LOW),
            keep_sem=dma((7,)),
            home_sem=dma((2,)),
            back_send=dma((3,)),
            back_recv=dma((3,)),
            x_send=dma((3, CubeGather.SENDS)),
            x_recv=dma((3, CubeGather.RECEIVES)),
            w_send=dma((1,)),
            w_recv=dma((1,)),
            rel_send=dma((2,)),
            rel_recv=dma((2,)),
            out_send=dma((2, GatherLate.SENDS)),
            out_recv=dma((2, GatherLate.RECEIVES)),
            in_send=dma((2, Gather.SENDS)),
            in_recv=dma((2, Gather.RECEIVES)),
            down_send=dma((2, Gather.SENDS)),
            down_recv=dma((2, Gather.RECEIVES)),
            msg_send=dma((1,)),
            msg_recv=dma((1,)),
            d_send=dma((1,)),
            d_recv=dma((1,)),
            g_in_send=dma((2, Reduce.SENDS)),
            g_in_recv=dma((2, Reduce.RECEIVES)),
            g_down_send=dma((2, Reduce.SENDS)),
            g_down_recv=dma((2, Reduce.RECEIVES)),
            g_out_send=dma((ReduceEarly.SENDS,)),
            g_out_recv=dma((ReduceEarly.RECEIVES,)),
            small_send=dma((6,)),
            small_recv=dma((6,)),
            d_x_send=dma((3, CubeReduce.SENDS)),
            d_x_recv=dma((3, CubeReduce.RECEIVES)),
            d_w_send=dma((1,)),
            d_w_recv=dma((1,)),
            d_rel_send=dma((2,)),
            d_rel_recv=dma((2,)),
            pair_send=dma((16,)),
            pair_recv=dma((16,)),
        ),
    )
    results = list(
        handed_over(
            [
                made.hidden_out,
                made.hidden_grad,
                made.qkv_grad,
                made.qkv_bias_grad,
                made.rel_tables_grad,
                made.out_w_grad,
                made.branch_grad,
                made.gain_grad,
                made.shift_grad,
                made.in_grad,
                made.bias_grad,
                made.down_grad,
            ]
        )
    )
    results[4] = results[4].transpose(0, 2, 1)
    results[10] = results[10].reshape(down_rows)
    return tuple(results)


def solution(mesh):
    by_heads = mesh.shape["grp"] == 2 and mesh.shape["blk"] == CHIPS == H
    return jax.shard_map(
        head_shards if by_heads else shards,
        mesh=mesh,
        in_specs=(
            P(("grp", "blk"), None),
            P(("grp", "blk")),
            P(("grp", "blk")),
            P(None, ("grp", "blk")),
            P(None, ("grp", "blk"), None),
            P(None, ("grp", "blk")),
            P(None, None, ("grp", "blk")),
            P(("grp", "blk"), None),
            P(None, ("grp", "blk")),
            P(None, ("grp", "blk")),
            P(None, ("grp", "blk")),
            P(("grp", "blk"), None),
            P(("grp", "blk")),
            P(("grp", "blk"), None),
            P(("grp", "blk"), None),
        ),
        out_specs=(
            P(("grp", "blk"), None),
            P(("grp", "blk"), None),
            P(None, ("grp", "blk"), None),
            P(None, ("grp", "blk")),
            P(None, None, ("grp", "blk")),
            P(("grp", "blk"), None),
            P(None, ("grp", "blk")),
            P(None, ("grp", "blk")),
            P(None, ("grp", "blk")),
            P(("grp", "blk"), None),
            P(("grp", "blk")),
            P(("grp", "blk"), None),
        ),
        check_vma=False,
    )
```
